32 devices in a mesh: dp: 8 (over y, x, core), expert: 4 (over z).
Axes of the slice: x: 2, y: 2, z: 4, core: 2. Of those that a mesh axis runs over, the one named last changes fastest.
Arguments:
- hidden_input: bfloat16 [40960, 768], P(('dp', 'expert')), may hold values from -6 to 6
- gate_carryover: float32 [40960, 8], P(('dp', 'expert')), may hold values from -2.5 to 2.5
- sequence_length: int32 [32, 5], P(('dp', 'expert')), may hold values from 1 to 1024, 1280 in all within a row
- token_stream_place: int32 [32, 1280], P(('dp', 'expert')), may hold values from 0 to 1279, each once within a row
- expert_choice_index: int32 [40960, 2], P(('dp', 'expert')), may hold values from 0 to 7, as said below
- sequence_adapter: int32 [32, 5], P(('dp', 'expert')), may hold values from 0 to 7
- attention_gain: bfloat16 [768], replicated, may hold values from 0.25 to 1.75
- query_key_weight: bfloat16 [768, 2304], P(('dp', 'expert')), may hold values from -0.21875 to 0.21875
- output_weight: bfloat16 [768, 768], P(('dp', 'expert')), may hold values from -0.625 to 0.625
- adapter_in_query: bfloat16 [768, 128], P(('dp', 'expert')), may hold values from -0.21875 to 0.21875
- adapter_out_query: bfloat16 [128, 2304], P(('dp', 'expert')), may hold values from -0.5 to 0.5
- adapter_in_output: bfloat16 [768, 128], P(('dp', 'expert')), may hold values from -0.21875 to 0.21875
- adapter_out_output: bfloat16 [128, 768], P(('dp', 'expert')), may hold values from -1.5 to 1.5
- feedfwd_gain: bfloat16 [768], replicated, may hold values from 0.25 to 1.75
- router_weight: bfloat16 [768, 8], replicated, may hold values from -0.15625 to 0.15625
- constant_gate: bfloat16 [768, 4], replicated, may hold values from -0.21875 to 0.21875
- constant_value: bfloat16 [2, 768], replicated, may hold values from -6 to 6
- gate_upward_weight: bfloat16 [4, 768, 4096], P('expert', 'dp'), may hold values from -0.21875 to 0.21875
- down_weight: bfloat16 [4, 2048, 768], P('expert', 'dp'), may hold values from -1.5 to 1.5
- adapter_in_gate: bfloat16 [4, 768, 128], P('expert', 'dp'), may hold values from -0.21875 to 0.21875
- adapter_out_gate: bfloat16 [4, 128, 4096], P('expert', 'dp'), may hold values from -0.5 to 0.5
- adapter_in_down: bfloat16 [4, 2048, 128], P('expert', 'dp'), may hold values from -0.125 to 0.125
- adapter_out_down: bfloat16 [4, 128, 768], P('expert', 'dp'), may hold values from -6 to 6
- output_gradient: bfloat16 [40960, 768], P(('dp', 'expert')), may hold values from -6 to 6
Outputs:
- out_hidden: bfloat16 [40960, 768], P(('dp', 'expert'))
- grad_hidden: float32 [40960, 768], P(('dp', 'expert'))
- grad_gate_res: float32 [40960, 8], P(('dp', 'expert'))
- grad_a_qkv: float32 [768, 128], P(('dp', 'expert'))
- grad_b_qkv: float32 [128, 2304], P(('dp', 'expert'))
- grad_a_out: float32 [768, 128], P(('dp', 'expert'))
- grad_b_out: float32 [128, 768], P(('dp', 'expert'))
- grad_a_gu: float32 [4, 768, 128], P('expert', 'dp')
- grad_b_gu: float32 [4, 128, 4096], P('expert', 'dp')
- grad_a_down: float32 [4, 2048, 128], P('expert', 'dp')
- grad_b_down: float32 [4, 128, 768], P('expert', 'dp')
The draws below stay inside these ranges and needn't reach their ends.
Inputs may be any that keep to these rules, and one draw needn't show every extreme that they name: `expert_choice_index`: each row names two different experts. Ids under 4 are feed-forward experts, 4 is the zero expert, 5 the copy expert, 6 and 7 the constant experts. Among the rows of one device no id under 4 appears more than 408 times; on every device of one index of dp some such id appears exactly 408 times.
All inputs are finite; a program needn't handle non-finite values.
Results may differ from the reference program's by a relative error of at most 0.019.
Values may be sent and summed in bfloat16 or wider, within the bound.
A program may use at most 384 MiB of HBM per device.

```python
import math
import jax
import jax.numpy as jnp
import numpy as np
from jax import lax

MODEL_WIDTH = 768
HEAD_COUNT = 12
HEAD_DIM = 64
FEEDFWD_WIDTH = 2048
ADAPTER_RANK = 16
ADAPTERS = 8
LONGEST = 1024
TOK_DEV = 1280
ADAPTER_COLUMNS = 128
EXPERT_TOTAL = 4
CHOICE_KINDS = 8
CAPACITY = 408
SEQ_DEV = 5
TOKENS = 40960
DEVICES = 32


def draw_expert_choice_index(key, part):
    key = jax.random.fold_in(key, 7)
    kind_count = EXPERT_TOTAL + 4
    others = kind_count - 1
    slot_count = 2 * TOK_DEV
    base_count = (slot_count - CAPACITY) // others
    extra_count = slot_count - CAPACITY - base_count * others
    spread_top = max(1, min(base_count, CAPACITY - base_count - extra_count))
    group_count = DEVICES // EXPERT_TOTAL
    key_full, key_rest = jax.random.split(key)
    full_ids = jax.random.randint(key_full, (group_count,), 0, EXPERT_TOTAL)

    def one_device(device):
        dev_key = jax.random.fold_in(key_rest, device)
        key_order, key_shift, key_perm, key_swap = jax.random.split(dev_key, 4)
        full_id = full_ids[device // EXPERT_TOTAL]
        rest_ids = (full_id + 1 + jax.random.permutation(key_order, others)) % kind_count
        shifts = jax.random.randint(key_shift, (others // 2,), 0, spread_top)
        rest_counts = base_count + jnp.concatenate([shifts, -shifts, jnp.full((1,), extra_count, jnp.int32)])
        all_ids = jnp.concatenate([full_id[None], rest_ids])
        all_counts = jnp.concatenate([jnp.full((1,), CAPACITY, jnp.int32), rest_counts])
        count_ends = jnp.cumsum(all_counts)
        slot_index = jnp.arange(slot_count)
        slot_group = jnp.sum((slot_index[:, None] >= count_ends[None, :]).astype(jnp.int32), axis=1)
        slot_ids = jnp.sum(jnp.where(slot_group[:, None] == jnp.arange(kind_count)[None, :], all_ids[None, :], 0), axis=1)
        pair_ids = jnp.stack([slot_ids[:TOK_DEV], slot_ids[TOK_DEV:]], axis=1)
        pair_ids = pair_ids[jax.random.permutation(key_perm, TOK_DEV)]
        swap_bits = jax.random.randint(key_swap, (TOK_DEV, 1), 0, 2)
        return jnp.where(swap_bits == 1, pair_ids[:, ::-1], pair_ids).astype(jnp.int32)
    return jax.vmap(one_device)(jnp.arange(DEVICES)).reshape(TOKENS, 2)


def plant(values, key, low, largest):
    longest = values.shape.index(max(values.shape))
    spots = []
    for shift in (0, 1):
        where = [jax.random.randint(jax.random.fold_in(key, axis), (), 0, length) for axis, length in enumerate(values.shape)]
        where[longest] = (where[longest] + shift) % values.shape[longest]
        spots.append(tuple(where))
    return values.at[spots[0]].set(low).at[spots[1]].set(largest)


def level_of(own_key, dims, cuts, least, high):
    level = 1.0
    for position, parts in cuts:
        draws = jax.random.uniform(jax.random.fold_in(jax.random.fold_in(own_key, 6), position), (parts,), jnp.float32, least / len(cuts), high / len(cuts))
        level = level * jnp.repeat(jnp.exp(draws), dims[position] // parts).reshape((-1,) + (1,) * (len(dims) - 1 - position))
    return level


def profile(amount, total, reach, lean):
    loads = [(1 << 20) // math.isqrt(rank ** lean) + 1 for rank in range(2, amount + 1)]
    rest, holding = total - reach - (amount - 1), [1] * (amount - 1)
    while rest > 0:
        movable = [i for i in range(amount - 1) if holding[i] < reach]
        pool, left = sum([loads[i] for i in movable]), rest
        for i in movable:
            more = min(reach - holding[i], max(1, left * loads[i] // pool), rest)
            holding[i] = holding[i] + more
            rest = rest - more
    return np.array([reach] + holding)


def ragged(key, amount, total, reach, slope):
    if amount == 2:
        one = jax.random.randint(key, (), max(1, total - reach), min(reach, total - 1) + 1)
        return jnp.stack([one, total - one])
    tallies = jnp.asarray(profile(amount, total, reach, slope), jnp.int32)
    couples = (amount - 1) // 2
    donor, taker = tallies[1:1 + 2 * couples:2], tallies[2:2 + 2 * couples:2]
    slack = jnp.minimum(donor - 1, reach - taker)
    moved = jax.random.randint(jax.random.fold_in(key, 1), (couples,), 0, 1 << 20) % (slack + 1)
    tallies = tallies.at[1:1 + 2 * couples:2].set(donor - moved).at[2:2 + 2 * couples:2].set(taker + moved)
    return tallies[jax.random.permutation(jax.random.fold_in(key, 2), amount)]


def normal_values(rng, extent, width, limit, shards=(), held_as=jnp.bfloat16):
    array = width * jax.random.normal(rng, extent, jnp.float32)
    if shards:
        array = array * level_of(rng, extent, shards, -0.22, 0.18)
    return jnp.clip(array, -limit, limit).astype(held_as)


def setup_inputs(seed: int = 0) -> dict:
    streams_of = jax.random.split(jax.random.key(seed), 25)
    return {
        "hidden_input": normal_values(streams_of[0], (TOKENS, MODEL_WIDTH), 1.0, 6.0, ((0, 32),)),
        "gate_carryover": normal_values(streams_of[1], (TOKENS, CHOICE_KINDS), 0.3, 2.5, ((0, 32),), jnp.float32),
        "sequence_length": jax.vmap(lambda own: ragged(own, SEQ_DEV, TOK_DEV, LONGEST, 2))(jax.random.split(streams_of[2], DEVICES)).reshape((DEVICES, SEQ_DEV)).astype(jnp.int32),
        "token_stream_place": jax.vmap(lambda own: jax.random.permutation(own, TOK_DEV))(jax.random.split(streams_of[3], DEVICES)).reshape((DEVICES, TOK_DEV)).astype(jnp.int32),
        "expert_choice_index": draw_expert_choice_index(jax.random.fold_in(streams_of[24], 71), 0),
        "sequence_adapter": plant(jax.random.randint(streams_of[5], (DEVICES, SEQ_DEV), 0, ADAPTERS), jax.random.fold_in(streams_of[5], 1), 0, ADAPTERS - 1).astype(jnp.int32),
        "attention_gain": jnp.clip(1.0 + 0.15 * jax.random.normal(streams_of[6], (MODEL_WIDTH,), jnp.float32), 0.25, 1.75).astype(jnp.bfloat16),
        "query_key_weight": normal_values(streams_of[7], (MODEL_WIDTH, 3 * MODEL_WIDTH), MODEL_WIDTH ** -0.5, 0.21875, ((0, 32),)),
        "output_weight": normal_values(streams_of[8], (MODEL_WIDTH, MODEL_WIDTH), (MODEL_WIDTH // 8) ** -0.5, 0.625, ((0, 32),)),
        "adapter_in_query": normal_values(streams_of[9], (MODEL_WIDTH, ADAPTER_COLUMNS), MODEL_WIDTH ** -0.5, 0.21875, ((0, 32),)),
        "adapter_out_query": normal_values(streams_of[10], (ADAPTER_COLUMNS, 3 * MODEL_WIDTH), ADAPTER_COLUMNS ** -0.5, 0.5, ((0, 32),)),
        "adapter_in_output": normal_values(streams_of[11], (MODEL_WIDTH, ADAPTER_COLUMNS), MODEL_WIDTH ** -0.5, 0.21875, ((0, 32),)),
        "adapter_out_output": normal_values(streams_of[12], (ADAPTER_COLUMNS, MODEL_WIDTH), (ADAPTER_COLUMNS // 8) ** -0.5, 1.5, ((0, 32),)),
        "feedfwd_gain": jnp.clip(1.0 + 0.15 * jax.random.normal(streams_of[13], (MODEL_WIDTH,), jnp.float32), 0.25, 1.75).astype(jnp.bfloat16),
        "router_weight": normal_values(streams_of[14], (MODEL_WIDTH, CHOICE_KINDS), (2 * MODEL_WIDTH) ** -0.5, 0.15625),
        "constant_gate": normal_values(streams_of[15], (MODEL_WIDTH, 4), MODEL_WIDTH ** -0.5, 0.21875),
        "constant_value": normal_values(streams_of[16], (2, MODEL_WIDTH), 1.0, 6.0),
        "gate_upward_weight": normal_values(streams_of[17], (EXPERT_TOTAL, MODEL_WIDTH, 2 * FEEDFWD_WIDTH), MODEL_WIDTH ** -0.5, 0.21875, ((0, 4), (1, 8))),
        "down_weight": normal_values(streams_of[18], (EXPERT_TOTAL, FEEDFWD_WIDTH, MODEL_WIDTH), (FEEDFWD_WIDTH // 128) ** -0.5, 1.5, ((0, 4), (1, 8))),
        "adapter_in_gate": normal_values(streams_of[19], (EXPERT_TOTAL, MODEL_WIDTH, ADAPTER_COLUMNS), MODEL_WIDTH ** -0.5, 0.21875, ((0, 4), (1, 8))),
        "adapter_out_gate": normal_values(streams_of[20], (EXPERT_TOTAL, ADAPTER_COLUMNS, 2 * FEEDFWD_WIDTH), ADAPTER_COLUMNS ** -0.5, 0.5, ((0, 4), (1, 8))),
        "adapter_in_down": normal_values(streams_of[21], (EXPERT_TOTAL, FEEDFWD_WIDTH, ADAPTER_COLUMNS), FEEDFWD_WIDTH ** -0.5, 0.125, ((0, 4), (1, 8))),
        "adapter_out_down": normal_values(streams_of[22], (EXPERT_TOTAL, ADAPTER_COLUMNS, MODEL_WIDTH), (max(1, ADAPTER_COLUMNS // 128)) ** -0.5, 6.0, ((0, 4), (1, 8))),
        "output_gradient": normal_values(streams_of[23], (TOKENS, MODEL_WIDTH), 1.0, 6.0, ((0, 32),)),
    }


@jax.custom_vjp
def low(v):
    return lax.optimization_barrier(v.astype(jnp.bfloat16)).astype(jnp.float32)

@jax.custom_vjp
def low_back(v):
    return v

def low_keep(v):
    return (low(v), None)

def low_pass(kept, grad):
    return (grad,)

def back_keep(v):
    return (v, None)

def back_low(kept, grad):
    return (low(grad),)
low.defvjp(low_keep, low_pass)
low_back.defvjp(back_keep, back_low)

def matmul_hi(left_arr, right_arr):
    return jnp.dot(left_arr, right_arr, precision=lax.Precision.HIGHEST)

def einsum_hi(form, left_arr, right_arr):
    return jnp.einsum(form, left_arr, right_arr, precision=lax.Precision.HIGHEST)

def norm_rows(values, gain_vec):
    return values * lax.rsqrt(lax.optimization_barrier(jnp.mean(values * values, axis=-1, keepdims=True)) + 1e-06) * gain_vec

def token_layout(order_row, lengths_row, adapter_row):
    row_count = order_row.shape[0]
    seq_count = lengths_row.shape[0]
    seq_ends = jnp.cumsum(lengths_row).astype(jnp.int32)
    seq_starts = (seq_ends - lengths_row).astype(jnp.int32)
    stream = jnp.arange(row_count, dtype=jnp.int32)
    seg_stream = lax.optimization_barrier(jnp.sum((stream[:, None] >= seq_ends[None, :]).astype(jnp.int32), axis=1)).astype(jnp.int32)
    seg_hot = seg_stream[:, None] == jnp.arange(seq_count, dtype=jnp.int32)[None, :]
    pos_stream = (stream - lax.optimization_barrier(jnp.sum(jnp.where(seg_hot, seq_starts[None, :], 0), axis=1))).astype(jnp.int32)
    adapt_stream = lax.optimization_barrier(jnp.sum(jnp.where(seg_hot, adapter_row[None, :], 0), axis=1)).astype(jnp.int32)
    inverse = jnp.zeros((row_count,), jnp.int32).at[order_row].set(stream)
    return (seg_stream, inverse, pos_stream[order_row], adapt_stream[order_row])

def rope_tables(positions, half_dim):
    freq_vals = jnp.exp(jnp.arange(half_dim, dtype=jnp.float32) * (-math.log(10000.0) / half_dim))
    angles = positions.astype(jnp.float32)[:, None] * freq_vals[None, :]
    return (jnp.cos(angles)[:, None, :], jnp.sin(angles)[:, None, :])

def rotate(values, cosine, sine_vals):
    half_dim = values.shape[-1] // 2
    first_half = values[..., :half_dim]
    second = values[..., half_dim:]
    return jnp.concatenate([first_half * cosine - second * sine_vals, second * cosine + first_half * sine_vals], axis=-1)

def block_layer(adapter_list, frozen, pieces):
    qkv_down, qkv_up, out_down, out_up, gu_down, gu_up, dn_down, dn_up = adapter_list
    attention_gain, query_key_weight, output_weight, feedfwd_gain, router_weight, constant_gate, constant_value, gate_upward_weight, down_weight = frozen
    hidden, gate_carryover, lengths_row, order_row, choice_row, adapter_row = pieces
    row_count = hidden.shape[0]
    seg_stream, inverse, positions, token_adapter_index = token_layout(order_row, lengths_row, adapter_row)
    cosine, sine_vals = rope_tables(positions, HEAD_DIM // 2)
    adapter_col_mask = (jnp.arange(ADAPTER_COLUMNS)[None, :] // ADAPTER_RANK == token_adapter_index[:, None]).astype(jnp.float32)
    act_one = low(norm_rows(hidden, attention_gain))
    low_qkv = low(low_back(adapter_col_mask * matmul_hi(act_one, qkv_down)))
    qkv_vals = low_back(matmul_hi(act_one, query_key_weight) + matmul_hi(low_qkv, qkv_up))
    qkv_split = qkv_vals.reshape(row_count, 3, HEAD_COUNT, HEAD_DIM)
    query_vals = low(rotate(qkv_split[:, 0], cosine, sine_vals))[inverse]
    key_vals = low(rotate(qkv_split[:, 1], cosine, sine_vals))[inverse]
    value_vals = low(qkv_split[:, 2])[inverse]
    stream = jnp.arange(row_count)
    allowed = (seg_stream[:, None] == seg_stream[None, :]) & (stream[None, :] <= stream[:, None])
    scores = low_back(einsum_hi('qhd,khd->hqk', query_vals, key_vals) * (1.0 / math.sqrt(HEAD_DIM)))
    prob_vals = jax.nn.softmax(jnp.where(allowed[None], scores, -1000000000.0), axis=-1)
    attended = einsum_hi('hqk,khd->qhd', low(prob_vals), value_vals)
    attn_low = low(low_back(attended[order_row].reshape(row_count, MODEL_WIDTH)))
    low_out = low(low_back(adapter_col_mask * matmul_hi(attn_low, out_down)))
    residual = hidden + low_back(matmul_hi(attn_low, output_weight) + matmul_hi(low_out, out_up))
    act_two = low(norm_rows(residual, feedfwd_gain))
    gate_prob = jax.nn.softmax(matmul_hi(act_two, router_weight) + gate_carryover, axis=-1)
    choice_hot = (choice_row[:, :, None] == jnp.arange(CHOICE_KINDS)[None, None, :]).astype(jnp.float32)
    gate_vals = lax.optimization_barrier(jnp.sum(choice_hot * gate_prob[:, None, :], axis=-1))
    flat_ids = choice_row.reshape(-1)
    expert_hot = (flat_ids[:, None] == jnp.arange(EXPERT_TOTAL)[None, :]).astype(jnp.int32)
    slot_rank = lax.optimization_barrier(jnp.sum((jnp.cumsum(expert_hot, axis=0) - 1) * expert_hot, axis=1)).astype(jnp.int32)
    buffer_rows = EXPERT_TOTAL * CAPACITY
    slot_dest = jnp.where(flat_ids < EXPERT_TOTAL, flat_ids * CAPACITY + slot_rank, buffer_rows).astype(jnp.int32)
    choice_index = jnp.arange(2 * row_count, dtype=jnp.int32)
    slot_source = jnp.zeros((buffer_rows + 1,), jnp.int32).at[slot_dest].set(choice_index)[:buffer_rows]
    slot_used = jnp.zeros((buffer_rows + 1,), jnp.int32).at[slot_dest].set(1)[:buffer_rows]
    source_token = (slot_source // 2).astype(jnp.int32)
    row_values = low_back((act_two[source_token] * slot_used[:, None].astype(jnp.float32)).reshape(EXPERT_TOTAL, CAPACITY, MODEL_WIDTH))
    row_adapter = (token_adapter_index[source_token] * slot_used).reshape(EXPERT_TOTAL, CAPACITY)
    row_mask_full = (jnp.arange(ADAPTER_COLUMNS)[None, None, :] // ADAPTER_RANK == row_adapter[:, :, None]).astype(jnp.float32)
    lowrank_gate = low(low_back(row_mask_full * einsum_hi('ecd,edr->ecr', row_values, gu_down)))
    gate_upward = low_back(einsum_hi('ecd,edf->ecf', row_values, gate_upward_weight) + einsum_hi('ecr,erf->ecf', lowrank_gate, gu_up))
    middle_state = low(low_back(jax.nn.silu(gate_upward[..., :FEEDFWD_WIDTH]) * gate_upward[..., FEEDFWD_WIDTH:]))
    lowrank_down = low(low_back(row_mask_full * einsum_hi('ecf,efr->ecr', middle_state, dn_down)))
    result = low(low_back(einsum_hi('ecf,efd->ecd', middle_state, down_weight) + einsum_hi('ecr,erd->ecd', lowrank_down, dn_up)))
    result_flat = jnp.concatenate([result.reshape(buffer_rows, MODEL_WIDTH), jnp.zeros((1, MODEL_WIDTH), jnp.float32)], axis=0)
    ffn_vals = result_flat[slot_dest].reshape(row_count, 2, MODEL_WIDTH)
    const_logits = matmul_hi(act_two, constant_gate)
    alpha_zero = jax.nn.softmax(const_logits[:, 0:2], axis=-1)
    alpha_one = jax.nn.softmax(const_logits[:, 2:4], axis=-1)
    const_zero = alpha_zero[:, 0:1] * act_two + alpha_zero[:, 1:2] * constant_value[0][None, :]
    const_one = alpha_one[:, 0:1] * act_two + alpha_one[:, 1:2] * constant_value[1][None, :]
    is_copy = (choice_row == EXPERT_TOTAL + 1).astype(jnp.float32)[:, :, None]
    is_first = (choice_row == EXPERT_TOTAL + 2).astype(jnp.float32)[:, :, None]
    is_second = (choice_row == EXPERT_TOTAL + 3).astype(jnp.float32)[:, :, None]
    choice_out = ffn_vals + is_copy * act_two[:, None, :] + is_first * const_zero[:, None, :] + is_second * const_one[:, None, :]
    return residual + lax.optimization_barrier(jnp.sum(gate_vals[:, :, None] * choice_out, axis=1))

def reference(hidden_input, gate_carryover, sequence_length, token_stream_place, expert_choice_index, sequence_adapter, attention_gain, query_key_weight, output_weight, adapter_in_query, adapter_out_query, adapter_in_output, adapter_out_output, feedfwd_gain, router_weight, constant_gate, constant_value, gate_upward_weight, down_weight, adapter_in_gate, adapter_out_gate, adapter_in_down, adapter_out_down, output_gradient):
    frozen = tuple((stacked_rows.astype(jnp.float32) for stacked_rows in (attention_gain, query_key_weight, output_weight, feedfwd_gain, router_weight, constant_gate, constant_value, gate_upward_weight, down_weight)))
    adapter_list = tuple((stacked_rows.astype(jnp.float32) for stacked_rows in (adapter_in_query, adapter_out_query, adapter_in_output, adapter_out_output, adapter_in_gate, adapter_out_gate, adapter_in_down, adapter_out_down)))
    hidden_all = hidden_input.astype(jnp.float32).reshape(DEVICES, TOK_DEV, MODEL_WIDTH)
    gate_all = gate_carryover.astype(jnp.float32).reshape(DEVICES, TOK_DEV, CHOICE_KINDS)
    choice_all = expert_choice_index.reshape(DEVICES, TOK_DEV, 2)

    def whole_layer(hidden_blocks, gate_blocks, adapter_set):
        block_step = jax.checkpoint(lambda pieces: block_layer(adapter_set, frozen, pieces))

        def scan_step(carried, pieces):
            return (carried, block_step(pieces))
        final_carry, block_outs = lax.scan(scan_step, jnp.zeros((), jnp.float32), (hidden_blocks, gate_blocks, sequence_length, token_stream_place, choice_all, sequence_adapter))
        return block_outs
    output, pullback = jax.vjp(whole_layer, hidden_all, gate_all, adapter_list)
    grad_hidden, grad_gate, grad_adapt = pullback(output_gradient.astype(jnp.float32).reshape(DEVICES, TOK_DEV, MODEL_WIDTH))
    return (output.reshape(TOKENS, MODEL_WIDTH).astype(jnp.bfloat16), grad_hidden.reshape(TOKENS, MODEL_WIDTH), grad_gate.reshape(TOKENS, CHOICE_KINDS), grad_adapt[0], grad_adapt[1], grad_adapt[2], grad_adapt[3], grad_adapt[4], grad_adapt[5], grad_adapt[6], grad_adapt[7])
```

```python
import functools
import math

import jax
import jax.numpy as jnp
from jax import lax
from jax.experimental import pallas as pl
from jax.experimental.pallas import tpu as pltpu
from jax.sharding import PartitionSpec as P

MODEL_WIDTH = 768
HEAD_COUNT = 12
HEAD_DIM = 64
FEEDFWD_WIDTH = 2048
ADAPTER_RANK = 16
ROW_BLOCK = 256
HIDDEN_BLOCK = 512
LANES = 128
CONST_LANE = 64
CHOICE_LANE = 48
EPSILON = 1e-06
VMEM_BYTES = 60 * 2**20

F32 = jnp.float32
BF16 = jnp.bfloat16


def dot(a, b):
    return jnp.dot(a, b, preferred_element_type=F32)


def dot_nt(a, b):
    return lax.dot_general(a, b, (((1,), (1,)), ((), ())), preferred_element_type=F32)


def dot_tn(a, b):
    return lax.dot_general(a, b, (((0,), (0,)), ((), ())), preferred_element_type=F32)


def iota(shape, dim):
    return lax.broadcasted_iota(jnp.int32, shape, dim)


def hot_matrix(condition):
    return jnp.where(condition, 1.0, 0.0).astype(BF16)


def whole(shape):
    zeros = (0,) * len(shape)
    return pl.BlockSpec(shape, lambda *_: zeros)


def row_spec(width, rows=ROW_BLOCK):
    return pl.BlockSpec((rows, width), lambda i: (i, 0))


def col_spec(rows, width=LANES):
    return pl.BlockSpec((rows, width), lambda j: (0, j))


def sds(shape, dtype):
    return jax.ShapeDtypeStruct(shape, dtype)


def call(body, grid, in_specs, out_specs, out_shape, scratch=(), name=None):
    return pl.pallas_call(
        body,
        grid=grid,
        in_specs=in_specs,
        out_specs=out_specs,
        out_shape=out_shape,
        scratch_shapes=list(scratch),
        compiler_params=pltpu.CompilerParams(vmem_limit_bytes=VMEM_BYTES),
        name=name,
    )


def half_swap(values):
    lane = iota(values.shape, 1)
    up = pltpu.roll(values, 32, 1)
    down = pltpu.roll(values, LANES - 32, 1)
    return jnp.where(lane % HEAD_DIM < HEAD_DIM // 2, down, up)


def lane_value(values, lane_id):
    return jnp.sum(jnp.where(iota(values.shape, 1) == lane_id, values, 0.0), axis=1, keepdims=True)


def proj_in_body(
    place_row, hidden, upstream, small, cosine, sine, mask, gain, w_qkv, a_in, b_out,
    hid_s, dy_s, small_s, act_one, low_qkv, query, key, value,
):
    rows = hid_s.shape[0]
    base = pl.program_id(0) * rows
    perm = hot_matrix(place_row[...] == base + iota((rows, place_row.shape[1]), 0))
    hid = dot(perm, hidden[...])
    hid_s[...] = hid.astype(BF16)
    dy_s[...] = dot(perm, upstream[...]).astype(BF16)
    small_s[...] = dot(perm, small[...])
    scale = lax.rsqrt(jnp.mean(hid * hid, axis=-1, keepdims=True) + EPSILON)
    act = (hid * scale * gain[...]).astype(BF16)
    act_one[...] = act
    low = (dot(act, a_in[...]) * mask[...].astype(F32)).astype(BF16)
    low_qkv[...] = low
    cos, sin = cosine[...], sine[...]
    for out, start, factor in ((query, 0, HEAD_DIM**-0.5), (key, MODEL_WIDTH, 1.0)):
        vals = dot(act, w_qkv[:, start : start + MODEL_WIDTH]) + dot(
            low, b_out[:, start : start + MODEL_WIDTH]
        )
        for c in range(MODEL_WIDTH // LANES):
            piece = vals[:, c * LANES : (c + 1) * LANES]
            turned = (piece * cos + half_swap(piece) * sin).astype(BF16)
            if factor != 1.0:
                turned = turned * jnp.asarray(factor, BF16)
            out[:, c * LANES : (c + 1) * LANES] = turned
    value[...] = (
        dot(act, w_qkv[:, 2 * MODEL_WIDTH :]) + dot(low, b_out[:, 2 * MODEL_WIDTH :])
    ).astype(BF16)


def head_mask(shape, head):
    lane = iota(shape, 1)
    return (lane >= head * HEAD_DIM) & (lane < (head + 1) * HEAD_DIM)


def attention_fwd_body(query, key, value, starts, attended, lse):
    tok = query.shape[0]
    size = ROW_BLOCK
    zero = jnp.zeros((), BF16)
    for blk in range(tok // size):
        lo, hi = blk * size, (blk + 1) * size
        q_blk = query[lo:hi, :]
        k_all = key[:hi, :]
        v_all = value[:hi, :]
        begin = starts[lo:hi, :]
        col = iota((size, hi), 1)
        allowed = (col <= lo + iota((size, hi), 0)) & (col >= begin)
        total = jnp.zeros((size, LANES), F32)
        stats = jnp.zeros((size, LANES), F32)
        for head in range(2):
            mine = head_mask((size, LANES), head)
            scores = dot_nt(jnp.where(mine, q_blk, zero), k_all)
            scores = jnp.where(allowed, scores, -1000000000.0)
            top = jnp.max(scores, axis=1, keepdims=True)
            expo = jnp.exp(scores - top)
            norm = jnp.sum(expo, axis=1, keepdims=True)
            v_head = jnp.where(head_mask((hi, LANES), head), v_all, zero)
            total = total + dot(expo.astype(BF16), v_head) * (1.0 / norm)
            stats = jnp.where(mine, top + jnp.log(norm), stats)
        attended[lo:hi, :] = total.astype(BF16)
        lse[lo:hi, :] = stats


def attention_bwd_body(
    query, key, value, dout, attended, lse, starts, cosine, sine, d_query, d_key, d_value, kacc, vacc
):
    tok = query.shape[0]
    size = ROW_BLOCK
    zero = jnp.zeros((), BF16)
    kacc[...] = jnp.zeros_like(kacc)
    vacc[...] = jnp.zeros_like(vacc)
    for blk in range(tok // size):
        lo, hi = blk * size, (blk + 1) * size
        q_blk = query[lo:hi, :]
        do_blk = dout[lo:hi, :]
        k_all = key[:hi, :]
        v_all = value[:hi, :]
        begin = starts[lo:hi, :]
        col = iota((size, hi), 1)
        allowed = (col <= lo + iota((size, hi), 0)) & (col >= begin)
        prod = do_blk.astype(F32) * attended[lo:hi, :].astype(F32)
        q_total = jnp.zeros((size, LANES), F32)
        for head in range(2):
            mine = head_mask((size, LANES), head)
            q_head = jnp.where(mine, q_blk, zero)
            do_head = jnp.where(mine, do_blk, zero)
            lse_head = lse[lo:hi, head * HEAD_DIM : head * HEAD_DIM + 1]
            delta = jnp.sum(jnp.where(mine, prod, 0.0), axis=1, keepdims=True)
            scores = dot_nt(q_head, k_all)
            prob = jnp.where(allowed, jnp.exp(jnp.minimum(scores - lse_head, 0.0)), 0.0)
            dprob = dot_nt(do_head, v_all)
            dscore = (prob * (dprob - delta)).astype(BF16)
            k_head = jnp.where(head_mask((hi, LANES), head), k_all, zero)
            q_total = q_total + dot(dscore, k_head)
            kacc[:hi, :] += dot_tn(dscore, q_head)
            vacc[:hi, :] += dot_tn(prob.astype(BF16), do_head)
        q_total = q_total * HEAD_DIM**-0.5
        d_query[lo:hi, :] = (
            q_total * cosine[lo:hi, :] - half_swap(q_total) * sine[lo:hi, :]
        ).astype(BF16)
    for blk in range(tok // size):
        lo, hi = blk * size, (blk + 1) * size
        k_total = kacc[lo:hi, :]
        d_key[lo:hi, :] = (
            k_total * cosine[lo:hi, :] - half_swap(k_total) * sine[lo:hi, :]
        ).astype(BF16)
    d_value[...] = vacc[...].astype(BF16)


def post_attn_body(
    kinds, attn_low, hid_s, mask, small_s, w_out, a_out, b_out, router, gain,
    low_out, resid, act_two, gate,
):
    attn = attn_low[...]
    low = (dot(attn, a_out[...]) * mask[...].astype(F32)).astype(BF16)
    low_out[...] = low
    res = hid_s[...].astype(F32) + (dot(attn, w_out[...]) + dot(low, b_out[...]))
    resid[...] = res
    scale = lax.rsqrt(jnp.mean(res * res, axis=-1, keepdims=True) + EPSILON)
    act = (res * scale * gain[...]).astype(BF16)
    act_two[...] = act
    sm = small_s[...]
    carry = sm + (pltpu.roll(sm, LANES - 16, 1) + pltpu.roll(sm, LANES - 32, 1))
    logits = dot(act, router[...])
    lane = iota(logits.shape, 1)
    routed = jnp.where(lane < kinds, logits + carry, -1e30)
    top = jnp.max(routed, axis=1, keepdims=True)
    expo = jnp.exp(routed - top)
    prob = expo / jnp.sum(expo, axis=1, keepdims=True)
    gate[...] = jnp.where(lane < kinds, prob, logits)


def dispatch_body(experts, eids, small_s, gate, act_two, dy_s, mask, slot, sent, slot_rows):
    tok = act_two.shape[0]
    cap = sent.shape[1]
    step = pl.program_id(0)

    @pl.when(step == 0)
    def _():
        lane = iota((tok, LANES), 1)
        first = small_s[:, CHOICE_LANE : CHOICE_LANE + 1].astype(jnp.int32)
        second = small_s[:, CHOICE_LANE + 1 : CHOICE_LANE + 2].astype(jnp.int32)
        hot = ((first == lane) | (second == lane)) & (lane < experts)
        hot_low = hot_matrix(hot)
        for blk in range(tok // ROW_BLOCK):
            lo, hi = blk * ROW_BLOCK, (blk + 1) * ROW_BLOCK
            tri = hot_matrix(iota((ROW_BLOCK, hi), 1) < lo + iota((ROW_BLOCK, hi), 0))
            rank = dot(tri, hot_low[:hi, :])
            slot[lo:hi, :] = jnp.where(hot[lo:hi, :], rank, -1.0)
        slot_rows[...] = slot[...].T

    eid = eids[step]
    row = slot_rows[pl.ds(eid, 1), :].astype(jnp.int32)
    pick = hot_matrix(row == iota((cap, tok), 0))
    value = lane_value(gate[...], eid)
    scaled = (dy_s[...].astype(F32) * value).astype(BF16)
    sent[0, :, :MODEL_WIDTH] = dot(pick, act_two[...]).astype(BF16)
    sent[0, :, MODEL_WIDTH : 2 * MODEL_WIDTH] = dot(pick, scaled).astype(BF16)
    sent[0, :, 2 * MODEL_WIDTH :] = dot(pick, mask[...]).astype(BF16)


def ffn_body(
    came, w_gu, w_dn, a_gu, b_gu, a_dn, b_dn,
    back, ga_gu, gb_gu, ga_dn, gb_dn, acc_out, acc_dx, acc_low, acc_dlow,
):
    @pl.when(pl.program_id(0) == 0)
    def _():
        for ref in (ga_gu, gb_gu, ga_dn, gb_dn):
            ref[...] = jnp.zeros_like(ref)

    rows = came[0, :, :MODEL_WIDTH]
    d_out = came[0, :, MODEL_WIDTH : 2 * MODEL_WIDTH]
    mask = came[0, :, 2 * MODEL_WIDTH :].astype(F32)
    low_gu = (dot(rows, a_gu[...]) * mask).astype(BF16)
    dlow_dn = (dot_nt(d_out, b_dn[...]) * mask).astype(BF16)
    for ref in (acc_out, acc_dx, acc_low, acc_dlow):
        ref[...] = jnp.zeros_like(ref)

    def step(j, carry):
        lo = pl.multiple_of(j * HIDDEN_BLOCK, HIDDEN_BLOCK)
        g_cols = pl.ds(lo, HIDDEN_BLOCK)
        u_cols = pl.ds(pl.multiple_of(FEEDFWD_WIDTH + lo, HIDDEN_BLOCK), HIDDEN_BLOCK)
        gate = dot(rows, w_gu[:, g_cols]) + dot(low_gu, b_gu[:, g_cols])
        up = dot(rows, w_gu[:, u_cols]) + dot(low_gu, b_gu[:, u_cols])
        sig = 1.0 / (1.0 + jnp.exp(-gate))
        silu = gate * sig
        middle = (silu * up).astype(BF16)
        acc_out[...] += dot(middle, w_dn[g_cols, :])
        acc_low[...] += dot(middle, a_dn[g_cols, :])
        d_mid = dot_nt(d_out, w_dn[g_cols, :]) + dot_nt(dlow_dn, a_dn[g_cols, :])
        d_mid = d_mid.astype(BF16).astype(F32)
        d_gate = (d_mid * up * (sig * (1.0 + gate * (1.0 - sig)))).astype(BF16)
        d_up = (d_mid * silu).astype(BF16)
        acc_dx[...] += dot_nt(d_gate, w_gu[:, g_cols]) + dot_nt(d_up, w_gu[:, u_cols])
        acc_dlow[...] += dot_nt(d_gate, b_gu[:, g_cols]) + dot_nt(d_up, b_gu[:, u_cols])
        gb_gu[:, g_cols] += dot_tn(low_gu, d_gate)
        gb_gu[:, u_cols] += dot_tn(low_gu, d_up)
        ga_dn[g_cols, :] += dot_tn(middle, dlow_dn)
        return carry

    lax.fori_loop(0, FEEDFWD_WIDTH // HIDDEN_BLOCK, step, 0)
    low_dn = (acc_low[...] * mask).astype(BF16)
    back[0, :, :MODEL_WIDTH] = (acc_out[...] + dot(low_dn, b_dn[...])).astype(BF16)
    gb_dn[...] += dot_tn(low_dn, d_out)
    dlow_gu = (acc_dlow[...] * mask).astype(BF16)
    back[0, :, MODEL_WIDTH:] = (acc_dx[...] + dot_nt(dlow_gu, a_gu[...])).astype(BF16)
    ga_gu[...] += dot_tn(rows, dlow_gu)


def combine_body(
    experts, kinds, eids, resid, act_two, dy_s, gate, slot, small_s, low_out, attn_low, mask, came,
    w_out, a_out, b_out, router, const_value, gain,
    out_s, d_resid, d_attended, d_logits, ga_out, gb_out,
):
    @pl.when(pl.program_id(0) == 0)
    def _():
        ga_out[...] = jnp.zeros_like(ga_out)
        gb_out[...] = jnp.zeros_like(gb_out)

    rows = resid.shape[0]
    cap = came.shape[1]
    res = resid[...]
    act = act_two[...].astype(F32)
    dy = dy_s[...].astype(F32)
    prob = gate[...]
    lane = iota((rows, LANES), 1)
    out = res
    d_act = jnp.zeros((rows, MODEL_WIDTH), F32)
    d_gate = jnp.zeros((rows, LANES), F32)
    for k in range(came.shape[0]):
        eid = eids[k]
        place = lane_value(slot[...], eid).astype(jnp.int32)
        pick = hot_matrix(place == iota((rows, cap), 1))
        result = dot(pick, came[k, :, :MODEL_WIDTH])
        d_act = d_act + dot(pick, came[k, :, MODEL_WIDTH:])
        d_gate = jnp.where(lane == eid, jnp.sum(dy * result, axis=1, keepdims=True), d_gate)
        out = out + lane_value(prob, eid) * result
    sm = small_s[...]
    first = sm[:, CHOICE_LANE : CHOICE_LANE + 1]
    second = sm[:, CHOICE_LANE + 1 : CHOICE_LANE + 2]

    def chosen(kind):
        return jnp.where((first == kind) | (second == kind), 1.0, 0.0)

    has_copy, has_zero, has_one = chosen(experts + 1), chosen(experts + 2), chosen(experts + 3)
    g_copy = has_copy * prob[:, experts + 1 : experts + 2]
    g_zero = has_zero * prob[:, experts + 2 : experts + 3]
    g_one = has_one * prob[:, experts + 3 : experts + 4]

    def pair(at):
        left, right = prob[:, at : at + 1], prob[:, at + 1 : at + 2]
        top = jnp.maximum(left, right)
        e_left, e_right = jnp.exp(left - top), jnp.exp(right - top)
        return e_left / (e_left + e_right), e_right / (e_left + e_right)

    a00, a01 = pair(CONST_LANE)
    a10, a11 = pair(CONST_LANE + 2)
    v_zero, v_one = const_value[0:1, :], const_value[1:2, :]
    along_act = jnp.sum(dy * act, axis=1, keepdims=True)
    along_zero = jnp.sum(dy * v_zero, axis=1, keepdims=True)
    along_one = jnp.sum(dy * v_one, axis=1, keepdims=True)
    coef = g_copy + g_zero * a00 + g_one * a10
    out = out + coef * act + (g_zero * a01) * v_zero + (g_one * a11) * v_one
    out_s[...] = out.astype(BF16)
    d_gate = jnp.where(lane == experts + 1, has_copy * along_act, d_gate)
    d_gate = jnp.where(
        lane == experts + 2, has_zero * (a00 * along_act + a01 * along_zero), d_gate
    )
    d_gate = jnp.where(lane == experts + 3, has_one * (a10 * along_act + a11 * along_one), d_gate)
    prob = jnp.where(lane < kinds, prob, 0.0)
    d_logit = prob * (d_gate - jnp.sum(prob * d_gate, axis=1, keepdims=True))
    d_logits[...] = d_logit
    mix = d_logit
    for at, g_val, left, right, along in (
        (CONST_LANE, g_zero, a00, a01, along_zero),
        (CONST_LANE + 2, g_one, a10, a11, along_one),
    ):
        da_left, da_right = g_val * along_act, g_val * along
        level = left * da_left + right * da_right
        mix = jnp.where(lane == at, left * (da_left - level), mix)
        mix = jnp.where(lane == at + 1, right * (da_right - level), mix)
    mix_hi = mix.astype(BF16)
    mix_lo = (mix - mix_hi.astype(F32)).astype(BF16)
    d_act = d_act + coef * dy + (dot_nt(mix_hi, router[...]) + dot_nt(mix_lo, router[...]))
    scale = lax.rsqrt(jnp.mean(res * res, axis=-1, keepdims=True) + EPSILON)
    weighted = d_act * gain[...]
    d_res = dy + (
        scale * weighted
        - res * (scale * scale * scale) * jnp.mean(res * weighted, axis=-1, keepdims=True)
    )
    d_resid[...] = d_res
    d_attn = d_res.astype(BF16)
    dlow = (dot_nt(d_attn, b_out[...]) * mask[...].astype(F32)).astype(BF16)
    gb_out[...] += dot_tn(low_out[...], d_attn)
    ga_out[...] += dot_tn(attn_low[...], dlow)
    d_attended[...] = (dot_nt(d_attn, w_out[...]) + dot_nt(dlow, a_out[...])).astype(BF16)


def input_grad_body(
    d_query, d_key, d_value, low_qkv, act_one, mask, hid_s, d_resid, w_qkv, a_in, b_out, gain,
    high, lower, ga_qkv, gb_qkv,
):
    @pl.when(pl.program_id(0) == 0)
    def _():
        ga_qkv[...] = jnp.zeros_like(ga_qkv)
        gb_qkv[...] = jnp.zeros_like(gb_qkv)

    d_low = jnp.zeros((d_query.shape[0], LANES), F32)
    d_act = jnp.zeros((d_query.shape[0], MODEL_WIDTH), F32)
    for part, ref in enumerate((d_query, d_key, d_value)):
        cols = slice(part * MODEL_WIDTH, (part + 1) * MODEL_WIDTH)
        grad = ref[...]
        d_low = d_low + dot_nt(grad, b_out[:, cols])
        d_act = d_act + dot_nt(grad, w_qkv[:, cols])
        gb_qkv[:, cols] += dot_tn(low_qkv[...], grad)
    d_low = (d_low * mask[...].astype(F32)).astype(BF16)
    ga_qkv[...] += dot_tn(act_one[...], d_low)
    d_act = d_act + dot_nt(d_low, a_in[...])
    hid = hid_s[...].astype(F32)
    scale = lax.rsqrt(jnp.mean(hid * hid, axis=-1, keepdims=True) + EPSILON)
    weighted = d_act * gain[...]
    grad_hid = d_resid[...] + (
        scale * weighted
        - hid * (scale * scale * scale) * jnp.mean(hid * weighted, axis=-1, keepdims=True)
    )
    top = grad_hid.astype(BF16)
    high[...] = top
    lower[...] = (grad_hid - top.astype(F32)).astype(BF16)


def to_rows_body(place_col, out_s, d_logits, high, lower, out, grad_hidden, grad_gate):
    rows = out.shape[0]
    tok = out_s.shape[0]
    perm = hot_matrix(place_col[...] == iota((rows, tok), 1))
    out[...] = dot(perm, out_s[...]).astype(BF16)
    grad_hidden[...] = dot(perm, high[...]) + dot(perm, lower[...])
    logits = d_logits[...]
    top = logits.astype(BF16)
    rest = logits - top.astype(F32)
    mid = rest.astype(BF16)
    last = (rest - mid.astype(F32)).astype(BF16)
    grad_gate[...] = dot(perm, top) + (dot(perm, mid) + dot(perm, last))


def split_three(values):
    top = values.astype(BF16)
    rest = values - top.astype(F32)
    mid = rest.astype(BF16)
    return top, mid, (rest - mid.astype(F32)).astype(BF16)


class PairPlan:
    def __init__(self, dp, ex):
        self.axes = ("dp", "expert")
        self.dp, self.ex = dp, ex
        self.h = lax.axis_index("dp") & 1
        self.z = lax.axis_index("expert")
        self.own = (self.z & 1) + 2 * self.h
        self.local = (self.z >> 1) == self.h
        self.groups = [[2 * m + h for m in range(dp // 2)] for h in range(2)]

    def send(self, values, target):
        pairs = []
        for d in range(self.dp):
            for z in range(self.ex):
                goal = target(d, z)
                if goal is not None:
                    pairs.append((d * self.ex + z, goal[0] * self.ex + goal[1]))
        return lax.ppermute(values, self.axes, pairs)

    def gather(self, shard):
        near = self.send(shard, lambda d, z: (d, z ^ 2) if (z >> 1) == (d & 1) else None)
        cross = self.send(shard, lambda d, z: (d ^ 1, z ^ 2) if (z >> 1) != (d & 1) else None)
        over = self.send(shard, lambda d, z: (d ^ 1, z) if (z >> 1) != (d & 1) else None)
        mine = jnp.where(self.local, shard, near)
        other = jnp.where(self.local, over, cross)
        both = jnp.stack([jnp.where(self.h == 0, mine, other), jnp.where(self.h == 0, other, mine)])
        return lax.all_gather(both, "dp", axis=0, tiled=True, axis_index_groups=self.groups)

    def expert_ids(self):
        return self.own ^ jnp.arange(self.ex, dtype=jnp.int32)

    def exchange(self, values):
        moves = (
            lambda d, z: (d, z ^ 1),
            lambda d, z: (d ^ 1, z),
            lambda d, z: (d ^ 1, z ^ 1),
        )
        parts = [values[0]] + [self.send(values[k + 1], moves[k]) for k in range(3)]
        return jnp.stack(parts)

    def reduce(self, sums):
        part = lax.psum_scatter(
            sums, "dp", scatter_dimension=0, tiled=True, axis_index_groups=self.groups
        )
        same = jnp.where(self.h == 0, part[0], part[1])
        flip = jnp.where(self.h == 0, part[1], part[0])
        over = self.send(flip, lambda d, z: (d ^ 1, z) if (z >> 1) == (d & 1) else None)
        near = self.send(same, lambda d, z: (d, z ^ 2) if (z >> 1) != (d & 1) else None)
        cross = self.send(flip, lambda d, z: (d ^ 1, z ^ 2) if (z >> 1) != (d & 1) else None)
        first = jnp.where(self.local, same, over).astype(F32)
        return first + near.astype(F32) + cross.astype(F32)

    def reduce_all(self, sums):
        values = sums.reshape((self.dp // 2, 2, self.ex) + sums.shape[1:])
        move = lambda d, z: (d ^ 1, z)
        values = self._halve(values, 1, self.h, move)
        rest = self.dp // 2
        position = lax.axis_index("dp") >> 1
        while rest > 1:
            rest //= 2
            values = values.reshape((2, rest) + values.shape[1:])
            bit = position // rest % 2
            values = self._halve(values, 0, bit, functools.partial(self._flip_dp, 2 * rest))
        values = values[0]
        rest = self.ex
        while rest > 1:
            rest //= 2
            values = values.reshape((2, rest) + values.shape[1:])
            bit = self.z // rest % 2
            values = self._halve(values, 0, bit, functools.partial(self._flip_ex, rest))
        return values[0].astype(F32)

    @staticmethod
    def _flip_dp(bit, d, z):
        return (d ^ bit, z)

    @staticmethod
    def _flip_ex(bit, d, z):
        return (d, z ^ bit)

    def _halve(self, values, axis, bit, move):
        keep = lax.dynamic_index_in_dim(values, bit, axis, keepdims=False)
        give = lax.dynamic_index_in_dim(values, 1 - bit, axis, keepdims=False)
        return (keep.astype(F32) + self.send(give, move).astype(F32)).astype(BF16)


class AxisPlan:
    def __init__(self, dp, ex):
        self.dp, self.ex = dp, ex

    def gather(self, shard):
        return lax.all_gather(shard, "dp", axis=0)

    def expert_ids(self):
        return jnp.arange(self.ex, dtype=jnp.int32)

    def exchange(self, values):
        return lax.all_to_all(values, "expert", split_axis=0, concat_axis=0, tiled=True)

    def reduce(self, sums):
        return lax.psum_scatter(sums, "dp", scatter_dimension=0, tiled=True)[0].astype(F32)

    def reduce_all(self, sums):
        return lax.psum_scatter(
            sums, ("dp", "expert"), scatter_dimension=0, tiled=True
        )[0].astype(F32)


def shards(
    dp_size,
    expert_count,
    hidden_input,
    gate_carryover,
    sequence_length,
    token_stream_place,
    expert_choice_index,
    sequence_adapter,
    attention_gain,
    query_key_weight,
    output_weight,
    adapter_in_query,
    adapter_out_query,
    adapter_in_output,
    adapter_out_output,
    feedfwd_gain,
    router_weight,
    constant_gate,
    constant_value,
    gate_upward_weight,
    down_weight,
    adapter_in_gate,
    adapter_out_gate,
    adapter_in_down,
    adapter_out_down,
    output_gradient,
):
    tok = hidden_input.shape[0]
    width = MODEL_WIDTH
    kinds = expert_count + 4
    devices = dp_size * expert_count
    capacity = 5 * tok // (2 * kinds) // 8 * 8 + 8
    cap = -(-capacity // 16) * 16
    blocks = tok // ROW_BLOCK
    plan = (PairPlan if (dp_size, expert_count) == (8, 4) else AxisPlan)(dp_size, expert_count)

    a_rows, b_rows = query_key_weight.shape[0], adapter_out_query.shape[0]
    own_a = jnp.concatenate(
        [query_key_weight, output_weight, adapter_in_query, adapter_in_output], axis=1
    )
    own_b = jnp.concatenate([adapter_out_query, adapter_out_output], axis=1)
    pad_rows = -(a_rows + b_rows) % 8
    own_attn = jnp.concatenate(
        [
            own_a,
            jnp.pad(own_b, ((0, pad_rows), (0, own_a.shape[1] - own_b.shape[1]))),
        ],
        axis=0,
    )
    attn_all = lax.all_gather(own_attn, ("dp", "expert"), axis=0)
    in_rows = attn_all[:, :a_rows]
    out_rows = attn_all[:, a_rows : a_rows + b_rows]
    w_qkv = in_rows[:, :, : 3 * width].reshape(width, 3 * width)
    w_out = in_rows[:, :, 3 * width : 4 * width].reshape(width, width)
    a_qkv = in_rows[:, :, 4 * width : 4 * width + LANES].reshape(width, LANES)
    a_out = in_rows[:, :, 4 * width + LANES :].reshape(width, LANES)
    b_qkv = out_rows[:, :, : 3 * width].reshape(LANES, 3 * width)
    b_out = out_rows[:, :, 3 * width : 4 * width].reshape(LANES, width)

    gu_rows, up_rows, dn_rows = gate_upward_weight.shape[1], adapter_out_gate.shape[1], down_weight.shape[1]
    wide = plan.gather(jnp.concatenate([gate_upward_weight[0], adapter_out_gate[0]], axis=0))
    mid = plan.gather(jnp.concatenate([down_weight[0], adapter_out_down[0]], axis=0))
    thin = plan.gather(jnp.concatenate([adapter_in_gate[0], adapter_in_down[0]], axis=0))
    w_gu = wide[:, :gu_rows].reshape(width, 2 * FEEDFWD_WIDTH)
    b_gu = wide[:, gu_rows:].reshape(LANES, 2 * FEEDFWD_WIDTH)
    w_dn = mid[:, :dn_rows].reshape(FEEDFWD_WIDTH, width)
    b_dn = mid[:, dn_rows:].reshape(LANES, width)
    a_gu = thin[:, :gu_rows].reshape(width, LANES)
    a_dn = thin[:, gu_rows:].reshape(FEEDFWD_WIDTH, LANES)

    place = token_stream_place[0]
    ends = jnp.cumsum(sequence_length[0])
    begins = ends - sequence_length[0]
    stream = jnp.arange(tok, dtype=jnp.int32)
    seg = jnp.sum((stream[:, None] >= ends[None, :]).astype(jnp.int32), axis=1)
    seg_hot = seg[:, None] == jnp.arange(ends.shape[0], dtype=jnp.int32)[None, :]
    start = jnp.sum(jnp.where(seg_hot, begins[None, :], 0), axis=1)
    adapter = jnp.sum(jnp.where(seg_hot, sequence_adapter[0][None, :], 0), axis=1)
    half = HEAD_DIM // 2
    freq = jnp.exp(jnp.arange(half, dtype=F32) * (-math.log(10000.0) / half))
    angle = (stream - start).astype(F32)[:, None] * freq[None, :]
    cos, sin = jnp.cos(angle), jnp.sin(angle)
    cosine = jnp.concatenate([cos, cos, cos, cos], axis=1)
    sine = jnp.concatenate([-sin, sin, -sin, sin], axis=1)
    starts = start[:, None]
    mask = (jnp.arange(LANES)[None, :] // ADAPTER_RANK == adapter[:, None]).astype(BF16)
    top, middle, last = split_three(gate_carryover)
    gap = jnp.zeros((tok, 16 - kinds), BF16)
    small = jnp.concatenate(
        [top, gap, middle, gap, last, gap, expert_choice_index.astype(BF16),
         jnp.zeros((tok, LANES - CHOICE_LANE - 2), BF16)],
        axis=1,
    )
    gain_one = attention_gain.astype(F32)[None, :]
    gain_two = feedfwd_gain.astype(F32)[None, :]
    router = jnp.concatenate(
        [router_weight, jnp.zeros((width, CONST_LANE - kinds), BF16), constant_gate,
         jnp.zeros((width, LANES - CONST_LANE - 4), BF16)],
        axis=1,
    )
    const_value = constant_value.astype(F32)

    full = whole
    hid_s, dy_s, small_s, act_one, low_qkv, query, key, value = call(
        proj_in_body,
        (blocks,),
        [full((1, tok)), full((tok, width)), full((tok, width)), full((tok, LANES)),
         row_spec(LANES), row_spec(LANES), row_spec(LANES), full((1, width)),
         full((width, 3 * width)), full((width, LANES)), full((LANES, 3 * width))],
        [row_spec(width), row_spec(width), row_spec(LANES), row_spec(width), row_spec(LANES),
         row_spec(width), row_spec(width), row_spec(width)],
        [sds((tok, width), BF16), sds((tok, width), BF16), sds((tok, LANES), F32),
         sds((tok, width), BF16), sds((tok, LANES), BF16), sds((tok, width), BF16),
         sds((tok, width), BF16), sds((tok, width), BF16)],
        name="proj_in",
    )(place[None, :], hidden_input, output_gradient, small, cosine, sine, mask, gain_one,
      w_qkv, a_qkv, b_qkv)

    pairs = HEAD_COUNT // 2
    attn_low, lse = call(
        attention_fwd_body,
        (pairs,),
        [col_spec(tok)] * 3 + [full((tok, 1))],
        [col_spec(tok), col_spec(tok)],
        [sds((tok, width), BF16), sds((tok, width), F32)],
        name="attention_fwd",
    )(query, key, value, starts)

    low_out, resid, act_two, gate = call(
        functools.partial(post_attn_body, kinds),
        (blocks,),
        [row_spec(width), row_spec(width), row_spec(LANES), row_spec(LANES), full((width, width)),
         full((width, LANES)), full((LANES, width)), full((width, LANES)), full((1, width))],
        [row_spec(LANES), row_spec(width), row_spec(width), row_spec(LANES)],
        [sds((tok, LANES), BF16), sds((tok, width), F32), sds((tok, width), BF16),
         sds((tok, LANES), F32)],
        name="post_attn",
    )(attn_low, hid_s, mask, small_s, w_out, a_out, b_out, router, gain_two)

    eids = plan.expert_ids()
    smem = pl.BlockSpec(memory_space=pltpu.SMEM)
    sent_width = 2 * width + LANES
    slot, sent = call(
        functools.partial(dispatch_body, expert_count),
        (expert_count,),
        [smem, full((tok, LANES)), full((tok, LANES)), full((tok, width)), full((tok, width)),
         full((tok, LANES))],
        [full((tok, LANES)), pl.BlockSpec((1, cap, sent_width), lambda i: (i, 0, 0))],
        [sds((tok, LANES), F32), sds((expert_count, cap, sent_width), BF16)],
        scratch=[pltpu.VMEM((LANES, tok), F32)],
        name="dispatch",
    )(eids, small_s, gate, act_two, dy_s, mask)

    came = plan.exchange(sent)
    back, ga_gu, gb_gu, ga_dn, gb_dn = call(
        ffn_body,
        (expert_count,),
        [pl.BlockSpec((1, cap, sent_width), lambda i: (i, 0, 0)), full((width, 2 * FEEDFWD_WIDTH)),
         full((FEEDFWD_WIDTH, width)), full((width, LANES)), full((LANES, 2 * FEEDFWD_WIDTH)),
         full((FEEDFWD_WIDTH, LANES)), full((LANES, width))],
        [pl.BlockSpec((1, cap, 2 * width), lambda i: (i, 0, 0)), full((width, LANES)),
         full((LANES, 2 * FEEDFWD_WIDTH)), full((FEEDFWD_WIDTH, LANES)), full((LANES, width))],
        [sds((expert_count, cap, 2 * width), BF16), sds((width, LANES), F32),
         sds((LANES, 2 * FEEDFWD_WIDTH), F32), sds((FEEDFWD_WIDTH, LANES), F32),
         sds((LANES, width), F32)],
        scratch=[pltpu.VMEM((cap, width), F32), pltpu.VMEM((cap, width), F32),
                 pltpu.VMEM((cap, LANES), F32), pltpu.VMEM((cap, LANES), F32)],
        name="ffn",
    )(came, w_gu, w_dn, a_gu, b_gu, a_dn, b_dn)
    returned = plan.exchange(back)

    owned_wide = plan.reduce(
        jnp.concatenate([gb_gu, gb_dn], axis=1).astype(BF16).reshape(dp_size, up_rows, -1)
    )
    owned_thin = plan.reduce(
        jnp.concatenate(
            [ga_gu.reshape(dp_size, gu_rows, LANES), ga_dn.reshape(dp_size, dn_rows, LANES)], axis=1
        ).astype(BF16)
    )

    out_s, d_resid, d_attended, d_logits, ga_out, gb_out = call(
        functools.partial(combine_body, expert_count, kinds),
        (blocks,),
        [smem, row_spec(width), row_spec(width), row_spec(width), row_spec(LANES), row_spec(LANES),
         row_spec(LANES), row_spec(LANES), row_spec(width), row_spec(LANES),
         full((expert_count, cap, 2 * width)), full((width, width)), full((width, LANES)),
         full((LANES, width)), full((width, LANES)), full((2, width)), full((1, width))],
        [row_spec(width), row_spec(width), row_spec(width), row_spec(LANES), full((width, LANES)),
         full((LANES, width))],
        [sds((tok, width), BF16), sds((tok, width), F32), sds((tok, width), BF16),
         sds((tok, LANES), F32), sds((width, LANES), F32), sds((LANES, width), F32)],
        name="combine",
    )(eids, resid, act_two, dy_s, gate, slot, small_s, low_out, attn_low, mask, returned,
      w_out, a_out, b_out, router, const_value, gain_two)

    d_query, d_key, d_value = call(
        attention_bwd_body,
        (pairs,),
        [col_spec(tok)] * 6 + [full((tok, 1)), full((tok, LANES)), full((tok, LANES))],
        [col_spec(tok)] * 3,
        [sds((tok, width), BF16)] * 3,
        scratch=[pltpu.VMEM((tok, LANES), F32), pltpu.VMEM((tok, LANES), F32)],
        name="attention_bwd",
    )(query, key, value, d_attended, attn_low, lse, starts, cosine, sine)

    high, lower, ga_qkv, gb_qkv = call(
        input_grad_body,
        (blocks,),
        [row_spec(width)] * 3 + [row_spec(LANES), row_spec(width), row_spec(LANES), row_spec(width),
         row_spec(width), full((width, 3 * width)), full((width, LANES)), full((LANES, 3 * width)),
         full((1, width))],
        [row_spec(width), row_spec(width), full((width, LANES)), full((LANES, 3 * width))],
        [sds((tok, width), BF16), sds((tok, width), BF16), sds((width, LANES), F32),
         sds((LANES, 3 * width), F32)],
        name="input_grad",
    )(d_query, d_key, d_value, low_qkv, act_one, mask, hid_s, d_resid, w_qkv, a_qkv, b_qkv,
      gain_one)

    owned = plan.reduce_all(
        jnp.concatenate(
            [
                ga_qkv.reshape(devices, b_rows, -1),
                ga_out.reshape(devices, b_rows, -1),
                gb_qkv.reshape(devices, b_rows, -1),
                gb_out.reshape(devices, b_rows, -1),
            ],
            axis=2,
        ).astype(BF16)
    )

    output, grad_hidden, grad_gate = call(
        to_rows_body,
        (blocks,),
        [row_spec(1), full((tok, width)), full((tok, LANES)), full((tok, width)),
         full((tok, width))],
        [row_spec(width), row_spec(width), row_spec(LANES)],
        [sds((tok, width), BF16), sds((tok, width), F32), sds((tok, LANES), F32)],
        name="to_rows",
    )(place[:, None], out_s, d_logits, high, lower)

    return (
        output,
        grad_hidden,
        grad_gate[:, :kinds],
        owned[:, :width].reshape(a_rows, LANES),
        owned[:, 2 * width : 5 * width],
        owned[:, width : 2 * width].reshape(a_rows, LANES),
        owned[:, 5 * width :],
        owned_thin[None, :gu_rows],
        owned_wide[None, :, : 2 * FEEDFWD_WIDTH],
        owned_thin[None, gu_rows:],
        owned_wide[None, :, 2 * FEEDFWD_WIDTH :],
    )


def solution(mesh):
    rows = P(("dp", "expert"), None)
    expert_rows = P("expert", "dp", None)
    in_specs = (
        (rows,) * 6 + (P(),) + (rows,) * 6 + (P(),) * 4 + (expert_rows,) * 6 + (rows,)
    )
    out_specs = (rows,) * 7 + (expert_rows,) * 4
    body = functools.partial(shards, mesh.shape["dp"], mesh.shape["expert"])
    return jax.shard_map(body, mesh=mesh, in_specs=in_specs, out_specs=out_specs, check_vma=False)
```

```python
import functools
import math

import jax
import jax.numpy as jnp
from jax import lax
from jax.experimental import pallas as pl
from jax.experimental.pallas import tpu as pltpu
from jax.sharding import PartitionSpec as P

MODEL_WIDTH = 768
HEAD_COUNT = 12
HEAD_DIM = 64
FEEDFWD_WIDTH = 2048
ADAPTER_RANK = 16
ROW_BLOCK = 256
HIDDEN_BLOCK = 512
LANES = 128
CONST_LANE = 64
CHOICE_LANE = 48
EPSILON = 1e-06
VMEM_BYTES = 60 * 2**20

F32 = jnp.float32
BF16 = jnp.bfloat16


def dot(a, b):
    return jnp.dot(a, b, preferred_element_type=F32)


def dot_nt(a, b):
    return lax.dot_general(a, b, (((1,), (1,)), ((), ())), preferred_element_type=F32)


def dot_tn(a, b):
    return lax.dot_general(a, b, (((0,), (0,)), ((), ())), preferred_element_type=F32)


def iota(shape, dim):
    return lax.broadcasted_iota(jnp.int32, shape, dim)


def hot_matrix(condition):
    return jnp.where(condition, 1.0, 0.0).astype(BF16)


def whole(shape):
    zeros = (0,) * len(shape)
    return pl.BlockSpec(shape, lambda *_: zeros)


def row_spec(width, rows=ROW_BLOCK):
    return pl.BlockSpec((rows, width), lambda i: (i, 0))


def col_spec(rows, width=LANES):
    return pl.BlockSpec((rows, width), lambda j: (0, j))


def sds(shape, dtype):
    return jax.ShapeDtypeStruct(shape, dtype)


def call(body, grid, in_specs, out_specs, out_shape, scratch=(), name=None):
    return pl.pallas_call(
        body,
        grid=grid,
        in_specs=in_specs,
        out_specs=out_specs,
        out_shape=out_shape,
        scratch_shapes=list(scratch),
        compiler_params=pltpu.CompilerParams(vmem_limit_bytes=VMEM_BYTES),
        name=name,
    )


def half_swap(values):
    lane = iota(values.shape, 1)
    up = pltpu.roll(values, 32, 1)
    down = pltpu.roll(values, LANES - 32, 1)
    return jnp.where(lane % HEAD_DIM < HEAD_DIM // 2, down, up)


def lane_value(values, lane_id):
    return jnp.sum(jnp.where(iota(values.shape, 1) == lane_id, values, 0.0), axis=1, keepdims=True)


def proj_in_body(
    place_row, hidden, upstream, small, cosine, sine, mask, gain, w_qkv, a_in, b_out,
    hid_s, dy_s, small_s, act_one, low_qkv, query, key, value,
):
    rows = hid_s.shape[0]
    base = pl.program_id(0) * rows
    perm = hot_matrix(place_row[...] == base + iota((rows, place_row.shape[1]), 0))
    hid = dot(perm, hidden[...])
    hid_s[...] = hid.astype(BF16)
    dy_s[...] = dot(perm, upstream[...]).astype(BF16)
    small_s[...] = dot(perm, small[...])
    scale = lax.rsqrt(jnp.mean(hid * hid, axis=-1, keepdims=True) + EPSILON)
    act = (hid * scale * gain[...]).astype(BF16)
    act_one[...] = act
    low = (dot(act, a_in[...]) * mask[...].astype(F32)).astype(BF16)
    low_qkv[...] = low
    cos, sin = cosine[...], sine[...]
    for out, start, factor in ((query, 0, HEAD_DIM**-0.5), (key, MODEL_WIDTH, 1.0)):
        vals = dot(act, w_qkv[:, start : start + MODEL_WIDTH]) + dot(
            low, b_out[:, start : start + MODEL_WIDTH]
        )
        for c in range(MODEL_WIDTH // LANES):
            piece = vals[:, c * LANES : (c + 1) * LANES]
            turned = (piece * cos + half_swap(piece) * sin).astype(BF16)
            if factor != 1.0:
                turned = turned * jnp.asarray(factor, BF16)
            out[:, c * LANES : (c + 1) * LANES] = turned
    value[...] = (
        dot(act, w_qkv[:, 2 * MODEL_WIDTH :]) + dot(low, b_out[:, 2 * MODEL_WIDTH :])
    ).astype(BF16)


def head_mask(shape, head):
    lane = iota(shape, 1)
    return (lane >= head * HEAD_DIM) & (lane < (head + 1) * HEAD_DIM)


def attention_fwd_body(query, key, value, starts, attended, lse):
    tok = query.shape[0]
    size = ROW_BLOCK
    zero = jnp.zeros((), BF16)
    for blk in range(tok // size):
        lo, hi = blk * size, (blk + 1) * size
        q_blk = query[lo:hi, :]
        k_all = key[:hi, :]
        v_all = value[:hi, :]
        begin = starts[lo:hi, :]
        col = iota((size, hi), 1)
        allowed = (col <= lo + iota((size, hi), 0)) & (col >= begin)
        total = jnp.zeros((size, LANES), F32)
        stats = jnp.zeros((size, LANES), F32)
        for head in range(2):
            mine = head_mask((size, LANES), head)
            scores = dot_nt(jnp.where(mine, q_blk, zero), k_all)
            scores = jnp.where(allowed, scores, -1000000000.0)
            top = jnp.max(scores, axis=1, keepdims=True)
            expo = jnp.exp(scores - top)
            norm = jnp.sum(expo, axis=1, keepdims=True)
            v_head = jnp.where(head_mask((hi, LANES), head), v_all, zero)
            total = total + dot(expo.astype(BF16), v_head) * (1.0 / norm)
            stats = jnp.where(mine, top + jnp.log(norm), stats)
        attended[lo:hi, :] = total.astype(BF16)
        lse[lo:hi, :] = stats


def attention_bwd_body(
    query, key, value, dout, attended, lse, starts, cosine, sine, d_query, d_key, d_value, kacc, vacc
):
    tok = query.shape[0]
    size = ROW_BLOCK
    zero = jnp.zeros((), BF16)
    kacc[...] = jnp.zeros_like(kacc)
    vacc[...] = jnp.zeros_like(vacc)
    for blk in range(tok // size):
        lo, hi = blk * size, (blk + 1) * size
        q_blk = query[lo:hi, :]
        do_blk = dout[lo:hi, :]
        k_all = key[:hi, :]
        v_all = value[:hi, :]
        begin = starts[lo:hi, :]
        col = iota((size, hi), 1)
        allowed = (col <= lo + iota((size, hi), 0)) & (col >= begin)
        prod = do_blk.astype(F32) * attended[lo:hi, :].astype(F32)
        q_total = jnp.zeros((size, LANES), F32)
        for head in range(2):
            mine = head_mask((size, LANES), head)
            q_head = jnp.where(mine, q_blk, zero)
            do_head = jnp.where(mine, do_blk, zero)
            lse_head = lse[lo:hi, head * HEAD_DIM : head * HEAD_DIM + 1]
            delta = jnp.sum(jnp.where(mine, prod, 0.0), axis=1, keepdims=True)
            scores = dot_nt(q_head, k_all)
            prob = jnp.where(allowed, jnp.exp(jnp.minimum(scores - lse_head, 0.0)), 0.0)
            dprob = dot_nt(do_head, v_all)
            dscore = (prob * (dprob - delta)).astype(BF16)
            k_head = jnp.where(head_mask((hi, LANES), head), k_all, zero)
            q_total = q_total + dot(dscore, k_head)
            kacc[:hi, :] += dot_tn(dscore, q_head)
            vacc[:hi, :] += dot_tn(prob.astype(BF16), do_head)
        q_total = q_total * HEAD_DIM**-0.5
        d_query[lo:hi, :] = (
            q_total * cosine[lo:hi, :] - half_swap(q_total) * sine[lo:hi, :]
        ).astype(BF16)
    for blk in range(tok // size):
        lo, hi = blk * size, (blk + 1) * size
        k_total = kacc[lo:hi, :]
        d_key[lo:hi, :] = (
            k_total * cosine[lo:hi, :] - half_swap(k_total) * sine[lo:hi, :]
        ).astype(BF16)
    d_value[...] = vacc[...].astype(BF16)


def post_attn_body(
    kinds, attn_low, hid_s, mask, small_s, w_out, a_out, b_out, router, gain,
    low_out, resid, act_two, gate,
):
    attn = attn_low[...]
    low = (dot(attn, a_out[...]) * mask[...].astype(F32)).astype(BF16)
    low_out[...] = low
    res = hid_s[...].astype(F32) + (dot(attn, w_out[...]) + dot(low, b_out[...]))
    resid[...] = res
    scale = lax.rsqrt(jnp.mean(res * res, axis=-1, keepdims=True) + EPSILON)
    act = (res * scale * gain[...]).astype(BF16)
    act_two[...] = act
    sm = small_s[...]
    carry = sm + (pltpu.roll(sm, LANES - 16, 1) + pltpu.roll(sm, LANES - 32, 1))
    logits = dot(act, router[...])
    lane = iota(logits.shape, 1)
    routed = jnp.where(lane < kinds, logits + carry, -1e30)
    top = jnp.max(routed, axis=1, keepdims=True)
    expo = jnp.exp(routed - top)
    prob = expo / jnp.sum(expo, axis=1, keepdims=True)
    gate[...] = jnp.where(lane < kinds, prob, logits)


def dispatch_body(experts, eids, small_s, gate, act_two, dy_s, mask, slot, sent, slot_rows):
    tok = act_two.shape[0]
    cap = sent.shape[1]
    step = pl.program_id(0)

    @pl.when(step == 0)
    def _():
        lane = iota((tok, LANES), 1)
        first = small_s[:, CHOICE_LANE : CHOICE_LANE + 1].astype(jnp.int32)
        second = small_s[:, CHOICE_LANE + 1 : CHOICE_LANE + 2].astype(jnp.int32)
        hot = ((first == lane) | (second == lane)) & (lane < experts)
        hot_low = hot_matrix(hot)
        for blk in range(tok // ROW_BLOCK):
            lo, hi = blk * ROW_BLOCK, (blk + 1) * ROW_BLOCK
            tri = hot_matrix(iota((ROW_BLOCK, hi), 1) < lo + iota((ROW_BLOCK, hi), 0))
            rank = dot(tri, hot_low[:hi, :])
            slot[lo:hi, :] = jnp.where(hot[lo:hi, :], rank, -1.0)
        slot_rows[...] = slot[...].T

    eid = eids[step]
    row = slot_rows[pl.ds(eid, 1), :].astype(jnp.int32)
    pick = hot_matrix(row == iota((cap, tok), 0))
    value = lane_value(gate[...], eid)
    scaled = (dy_s[...].astype(F32) * value).astype(BF16)
    sent[0, :, :MODEL_WIDTH] = dot(pick, act_two[...]).astype(BF16)
    sent[0, :, MODEL_WIDTH : 2 * MODEL_WIDTH] = dot(pick, scaled).astype(BF16)
    sent[0, :, 2 * MODEL_WIDTH :] = dot(pick, mask[...]).astype(BF16)


def ffn_math(
    rows, d_out, mask, w_gu, w_dn, a_gu, b_gu, a_dn, b_dn,
    ga_gu, gb_gu, ga_dn, gb_dn, acc_out, acc_dx, acc_low, acc_dlow,
):
    low_gu = (dot(rows, a_gu[...]) * mask).astype(BF16)
    dlow_dn = (dot_nt(d_out, b_dn[...]) * mask).astype(BF16)
    for ref in (acc_out, acc_dx, acc_low, acc_dlow):
        ref[...] = jnp.zeros_like(ref)

    def step(j, carry):
        lo = pl.multiple_of(j * HIDDEN_BLOCK, HIDDEN_BLOCK)
        g_cols = pl.ds(lo, HIDDEN_BLOCK)
        u_cols = pl.ds(pl.multiple_of(FEEDFWD_WIDTH + lo, HIDDEN_BLOCK), HIDDEN_BLOCK)
        gate = dot(rows, w_gu[:, g_cols]) + dot(low_gu, b_gu[:, g_cols])
        up = dot(rows, w_gu[:, u_cols]) + dot(low_gu, b_gu[:, u_cols])
        sig = 1.0 / (1.0 + jnp.exp(-gate))
        silu = gate * sig
        middle = (silu * up).astype(BF16)
        acc_out[...] += dot(middle, w_dn[g_cols, :])
        acc_low[...] += dot(middle, a_dn[g_cols, :])
        d_mid = dot_nt(d_out, w_dn[g_cols, :]) + dot_nt(dlow_dn, a_dn[g_cols, :])
        d_mid = d_mid.astype(BF16).astype(F32)
        d_gate = (d_mid * up * (sig * (1.0 + gate * (1.0 - sig)))).astype(BF16)
        d_up = (d_mid * silu).astype(BF16)
        acc_dx[...] += dot_nt(d_gate, w_gu[:, g_cols]) + dot_nt(d_up, w_gu[:, u_cols])
        acc_dlow[...] += dot_nt(d_gate, b_gu[:, g_cols]) + dot_nt(d_up, b_gu[:, u_cols])
        gb_gu[:, g_cols] += dot_tn(low_gu, d_gate)
        gb_gu[:, u_cols] += dot_tn(low_gu, d_up)
        ga_dn[g_cols, :] += dot_tn(middle, dlow_dn)
        return carry

    lax.fori_loop(0, FEEDFWD_WIDTH // HIDDEN_BLOCK, step, 0)
    low_dn = (acc_low[...] * mask).astype(BF16)
    result = (acc_out[...] + dot(low_dn, b_dn[...])).astype(BF16)
    gb_dn[...] += dot_tn(low_dn, d_out)
    dlow_gu = (acc_dlow[...] * mask).astype(BF16)
    d_rows = (acc_dx[...] + dot_nt(dlow_gu, a_gu[...])).astype(BF16)
    ga_gu[...] += dot_tn(rows, dlow_gu)
    return result, d_rows


def ffn_body(
    came, w_gu, w_dn, a_gu, b_gu, a_dn, b_dn,
    back, ga_gu, gb_gu, ga_dn, gb_dn, acc_out, acc_dx, acc_low, acc_dlow,
):
    @pl.when(pl.program_id(0) == 0)
    def _():
        for ref in (ga_gu, gb_gu, ga_dn, gb_dn):
            ref[...] = jnp.zeros_like(ref)

    back[0, :, :MODEL_WIDTH], back[0, :, MODEL_WIDTH:] = ffn_math(
        came[0, :, :MODEL_WIDTH], came[0, :, MODEL_WIDTH : 2 * MODEL_WIDTH],
        came[0, :, 2 * MODEL_WIDTH :].astype(F32), w_gu, w_dn, a_gu, b_gu, a_dn, b_dn,
        ga_gu, gb_gu, ga_dn, gb_dn, acc_out, acc_dx, acc_low, acc_dlow,
    )


def pair_ffn_body(
    sent, wide, mid, thin,
    returned, ga_gu, gb_gu, ga_dn, gb_dn,
    came, back, w_gu, w_dn, a_gu, b_gu, a_dn, b_dn, acc_out, acc_dx, acc_low, acc_dlow,
    load_sems, send_sems, came_sems, back_sems, done_sems,
):
    dp, z = lax.axis_index("dp"), lax.axis_index("expert")
    core, plane = dp % 2, z % 2
    mesh_id = pl.DeviceIdType.MESH

    def peer(k):
        return (dp + (k // 2) * (1 - 2 * core), z + (k % 2) * (1 - 2 * plane))

    barrier = pltpu.get_barrier_semaphore()
    for k in (1, 2, 3):
        pl.semaphore_signal(barrier, inc=1, device_id=peer(k), device_id_type=mesh_id)
    pl.semaphore_wait(barrier, 3)

    def rows_out(k):
        return pltpu.make_async_remote_copy(
            src_ref=sent.at[k], dst_ref=came.at[k], send_sem=send_sems.at[k],
            recv_sem=came_sems.at[k], device_id=peer(k), device_id_type=mesh_id,
        )

    def result_out(k):
        return pltpu.make_async_remote_copy(
            src_ref=back.at[k], dst_ref=returned.at[k], send_sem=back_sems.at[k],
            recv_sem=done_sems.at[k], device_id=peer(k), device_id_type=mesh_id,
        )

    for k in (1, 2, 3):
        rows_out(k).start()
    own_in = pltpu.make_async_copy(sent.at[0], came.at[0], came_sems.at[0])
    own_in.start()

    gu_rows = w_gu.shape[0] // wide.shape[0]
    up_rows = b_gu.shape[0] // wide.shape[0]
    dn_rows = w_dn.shape[0] // wide.shape[0]
    plans = (
        (wide, 0, gu_rows, w_gu), (wide, gu_rows, up_rows, b_gu), (mid, 0, dn_rows, w_dn),
        (mid, dn_rows, up_rows, b_dn), (thin, 0, gu_rows, a_gu), (thin, gu_rows, dn_rows, a_dn),
    )

    def load(d, carry):
        for i, (source, at, count, target) in enumerate(plans):
            pltpu.make_async_copy(
                source.at[d, pl.ds(at, count)],
                target.at[pl.ds(pl.multiple_of(d * count, 16), count)],
                load_sems.at[i],
            ).start()
        return carry

    lax.fori_loop(0, wide.shape[0], load, 0)
    for ref in (ga_gu, gb_gu, ga_dn, gb_dn):
        ref[...] = jnp.zeros_like(ref)
    for i, (_, _, _, target) in enumerate(plans):
        pltpu.make_async_copy(target, target, load_sems.at[i]).wait()

    def source_step(s, carry):
        k = (s % 2) * 2 + s // 2

        @pl.when(s == 0)
        def _():
            own_in.wait()

        @pl.when(s > 0)
        def _():
            rows_out(k).wait_recv()

        back[k, :, :MODEL_WIDTH], back[k, :, MODEL_WIDTH:] = ffn_math(
            came[k, :, :MODEL_WIDTH], came[k, :, MODEL_WIDTH : 2 * MODEL_WIDTH],
            came[k, :, 2 * MODEL_WIDTH :].astype(F32), w_gu, w_dn, a_gu, b_gu, a_dn, b_dn,
            ga_gu, gb_gu, ga_dn, gb_dn, acc_out, acc_dx, acc_low, acc_dlow,
        )

        @pl.when(s > 0)
        def _():
            result_out(k).start()

        return carry

    lax.fori_loop(0, 4, source_step, 0)
    own_out = pltpu.make_async_copy(back.at[0], returned.at[0], done_sems.at[0])
    own_out.start()
    own_out.wait()
    for k in (1, 2, 3):
        rows_out(k).wait_send()
        result_out(k).wait_send()
        result_out(k).wait_recv()


def combine_body(
    experts, kinds, eids, resid, act_two, dy_s, gate, slot, small_s, low_out, attn_low, mask, came,
    w_out, a_out, b_out, router, const_value, gain,
    out_s, d_resid, d_attended, d_logits, ga_out, gb_out,
):
    @pl.when(pl.program_id(0) == 0)
    def _():
        ga_out[...] = jnp.zeros_like(ga_out)
        gb_out[...] = jnp.zeros_like(gb_out)

    rows = resid.shape[0]
    cap = came.shape[1]
    res = resid[...]
    act = act_two[...].astype(F32)
    dy = dy_s[...].astype(F32)
    prob = gate[...]
    lane = iota((rows, LANES), 1)
    out = res
    d_act = jnp.zeros((rows, MODEL_WIDTH), F32)
    d_gate = jnp.zeros((rows, LANES), F32)
    for k in range(came.shape[0]):
        eid = eids[k]
        place = lane_value(slot[...], eid).astype(jnp.int32)
        pick = hot_matrix(place == iota((rows, cap), 1))
        result = dot(pick, came[k, :, :MODEL_WIDTH])
        d_act = d_act + dot(pick, came[k, :, MODEL_WIDTH:])
        d_gate = jnp.where(lane == eid, jnp.sum(dy * result, axis=1, keepdims=True), d_gate)
        out = out + lane_value(prob, eid) * result
    sm = small_s[...]
    first = sm[:, CHOICE_LANE : CHOICE_LANE + 1]
    second = sm[:, CHOICE_LANE + 1 : CHOICE_LANE + 2]

    def chosen(kind):
        return jnp.where((first == kind) | (second == kind), 1.0, 0.0)

    has_copy, has_zero, has_one = chosen(experts + 1), chosen(experts + 2), chosen(experts + 3)
    g_copy = has_copy * prob[:, experts + 1 : experts + 2]
    g_zero = has_zero * prob[:, experts + 2 : experts + 3]
    g_one = has_one * prob[:, experts + 3 : experts + 4]

    def pair(at):
        left, right = prob[:, at : at + 1], prob[:, at + 1 : at + 2]
        top = jnp.maximum(left, right)
        e_left, e_right = jnp.exp(left - top), jnp.exp(right - top)
        return e_left / (e_left + e_right), e_right / (e_left + e_right)

    a00, a01 = pair(CONST_LANE)
    a10, a11 = pair(CONST_LANE + 2)
    v_zero, v_one = const_value[0:1, :], const_value[1:2, :]
    along_act = jnp.sum(dy * act, axis=1, keepdims=True)
    along_zero = jnp.sum(dy * v_zero, axis=1, keepdims=True)
    along_one = jnp.sum(dy * v_one, axis=1, keepdims=True)
    coef = g_copy + g_zero * a00 + g_one * a10
    out = out + coef * act + (g_zero * a01) * v_zero + (g_one * a11) * v_one
    out_s[...] = out.astype(BF16)
    d_gate = jnp.where(lane == experts + 1, has_copy * along_act, d_gate)
    d_gate = jnp.where(
        lane == experts + 2, has_zero * (a00 * along_act + a01 * along_zero), d_gate
    )
    d_gate = jnp.where(lane == experts + 3, has_one * (a10 * along_act + a11 * along_one), d_gate)
    prob = jnp.where(lane < kinds, prob, 0.0)
    d_logit = prob * (d_gate - jnp.sum(prob * d_gate, axis=1, keepdims=True))
    d_logits[...] = d_logit
    mix = d_logit
    for at, g_val, left, right, along in (
        (CONST_LANE, g_zero, a00, a01, along_zero),
        (CONST_LANE + 2, g_one, a10, a11, along_one),
    ):
        da_left, da_right = g_val * along_act, g_val * along
        level = left * da_left + right * da_right
        mix = jnp.where(lane == at, left * (da_left - level), mix)
        mix = jnp.where(lane == at + 1, right * (da_right - level), mix)
    mix_hi = mix.astype(BF16)
    mix_lo = (mix - mix_hi.astype(F32)).astype(BF16)
    d_act = d_act + coef * dy + (dot_nt(mix_hi, router[...]) + dot_nt(mix_lo, router[...]))
    scale = lax.rsqrt(jnp.mean(res * res, axis=-1, keepdims=True) + EPSILON)
    weighted = d_act * gain[...]
    d_res = dy + (
        scale * weighted
        - res * (scale * scale * scale) * jnp.mean(res * weighted, axis=-1, keepdims=True)
    )
    d_resid[...] = d_res
    d_attn = d_res.astype(BF16)
    dlow = (dot_nt(d_attn, b_out[...]) * mask[...].astype(F32)).astype(BF16)
    gb_out[...] += dot_tn(low_out[...], d_attn)
    ga_out[...] += dot_tn(attn_low[...], dlow)
    d_attended[...] = (dot_nt(d_attn, w_out[...]) + dot_nt(dlow, a_out[...])).astype(BF16)


def input_grad_body(
    d_query, d_key, d_value, low_qkv, act_one, mask, hid_s, d_resid, w_qkv, a_in, b_out, gain,
    high, lower, ga_qkv, gb_qkv,
):
    @pl.when(pl.program_id(0) == 0)
    def _():
        ga_qkv[...] = jnp.zeros_like(ga_qkv)
        gb_qkv[...] = jnp.zeros_like(gb_qkv)

    d_low = jnp.zeros((d_query.shape[0], LANES), F32)
    d_act = jnp.zeros((d_query.shape[0], MODEL_WIDTH), F32)
    for part, ref in enumerate((d_query, d_key, d_value)):
        cols = slice(part * MODEL_WIDTH, (part + 1) * MODEL_WIDTH)
        grad = ref[...]
        d_low = d_low + dot_nt(grad, b_out[:, cols])
        d_act = d_act + dot_nt(grad, w_qkv[:, cols])
        gb_qkv[:, cols] += dot_tn(low_qkv[...], grad)
    d_low = (d_low * mask[...].astype(F32)).astype(BF16)
    ga_qkv[...] += dot_tn(act_one[...], d_low)
    d_act = d_act + dot_nt(d_low, a_in[...])
    hid = hid_s[...].astype(F32)
    scale = lax.rsqrt(jnp.mean(hid * hid, axis=-1, keepdims=True) + EPSILON)
    weighted = d_act * gain[...]
    grad_hid = d_resid[...] + (
        scale * weighted
        - hid * (scale * scale * scale) * jnp.mean(hid * weighted, axis=-1, keepdims=True)
    )
    top = grad_hid.astype(BF16)
    high[...] = top
    lower[...] = (grad_hid - top.astype(F32)).astype(BF16)


def to_rows_body(place_col, out_s, d_logits, high, lower, out, grad_hidden, grad_gate):
    rows = out.shape[0]
    tok = out_s.shape[0]
    perm = hot_matrix(place_col[...] == iota((rows, tok), 1))
    out[...] = dot(perm, out_s[...]).astype(BF16)
    grad_hidden[...] = dot(perm, high[...]) + dot(perm, lower[...])
    logits = d_logits[...]
    top = logits.astype(BF16)
    rest = logits - top.astype(F32)
    mid = rest.astype(BF16)
    last = (rest - mid.astype(F32)).astype(BF16)
    grad_gate[...] = dot(perm, top) + (dot(perm, mid) + dot(perm, last))


def split_three(values):
    top = values.astype(BF16)
    rest = values - top.astype(F32)
    mid = rest.astype(BF16)
    return top, mid, (rest - mid.astype(F32)).astype(BF16)


class PairPlan:
    paired = True

    def __init__(self, dp, ex):
        self.axes = ("dp", "expert")
        self.dp, self.ex = dp, ex
        self.h = lax.axis_index("dp") & 1
        self.z = lax.axis_index("expert")
        self.own = (self.z & 1) + 2 * self.h
        self.local = (self.z >> 1) == self.h
        self.groups = [[2 * m + h for m in range(dp // 2)] for h in range(2)]

    def send(self, values, target):
        pairs = []
        for d in range(self.dp):
            for z in range(self.ex):
                goal = target(d, z)
                if goal is not None:
                    pairs.append((d * self.ex + z, goal[0] * self.ex + goal[1]))
        return lax.ppermute(values, self.axes, pairs)

    def gather(self, shard):
        near = self.send(shard, lambda d, z: (d, z ^ 2) if (z >> 1) == (d & 1) else None)
        cross = self.send(shard, lambda d, z: (d ^ 1, z ^ 2) if (z >> 1) != (d & 1) else None)
        over = self.send(shard, lambda d, z: (d ^ 1, z) if (z >> 1) != (d & 1) else None)
        mine = jnp.where(self.local, shard, near)
        other = jnp.where(self.local, over, cross)
        both = jnp.stack([jnp.where(self.h == 0, mine, other), jnp.where(self.h == 0, other, mine)])
        return lax.all_gather(both, "dp", axis=0, tiled=True, axis_index_groups=self.groups)

    def expert_ids(self):
        return self.own ^ jnp.arange(self.ex, dtype=jnp.int32)

    def reduce(self, sums):
        part = lax.psum_scatter(
            sums, "dp", scatter_dimension=0, tiled=True, axis_index_groups=self.groups
        )
        same = jnp.where(self.h == 0, part[0], part[1])
        flip = jnp.where(self.h == 0, part[1], part[0])
        over = self.send(flip, lambda d, z: (d ^ 1, z) if (z >> 1) == (d & 1) else None)
        near = self.send(same, lambda d, z: (d, z ^ 2) if (z >> 1) != (d & 1) else None)
        cross = self.send(flip, lambda d, z: (d ^ 1, z ^ 2) if (z >> 1) != (d & 1) else None)
        first = jnp.where(self.local, same, over).astype(F32)
        return first + near.astype(F32) + cross.astype(F32)

    def reduce_all(self, sums):
        values = sums.reshape((self.dp // 2, 2, self.ex) + sums.shape[1:])
        move = lambda d, z: (d ^ 1, z)
        values = self._halve(values, 1, self.h, move)
        rest = self.dp // 2
        position = lax.axis_index("dp") >> 1
        while rest > 1:
            rest //= 2
            values = values.reshape((2, rest) + values.shape[1:])
            bit = position // rest % 2
            values = self._halve(values, 0, bit, functools.partial(self._flip_dp, 2 * rest))
        values = values[0]
        rest = self.ex
        while rest > 1:
            rest //= 2
            values = values.reshape((2, rest) + values.shape[1:])
            bit = self.z // rest % 2
            values = self._halve(values, 0, bit, functools.partial(self._flip_ex, rest))
        return values[0].astype(F32)

    @staticmethod
    def _flip_dp(bit, d, z):
        return (d ^ bit, z)

    @staticmethod
    def _flip_ex(bit, d, z):
        return (d, z ^ bit)

    def _halve(self, values, axis, bit, move):
        keep = lax.dynamic_index_in_dim(values, bit, axis, keepdims=False)
        give = lax.dynamic_index_in_dim(values, 1 - bit, axis, keepdims=False)
        return (keep.astype(F32) + self.send(give, move).astype(F32)).astype(BF16)


class AxisPlan:
    paired = False

    def __init__(self, dp, ex):
        self.dp, self.ex = dp, ex

    def gather(self, shard):
        return lax.all_gather(shard, "dp", axis=0)

    def expert_ids(self):
        return jnp.arange(self.ex, dtype=jnp.int32)

    def exchange(self, values):
        return lax.all_to_all(values, "expert", split_axis=0, concat_axis=0, tiled=True)

    def reduce(self, sums):
        return lax.psum_scatter(sums, "dp", scatter_dimension=0, tiled=True)[0].astype(F32)

    def reduce_all(self, sums):
        return lax.psum_scatter(
            sums, ("dp", "expert"), scatter_dimension=0, tiled=True
        )[0].astype(F32)


def shards(
    dp_size,
    expert_count,
    hidden_input,
    gate_carryover,
    sequence_length,
    token_stream_place,
    expert_choice_index,
    sequence_adapter,
    attention_gain,
    query_key_weight,
    output_weight,
    adapter_in_query,
    adapter_out_query,
    adapter_in_output,
    adapter_out_output,
    feedfwd_gain,
    router_weight,
    constant_gate,
    constant_value,
    gate_upward_weight,
    down_weight,
    adapter_in_gate,
    adapter_out_gate,
    adapter_in_down,
    adapter_out_down,
    output_gradient,
):
    tok = hidden_input.shape[0]
    width = MODEL_WIDTH
    kinds = expert_count + 4
    devices = dp_size * expert_count
    capacity = 5 * tok // (2 * kinds) // 8 * 8 + 8
    cap = -(-capacity // 16) * 16
    blocks = tok // ROW_BLOCK
    plan = (PairPlan if (dp_size, expert_count) == (8, 4) else AxisPlan)(dp_size, expert_count)

    a_rows, b_rows = query_key_weight.shape[0], adapter_out_query.shape[0]
    own_a = jnp.concatenate(
        [query_key_weight, output_weight, adapter_in_query, adapter_in_output], axis=1
    )
    own_b = jnp.concatenate([adapter_out_query, adapter_out_output], axis=1)
    pad_rows = -(a_rows + b_rows) % 8
    own_attn = jnp.concatenate(
        [
            own_a,
            jnp.pad(own_b, ((0, pad_rows), (0, own_a.shape[1] - own_b.shape[1]))),
        ],
        axis=0,
    )
    attn_all = lax.all_gather(own_attn, ("dp", "expert"), axis=0)
    in_rows = attn_all[:, :a_rows]
    out_rows = attn_all[:, a_rows : a_rows + b_rows]
    w_qkv = in_rows[:, :, : 3 * width].reshape(width, 3 * width)
    w_out = in_rows[:, :, 3 * width : 4 * width].reshape(width, width)
    a_qkv = in_rows[:, :, 4 * width : 4 * width + LANES].reshape(width, LANES)
    a_out = in_rows[:, :, 4 * width + LANES :].reshape(width, LANES)
    b_qkv = out_rows[:, :, : 3 * width].reshape(LANES, 3 * width)
    b_out = out_rows[:, :, 3 * width : 4 * width].reshape(LANES, width)

    gu_rows, up_rows, dn_rows = gate_upward_weight.shape[1], adapter_out_gate.shape[1], down_weight.shape[1]
    wide = plan.gather(jnp.concatenate([gate_upward_weight[0], adapter_out_gate[0]], axis=0))
    mid = plan.gather(jnp.concatenate([down_weight[0], adapter_out_down[0]], axis=0))
    thin = plan.gather(jnp.concatenate([adapter_in_gate[0], adapter_in_down[0]], axis=0))

    place = token_stream_place[0]
    ends = jnp.cumsum(sequence_length[0])
    begins = ends - sequence_length[0]
    stream = jnp.arange(tok, dtype=jnp.int32)
    seg = jnp.sum((stream[:, None] >= ends[None, :]).astype(jnp.int32), axis=1)
    seg_hot = seg[:, None] == jnp.arange(ends.shape[0], dtype=jnp.int32)[None, :]
    start = jnp.sum(jnp.where(seg_hot, begins[None, :], 0), axis=1)
    adapter = jnp.sum(jnp.where(seg_hot, sequence_adapter[0][None, :], 0), axis=1)
    half = HEAD_DIM // 2
    freq = jnp.exp(jnp.arange(half, dtype=F32) * (-math.log(10000.0) / half))
    angle = (stream - start).astype(F32)[:, None] * freq[None, :]
    cos, sin = jnp.cos(angle), jnp.sin(angle)
    cosine = jnp.concatenate([cos, cos, cos, cos], axis=1)
    sine = jnp.concatenate([-sin, sin, -sin, sin], axis=1)
    starts = start[:, None]
    mask = (jnp.arange(LANES)[None, :] // ADAPTER_RANK == adapter[:, None]).astype(BF16)
    top, middle, last = split_three(gate_carryover)
    gap = jnp.zeros((tok, 16 - kinds), BF16)
    small = jnp.concatenate(
        [top, gap, middle, gap, last, gap, expert_choice_index.astype(BF16),
         jnp.zeros((tok, LANES - CHOICE_LANE - 2), BF16)],
        axis=1,
    )
    gain_one = attention_gain.astype(F32)[None, :]
    gain_two = feedfwd_gain.astype(F32)[None, :]
    router = jnp.concatenate(
        [router_weight, jnp.zeros((width, CONST_LANE - kinds), BF16), constant_gate,
         jnp.zeros((width, LANES - CONST_LANE - 4), BF16)],
        axis=1,
    )
    const_value = constant_value.astype(F32)

    full = whole
    hid_s, dy_s, small_s, act_one, low_qkv, query, key, value = call(
        proj_in_body,
        (blocks,),
        [full((1, tok)), full((tok, width)), full((tok, width)), full((tok, LANES)),
         row_spec(LANES), row_spec(LANES), row_spec(LANES), full((1, width)),
         full((width, 3 * width)), full((width, LANES)), full((LANES, 3 * width))],
        [row_spec(width), row_spec(width), row_spec(LANES), row_spec(width), row_spec(LANES),
         row_spec(width), row_spec(width), row_spec(width)],
        [sds((tok, width), BF16), sds((tok, width), BF16), sds((tok, LANES), F32),
         sds((tok, width), BF16), sds((tok, LANES), BF16), sds((tok, width), BF16),
         sds((tok, width), BF16), sds((tok, width), BF16)],
        name="proj_in",
    )(place[None, :], hidden_input, output_gradient, small, cosine, sine, mask, gain_one,
      w_qkv, a_qkv, b_qkv)

    pairs = HEAD_COUNT // 2
    attn_low, lse = call(
        attention_fwd_body,
        (pairs,),
        [col_spec(tok)] * 3 + [full((tok, 1))],
        [col_spec(tok), col_spec(tok)],
        [sds((tok, width), BF16), sds((tok, width), F32)],
        name="attention_fwd",
    )(query, key, value, starts)

    low_out, resid, act_two, gate = call(
        functools.partial(post_attn_body, kinds),
        (blocks,),
        [row_spec(width), row_spec(width), row_spec(LANES), row_spec(LANES), full((width, width)),
         full((width, LANES)), full((LANES, width)), full((width, LANES)), full((1, width))],
        [row_spec(LANES), row_spec(width), row_spec(width), row_spec(LANES)],
        [sds((tok, LANES), BF16), sds((tok, width), F32), sds((tok, width), BF16),
         sds((tok, LANES), F32)],
        name="post_attn",
    )(attn_low, hid_s, mask, small_s, w_out, a_out, b_out, router, gain_two)

    eids = plan.expert_ids()
    smem = pl.BlockSpec(memory_space=pltpu.SMEM)
    sent_width = 2 * width + LANES
    slot, sent = call(
        functools.partial(dispatch_body, expert_count),
        (expert_count,),
        [smem, full((tok, LANES)), full((tok, LANES)), full((tok, width)), full((tok, width)),
         full((tok, LANES))],
        [full((tok, LANES)), pl.BlockSpec((1, cap, sent_width), lambda i: (i, 0, 0))],
        [sds((tok, LANES), F32), sds((expert_count, cap, sent_width), BF16)],
        scratch=[pltpu.VMEM((LANES, tok), F32)],
        name="dispatch",
    )(eids, small_s, gate, act_two, dy_s, mask)

    grad_shapes = [
        sds((width, LANES), F32), sds((LANES, 2 * FEEDFWD_WIDTH), F32),
        sds((FEEDFWD_WIDTH, LANES), F32), sds((LANES, width), F32),
    ]
    accumulators = [
        pltpu.VMEM((cap, width), F32), pltpu.VMEM((cap, width), F32),
        pltpu.VMEM((cap, LANES), F32), pltpu.VMEM((cap, LANES), F32),
    ]
    if plan.paired:
        hbm = pl.BlockSpec(memory_space=pl.ANY)
        vmem = pl.BlockSpec(memory_space=pltpu.VMEM)
        returned, ga_gu, gb_gu, ga_dn, gb_dn = pl.pallas_call(
            pair_ffn_body,
            in_specs=[hbm] * 4,
            out_specs=[hbm] + [vmem] * 4,
            out_shape=[sds((expert_count, cap, 2 * width), BF16)] + grad_shapes,
            scratch_shapes=[
                pltpu.VMEM((expert_count, cap, sent_width), BF16),
                pltpu.VMEM((expert_count, cap, 2 * width), BF16),
                pltpu.VMEM((width, 2 * FEEDFWD_WIDTH), BF16), pltpu.VMEM((FEEDFWD_WIDTH, width), BF16),
                pltpu.VMEM((width, LANES), BF16), pltpu.VMEM((LANES, 2 * FEEDFWD_WIDTH), BF16),
                pltpu.VMEM((FEEDFWD_WIDTH, LANES), BF16), pltpu.VMEM((LANES, width), BF16),
                *accumulators,
                pltpu.SemaphoreType.DMA((6,)),
                *[pltpu.SemaphoreType.DMA((expert_count,)) for _ in range(4)],
            ],
            compiler_params=pltpu.CompilerParams(
                vmem_limit_bytes=VMEM_BYTES, collective_id=1, has_side_effects=True
            ),
            name="pair_ffn",
        )(sent, wide, mid, thin)
    else:
        w_gu = wide[:, :gu_rows].reshape(width, 2 * FEEDFWD_WIDTH)
        b_gu = wide[:, gu_rows:].reshape(LANES, 2 * FEEDFWD_WIDTH)
        w_dn = mid[:, :dn_rows].reshape(FEEDFWD_WIDTH, width)
        b_dn = mid[:, dn_rows:].reshape(LANES, width)
        a_gu = thin[:, :gu_rows].reshape(width, LANES)
        a_dn = thin[:, gu_rows:].reshape(FEEDFWD_WIDTH, LANES)
        came = plan.exchange(sent)
        back, ga_gu, gb_gu, ga_dn, gb_dn = call(
            ffn_body,
            (expert_count,),
            [pl.BlockSpec((1, cap, sent_width), lambda i: (i, 0, 0)),
             full((width, 2 * FEEDFWD_WIDTH)), full((FEEDFWD_WIDTH, width)), full((width, LANES)),
             full((LANES, 2 * FEEDFWD_WIDTH)), full((FEEDFWD_WIDTH, LANES)), full((LANES, width))],
            [pl.BlockSpec((1, cap, 2 * width), lambda i: (i, 0, 0)), full((width, LANES)),
             full((LANES, 2 * FEEDFWD_WIDTH)), full((FEEDFWD_WIDTH, LANES)), full((LANES, width))],
            [sds((expert_count, cap, 2 * width), BF16)] + grad_shapes,
            scratch=accumulators,
            name="ffn",
        )(came, w_gu, w_dn, a_gu, b_gu, a_dn, b_dn)
        returned = plan.exchange(back)

    owned_wide = plan.reduce(
        jnp.concatenate([gb_gu, gb_dn], axis=1).astype(BF16).reshape(dp_size, up_rows, -1)
    )
    owned_thin = plan.reduce(
        jnp.concatenate(
            [ga_gu.reshape(dp_size, gu_rows, LANES), ga_dn.reshape(dp_size, dn_rows, LANES)], axis=1
        ).astype(BF16)
    )

    out_s, d_resid, d_attended, d_logits, ga_out, gb_out = call(
        functools.partial(combine_body, expert_count, kinds),
        (blocks,),
        [smem, row_spec(width), row_spec(width), row_spec(width), row_spec(LANES), row_spec(LANES),
         row_spec(LANES), row_spec(LANES), row_spec(width), row_spec(LANES),
         full((expert_count, cap, 2 * width)), full((width, width)), full((width, LANES)),
         full((LANES, width)), full((width, LANES)), full((2, width)), full((1, width))],
        [row_spec(width), row_spec(width), row_spec(width), row_spec(LANES), full((width, LANES)),
         full((LANES, width))],
        [sds((tok, width), BF16), sds((tok, width), F32), sds((tok, width), BF16),
         sds((tok, LANES), F32), sds((width, LANES), F32), sds((LANES, width), F32)],
        name="combine",
    )(eids, resid, act_two, dy_s, gate, slot, small_s, low_out, attn_low, mask, returned,
      w_out, a_out, b_out, router, const_value, gain_two)

    d_query, d_key, d_value = call(
        attention_bwd_body,
        (pairs,),
        [col_spec(tok)] * 6 + [full((tok, 1)), full((tok, LANES)), full((tok, LANES))],
        [col_spec(tok)] * 3,
        [sds((tok, width), BF16)] * 3,
        scratch=[pltpu.VMEM((tok, LANES), F32), pltpu.VMEM((tok, LANES), F32)],
        name="attention_bwd",
    )(query, key, value, d_attended, attn_low, lse, starts, cosine, sine)

    high, lower, ga_qkv, gb_qkv = call(
        input_grad_body,
        (blocks,),
        [row_spec(width)] * 3 + [row_spec(LANES), row_spec(width), row_spec(LANES), row_spec(width),
         row_spec(width), full((width, 3 * width)), full((width, LANES)), full((LANES, 3 * width)),
         full((1, width))],
        [row_spec(width), row_spec(width), full((width, LANES)), full((LANES, 3 * width))],
        [sds((tok, width), BF16), sds((tok, width), BF16), sds((width, LANES), F32),
         sds((LANES, 3 * width), F32)],
        name="input_grad",
    )(d_query, d_key, d_value, low_qkv, act_one, mask, hid_s, d_resid, w_qkv, a_qkv, b_qkv,
      gain_one)

    owned = plan.reduce_all(
        jnp.concatenate(
            [
                ga_qkv.reshape(devices, b_rows, -1),
                ga_out.reshape(devices, b_rows, -1),
                gb_qkv.reshape(devices, b_rows, -1),
                gb_out.reshape(devices, b_rows, -1),
            ],
            axis=2,
        ).astype(BF16)
    )

    output, grad_hidden, grad_gate = call(
        to_rows_body,
        (blocks,),
        [row_spec(1), full((tok, width)), full((tok, LANES)), full((tok, width)),
         full((tok, width))],
        [row_spec(width), row_spec(width), row_spec(LANES)],
        [sds((tok, width), BF16), sds((tok, width), F32), sds((tok, LANES), F32)],
        name="to_rows",
    )(place[:, None], out_s, d_logits, high, lower)

    return (
        output,
        grad_hidden,
        grad_gate[:, :kinds],
        owned[:, :width].reshape(a_rows, LANES),
        owned[:, 2 * width : 5 * width],
        owned[:, width : 2 * width].reshape(a_rows, LANES),
        owned[:, 5 * width :],
        owned_thin[None, :gu_rows],
        owned_wide[None, :, : 2 * FEEDFWD_WIDTH],
        owned_thin[None, gu_rows:],
        owned_wide[None, :, 2 * FEEDFWD_WIDTH :],
    )


def solution(mesh):
    rows = P(("dp", "expert"), None)
    expert_rows = P("expert", "dp", None)
    in_specs = (
        (rows,) * 6 + (P(),) + (rows,) * 6 + (P(),) * 4 + (expert_rows,) * 6 + (rows,)
    )
    out_specs = (rows,) * 7 + (expert_rows,) * 4
    body = functools.partial(shards, mesh.shape["dp"], mesh.shape["expert"])
    return jax.shard_map(body, mesh=mesh, in_specs=in_specs, out_specs=out_specs, check_vma=False)
```

```python
import functools
import math

import jax
import jax.numpy as jnp
from jax import lax
from jax.experimental import pallas as pl
from jax.experimental.pallas import tpu as pltpu
from jax.sharding import PartitionSpec as P

MODEL_WIDTH = 768
HEAD_COUNT = 12
HEAD_DIM = 64
FEEDFWD_WIDTH = 2048
ADAPTER_RANK = 16
ROW_BLOCK = 256
HIDDEN_BLOCK = 512
LANES = 128
CONST_LANE = 64
CHOICE_LANE = 48
EPSILON = 1e-06
VMEM_BYTES = 60 * 2**20
MESH_ID = pl.DeviceIdType.MESH

F32 = jnp.float32
BF16 = jnp.bfloat16


def dot(a, b):
    return jnp.dot(a, b, preferred_element_type=F32)


def dot_nt(a, b):
    return lax.dot_general(a, b, (((1,), (1,)), ((), ())), preferred_element_type=F32)


def dot_tn(a, b):
    return lax.dot_general(a, b, (((0,), (0,)), ((), ())), preferred_element_type=F32)


def iota(shape, dim):
    return lax.broadcasted_iota(jnp.int32, shape, dim)


def hot_matrix(condition):
    return jnp.where(condition, 1.0, 0.0).astype(BF16)


def whole(shape):
    zeros = (0,) * len(shape)
    return pl.BlockSpec(shape, lambda *_: zeros)


def row_spec(width, rows=ROW_BLOCK):
    return pl.BlockSpec((rows, width), lambda i: (i, 0))


def col_spec(rows, width=LANES):
    return pl.BlockSpec((rows, width), lambda j: (0, j))


def sds(shape, dtype):
    return jax.ShapeDtypeStruct(shape, dtype)


def call(body, grid, in_specs, out_specs, out_shape, scratch=(), name=None):
    return pl.pallas_call(
        body,
        grid=grid,
        in_specs=in_specs,
        out_specs=out_specs,
        out_shape=out_shape,
        scratch_shapes=list(scratch),
        compiler_params=pltpu.CompilerParams(vmem_limit_bytes=VMEM_BYTES),
        name=name,
    )


def half_swap(values):
    lane = iota(values.shape, 1)
    up = pltpu.roll(values, 32, 1)
    down = pltpu.roll(values, LANES - 32, 1)
    return jnp.where(lane % HEAD_DIM < HEAD_DIM // 2, down, up)


def lane_value(values, lane_id):
    return jnp.sum(jnp.where(iota(values.shape, 1) == lane_id, values, 0.0), axis=1, keepdims=True)


def proj_in_body(
    place_row, hidden, upstream, small, cosine, sine, mask, gain, w_qkv, a_in, b_out,
    hid_s, dy_s, small_s, act_one, low_qkv, query, key, value,
):
    rows = hid_s.shape[0]
    base = pl.program_id(0) * rows
    perm = hot_matrix(place_row[...] == base + iota((rows, place_row.shape[1]), 0))
    hid = dot(perm, hidden[...])
    hid_s[...] = hid.astype(BF16)
    dy_s[...] = dot(perm, upstream[...]).astype(BF16)
    small_s[...] = dot(perm, small[...])
    scale = lax.rsqrt(jnp.mean(hid * hid, axis=-1, keepdims=True) + EPSILON)
    act = (hid * scale * gain[...]).astype(BF16)
    act_one[...] = act
    low = (dot(act, a_in[...]) * mask[...].astype(F32)).astype(BF16)
    low_qkv[...] = low
    cos, sin = cosine[...], sine[...]
    for out, start, factor in ((query, 0, HEAD_DIM**-0.5), (key, MODEL_WIDTH, 1.0)):
        vals = dot(act, w_qkv[:, start : start + MODEL_WIDTH]) + dot(
            low, b_out[:, start : start + MODEL_WIDTH]
        )
        for c in range(MODEL_WIDTH // LANES):
            piece = vals[:, c * LANES : (c + 1) * LANES]
            turned = (piece * cos + half_swap(piece) * sin).astype(BF16)
            if factor != 1.0:
                turned = turned * jnp.asarray(factor, BF16)
            out[:, c * LANES : (c + 1) * LANES] = turned
    value[...] = (
        dot(act, w_qkv[:, 2 * MODEL_WIDTH :]) + dot(low, b_out[:, 2 * MODEL_WIDTH :])
    ).astype(BF16)


def head_mask(shape, head):
    lane = iota(shape, 1)
    return (lane >= head * HEAD_DIM) & (lane < (head + 1) * HEAD_DIM)


def attention_fwd_body(query, key, value, starts, attended, lse):
    tok = query.shape[0]
    size = ROW_BLOCK
    zero = jnp.zeros((), BF16)
    for blk in range(tok // size):
        lo, hi = blk * size, (blk + 1) * size
        q_blk = query[lo:hi, :]
        k_all = key[:hi, :]
        v_all = value[:hi, :]
        begin = starts[lo:hi, :]
        col = iota((size, hi), 1)
        allowed = (col <= lo + iota((size, hi), 0)) & (col >= begin)
        total = jnp.zeros((size, LANES), F32)
        stats = jnp.zeros((size, LANES), F32)
        for head in range(2):
            mine = head_mask((size, LANES), head)
            scores = dot_nt(jnp.where(mine, q_blk, zero), k_all)
            scores = jnp.where(allowed, scores, -1000000000.0)
            top = jnp.max(scores, axis=1, keepdims=True)
            expo = jnp.exp(scores - top)
            norm = jnp.sum(expo, axis=1, keepdims=True)
            v_head = jnp.where(head_mask((hi, LANES), head), v_all, zero)
            total = total + dot(expo.astype(BF16), v_head) * (1.0 / norm)
            stats = jnp.where(mine, top + jnp.log(norm), stats)
        attended[lo:hi, :] = total.astype(BF16)
        lse[lo:hi, :] = stats


def attention_bwd_body(
    query, key, value, dout, attended, lse, starts, cosine, sine, d_query, d_key, d_value, kacc, vacc
):
    tok = query.shape[0]
    size = ROW_BLOCK
    zero = jnp.zeros((), BF16)
    kacc[...] = jnp.zeros_like(kacc)
    vacc[...] = jnp.zeros_like(vacc)
    for blk in range(tok // size):
        lo, hi = blk * size, (blk + 1) * size
        q_blk = query[lo:hi, :]
        do_blk = dout[lo:hi, :]
        k_all = key[:hi, :]
        v_all = value[:hi, :]
        begin = starts[lo:hi, :]
        col = iota((size, hi), 1)
        allowed = (col <= lo + iota((size, hi), 0)) & (col >= begin)
        prod = do_blk.astype(F32) * attended[lo:hi, :].astype(F32)
        q_total = jnp.zeros((size, LANES), F32)
        for head in range(2):
            mine = head_mask((size, LANES), head)
            q_head = jnp.where(mine, q_blk, zero)
            do_head = jnp.where(mine, do_blk, zero)
            lse_head = lse[lo:hi, head * HEAD_DIM : head * HEAD_DIM + 1]
            delta = jnp.sum(jnp.where(mine, prod, 0.0), axis=1, keepdims=True)
            scores = dot_nt(q_head, k_all)
            prob = jnp.where(allowed, jnp.exp(jnp.minimum(scores - lse_head, 0.0)), 0.0)
            dprob = dot_nt(do_head, v_all)
            dscore = (prob * (dprob - delta)).astype(BF16)
            k_head = jnp.where(head_mask((hi, LANES), head), k_all, zero)
            q_total = q_total + dot(dscore, k_head)
            kacc[:hi, :] += dot_tn(dscore, q_head)
            vacc[:hi, :] += dot_tn(prob.astype(BF16), do_head)
        q_total = q_total * HEAD_DIM**-0.5
        d_query[lo:hi, :] = (
            q_total * cosine[lo:hi, :] - half_swap(q_total) * sine[lo:hi, :]
        ).astype(BF16)
    for blk in range(tok // size):
        lo, hi = blk * size, (blk + 1) * size
        k_total = kacc[lo:hi, :]
        d_key[lo:hi, :] = (
            k_total * cosine[lo:hi, :] - half_swap(k_total) * sine[lo:hi, :]
        ).astype(BF16)
    d_value[...] = vacc[...].astype(BF16)


def start_kernel(send_to, hear_from, count):
    barrier = pltpu.get_barrier_semaphore()
    for device, remote in hear_from:
        if remote is None:
            pl.semaphore_signal(barrier, inc=1, device_id=device, device_id_type=MESH_ID)
        else:

            @pl.when(remote)
            def _(device=device):
                pl.semaphore_signal(barrier, inc=1, device_id=device, device_id_type=MESH_ID)

    pl.semaphore_wait(barrier, count)


def pair_attention_bwd_body(
    query, key, value, dout, attended, lse, starts, cosine, sine, ga_gu, gb_gu, ga_dn, gb_dn,
    d_query, d_key, d_value, own_ga_gu, own_gb_gu, own_ga_dn, own_gb_dn,
    kacc, vacc, r_ga_gu, r_gb_gu, r_ga_dn, r_gb_dn, send_sems, recv_sems,
):
    dp, z = lax.axis_index("dp"), lax.axis_index("expert")
    core, spot, half = dp % 2, dp // 2, z // 2
    own = z % 2 + 2 * core
    far = (z + 2) % 4
    at_home = core == half
    away = 1 - (core * half + (1 - core) * (1 - half))
    slot = 2 * spot + away
    groups = (
        (ga_gu, r_ga_gu, own_ga_gu), (gb_gu, r_gb_gu, own_gb_gu),
        (ga_dn, r_ga_dn, own_ga_dn), (gb_dn, r_gb_dn, own_gb_dn),
    )
    owners = 8

    def piece(i, d):
        source, target, _ = groups[i]
        count = target.shape[1]
        return source.at[pl.ds(pl.multiple_of(d * count, 16), count)]

    def push(i, d):
        return pltpu.make_async_remote_copy(
            src_ref=piece(i, d), dst_ref=groups[i][1].at[slot], send_sem=send_sems.at[i, d],
            recv_sem=recv_sems.at[i, slot], device_id=(d, own), device_id_type=MESH_ID,
        )

    def keep(i):
        return pltpu.make_async_copy(
            piece(i, dp), groups[i][1].at[2 * spot], recv_sems.at[i, 2 * spot]
        )

    def arrival(i, s):
        return pltpu.make_async_remote_copy(
            src_ref=piece(i, 0), dst_ref=groups[i][1].at[s], send_sem=send_sems.at[i, 0],
            recv_sem=recv_sems.at[i, s], device_id=(0, own), device_id_type=MESH_ID,
        )

    @pl.when(pl.program_id(0) == 0)
    def _():
        senders = []
        for m in range(owners // 2):
            device = 2 * m + half
            senders.append(((device, z), device != dp))
            senders.append(((device, far), None))
        start_kernel(None, senders, owners - 1 + away)

        def send(d, carry):
            mine = at_home & (d == dp)

            @pl.when(mine)
            def _():
                for i in range(4):
                    keep(i).start()

            @pl.when(jnp.logical_not(mine))
            def _():
                for i in range(4):
                    push(i, d).start()

            return carry

        lax.fori_loop(0, owners, send, 0)

    attention_bwd_body(
        query, key, value, dout, attended, lse, starts, cosine, sine, d_query, d_key, d_value,
        kacc, vacc,
    )

    @pl.when(pl.program_id(0) == pl.num_programs(0) - 1)
    def _():
        def finish(s, carry):
            mine = at_home & (s == 2 * spot)

            @pl.when(mine)
            def _():
                for i in range(4):
                    keep(i).wait()

            @pl.when(jnp.logical_not(mine))
            def _():
                for i in range(4):
                    arrival(i, s).wait_recv()

            @pl.when(jnp.logical_not(at_home & (s == dp)))
            def _():
                for i in range(4):
                    push(i, s).wait_send()

            return carry

        lax.fori_loop(0, owners, finish, 0)
        for _, target, out in groups:
            total = target[0].astype(F32)
            for s in range(1, owners):
                total = total + target[s].astype(F32)
            out[...] = total


def pair_tail_body(
    place_col, d_query, d_key, d_value, low_qkv, act_one, mask, a_in, b_out, gain, ga_out, gb_out,
    d_logits, hid_hbm, resid_hbm, w_hbm, out_hbm,
    out, grad_hidden, grad_gate, own_ga_qkv, own_gb_qkv, own_ga_out, own_gb_out,
    hid_s, d_resid, w_qkv, out_s, high, lower, d_low_all, ga_sum, gb_sum,
    s_ga_qkv, s_gb_qkv, s_ga_out, s_gb_out, r_ga_qkv, r_gb_qkv, r_ga_out, r_gb_out,
    thin_out, wide_out, thin_in, wide_in, load_sems, send_sems, recv_sems, far_send, far_recv,
):
    dp, z = lax.axis_index("dp"), lax.axis_index("expert")
    others, planes = 7, 3
    tok = place_col.shape[0]
    blocks = tok // ROW_BLOCK
    loads = [
        pltpu.make_async_copy(source, target, load_sems.at[i])
        for i, (source, target) in enumerate(
            ((w_hbm, w_qkv), (hid_hbm, hid_s), (resid_hbm, d_resid), (out_hbm, out_s))
        )
    ]
    for load in loads:
        load.start()
    start_kernel(
        None,
        [(((dp + i) % 8, z), None) for i in range(1, 8)] + [((dp, (z + j) % 4), None) for j in (1, 2, 3)],
        others + planes,
    )
    ga_sum[...] = jnp.zeros_like(ga_sum)
    gb_sum[...] = jnp.zeros_like(gb_sum)
    parts = [slice(p * MODEL_WIDTH, (p + 1) * MODEL_WIDTH) for p in range(3)]
    d_refs = (d_query, d_key, d_value)

    def block_rows(b):
        return pl.ds(pl.multiple_of(b * ROW_BLOCK, ROW_BLOCK), ROW_BLOCK)

    def sums(b, carry):
        rows = block_rows(b)
        low = low_qkv[rows, :]
        d_low = jnp.zeros((ROW_BLOCK, LANES), F32)
        for cols, ref in zip(parts, d_refs):
            grad = ref[rows, :]
            d_low = d_low + dot_nt(grad, b_out[:, cols])
            gb_sum[:, cols] += dot_tn(low, grad)
        d_low = (d_low * mask[rows, :].astype(F32)).astype(BF16)
        d_low_all[rows, :] = d_low
        ga_sum[...] += dot_tn(act_one[rows, :], d_low)
        return carry

    lax.fori_loop(0, blocks, sums, 0)
    s_ga_qkv[...] = ga_sum[...].astype(BF16)
    s_gb_qkv[...] = gb_sum[...].astype(BF16)
    s_ga_out[...] = ga_out[...].astype(BF16)
    s_gb_out[...] = gb_out[...].astype(BF16)
    groups = (
        (s_ga_qkv, r_ga_qkv), (s_gb_qkv, r_gb_qkv), (s_ga_out, r_ga_out), (s_gb_out, r_gb_out),
    )

    def share(i, d):
        count = groups[i][1].shape[1]
        return groups[i][0].at[pl.ds(pl.multiple_of(d * count, 16), count)]

    def near(i, n):
        goal = (dp + n + 1) % 8
        return pltpu.make_async_remote_copy(
            src_ref=share(i, goal), dst_ref=groups[i][1].at[n], send_sem=send_sems.at[i, n],
            recv_sem=recv_sems.at[i, n], device_id=(goal, z), device_id_type=MESH_ID,
        )

    def send_near(n, carry):
        for i in range(4):
            near(i, n).start()
        return carry

    lax.fori_loop(0, others, send_near, 0)

    for load in loads[:3]:
        load.wait()

    def back(b, carry):
        rows = block_rows(b)
        d_act = dot_nt(d_low_all[rows, :], a_in[...])
        for cols, ref in zip(parts, d_refs):
            d_act = d_act + dot_nt(ref[rows, :], w_qkv[:, cols])
        hid = hid_s[rows, :].astype(F32)
        scale = lax.rsqrt(jnp.mean(hid * hid, axis=-1, keepdims=True) + EPSILON)
        weighted = d_act * gain[...]
        grad_hid = d_resid[rows, :] + (
            scale * weighted
            - hid * (scale * scale * scale) * jnp.mean(hid * weighted, axis=-1, keepdims=True)
        )
        top = grad_hid.astype(BF16)
        high[rows, :] = top
        lower[rows, :] = (grad_hid - top.astype(F32)).astype(BF16)
        return carry

    lax.fori_loop(0, blocks, back, 0)

    def near_done(n, carry):
        for i in range(4):
            near(i, n).wait_recv()
        return carry

    lax.fori_loop(0, others, near_done, 0)
    totals = []
    for i in range(4):
        total = share(i, dp)[...].astype(F32)
        for n in range(others):
            total = total + groups[i][1][n].astype(F32)
        totals.append(total)
    a_qkv, b_qkv, a_o, b_o = totals
    a_count, b_count = a_qkv.shape[0] // 4, b_qkv.shape[0] // 4
    for p in range(4):
        a_rows, b_rows = slice(p * a_count, (p + 1) * a_count), slice(p * b_count, (p + 1) * b_count)
        thin_out[p, :a_count, :LANES] = a_qkv[a_rows].astype(BF16)
        thin_out[p, :a_count, LANES:] = a_o[a_rows].astype(BF16)
        thin_out[p, a_count:, :] = jnp.zeros((thin_out.shape[1] - a_count, 2 * LANES), BF16)
        wide_out[p] = jnp.concatenate(
            [b_qkv[b_rows, cols] for cols in parts] + [b_o[b_rows]], axis=0
        ).astype(BF16)

    def far(i, j):
        goal = (z + j + 1) % 4
        source, target = ((thin_out, thin_in), (wide_out, wide_in))[i]
        return pltpu.make_async_remote_copy(
            src_ref=source.at[goal], dst_ref=target.at[j], send_sem=far_send.at[i, j],
            recv_sem=far_recv.at[i, j], device_id=(dp, goal), device_id_type=MESH_ID,
        )

    for j in range(planes):
        for i in range(2):
            far(i, j).start()
    loads[3].wait()

    def to_rows(b, carry):
        rows = block_rows(b)
        perm = hot_matrix(place_col[rows, :] == iota((ROW_BLOCK, tok), 1))
        out[rows, :] = dot(perm, out_s[...]).astype(BF16)
        grad_hidden[rows, :] = dot(perm, high[...]) + dot(perm, lower[...])
        top, mid, last = split_three(d_logits[...])
        grad_gate[rows, :] = dot(perm, top) + (dot(perm, mid) + dot(perm, last))
        return carry

    lax.fori_loop(0, blocks, to_rows, 0)
    for j in range(planes):
        for i in range(2):
            far(i, j).wait_recv()
    thin = thin_out[z].astype(F32)
    wide = wide_out[z].astype(F32)
    for j in range(planes):
        thin = thin + thin_in[j].astype(F32)
        wide = wide + wide_in[j].astype(F32)
    own_ga_qkv[...] = thin[:a_count, :LANES]
    own_ga_out[...] = thin[:a_count, LANES:]
    for p, cols in enumerate(parts):
        own_gb_qkv[:, cols] = wide[p * b_count : (p + 1) * b_count]
    own_gb_out[...] = wide[3 * b_count : 4 * b_count]

    def sent(n, carry):
        for i in range(4):
            near(i, n).wait_send()
        return carry

    lax.fori_loop(0, others, sent, 0)
    for j in range(planes):
        for i in range(2):
            far(i, j).wait_send()


def split_three(values):
    top = values.astype(BF16)
    rest = values - top.astype(F32)
    mid = rest.astype(BF16)
    return top, mid, (rest - mid.astype(F32)).astype(BF16)


def post_attn_body(
    kinds, attn_low, hid_s, mask, small_s, w_out, a_out, b_out, router, gain,
    low_out, resid, act_two, gate,
):
    attn = attn_low[...]
    low = (dot(attn, a_out[...]) * mask[...].astype(F32)).astype(BF16)
    low_out[...] = low
    res = hid_s[...].astype(F32) + (dot(attn, w_out[...]) + dot(low, b_out[...]))
    resid[...] = res
    scale = lax.rsqrt(jnp.mean(res * res, axis=-1, keepdims=True) + EPSILON)
    act = (res * scale * gain[...]).astype(BF16)
    act_two[...] = act
    sm = small_s[...]
    carry = sm + (pltpu.roll(sm, LANES - 16, 1) + pltpu.roll(sm, LANES - 32, 1))
    logits = dot(act, router[...])
    lane = iota(logits.shape, 1)
    routed = jnp.where(lane < kinds, logits + carry, -1e30)
    top = jnp.max(routed, axis=1, keepdims=True)
    expo = jnp.exp(routed - top)
    prob = expo / jnp.sum(expo, axis=1, keepdims=True)
    gate[...] = jnp.where(lane < kinds, prob, logits)


def dispatch_body(experts, eids, small_s, gate, act_two, dy_s, mask, slot, sent, slot_rows):
    tok = act_two.shape[0]
    cap = sent.shape[1]
    step = pl.program_id(0)

    @pl.when(step == 0)
    def _():
        lane = iota((tok, LANES), 1)
        first = small_s[:, CHOICE_LANE : CHOICE_LANE + 1].astype(jnp.int32)
        second = small_s[:, CHOICE_LANE + 1 : CHOICE_LANE + 2].astype(jnp.int32)
        hot = ((first == lane) | (second == lane)) & (lane < experts)
        hot_low = hot_matrix(hot)
        for blk in range(tok // ROW_BLOCK):
            lo, hi = blk * ROW_BLOCK, (blk + 1) * ROW_BLOCK
            tri = hot_matrix(iota((ROW_BLOCK, hi), 1) < lo + iota((ROW_BLOCK, hi), 0))
            rank = dot(tri, hot_low[:hi, :])
            slot[lo:hi, :] = jnp.where(hot[lo:hi, :], rank, -1.0)
        slot_rows[...] = slot[...].T

    eid = eids[step]
    row = slot_rows[pl.ds(eid, 1), :].astype(jnp.int32)
    pick = hot_matrix(row == iota((cap, tok), 0))
    value = lane_value(gate[...], eid)
    scaled = (dy_s[...].astype(F32) * value).astype(BF16)
    sent[0, :, :MODEL_WIDTH] = dot(pick, act_two[...]).astype(BF16)
    sent[0, :, MODEL_WIDTH : 2 * MODEL_WIDTH] = dot(pick, scaled).astype(BF16)
    sent[0, :, 2 * MODEL_WIDTH :] = dot(pick, mask[...]).astype(BF16)


def ffn_math(
    rows, d_out, mask, w_gu, w_dn, a_gu, b_gu, a_dn, b_dn,
    ga_gu, gb_gu, ga_dn, gb_dn, acc_out, acc_dx, acc_low, acc_dlow,
):
    low_gu = (dot(rows, a_gu[...]) * mask).astype(BF16)
    dlow_dn = (dot_nt(d_out, b_dn[...]) * mask).astype(BF16)
    for ref in (acc_out, acc_dx, acc_low, acc_dlow):
        ref[...] = jnp.zeros_like(ref)

    def step(j, carry):
        lo = pl.multiple_of(j * HIDDEN_BLOCK, HIDDEN_BLOCK)
        g_cols = pl.ds(lo, HIDDEN_BLOCK)
        u_cols = pl.ds(pl.multiple_of(FEEDFWD_WIDTH + lo, HIDDEN_BLOCK), HIDDEN_BLOCK)
        gate = dot(rows, w_gu[:, g_cols]) + dot(low_gu, b_gu[:, g_cols])
        up = dot(rows, w_gu[:, u_cols]) + dot(low_gu, b_gu[:, u_cols])
        sig = 1.0 / (1.0 + jnp.exp(-gate))
        silu = gate * sig
        middle = (silu * up).astype(BF16)
        acc_out[...] += dot(middle, w_dn[g_cols, :])
        acc_low[...] += dot(middle, a_dn[g_cols, :])
        d_mid = dot_nt(d_out, w_dn[g_cols, :]) + dot_nt(dlow_dn, a_dn[g_cols, :])
        d_mid = d_mid.astype(BF16).astype(F32)
        d_gate = (d_mid * up * (sig * (1.0 + gate * (1.0 - sig)))).astype(BF16)
        d_up = (d_mid * silu).astype(BF16)
        acc_dx[...] += dot_nt(d_gate, w_gu[:, g_cols]) + dot_nt(d_up, w_gu[:, u_cols])
        acc_dlow[...] += dot_nt(d_gate, b_gu[:, g_cols]) + dot_nt(d_up, b_gu[:, u_cols])
        gb_gu[:, g_cols] += dot_tn(low_gu, d_gate)
        gb_gu[:, u_cols] += dot_tn(low_gu, d_up)
        ga_dn[g_cols, :] += dot_tn(middle, dlow_dn)
        return carry

    lax.fori_loop(0, FEEDFWD_WIDTH // HIDDEN_BLOCK, step, 0)
    low_dn = (acc_low[...] * mask).astype(BF16)
    result = (acc_out[...] + dot(low_dn, b_dn[...])).astype(BF16)
    gb_dn[...] += dot_tn(low_dn, d_out)
    dlow_gu = (acc_dlow[...] * mask).astype(BF16)
    d_rows = (acc_dx[...] + dot_nt(dlow_gu, a_gu[...])).astype(BF16)
    ga_gu[...] += dot_tn(rows, dlow_gu)
    return result, d_rows


def ffn_body(
    came, w_gu, w_dn, a_gu, b_gu, a_dn, b_dn,
    back, ga_gu, gb_gu, ga_dn, gb_dn, acc_out, acc_dx, acc_low, acc_dlow,
):
    @pl.when(pl.program_id(0) == 0)
    def _():
        for ref in (ga_gu, gb_gu, ga_dn, gb_dn):
            ref[...] = jnp.zeros_like(ref)

    back[0, :, :MODEL_WIDTH], back[0, :, MODEL_WIDTH:] = ffn_math(
        came[0, :, :MODEL_WIDTH], came[0, :, MODEL_WIDTH : 2 * MODEL_WIDTH],
        came[0, :, 2 * MODEL_WIDTH :].astype(F32), w_gu, w_dn, a_gu, b_gu, a_dn, b_dn,
        ga_gu, gb_gu, ga_dn, gb_dn, acc_out, acc_dx, acc_low, acc_dlow,
    )


def pair_ffn_body(
    sent, wide, mid, thin,
    returned, out_ga_gu, out_gb_gu, out_ga_dn, out_gb_dn,
    came, back, ga_gu, gb_gu, ga_dn, gb_dn, w_gu, w_dn, a_gu, b_gu, a_dn, b_dn, acc_out, acc_dx, acc_low, acc_dlow,
    load_sems, send_sems, came_sems, back_sems, done_sems,
):
    dp, z = lax.axis_index("dp"), lax.axis_index("expert")
    core, plane = dp % 2, z % 2

    def peer(k):
        return (dp + (k // 2) * (1 - 2 * core), z + (k % 2) * (1 - 2 * plane))

    barrier = pltpu.get_barrier_semaphore()
    for k in (1, 2, 3):
        pl.semaphore_signal(barrier, inc=1, device_id=peer(k), device_id_type=MESH_ID)
    pl.semaphore_wait(barrier, 3)

    def rows_out(k):
        return pltpu.make_async_remote_copy(
            src_ref=sent.at[k], dst_ref=came.at[k], send_sem=send_sems.at[k],
            recv_sem=came_sems.at[k], device_id=peer(k), device_id_type=MESH_ID,
        )

    def result_out(k):
        return pltpu.make_async_remote_copy(
            src_ref=back.at[k], dst_ref=returned.at[k], send_sem=back_sems.at[k],
            recv_sem=done_sems.at[k], device_id=peer(k), device_id_type=MESH_ID,
        )

    for k in (1, 2, 3):
        rows_out(k).start()
    own_in = pltpu.make_async_copy(sent.at[0], came.at[0], came_sems.at[0])
    own_in.start()

    gu_rows = w_gu.shape[0] // wide.shape[0]
    up_rows = b_gu.shape[0] // wide.shape[0]
    dn_rows = w_dn.shape[0] // wide.shape[0]
    plans = (
        (wide, 0, gu_rows, w_gu), (wide, gu_rows, up_rows, b_gu), (mid, 0, dn_rows, w_dn),
        (mid, dn_rows, up_rows, b_dn), (thin, 0, gu_rows, a_gu), (thin, gu_rows, dn_rows, a_dn),
    )

    def load(d, carry):
        for i, (source, at, count, target) in enumerate(plans):
            pltpu.make_async_copy(
                source.at[d, pl.ds(at, count)],
                target.at[pl.ds(pl.multiple_of(d * count, 16), count)],
                load_sems.at[i],
            ).start()
        return carry

    lax.fori_loop(0, wide.shape[0], load, 0)
    for ref in (ga_gu, gb_gu, ga_dn, gb_dn):
        ref[...] = jnp.zeros_like(ref)
    for i, (_, _, _, target) in enumerate(plans):
        pltpu.make_async_copy(target, target, load_sems.at[i]).wait()

    def source_step(s, carry):
        k = (s % 2) * 2 + s // 2

        @pl.when(s == 0)
        def _():
            own_in.wait()

        @pl.when(s > 0)
        def _():
            rows_out(k).wait_recv()

        back[k, :, :MODEL_WIDTH], back[k, :, MODEL_WIDTH:] = ffn_math(
            came[k, :, :MODEL_WIDTH], came[k, :, MODEL_WIDTH : 2 * MODEL_WIDTH],
            came[k, :, 2 * MODEL_WIDTH :].astype(F32), w_gu, w_dn, a_gu, b_gu, a_dn, b_dn,
            ga_gu, gb_gu, ga_dn, gb_dn, acc_out, acc_dx, acc_low, acc_dlow,
        )

        @pl.when(s > 0)
        def _():
            result_out(k).start()

        return carry

    lax.fori_loop(0, 4, source_step, 0)
    for out, total in (
        (out_ga_gu, ga_gu), (out_gb_gu, gb_gu), (out_ga_dn, ga_dn), (out_gb_dn, gb_dn),
    ):
        out[...] = total[...].astype(BF16)
    own_out = pltpu.make_async_copy(back.at[0], returned.at[0], done_sems.at[0])
    own_out.start()
    own_out.wait()
    for k in (1, 2, 3):
        rows_out(k).wait_send()
        result_out(k).wait_send()
        result_out(k).wait_recv()


def combine_body(
    experts, kinds, eids, resid, act_two, dy_s, gate, slot, small_s, low_out, attn_low, mask, came,
    w_out, a_out, b_out, router, const_value, gain,
    out_s, d_resid, d_attended, d_logits, ga_out, gb_out,
):
    @pl.when(pl.program_id(0) == 0)
    def _():
        ga_out[...] = jnp.zeros_like(ga_out)
        gb_out[...] = jnp.zeros_like(gb_out)

    rows = resid.shape[0]
    cap = came.shape[1]
    res = resid[...]
    act = act_two[...].astype(F32)
    dy = dy_s[...].astype(F32)
    prob = gate[...]
    lane = iota((rows, LANES), 1)
    out = res
    d_act = jnp.zeros((rows, MODEL_WIDTH), F32)
    d_gate = jnp.zeros((rows, LANES), F32)
    for k in range(came.shape[0]):
        eid = eids[k]
        place = lane_value(slot[...], eid).astype(jnp.int32)
        pick = hot_matrix(place == iota((rows, cap), 1))
        result = dot(pick, came[k, :, :MODEL_WIDTH])
        d_act = d_act + dot(pick, came[k, :, MODEL_WIDTH:])
        d_gate = jnp.where(lane == eid, jnp.sum(dy * result, axis=1, keepdims=True), d_gate)
        out = out + lane_value(prob, eid) * result
    sm = small_s[...]
    first = sm[:, CHOICE_LANE : CHOICE_LANE + 1]
    second = sm[:, CHOICE_LANE + 1 : CHOICE_LANE + 2]

    def chosen(kind):
        return jnp.where((first == kind) | (second == kind), 1.0, 0.0)

    has_copy, has_zero, has_one = chosen(experts + 1), chosen(experts + 2), chosen(experts + 3)
    g_copy = has_copy * prob[:, experts + 1 : experts + 2]
    g_zero = has_zero * prob[:, experts + 2 : experts + 3]
    g_one = has_one * prob[:, experts + 3 : experts + 4]

    def pair(at):
        left, right = prob[:, at : at + 1], prob[:, at + 1 : at + 2]
        top = jnp.maximum(left, right)
        e_left, e_right = jnp.exp(left - top), jnp.exp(right - top)
        return e_left / (e_left + e_right), e_right / (e_left + e_right)

    a00, a01 = pair(CONST_LANE)
    a10, a11 = pair(CONST_LANE + 2)
    v_zero, v_one = const_value[0:1, :], const_value[1:2, :]
    along_act = jnp.sum(dy * act, axis=1, keepdims=True)
    along_zero = jnp.sum(dy * v_zero, axis=1, keepdims=True)
    along_one = jnp.sum(dy * v_one, axis=1, keepdims=True)
    coef = g_copy + g_zero * a00 + g_one * a10
    out = out + coef * act + (g_zero * a01) * v_zero + (g_one * a11) * v_one
    out_s[...] = out.astype(BF16)
    d_gate = jnp.where(lane == experts + 1, has_copy * along_act, d_gate)
    d_gate = jnp.where(
        lane == experts + 2, has_zero * (a00 * along_act + a01 * along_zero), d_gate
    )
    d_gate = jnp.where(lane == experts + 3, has_one * (a10 * along_act + a11 * along_one), d_gate)
    prob = jnp.where(lane < kinds, prob, 0.0)
    d_logit = prob * (d_gate - jnp.sum(prob * d_gate, axis=1, keepdims=True))
    d_logits[...] = d_logit
    mix = d_logit
    for at, g_val, left, right, along in (
        (CONST_LANE, g_zero, a00, a01, along_zero),
        (CONST_LANE + 2, g_one, a10, a11, along_one),
    ):
        da_left, da_right = g_val * along_act, g_val * along
        level = left * da_left + right * da_right
        mix = jnp.where(lane == at, left * (da_left - level), mix)
        mix = jnp.where(lane == at + 1, right * (da_right - level), mix)
    mix_hi = mix.astype(BF16)
    mix_lo = (mix - mix_hi.astype(F32)).astype(BF16)
    d_act = d_act + coef * dy + (dot_nt(mix_hi, router[...]) + dot_nt(mix_lo, router[...]))
    scale = lax.rsqrt(jnp.mean(res * res, axis=-1, keepdims=True) + EPSILON)
    weighted = d_act * gain[...]
    d_res = dy + (
        scale * weighted
        - res * (scale * scale * scale) * jnp.mean(res * weighted, axis=-1, keepdims=True)
    )
    d_resid[...] = d_res
    d_attn = d_res.astype(BF16)
    dlow = (dot_nt(d_attn, b_out[...]) * mask[...].astype(F32)).astype(BF16)
    gb_out[...] += dot_tn(low_out[...], d_attn)
    ga_out[...] += dot_tn(attn_low[...], dlow)
    d_attended[...] = (dot_nt(d_attn, w_out[...]) + dot_nt(dlow, a_out[...])).astype(BF16)


def input_grad_body(
    d_query, d_key, d_value, low_qkv, act_one, mask, hid_s, d_resid, w_qkv, a_in, b_out, gain,
    high, lower, ga_qkv, gb_qkv,
):
    @pl.when(pl.program_id(0) == 0)
    def _():
        ga_qkv[...] = jnp.zeros_like(ga_qkv)
        gb_qkv[...] = jnp.zeros_like(gb_qkv)

    d_low = jnp.zeros((d_query.shape[0], LANES), F32)
    d_act = jnp.zeros((d_query.shape[0], MODEL_WIDTH), F32)
    for part, ref in enumerate((d_query, d_key, d_value)):
        cols = slice(part * MODEL_WIDTH, (part + 1) * MODEL_WIDTH)
        grad = ref[...]
        d_low = d_low + dot_nt(grad, b_out[:, cols])
        d_act = d_act + dot_nt(grad, w_qkv[:, cols])
        gb_qkv[:, cols] += dot_tn(low_qkv[...], grad)
    d_low = (d_low * mask[...].astype(F32)).astype(BF16)
    ga_qkv[...] += dot_tn(act_one[...], d_low)
    d_act = d_act + dot_nt(d_low, a_in[...])
    hid = hid_s[...].astype(F32)
    scale = lax.rsqrt(jnp.mean(hid * hid, axis=-1, keepdims=True) + EPSILON)
    weighted = d_act * gain[...]
    grad_hid = d_resid[...] + (
        scale * weighted
        - hid * (scale * scale * scale) * jnp.mean(hid * weighted, axis=-1, keepdims=True)
    )
    top = grad_hid.astype(BF16)
    high[...] = top
    lower[...] = (grad_hid - top.astype(F32)).astype(BF16)


def to_rows_body(place_col, out_s, d_logits, high, lower, out, grad_hidden, grad_gate):
    rows = out.shape[0]
    tok = out_s.shape[0]
    perm = hot_matrix(place_col[...] == iota((rows, tok), 1))
    out[...] = dot(perm, out_s[...]).astype(BF16)
    grad_hidden[...] = dot(perm, high[...]) + dot(perm, lower[...])
    logits = d_logits[...]
    top = logits.astype(BF16)
    rest = logits - top.astype(F32)
    mid = rest.astype(BF16)
    last = (rest - mid.astype(F32)).astype(BF16)
    grad_gate[...] = dot(perm, top) + (dot(perm, mid) + dot(perm, last))


class PairPlan:
    paired = True

    def __init__(self, dp, ex):
        self.axes = ("dp", "expert")
        self.dp, self.ex = dp, ex
        self.h = lax.axis_index("dp") & 1
        self.z = lax.axis_index("expert")
        self.own = (self.z & 1) + 2 * self.h
        self.local = (self.z >> 1) == self.h
        self.groups = [[2 * m + h for m in range(dp // 2)] for h in range(2)]

    def send(self, values, target):
        pairs = []
        for d in range(self.dp):
            for z in range(self.ex):
                goal = target(d, z)
                if goal is not None:
                    pairs.append((d * self.ex + z, goal[0] * self.ex + goal[1]))
        return lax.ppermute(values, self.axes, pairs)

    def gather(self, shard):
        near = self.send(shard, lambda d, z: (d, z ^ 2) if (z >> 1) == (d & 1) else None)
        cross = self.send(shard, lambda d, z: (d ^ 1, z ^ 2) if (z >> 1) != (d & 1) else None)
        over = self.send(shard, lambda d, z: (d ^ 1, z) if (z >> 1) != (d & 1) else None)
        mine = jnp.where(self.local, shard, near)
        other = jnp.where(self.local, over, cross)
        both = jnp.stack([jnp.where(self.h == 0, mine, other), jnp.where(self.h == 0, other, mine)])
        return lax.all_gather(both, "dp", axis=0, tiled=True, axis_index_groups=self.groups)

    def expert_ids(self):
        return self.own ^ jnp.arange(self.ex, dtype=jnp.int32)


class AxisPlan:
    paired = False

    def __init__(self, dp, ex):
        self.dp, self.ex = dp, ex

    def gather(self, shard):
        return lax.all_gather(shard, "dp", axis=0)

    def expert_ids(self):
        return jnp.arange(self.ex, dtype=jnp.int32)

    def exchange(self, values):
        return lax.all_to_all(values, "expert", split_axis=0, concat_axis=0, tiled=True)

    def reduce(self, sums):
        return lax.psum_scatter(sums, "dp", scatter_dimension=0, tiled=True)[0].astype(F32)

    def reduce_all(self, sums):
        return lax.psum_scatter(
            sums, ("dp", "expert"), scatter_dimension=0, tiled=True
        )[0].astype(F32)


def shards(
    dp_size,
    expert_count,
    hidden_input,
    gate_carryover,
    sequence_length,
    token_stream_place,
    expert_choice_index,
    sequence_adapter,
    attention_gain,
    query_key_weight,
    output_weight,
    adapter_in_query,
    adapter_out_query,
    adapter_in_output,
    adapter_out_output,
    feedfwd_gain,
    router_weight,
    constant_gate,
    constant_value,
    gate_upward_weight,
    down_weight,
    adapter_in_gate,
    adapter_out_gate,
    adapter_in_down,
    adapter_out_down,
    output_gradient,
):
    tok = hidden_input.shape[0]
    width = MODEL_WIDTH
    kinds = expert_count + 4
    devices = dp_size * expert_count
    capacity = 5 * tok // (2 * kinds) // 8 * 8 + 8
    cap = -(-capacity // 16) * 16
    blocks = tok // ROW_BLOCK
    plan = (PairPlan if (dp_size, expert_count) == (8, 4) else AxisPlan)(dp_size, expert_count)

    a_rows, b_rows = query_key_weight.shape[0], adapter_out_query.shape[0]
    own_a = jnp.concatenate(
        [query_key_weight, output_weight, adapter_in_query, adapter_in_output], axis=1
    )
    own_b = jnp.concatenate([adapter_out_query, adapter_out_output], axis=1)
    pad_rows = -(a_rows + b_rows) % 8
    own_attn = jnp.concatenate(
        [
            own_a,
            jnp.pad(own_b, ((0, pad_rows), (0, own_a.shape[1] - own_b.shape[1]))),
        ],
        axis=0,
    )
    attn_all = lax.all_gather(own_attn, ("dp", "expert"), axis=0)
    in_rows = attn_all[:, :a_rows]
    out_rows = attn_all[:, a_rows : a_rows + b_rows]
    w_qkv = in_rows[:, :, : 3 * width].reshape(width, 3 * width)
    w_out = in_rows[:, :, 3 * width : 4 * width].reshape(width, width)
    a_qkv = in_rows[:, :, 4 * width : 4 * width + LANES].reshape(width, LANES)
    a_out = in_rows[:, :, 4 * width + LANES :].reshape(width, LANES)
    b_qkv = out_rows[:, :, : 3 * width].reshape(LANES, 3 * width)
    b_out = out_rows[:, :, 3 * width : 4 * width].reshape(LANES, width)

    gu_rows, up_rows, dn_rows = gate_upward_weight.shape[1], adapter_out_gate.shape[1], down_weight.shape[1]
    wide = plan.gather(jnp.concatenate([gate_upward_weight[0], adapter_out_gate[0]], axis=0))
    mid = plan.gather(jnp.concatenate([down_weight[0], adapter_out_down[0]], axis=0))
    thin = plan.gather(jnp.concatenate([adapter_in_gate[0], adapter_in_down[0]], axis=0))

    place = token_stream_place[0]
    ends = jnp.cumsum(sequence_length[0])
    begins = ends - sequence_length[0]
    stream = jnp.arange(tok, dtype=jnp.int32)
    seg = jnp.sum((stream[:, None] >= ends[None, :]).astype(jnp.int32), axis=1)
    seg_hot = seg[:, None] == jnp.arange(ends.shape[0], dtype=jnp.int32)[None, :]
    start = jnp.sum(jnp.where(seg_hot, begins[None, :], 0), axis=1)
    adapter = jnp.sum(jnp.where(seg_hot, sequence_adapter[0][None, :], 0), axis=1)
    half = HEAD_DIM // 2
    freq = jnp.exp(jnp.arange(half, dtype=F32) * (-math.log(10000.0) / half))
    angle = (stream - start).astype(F32)[:, None] * freq[None, :]
    cos, sin = jnp.cos(angle), jnp.sin(angle)
    cosine = jnp.concatenate([cos, cos, cos, cos], axis=1)
    sine = jnp.concatenate([-sin, sin, -sin, sin], axis=1)
    starts = start[:, None]
    mask = (jnp.arange(LANES)[None, :] // ADAPTER_RANK == adapter[:, None]).astype(BF16)
    top, middle, last = split_three(gate_carryover)
    gap = jnp.zeros((tok, 16 - kinds), BF16)
    small = jnp.concatenate(
        [top, gap, middle, gap, last, gap, expert_choice_index.astype(BF16),
         jnp.zeros((tok, LANES - CHOICE_LANE - 2), BF16)],
        axis=1,
    )
    gain_one = attention_gain.astype(F32)[None, :]
    gain_two = feedfwd_gain.astype(F32)[None, :]
    router = jnp.concatenate(
        [router_weight, jnp.zeros((width, CONST_LANE - kinds), BF16), constant_gate,
         jnp.zeros((width, LANES - CONST_LANE - 4), BF16)],
        axis=1,
    )
    const_value = constant_value.astype(F32)

    full = whole
    hid_s, dy_s, small_s, act_one, low_qkv, query, key, value = call(
        proj_in_body,
        (blocks,),
        [full((1, tok)), full((tok, width)), full((tok, width)), full((tok, LANES)),
         row_spec(LANES), row_spec(LANES), row_spec(LANES), full((1, width)),
         full((width, 3 * width)), full((width, LANES)), full((LANES, 3 * width))],
        [row_spec(width), row_spec(width), row_spec(LANES), row_spec(width), row_spec(LANES),
         row_spec(width), row_spec(width), row_spec(width)],
        [sds((tok, width), BF16), sds((tok, width), BF16), sds((tok, LANES), F32),
         sds((tok, width), BF16), sds((tok, LANES), BF16), sds((tok, width), BF16),
         sds((tok, width), BF16), sds((tok, width), BF16)],
        name="proj_in",
    )(place[None, :], hidden_input, output_gradient, small, cosine, sine, mask, gain_one,
      w_qkv, a_qkv, b_qkv)

    pairs = HEAD_COUNT // 2
    attn_low, lse = call(
        attention_fwd_body,
        (pairs,),
        [col_spec(tok)] * 3 + [full((tok, 1))],
        [col_spec(tok), col_spec(tok)],
        [sds((tok, width), BF16), sds((tok, width), F32)],
        name="attention_fwd",
    )(query, key, value, starts)

    low_out, resid, act_two, gate = call(
        functools.partial(post_attn_body, kinds),
        (blocks,),
        [row_spec(width), row_spec(width), row_spec(LANES), row_spec(LANES), full((width, width)),
         full((width, LANES)), full((LANES, width)), full((width, LANES)), full((1, width))],
        [row_spec(LANES), row_spec(width), row_spec(width), row_spec(LANES)],
        [sds((tok, LANES), BF16), sds((tok, width), F32), sds((tok, width), BF16),
         sds((tok, LANES), F32)],
        name="post_attn",
    )(attn_low, hid_s, mask, small_s, w_out, a_out, b_out, router, gain_two)

    eids = plan.expert_ids()
    smem = pl.BlockSpec(memory_space=pltpu.SMEM)
    sent_width = 2 * width + LANES
    slot, sent = call(
        functools.partial(dispatch_body, expert_count),
        (expert_count,),
        [smem, full((tok, LANES)), full((tok, LANES)), full((tok, width)), full((tok, width)),
         full((tok, LANES))],
        [full((tok, LANES)), pl.BlockSpec((1, cap, sent_width), lambda i: (i, 0, 0))],
        [sds((tok, LANES), F32), sds((expert_count, cap, sent_width), BF16)],
        scratch=[pltpu.VMEM((LANES, tok), F32)],
        name="dispatch",
    )(eids, small_s, gate, act_two, dy_s, mask)

    grad_shapes = [
        sds((width, LANES), F32), sds((LANES, 2 * FEEDFWD_WIDTH), F32),
        sds((FEEDFWD_WIDTH, LANES), F32), sds((LANES, width), F32),
    ]
    accumulators = [
        pltpu.VMEM((cap, width), F32), pltpu.VMEM((cap, width), F32),
        pltpu.VMEM((cap, LANES), F32), pltpu.VMEM((cap, LANES), F32),
    ]
    hbm = pl.BlockSpec(memory_space=pl.ANY)
    vmem = pl.BlockSpec(memory_space=pltpu.VMEM)
    if plan.paired:
        returned, ga_gu, gb_gu, ga_dn, gb_dn = pl.pallas_call(
            pair_ffn_body,
            in_specs=[hbm] * 4,
            out_specs=[hbm] + [vmem] * 4,
            out_shape=[sds((expert_count, cap, 2 * width), BF16)]
            + [sds(g.shape, BF16) for g in grad_shapes],
            scratch_shapes=[
                pltpu.VMEM((expert_count, cap, sent_width), BF16),
                pltpu.VMEM((expert_count, cap, 2 * width), BF16),
                *[pltpu.VMEM(g.shape, F32) for g in grad_shapes],
                pltpu.VMEM((width, 2 * FEEDFWD_WIDTH), BF16), pltpu.VMEM((FEEDFWD_WIDTH, width), BF16),
                pltpu.VMEM((width, LANES), BF16), pltpu.VMEM((LANES, 2 * FEEDFWD_WIDTH), BF16),
                pltpu.VMEM((FEEDFWD_WIDTH, LANES), BF16), pltpu.VMEM((LANES, width), BF16),
                *accumulators,
                pltpu.SemaphoreType.DMA((6,)),
                *[pltpu.SemaphoreType.DMA((expert_count,)) for _ in range(4)],
            ],
            compiler_params=pltpu.CompilerParams(
                vmem_limit_bytes=VMEM_BYTES, collective_id=1, has_side_effects=True
            ),
            name="pair_ffn",
        )(sent, wide, mid, thin)
    else:
        w_gu = wide[:, :gu_rows].reshape(width, 2 * FEEDFWD_WIDTH)
        b_gu = wide[:, gu_rows:].reshape(LANES, 2 * FEEDFWD_WIDTH)
        w_dn = mid[:, :dn_rows].reshape(FEEDFWD_WIDTH, width)
        b_dn = mid[:, dn_rows:].reshape(LANES, width)
        a_gu = thin[:, :gu_rows].reshape(width, LANES)
        a_dn = thin[:, gu_rows:].reshape(FEEDFWD_WIDTH, LANES)
        came = plan.exchange(sent)
        back, ga_gu, gb_gu, ga_dn, gb_dn = call(
            ffn_body,
            (expert_count,),
            [pl.BlockSpec((1, cap, sent_width), lambda i: (i, 0, 0)),
             full((width, 2 * FEEDFWD_WIDTH)), full((FEEDFWD_WIDTH, width)), full((width, LANES)),
             full((LANES, 2 * FEEDFWD_WIDTH)), full((FEEDFWD_WIDTH, LANES)), full((LANES, width))],
            [pl.BlockSpec((1, cap, 2 * width), lambda i: (i, 0, 0)), full((width, LANES)),
             full((LANES, 2 * FEEDFWD_WIDTH)), full((FEEDFWD_WIDTH, LANES)), full((LANES, width))],
            [sds((expert_count, cap, 2 * width), BF16)] + grad_shapes,
            scratch=accumulators,
            name="ffn",
        )(came, w_gu, w_dn, a_gu, b_gu, a_dn, b_dn)
        returned = plan.exchange(back)

    out_s, d_resid, d_attended, d_logits, ga_out, gb_out = call(
        functools.partial(combine_body, expert_count, kinds),
        (blocks,),
        [smem, row_spec(width), row_spec(width), row_spec(width), row_spec(LANES), row_spec(LANES),
         row_spec(LANES), row_spec(LANES), row_spec(width), row_spec(LANES),
         full((expert_count, cap, 2 * width)), full((width, width)), full((width, LANES)),
         full((LANES, width)), full((width, LANES)), full((2, width)), full((1, width))],
        [row_spec(width), row_spec(width), row_spec(width), row_spec(LANES), full((width, LANES)),
         full((LANES, width))],
        [sds((tok, width), BF16), sds((tok, width), F32), sds((tok, width), BF16),
         sds((tok, LANES), F32), sds((width, LANES), F32), sds((LANES, width), F32)],
        name="combine",
    )(eids, resid, act_two, dy_s, gate, slot, small_s, low_out, attn_low, mask, returned,
      w_out, a_out, b_out, router, const_value, gain_two)

    if plan.paired:
        flow = dict(vmem_limit_bytes=VMEM_BYTES, has_side_effects=True)
        own_shapes = [
            sds((gu_rows, LANES), F32), sds((up_rows, 2 * FEEDFWD_WIDTH), F32),
            sds((dn_rows, LANES), F32), sds((up_rows, width), F32),
        ]
        d_query, d_key, d_value, *expert_owned = pl.pallas_call(
            pair_attention_bwd_body,
            grid=(pairs,),
            in_specs=[col_spec(tok)] * 6
            + [full((tok, 1)), full((tok, LANES)), full((tok, LANES))]
            + [hbm] * 4,
            out_specs=[col_spec(tok)] * 3 + [full(s.shape) for s in own_shapes],
            out_shape=[sds((tok, width), BF16)] * 3 + own_shapes,
            scratch_shapes=[pltpu.VMEM((tok, LANES), F32), pltpu.VMEM((tok, LANES), F32)]
            + [pltpu.VMEM((dp_size,) + s.shape, BF16) for s in own_shapes]
            + [pltpu.SemaphoreType.DMA((4, dp_size)), pltpu.SemaphoreType.DMA((4, dp_size))],
            compiler_params=pltpu.CompilerParams(collective_id=2, **flow),
            name="pair_attention_bwd",
        )(query, key, value, d_attended, attn_low, lse, starts, cosine, sine,
          ga_gu, gb_gu, ga_dn, gb_dn)
        sum_shapes = [(width, LANES), (LANES, 3 * width), (width, LANES), (LANES, width)]
        got_shapes = [(dp_size - 1, a // dp_size, b) for a, b in sum_shapes]
        thin_rows = -(-a_rows // 16) * 16
        output, grad_hidden, grad_gate, *attn_owned = pl.pallas_call(
            pair_tail_body,
            in_specs=[vmem] * 13 + [hbm] * 4,
            out_specs=[vmem] * 7,
            out_shape=[
                sds((tok, width), BF16), sds((tok, width), F32), sds((tok, LANES), F32),
                sds((a_rows, LANES), F32), sds((b_rows, 3 * width), F32),
                sds((a_rows, LANES), F32), sds((b_rows, width), F32),
            ],
            scratch_shapes=[
                pltpu.VMEM((tok, width), BF16), pltpu.VMEM((tok, width), F32),
                pltpu.VMEM((width, 3 * width), BF16), pltpu.VMEM((tok, width), BF16),
                pltpu.VMEM((tok, width), BF16), pltpu.VMEM((tok, width), BF16),
                pltpu.VMEM((tok, LANES), BF16),
                pltpu.VMEM((width, LANES), F32), pltpu.VMEM((LANES, 3 * width), F32),
                *[pltpu.VMEM(shape, BF16) for shape in sum_shapes + got_shapes],
                pltpu.VMEM((expert_count, thin_rows, 2 * LANES), BF16),
                pltpu.VMEM((expert_count, 4 * b_rows, width), BF16),
                pltpu.VMEM((expert_count - 1, thin_rows, 2 * LANES), BF16),
                pltpu.VMEM((expert_count - 1, 4 * b_rows, width), BF16),
                pltpu.SemaphoreType.DMA((4,)),
                pltpu.SemaphoreType.DMA((4, dp_size - 1)), pltpu.SemaphoreType.DMA((4, dp_size - 1)),
                pltpu.SemaphoreType.DMA((2, expert_count - 1)),
                pltpu.SemaphoreType.DMA((2, expert_count - 1)),
            ],
            compiler_params=pltpu.CompilerParams(collective_id=3, **flow),
            name="pair_tail",
        )(place[:, None], d_query, d_key, d_value, low_qkv, act_one, mask, a_qkv, b_qkv, gain_one,
          ga_out, gb_out, d_logits, hid_s, d_resid, w_qkv, out_s)
        return (
            output, grad_hidden, grad_gate[:, :kinds], *attn_owned,
            *[expert_owned[i][None] for i in range(4)],
        )

    owned_wide = plan.reduce(
        jnp.concatenate([gb_gu, gb_dn], axis=1).astype(BF16).reshape(dp_size, up_rows, -1)
    )
    owned_thin = plan.reduce(
        jnp.concatenate(
            [ga_gu.reshape(dp_size, gu_rows, LANES), ga_dn.reshape(dp_size, dn_rows, LANES)], axis=1
        ).astype(BF16)
    )

    d_query, d_key, d_value = call(
        attention_bwd_body,
        (pairs,),
        [col_spec(tok)] * 6 + [full((tok, 1)), full((tok, LANES)), full((tok, LANES))],
        [col_spec(tok)] * 3,
        [sds((tok, width), BF16)] * 3,
        scratch=[pltpu.VMEM((tok, LANES), F32), pltpu.VMEM((tok, LANES), F32)],
        name="attention_bwd",
    )(query, key, value, d_attended, attn_low, lse, starts, cosine, sine)

    high, lower, ga_qkv, gb_qkv = call(
        input_grad_body,
        (blocks,),
        [row_spec(width)] * 3 + [row_spec(LANES), row_spec(width), row_spec(LANES), row_spec(width),
         row_spec(width), full((width, 3 * width)), full((width, LANES)), full((LANES, 3 * width)),
         full((1, width))],
        [row_spec(width), row_spec(width), full((width, LANES)), full((LANES, 3 * width))],
        [sds((tok, width), BF16), sds((tok, width), BF16), sds((width, LANES), F32),
         sds((LANES, 3 * width), F32)],
        name="input_grad",
    )(d_query, d_key, d_value, low_qkv, act_one, mask, hid_s, d_resid, w_qkv, a_qkv, b_qkv,
      gain_one)

    owned = plan.reduce_all(
        jnp.concatenate(
            [
                ga_qkv.reshape(devices, b_rows, -1),
                ga_out.reshape(devices, b_rows, -1),
                gb_qkv.reshape(devices, b_rows, -1),
                gb_out.reshape(devices, b_rows, -1),
            ],
            axis=2,
        ).astype(BF16)
    )

    output, grad_hidden, grad_gate = call(
        to_rows_body,
        (blocks,),
        [row_spec(1), full((tok, width)), full((tok, LANES)), full((tok, width)),
         full((tok, width))],
        [row_spec(width), row_spec(width), row_spec(LANES)],
        [sds((tok, width), BF16), sds((tok, width), F32), sds((tok, LANES), F32)],
        name="to_rows",
    )(place[:, None], out_s, d_logits, high, lower)

    return (
        output,
        grad_hidden,
        grad_gate[:, :kinds],
        owned[:, :width].reshape(a_rows, LANES),
        owned[:, 2 * width : 5 * width],
        owned[:, width : 2 * width].reshape(a_rows, LANES),
        owned[:, 5 * width :],
        owned_thin[None, :gu_rows],
        owned_wide[None, :, : 2 * FEEDFWD_WIDTH],
        owned_thin[None, gu_rows:],
        owned_wide[None, :, 2 * FEEDFWD_WIDTH :],
    )


def solution(mesh):
    rows = P(("dp", "expert"), None)
    expert_rows = P("expert", "dp", None)
    in_specs = (
        (rows,) * 6 + (P(),) + (rows,) * 6 + (P(),) * 4 + (expert_rows,) * 6 + (rows,)
    )
    out_specs = (rows,) * 7 + (expert_rows,) * 4
    body = functools.partial(shards, mesh.shape["dp"], mesh.shape["expert"])
    return jax.shard_map(body, mesh=mesh, in_specs=in_specs, out_specs=out_specs, check_vma=False)
```

```python
import functools
import math

import jax
import jax.numpy as jnp
from jax import lax
from jax.experimental import pallas as pl
from jax.experimental.pallas import tpu as pltpu
from jax.sharding import PartitionSpec as P

MODEL_WIDTH = 768
HEAD_COUNT = 12
HEAD_DIM = 64
FEEDFWD_WIDTH = 2048
ADAPTER_RANK = 16
ROW_BLOCK = 256
HIDDEN_BLOCK = 512
LANES = 128
CONST_LANE = 64
CHOICE_LANE = 48
EPSILON = 1e-06
VMEM_BYTES = 60 * 2**20
MESH_ID = pl.DeviceIdType.MESH

F32 = jnp.float32
BF16 = jnp.bfloat16


def dot(a, b):
    return jnp.dot(a, b, preferred_element_type=F32)


def dot_nt(a, b):
    return lax.dot_general(a, b, (((1,), (1,)), ((), ())), preferred_element_type=F32)


def dot_tn(a, b):
    return lax.dot_general(a, b, (((0,), (0,)), ((), ())), preferred_element_type=F32)


def iota(shape, dim):
    return lax.broadcasted_iota(jnp.int32, shape, dim)


def hot_matrix(condition):
    return jnp.where(condition, 1.0, 0.0).astype(BF16)


def whole(shape):
    zeros = (0,) * len(shape)
    return pl.BlockSpec(shape, lambda *_: zeros)


def row_spec(width, rows=ROW_BLOCK):
    return pl.BlockSpec((rows, width), lambda i: (i, 0))


def col_spec(rows, width=LANES):
    return pl.BlockSpec((rows, width), lambda j: (0, j))


def sds(shape, dtype):
    return jax.ShapeDtypeStruct(shape, dtype)


def call(body, grid, in_specs, out_specs, out_shape, scratch=(), name=None):
    return pl.pallas_call(
        body,
        grid=grid,
        in_specs=in_specs,
        out_specs=out_specs,
        out_shape=out_shape,
        scratch_shapes=list(scratch),
        compiler_params=pltpu.CompilerParams(vmem_limit_bytes=VMEM_BYTES),
        name=name,
    )


def half_swap(values):
    lane = iota(values.shape, 1)
    up = pltpu.roll(values, 32, 1)
    down = pltpu.roll(values, LANES - 32, 1)
    return jnp.where(lane % HEAD_DIM < HEAD_DIM // 2, down, up)


def lane_value(values, lane_id):
    return jnp.sum(jnp.where(iota(values.shape, 1) == lane_id, values, 0.0), axis=1, keepdims=True)


def proj_in_body(
    place_row, hidden, upstream, small, cosine, sine, mask, gain, w_qkv, a_in, b_out,
    hid_s, dy_s, small_s, act_one, low_qkv, query, key, value,
):
    rows = hid_s.shape[0]
    base = pl.program_id(0) * rows
    perm = hot_matrix(place_row[...] == base + iota((rows, place_row.shape[1]), 0))
    hid = dot(perm, hidden[...])
    hid_s[...] = hid.astype(BF16)
    dy_s[...] = dot(perm, upstream[...]).astype(BF16)
    small_s[...] = dot(perm, small[...])
    act = normed(hid, gain)
    act_one[...] = act
    low, q_val, k_val, value[...] = project(
        act, mask[...], cosine[...], sine[...], w_qkv, a_in, b_out
    )
    low_qkv[...] = low
    query[...], key[...] = q_val, k_val


def normed(values, gain):
    scale = lax.rsqrt(jnp.mean(values * values, axis=-1, keepdims=True) + EPSILON)
    return (values * scale * gain[...]).astype(BF16)


def project(act, mask, cos, sin, w_qkv, a_in, b_out):
    low = (dot(act, a_in[...]) * mask.astype(F32)).astype(BF16)
    turned = []
    for start, factor in ((0, HEAD_DIM**-0.5), (MODEL_WIDTH, 1.0)):
        cols = slice(start, start + MODEL_WIDTH)
        vals = dot(act, w_qkv[:, cols]) + dot(low, b_out[:, cols])
        pieces = []
        for c in range(MODEL_WIDTH // LANES):
            piece = vals[:, c * LANES : (c + 1) * LANES]
            piece = (piece * cos + half_swap(piece) * sin).astype(BF16)
            pieces.append(piece if factor == 1.0 else piece * jnp.asarray(factor, BF16))
        turned.append(jnp.concatenate(pieces, axis=1))
    value = dot(act, w_qkv[:, 2 * MODEL_WIDTH :]) + dot(low, b_out[:, 2 * MODEL_WIDTH :])
    return low, turned[0], turned[1], value.astype(BF16)


def head_mask(shape, head):
    lane = iota(shape, 1)
    return (lane >= head * HEAD_DIM) & (lane < (head + 1) * HEAD_DIM)


def attention_fwd_body(query, key, value, starts, attended, lse):
    @pl.when(pl.program_id(0) == 0)
    def _():
        lse[...] = jnp.zeros_like(lse)

    attention_fwd_pair(pl.program_id(0), query, key, value, starts, attended, lse)


def attention_fwd_pair(pair, query, key, value, starts, attended, lse):
    tok = query.shape[0]
    size = ROW_BLOCK
    zero = jnp.zeros((), BF16)
    for blk in range(tok // size):
        lo, hi = blk * size, (blk + 1) * size
        q_blk = query[lo:hi, :]
        k_all = key[:hi, :]
        v_all = value[:hi, :]
        begin = starts[lo:hi, :]
        col = iota((size, hi), 1)
        allowed = (col <= lo + iota((size, hi), 0)) & (col >= begin)
        total = jnp.zeros((size, LANES), F32)
        stats = lse[lo:hi, :]
        lane = iota((size, LANES), 1)
        for head in range(2):
            mine = head_mask((size, LANES), head)
            scores = dot_nt(jnp.where(mine, q_blk, zero), k_all)
            scores = jnp.where(allowed, scores, -1000000000.0)
            top = jnp.max(scores, axis=1, keepdims=True)
            expo = jnp.exp(scores - top)
            norm = jnp.sum(expo, axis=1, keepdims=True)
            v_head = jnp.where(head_mask((hi, LANES), head), v_all, zero)
            total = total + dot(expo.astype(BF16), v_head) * (1.0 / norm)
            stats = jnp.where(lane == 2 * pair + head, top + jnp.log(norm), stats)
        attended[lo:hi, :] = total.astype(BF16)
        lse[lo:hi, :] = stats


def attention_bwd_body(
    query, key, value, dout, attended, lse, starts, cosine, sine, d_query, d_key, d_value, kacc, vacc
):
    tok = query.shape[0]
    size = ROW_BLOCK
    zero = jnp.zeros((), BF16)
    kacc[...] = jnp.zeros_like(kacc)
    vacc[...] = jnp.zeros_like(vacc)
    for blk in range(tok // size):
        lo, hi = blk * size, (blk + 1) * size
        q_blk = query[lo:hi, :]
        do_blk = dout[lo:hi, :]
        k_all = key[:hi, :]
        v_all = value[:hi, :]
        begin = starts[lo:hi, :]
        col = iota((size, hi), 1)
        allowed = (col <= lo + iota((size, hi), 0)) & (col >= begin)
        prod = do_blk.astype(F32) * attended[lo:hi, :].astype(F32)
        q_total = jnp.zeros((size, LANES), F32)
        for head in range(2):
            mine = head_mask((size, LANES), head)
            q_head = jnp.where(mine, q_blk, zero)
            do_head = jnp.where(mine, do_blk, zero)
            lse_head = lane_value(lse[lo:hi, :], 2 * pl.program_id(0) + head)
            delta = jnp.sum(jnp.where(mine, prod, 0.0), axis=1, keepdims=True)
            scores = dot_nt(q_head, k_all)
            prob = jnp.where(allowed, jnp.exp(jnp.minimum(scores - lse_head, 0.0)), 0.0)
            dprob = dot_nt(do_head, v_all)
            dscore = (prob * (dprob - delta)).astype(BF16)
            k_head = jnp.where(head_mask((hi, LANES), head), k_all, zero)
            q_total = q_total + dot(dscore, k_head)
            kacc[:hi, :] += dot_tn(dscore, q_head)
            vacc[:hi, :] += dot_tn(prob.astype(BF16), do_head)
        q_total = q_total * HEAD_DIM**-0.5
        d_query[lo:hi, :] = (
            q_total * cosine[lo:hi, :] - half_swap(q_total) * sine[lo:hi, :]
        ).astype(BF16)
    for blk in range(tok // size):
        lo, hi = blk * size, (blk + 1) * size
        k_total = kacc[lo:hi, :]
        d_key[lo:hi, :] = (
            k_total * cosine[lo:hi, :] - half_swap(k_total) * sine[lo:hi, :]
        ).astype(BF16)
    d_value[...] = vacc[...].astype(BF16)


def start_kernel(send_to, hear_from, count):
    barrier = pltpu.get_barrier_semaphore()
    for device, remote in hear_from:
        if remote is None:
            pl.semaphore_signal(barrier, inc=1, device_id=device, device_id_type=MESH_ID)
        else:

            @pl.when(remote)
            def _(device=device):
                pl.semaphore_signal(barrier, inc=1, device_id=device, device_id_type=MESH_ID)

    pl.semaphore_wait(barrier, count)


def pair_front_body(
    kinds, a_rows, b_rows,
    place_row, hidden, upstream, small, cosine, sine, mask, starts, gain_one, gain_two, router,
    own_qkv, own_out, own_wide, own_mid, own_thin, *rest,
):
    outs, rest = rest[:20], rest[20:]
    all_wide, all_mid, all_thin, rest = *rest[:3], rest[3:]
    kept, rest = rest[:20], rest[20:]
    (
        hid_s, dy_s, small_s, act_one, low_qkv, query, key, value, w_qkv, a_qkv, b_qkv,
        w_out, a_out, b_out, attn_low, lse, low_out, resid, act_two, gate,
    ) = kept
    g_qkv, g_out, a_send, a_recv, e_send, e_recv, out_sems, own_sems = rest
    dp, z = lax.axis_index("dp"), lax.axis_index("expert")
    core, x_bit, y_bit = dp % 2, dp // 2 % 2, dp // 4
    across = dp + 1 - 2 * core
    x_dev, y_dev = dp + 2 - 4 * x_bit, dp + 4 - 8 * y_bit
    diag = x_dev + 4 - 8 * y_bit
    far = (z + 2) % 4
    home = z // 2
    columns = (dp, x_dev, y_dev, diag)
    tok = hidden.shape[0]
    blocks = tok // ROW_BLOCK

    def remote(source, target, send, recv, device):
        return pltpu.make_async_remote_copy(
            src_ref=source, dst_ref=target, send_sem=send, recv_sem=recv,
            device_id=device, device_id_type=MESH_ID,
        )

    packs = ((own_qkv, g_qkv), (own_out, g_out))

    def at(kind, back):
        return columns[kind] * 4 + (z + 4 - back) % 4

    def shard(p, kind, back, rows=None):
        view = packs[p][1].at[at(kind, back)]
        if rows is None:
            return view
        half = packs[p][1].shape[1] // 2
        return view.at[pl.ds(rows * half, half)]

    def along_z(p, j):
        return remote(
            packs[p][0], packs[p][1].at[at(0, 0)], a_send.at[p, j - 1], a_recv.at[p, j - 1],
            (dp, (z + j) % 4),
        )

    def z_arrival(p, j):
        return remote(
            packs[p][0], shard(p, 0, j), a_send.at[p, j - 1], a_recv.at[p, j - 1], (dp, (z + j) % 4)
        )

    def to_x(p, back):
        return remote(
            shard(p, 0, back), shard(p, 0, back), a_send.at[p, 3 + back], a_recv.at[p, 3 + back],
            (x_dev, z),
        )

    def to_y(p, back):
        return remote(
            shard(p, 0, back), shard(p, 0, back), a_send.at[p, 7 + back], a_recv.at[p, 7 + back],
            (y_dev, z),
        )

    def relay_y(p, back):
        return remote(
            shard(p, 1, back, 0), shard(p, 1, back, 0), a_send.at[p, 11 + back],
            a_recv.at[p, 11 + back], (y_dev, z),
        )

    def relay_x(p, back):
        return remote(
            shard(p, 2, back, 1), shard(p, 2, back, 1), a_send.at[p, 15 + back],
            a_recv.at[p, 15 + back], (x_dev, z),
        )

    def to_core(p, kind, back):
        sem = 19 + 4 * kind + back
        return remote(
            shard(p, kind, back), shard(p, kind, back), a_send.at[p, sem], a_recv.at[p, sem],
            (across, z),
        )

    def keep_own(p):
        return pltpu.make_async_copy(packs[p][0], shard(p, 0, 0), own_sems.at[p])

    half_wide = own_wide.shape[1] // 2
    parts = []
    for own, everything, cols in (
        (own_mid, all_mid, None), (own_thin, all_thin, None),
        (own_wide, all_wide, (0, half_wide)), (own_wide, all_wide, (half_wide, half_wide)),
    ):
        if cols is None:
            parts.append((own, lambda d, ref=everything: ref.at[d]))
        else:
            parts.append(
                (own.at[:, pl.ds(*cols)], lambda d, ref=everything, c=cols: ref.at[d, :, pl.ds(*c)])
            )
    chunks = ((0, 1), (2,), (3,))

    def first_far(a):
        return remote(
            parts[a][0], parts[a][1](dp), e_send.at[a, 0], e_recv.at[a, core],
            (dp - core + home, far),
        )

    def first_across(a):
        return remote(
            parts[a][0], parts[a][1](dp), e_send.at[a, 1], e_recv.at[a, core], (across, z)
        )

    def first_keep(a):
        return pltpu.make_async_copy(parts[a][0], parts[a][1](dp), e_recv.at[a, core])

    def first_arrival(a, i):
        view = parts[a][1](dp - core + i)
        return remote(view, view, e_send.at[a, 0], e_recv.at[a, i], (dp, far))

    def expert_hop(a, column, i, sem, device):
        view = parts[a][1](column - core + i)
        return remote(view, view, e_send.at[a, sem], e_recv.at[a, sem], (device, z))

    def expert_x(a, i):
        return expert_hop(a, dp, i, 2 + i, x_dev)

    def expert_y(a, i):
        return expert_hop(a, dp, i, 4 + i, y_dev)

    def expert_relay_y(a):
        return expert_hop(a, x_dev, 0, 6, y_dev)

    def expert_relay_x(a):
        return expert_hop(a, y_dev, 1, 7, x_dev)

    def expert_first(c):
        for a in chunks[c]:
            first_far(a).start()

            @pl.when(core == home)
            def _(a=a):
                first_keep(a).start()

            @pl.when(core != home)
            def _(a=a):
                first_across(a).start()

    def expert_spread(c):
        for a in chunks[c]:

            @pl.when(core == home)
            def _(a=a):
                first_keep(a).wait()
                first_arrival(a, 1 - core).wait_recv()

            @pl.when(core != home)
            def _(a=a):
                for i in range(2):
                    first_arrival(a, i).wait_recv()

            for i in range(2):
                expert_x(a, i).start()
                expert_y(a, i).start()

    def expert_relay(c):
        for a in chunks[c]:
            for i in range(2):
                expert_hop(a, x_dev, i, 2 + i, x_dev).wait_recv()
            expert_relay_y(a).start()
            for i in range(2):
                expert_hop(a, y_dev, i, 4 + i, y_dev).wait_recv()
            expert_relay_x(a).start()

    def expert_finish(c):
        for a in chunks[c]:
            expert_hop(a, diag, 0, 6, y_dev).wait_recv()
            expert_hop(a, diag, 1, 7, x_dev).wait_recv()
            first_far(a).wait_send()

            @pl.when(core != home)
            def _(a=a):
                first_across(a).wait_send()

            for i in range(2):
                expert_x(a, i).wait_send()
                expert_y(a, i).wait_send()
            expert_relay_y(a).wait_send()
            expert_relay_x(a).wait_send()

    peers = [(x_dev, z), (y_dev, z), (across, z), (across, far)]
    peers += [(dp, (z + j) % 4) for j in (1, 2, 3)]
    start_kernel(None, [(device, None) for device in peers], len(peers))
    for p in range(2):
        for j in (1, 2, 3):
            along_z(p, jnp.where(z < 2, 4 - j, j)).start()
        keep_own(p).start()
    for p in range(2):
        keep_own(p).wait()
        to_x(p, 0).start()
        to_y(p, 0).start()
        to_core(p, 0, 0).start()

    def block_rows(b):
        return pl.ds(pl.multiple_of(b * ROW_BLOCK, ROW_BLOCK), ROW_BLOCK)

    def arrange(b, carry):
        rows = block_rows(b)
        perm = hot_matrix(place_row[...] == b * ROW_BLOCK + iota((ROW_BLOCK, tok), 0))
        hid = dot(perm, hidden[...])
        hid_s[rows, :] = hid.astype(BF16)
        act_one[rows, :] = normed(hid, gain_one)
        dy_s[rows, :] = dot(perm, upstream[...]).astype(BF16)
        small_s[rows, :] = dot(perm, small[...])
        return carry

    lax.fori_loop(0, blocks, arrange, 0)

    for p in range(2):

        def from_z(j, carry, p=p):
            z_arrival(p, j).wait_recv()
            to_x(p, j).start()
            to_y(p, j).start()
            to_core(p, 0, j).start()
            return carry

        lax.fori_loop(1, 4, from_z, 0)
    for p in range(2):

        def from_sides(back, carry, p=p):
            remote(
                shard(p, 1, back), shard(p, 1, back), a_send.at[p, 3 + back], a_recv.at[p, 3 + back],
                (x_dev, z),
            ).wait_recv()
            relay_y(p, back).start()
            to_core(p, 1, back).start()
            remote(
                shard(p, 2, back), shard(p, 2, back), a_send.at[p, 7 + back], a_recv.at[p, 7 + back],
                (y_dev, z),
            ).wait_recv()
            relay_x(p, back).start()
            to_core(p, 2, back).start()
            return carry

        lax.fori_loop(0, 4, from_sides, 0)
    for c in range(len(chunks)):
        expert_first(c)
    for p in range(2):

        def from_diag(back, carry, p=p):
            remote(
                shard(p, 3, back, 0), shard(p, 3, back, 0), a_send.at[p, 11 + back],
                a_recv.at[p, 11 + back], (y_dev, z),
            ).wait_recv()
            remote(
                shard(p, 3, back, 1), shard(p, 3, back, 1), a_send.at[p, 15 + back],
                a_recv.at[p, 15 + back], (x_dev, z),
            ).wait_recv()
            to_core(p, 3, back).start()
            return carry

        lax.fori_loop(0, 4, from_diag, 0)
    core_columns = (across, x_dev + across - dp, y_dev + across - dp, diag + across - dp)

    def from_core(p):
        def body(back, carry):
            for kind in range(4):
                view = packs[p][1].at[core_columns[kind] * 4 + (z + 4 - back) % 4]
                sem = 19 + 4 * kind + back
                remote(view, view, a_send.at[p, sem], a_recv.at[p, sem], (across, z)).wait_recv()
            return carry

        lax.fori_loop(0, 4, body, 0)

    width = MODEL_WIDTH
    total = g_qkv.shape[0]

    def lay_rows(i, carry, gathered, targets):
        pair = [gathered[2 * i + n, :a_rows, :].astype(F32) for n in range(2)]
        both = jnp.concatenate(pair, axis=0).astype(BF16)
        rows = pl.ds(pl.multiple_of(i * 2 * a_rows, 16), 2 * a_rows)
        start = 0
        for target in targets:
            target[rows, :] = both[:, start : start + target.shape[1]]
            start += target.shape[1]
        return carry

    def lay_ups(i, carry, gathered, target):
        group = 16 // b_rows
        pieces = [
            gathered[group * i + n, a_rows : a_rows + b_rows, : target.shape[1]].astype(F32)
            for n in range(group)
        ]
        rows = pl.ds(pl.multiple_of(i * 16, 16), 16)
        target[rows, :] = jnp.concatenate(pieces, axis=0).astype(BF16)
        return carry

    def lay(gathered, targets, ups):
        lax.fori_loop(
            0, total // 2, functools.partial(lay_rows, gathered=gathered, targets=targets), 0
        )
        lax.fori_loop(
            0, total * b_rows // 16, functools.partial(lay_ups, gathered=gathered, target=ups), 0
        )

    def flush(first, last):
        return [
            pltpu.make_async_copy(kept[i], outs[i], out_sems.at[i]) for i in range(first, last)
        ]

    from_core(0)
    lay(g_qkv, (w_qkv, a_qkv), b_qkv)

    def projection(b, carry):
        rows = block_rows(b)
        low_qkv[rows, :], query[rows, :], key[rows, :], value[rows, :] = project(
            act_one[rows, :], mask[rows, :], cosine[rows, :], sine[rows, :], w_qkv, a_qkv, b_qkv
        )

        @pl.when(b == 1)
        def _():
            expert_spread(0)

        return carry

    lax.fori_loop(0, blocks, projection, 0)
    from_core(1)
    lay(g_out, (w_out, a_out), b_out)
    for copy in flush(0, 14):
        copy.start()
    lse[...] = jnp.zeros_like(lse)

    def attention(pair, carry):
        cols = pl.ds(pl.multiple_of(pair * LANES, LANES), LANES)
        attention_fwd_pair(
            pair, query.at[:, cols], key.at[:, cols], value.at[:, cols], starts,
            attn_low.at[:, cols], lse,
        )

        @pl.when(pair == 0)
        def _():
            expert_spread(1)

        @pl.when(pair == 1)
        def _():
            expert_relay(0)

        @pl.when(pair == 3)
        def _():
            expert_spread(2)

        @pl.when(pair == 5)
        def _():
            expert_relay(1)

        return carry

    lax.fori_loop(0, HEAD_COUNT // 2, attention, 0)
    for copy in flush(14, 16):
        copy.start()

    def after(b, carry):
        rows = block_rows(b)
        low_out[rows, :], resid[rows, :], act_two[rows, :], gate[rows, :] = post_attn(
            kinds, attn_low[rows, :], hid_s[rows, :], mask[rows, :], small_s[rows, :],
            w_out, a_out, b_out, router, gain_two,
        )
        return carry

    lax.fori_loop(0, blocks, after, 0)
    for copy in flush(16, 20):
        copy.start()
    expert_relay(2)
    for c in range(len(chunks)):
        expert_finish(c)

    def attn_sent(n, carry):
        for p in range(2):
            to_x(p, n).wait_send()
            to_y(p, n).wait_send()
            relay_x(p, n).wait_send()
            relay_y(p, n).wait_send()
            for kind in range(4):
                to_core(p, kind, n).wait_send()
        return carry

    lax.fori_loop(0, 4, attn_sent, 0)
    for p in range(2):
        for j in (1, 2, 3):
            along_z(p, j).wait_send()
    for copy in flush(0, 20):
        copy.wait()


def pair_attention_bwd_body(
    query, key, value, dout, attended, lse, starts, cosine, sine, ga_gu, gb_gu, ga_dn, gb_dn,
    d_query, d_key, d_value, own_ga_gu, own_gb_gu, own_ga_dn, own_gb_dn,
    kacc, vacc, r_ga_gu, r_gb_gu, r_ga_dn, r_gb_dn, send_sems, recv_sems,
):
    dp, z = lax.axis_index("dp"), lax.axis_index("expert")
    core, spot, half = dp % 2, dp // 2, z // 2
    own = z % 2 + 2 * core
    far = (z + 2) % 4
    at_home = core == half
    away = 1 - (core * half + (1 - core) * (1 - half))
    slot = 2 * spot + away
    groups = (
        (ga_gu, r_ga_gu, own_ga_gu), (gb_gu, r_gb_gu, own_gb_gu),
        (ga_dn, r_ga_dn, own_ga_dn), (gb_dn, r_gb_dn, own_gb_dn),
    )
    owners = 8

    def piece(i, d):
        source, target, _ = groups[i]
        count = target.shape[1]
        return source.at[pl.ds(pl.multiple_of(d * count, 16), count)]

    def push(i, d):
        return pltpu.make_async_remote_copy(
            src_ref=piece(i, d), dst_ref=groups[i][1].at[slot], send_sem=send_sems.at[i, d],
            recv_sem=recv_sems.at[i, slot], device_id=(d, own), device_id_type=MESH_ID,
        )

    def keep(i):
        return pltpu.make_async_copy(
            piece(i, dp), groups[i][1].at[2 * spot], recv_sems.at[i, 2 * spot]
        )

    def arrival(i, s):
        return pltpu.make_async_remote_copy(
            src_ref=piece(i, 0), dst_ref=groups[i][1].at[s], send_sem=send_sems.at[i, 0],
            recv_sem=recv_sems.at[i, s], device_id=(0, own), device_id_type=MESH_ID,
        )

    @pl.when(pl.program_id(0) == 0)
    def _():
        senders = []
        for m in range(owners // 2):
            device = 2 * m + half
            senders.append(((device, z), device != dp))
            senders.append(((device, far), None))
        start_kernel(None, senders, owners - 1 + away)

        def send(d, carry):
            mine = at_home & (d == dp)

            @pl.when(mine)
            def _():
                for i in range(4):
                    keep(i).start()

            @pl.when(jnp.logical_not(mine))
            def _():
                for i in range(4):
                    push(i, d).start()

            return carry

        lax.fori_loop(0, owners, send, 0)

    attention_bwd_body(
        query, key, value, dout, attended, lse, starts, cosine, sine, d_query, d_key, d_value,
        kacc, vacc,
    )

    @pl.when(pl.program_id(0) == pl.num_programs(0) - 1)
    def _():
        def finish(s, carry):
            mine = at_home & (s == 2 * spot)

            @pl.when(mine)
            def _():
                for i in range(4):
                    keep(i).wait()

            @pl.when(jnp.logical_not(mine))
            def _():
                for i in range(4):
                    arrival(i, s).wait_recv()

            @pl.when(jnp.logical_not(at_home & (s == dp)))
            def _():
                for i in range(4):
                    push(i, s).wait_send()

            return carry

        lax.fori_loop(0, owners, finish, 0)
        for _, target, out in groups:
            total = target[0].astype(F32)
            for s in range(1, owners):
                total = total + target[s].astype(F32)
            out[...] = total


def pair_tail_body(
    place_col, d_query, d_key, d_value, low_qkv, act_one, mask, a_in, b_out, gain, ga_out, gb_out,
    d_logits, hid_hbm, resid_hbm, w_hbm, out_hbm,
    out, grad_hidden, grad_gate, own_ga_qkv, own_gb_qkv, own_ga_out, own_gb_out,
    hid_s, d_resid, w_qkv, out_s, high, lower, d_low_all, ga_sum, gb_sum,
    s_ga_qkv, s_gb_qkv, s_ga_out, s_gb_out, r_ga_qkv, r_gb_qkv, r_ga_out, r_gb_out,
    thin_out, wide_out, thin_in, wide_in, load_sems, send_sems, recv_sems, far_send, far_recv,
):
    dp, z = lax.axis_index("dp"), lax.axis_index("expert")
    others, planes = 7, 3
    tok = place_col.shape[0]
    blocks = tok // ROW_BLOCK
    loads = [
        pltpu.make_async_copy(source, target, load_sems.at[i])
        for i, (source, target) in enumerate(
            ((w_hbm, w_qkv), (hid_hbm, hid_s), (resid_hbm, d_resid), (out_hbm, out_s))
        )
    ]
    for load in loads:
        load.start()
    start_kernel(
        None,
        [(((dp + i) % 8, z), None) for i in range(1, 8)] + [((dp, (z + j) % 4), None) for j in (1, 2, 3)],
        others + planes,
    )
    ga_sum[...] = jnp.zeros_like(ga_sum)
    gb_sum[...] = jnp.zeros_like(gb_sum)
    parts = [slice(p * MODEL_WIDTH, (p + 1) * MODEL_WIDTH) for p in range(3)]
    d_refs = (d_query, d_key, d_value)

    def block_rows(b):
        return pl.ds(pl.multiple_of(b * ROW_BLOCK, ROW_BLOCK), ROW_BLOCK)

    def sums(b, carry):
        rows = block_rows(b)
        low = low_qkv[rows, :]
        d_low = jnp.zeros((ROW_BLOCK, LANES), F32)
        for cols, ref in zip(parts, d_refs):
            grad = ref[rows, :]
            d_low = d_low + dot_nt(grad, b_out[:, cols])
            gb_sum[:, cols] += dot_tn(low, grad)
        d_low = (d_low * mask[rows, :].astype(F32)).astype(BF16)
        d_low_all[rows, :] = d_low
        ga_sum[...] += dot_tn(act_one[rows, :], d_low)
        return carry

    lax.fori_loop(0, blocks, sums, 0)
    s_ga_qkv[...] = ga_sum[...].astype(BF16)
    s_gb_qkv[...] = gb_sum[...].astype(BF16)
    s_ga_out[...] = ga_out[...].astype(BF16)
    s_gb_out[...] = gb_out[...].astype(BF16)
    groups = (
        (s_ga_qkv, r_ga_qkv), (s_gb_qkv, r_gb_qkv), (s_ga_out, r_ga_out), (s_gb_out, r_gb_out),
    )

    def share(i, d):
        count = groups[i][1].shape[1]
        return groups[i][0].at[pl.ds(pl.multiple_of(d * count, 16), count)]

    def near(i, n):
        goal = (dp + n + 1) % 8
        return pltpu.make_async_remote_copy(
            src_ref=share(i, goal), dst_ref=groups[i][1].at[n], send_sem=send_sems.at[i, n],
            recv_sem=recv_sems.at[i, n], device_id=(goal, z), device_id_type=MESH_ID,
        )

    def send_near(n, carry):
        for i in range(4):
            near(i, n).start()
        return carry

    lax.fori_loop(0, others, send_near, 0)

    for load in loads[:3]:
        load.wait()

    def back(b, carry):
        rows = block_rows(b)
        d_act = dot_nt(d_low_all[rows, :], a_in[...])
        for cols, ref in zip(parts, d_refs):
            d_act = d_act + dot_nt(ref[rows, :], w_qkv[:, cols])
        hid = hid_s[rows, :].astype(F32)
        scale = lax.rsqrt(jnp.mean(hid * hid, axis=-1, keepdims=True) + EPSILON)
        weighted = d_act * gain[...]
        grad_hid = d_resid[rows, :] + (
            scale * weighted
            - hid * (scale * scale * scale) * jnp.mean(hid * weighted, axis=-1, keepdims=True)
        )
        top = grad_hid.astype(BF16)
        high[rows, :] = top
        lower[rows, :] = (grad_hid - top.astype(F32)).astype(BF16)
        return carry

    lax.fori_loop(0, blocks, back, 0)

    def near_done(n, carry):
        for i in range(4):
            near(i, n).wait_recv()
        return carry

    lax.fori_loop(0, others, near_done, 0)
    totals = []
    for i in range(4):
        total = share(i, dp)[...].astype(F32)
        for n in range(others):
            total = total + groups[i][1][n].astype(F32)
        totals.append(total)
    a_qkv, b_qkv, a_o, b_o = totals
    a_count, b_count = a_qkv.shape[0] // 4, b_qkv.shape[0] // 4
    for p in range(4):
        a_rows, b_rows = slice(p * a_count, (p + 1) * a_count), slice(p * b_count, (p + 1) * b_count)
        thin_out[p, :a_count, :LANES] = a_qkv[a_rows].astype(BF16)
        thin_out[p, :a_count, LANES:] = a_o[a_rows].astype(BF16)
        thin_out[p, a_count:, :] = jnp.zeros((thin_out.shape[1] - a_count, 2 * LANES), BF16)
        wide_out[p] = jnp.concatenate(
            [b_qkv[b_rows, cols] for cols in parts] + [b_o[b_rows]], axis=0
        ).astype(BF16)

    def far(i, j):
        goal = (z + j + 1) % 4
        source, target = ((thin_out, thin_in), (wide_out, wide_in))[i]
        return pltpu.make_async_remote_copy(
            src_ref=source.at[goal], dst_ref=target.at[j], send_sem=far_send.at[i, j],
            recv_sem=far_recv.at[i, j], device_id=(dp, goal), device_id_type=MESH_ID,
        )

    for j in range(planes):
        for i in range(2):
            far(i, j).start()
    loads[3].wait()

    def to_rows(b, carry):
        rows = block_rows(b)
        perm = hot_matrix(place_col[rows, :] == iota((ROW_BLOCK, tok), 1))
        out[rows, :] = dot(perm, out_s[...]).astype(BF16)
        grad_hidden[rows, :] = dot(perm, high[...]) + dot(perm, lower[...])
        top, mid, last = split_three(d_logits[...])
        grad_gate[rows, :] = dot(perm, top) + (dot(perm, mid) + dot(perm, last))
        return carry

    lax.fori_loop(0, blocks, to_rows, 0)
    for j in range(planes):
        for i in range(2):
            far(i, j).wait_recv()
    thin = thin_out[z].astype(F32)
    wide = wide_out[z].astype(F32)
    for j in range(planes):
        thin = thin + thin_in[j].astype(F32)
        wide = wide + wide_in[j].astype(F32)
    own_ga_qkv[...] = thin[:a_count, :LANES]
    own_ga_out[...] = thin[:a_count, LANES:]
    for p, cols in enumerate(parts):
        own_gb_qkv[:, cols] = wide[p * b_count : (p + 1) * b_count]
    own_gb_out[...] = wide[3 * b_count : 4 * b_count]

    def sent(n, carry):
        for i in range(4):
            near(i, n).wait_send()
        return carry

    lax.fori_loop(0, others, sent, 0)
    for j in range(planes):
        for i in range(2):
            far(i, j).wait_send()


def split_three(values):
    top = values.astype(BF16)
    rest = values - top.astype(F32)
    mid = rest.astype(BF16)
    return top, mid, (rest - mid.astype(F32)).astype(BF16)


def post_attn_body(
    kinds, attn_low, hid_s, mask, small_s, w_out, a_out, b_out, router, gain,
    low_out, resid, act_two, gate,
):
    low_out[...], resid[...], act_two[...], gate[...] = post_attn(
        kinds, attn_low[...], hid_s[...], mask[...], small_s[...], w_out, a_out, b_out, router, gain
    )


def post_attn(kinds, attn, hid, mask, sm, w_out, a_out, b_out, router, gain):
    low = (dot(attn, a_out[...]) * mask.astype(F32)).astype(BF16)
    res = hid.astype(F32) + (dot(attn, w_out[...]) + dot(low, b_out[...]))
    act = normed(res, gain)
    carry = sm + (pltpu.roll(sm, LANES - 16, 1) + pltpu.roll(sm, LANES - 32, 1))
    logits = dot(act, router[...])
    lane = iota(logits.shape, 1)
    routed = jnp.where(lane < kinds, logits + carry, -1e30)
    top = jnp.max(routed, axis=1, keepdims=True)
    expo = jnp.exp(routed - top)
    prob = expo / jnp.sum(expo, axis=1, keepdims=True)
    return low, res, act, jnp.where(lane < kinds, prob, logits)


def start_kernel(send_to, hear_from, count):
    barrier = pltpu.get_barrier_semaphore()
    for device, remote in hear_from:
        if remote is None:
            pl.semaphore_signal(barrier, inc=1, device_id=device, device_id_type=MESH_ID)
        else:

            @pl.when(remote)
            def _(device=device):
                pl.semaphore_signal(barrier, inc=1, device_id=device, device_id_type=MESH_ID)

    pl.semaphore_wait(barrier, count)


def pair_attention_bwd_body(
    query, key, value, dout, attended, lse, starts, cosine, sine, ga_gu, gb_gu, ga_dn, gb_dn,
    d_query, d_key, d_value, own_ga_gu, own_gb_gu, own_ga_dn, own_gb_dn,
    kacc, vacc, r_ga_gu, r_gb_gu, r_ga_dn, r_gb_dn, send_sems, recv_sems,
):
    dp, z = lax.axis_index("dp"), lax.axis_index("expert")
    core, spot, half = dp % 2, dp // 2, z // 2
    own = z % 2 + 2 * core
    far = (z + 2) % 4
    at_home = core == half
    away = 1 - (core * half + (1 - core) * (1 - half))
    slot = 2 * spot + away
    groups = (
        (ga_gu, r_ga_gu, own_ga_gu), (gb_gu, r_gb_gu, own_gb_gu),
        (ga_dn, r_ga_dn, own_ga_dn), (gb_dn, r_gb_dn, own_gb_dn),
    )
    owners = 8

    def piece(i, d):
        source, target, _ = groups[i]
        count = target.shape[1]
        return source.at[pl.ds(pl.multiple_of(d * count, 16), count)]

    def push(i, d):
        return pltpu.make_async_remote_copy(
            src_ref=piece(i, d), dst_ref=groups[i][1].at[slot], send_sem=send_sems.at[i, d],
            recv_sem=recv_sems.at[i, slot], device_id=(d, own), device_id_type=MESH_ID,
        )

    def keep(i):
        return pltpu.make_async_copy(
            piece(i, dp), groups[i][1].at[2 * spot], recv_sems.at[i, 2 * spot]
        )

    def arrival(i, s):
        return pltpu.make_async_remote_copy(
            src_ref=piece(i, 0), dst_ref=groups[i][1].at[s], send_sem=send_sems.at[i, 0],
            recv_sem=recv_sems.at[i, s], device_id=(0, own), device_id_type=MESH_ID,
        )

    @pl.when(pl.program_id(0) == 0)
    def _():
        senders = []
        for m in range(owners // 2):
            device = 2 * m + half
            senders.append(((device, z), device != dp))
            senders.append(((device, far), None))
        start_kernel(None, senders, owners - 1 + away)

        def send(d, carry):
            mine = at_home & (d == dp)

            @pl.when(mine)
            def _():
                for i in range(4):
                    keep(i).start()

            @pl.when(jnp.logical_not(mine))
            def _():
                for i in range(4):
                    push(i, d).start()

            return carry

        lax.fori_loop(0, owners, send, 0)

    attention_bwd_body(
        query, key, value, dout, attended, lse, starts, cosine, sine, d_query, d_key, d_value,
        kacc, vacc,
    )

    @pl.when(pl.program_id(0) == pl.num_programs(0) - 1)
    def _():
        def finish(s, carry):
            mine = at_home & (s == 2 * spot)

            @pl.when(mine)
            def _():
                for i in range(4):
                    keep(i).wait()

            @pl.when(jnp.logical_not(mine))
            def _():
                for i in range(4):
                    arrival(i, s).wait_recv()

            @pl.when(jnp.logical_not(at_home & (s == dp)))
            def _():
                for i in range(4):
                    push(i, s).wait_send()

            return carry

        lax.fori_loop(0, owners, finish, 0)
        for _, target, out in groups:
            total = target[0].astype(F32)
            for s in range(1, owners):
                total = total + target[s].astype(F32)
            out[...] = total


def pair_tail_body(
    place_col, d_query, d_key, d_value, low_qkv, act_one, mask, a_in, b_out, gain, ga_out, gb_out,
    d_logits, hid_hbm, resid_hbm, w_hbm, out_hbm,
    out, grad_hidden, grad_gate, own_ga_qkv, own_gb_qkv, own_ga_out, own_gb_out,
    hid_s, d_resid, w_qkv, out_s, high, lower, d_low_all, ga_sum, gb_sum,
    s_ga_qkv, s_gb_qkv, s_ga_out, s_gb_out, r_ga_qkv, r_gb_qkv, r_ga_out, r_gb_out,
    thin_out, wide_out, thin_in, wide_in, load_sems, send_sems, recv_sems, far_send, far_recv,
):
    dp, z = lax.axis_index("dp"), lax.axis_index("expert")
    others, planes = 7, 3
    tok = place_col.shape[0]
    blocks = tok // ROW_BLOCK
    loads = [
        pltpu.make_async_copy(source, target, load_sems.at[i])
        for i, (source, target) in enumerate(
            ((w_hbm, w_qkv), (hid_hbm, hid_s), (resid_hbm, d_resid), (out_hbm, out_s))
        )
    ]
    for load in loads:
        load.start()
    start_kernel(
        None,
        [(((dp + i) % 8, z), None) for i in range(1, 8)] + [((dp, (z + j) % 4), None) for j in (1, 2, 3)],
        others + planes,
    )
    ga_sum[...] = jnp.zeros_like(ga_sum)
    gb_sum[...] = jnp.zeros_like(gb_sum)
    parts = [slice(p * MODEL_WIDTH, (p + 1) * MODEL_WIDTH) for p in range(3)]
    d_refs = (d_query, d_key, d_value)

    def block_rows(b):
        return pl.ds(pl.multiple_of(b * ROW_BLOCK, ROW_BLOCK), ROW_BLOCK)

    def sums(b, carry):
        rows = block_rows(b)
        low = low_qkv[rows, :]
        d_low = jnp.zeros((ROW_BLOCK, LANES), F32)
        for cols, ref in zip(parts, d_refs):
            grad = ref[rows, :]
            d_low = d_low + dot_nt(grad, b_out[:, cols])
            gb_sum[:, cols] += dot_tn(low, grad)
        d_low = (d_low * mask[rows, :].astype(F32)).astype(BF16)
        d_low_all[rows, :] = d_low
        ga_sum[...] += dot_tn(act_one[rows, :], d_low)
        return carry

    lax.fori_loop(0, blocks, sums, 0)
    s_ga_qkv[...] = ga_sum[...].astype(BF16)
    s_gb_qkv[...] = gb_sum[...].astype(BF16)
    s_ga_out[...] = ga_out[...].astype(BF16)
    s_gb_out[...] = gb_out[...].astype(BF16)
    groups = (
        (s_ga_qkv, r_ga_qkv), (s_gb_qkv, r_gb_qkv), (s_ga_out, r_ga_out), (s_gb_out, r_gb_out),
    )

    def share(i, d):
        count = groups[i][1].shape[1]
        return groups[i][0].at[pl.ds(pl.multiple_of(d * count, 16), count)]

    def near(i, n):
        goal = (dp + n + 1) % 8
        return pltpu.make_async_remote_copy(
            src_ref=share(i, goal), dst_ref=groups[i][1].at[n], send_sem=send_sems.at[i, n],
            recv_sem=recv_sems.at[i, n], device_id=(goal, z), device_id_type=MESH_ID,
        )

    def send_near(n, carry):
        for i in range(4):
            near(i, n).start()
        return carry

    lax.fori_loop(0, others, send_near, 0)

    for load in loads[:3]:
        load.wait()

    def back(b, carry):
        rows = block_rows(b)
        d_act = dot_nt(d_low_all[rows, :], a_in[...])
        for cols, ref in zip(parts, d_refs):
            d_act = d_act + dot_nt(ref[rows, :], w_qkv[:, cols])
        hid = hid_s[rows, :].astype(F32)
        scale = lax.rsqrt(jnp.mean(hid * hid, axis=-1, keepdims=True) + EPSILON)
        weighted = d_act * gain[...]
        grad_hid = d_resid[rows, :] + (
            scale * weighted
            - hid * (scale * scale * scale) * jnp.mean(hid * weighted, axis=-1, keepdims=True)
        )
        top = grad_hid.astype(BF16)
        high[rows, :] = top
        lower[rows, :] = (grad_hid - top.astype(F32)).astype(BF16)
        return carry

    lax.fori_loop(0, blocks, back, 0)

    def near_done(n, carry):
        for i in range(4):
            near(i, n).wait_recv()
        return carry

    lax.fori_loop(0, others, near_done, 0)
    totals = []
    for i in range(4):
        total = share(i, dp)[...].astype(F32)
        for n in range(others):
            total = total + groups[i][1][n].astype(F32)
        totals.append(total)
    a_qkv, b_qkv, a_o, b_o = totals
    a_count, b_count = a_qkv.shape[0] // 4, b_qkv.shape[0] // 4
    for p in range(4):
        a_rows, b_rows = slice(p * a_count, (p + 1) * a_count), slice(p * b_count, (p + 1) * b_count)
        thin_out[p, :a_count, :LANES] = a_qkv[a_rows].astype(BF16)
        thin_out[p, :a_count, LANES:] = a_o[a_rows].astype(BF16)
        thin_out[p, a_count:, :] = jnp.zeros((thin_out.shape[1] - a_count, 2 * LANES), BF16)
        wide_out[p] = jnp.concatenate(
            [b_qkv[b_rows, cols] for cols in parts] + [b_o[b_rows]], axis=0
        ).astype(BF16)

    def far(i, j):
        goal = (z + j + 1) % 4
        source, target = ((thin_out, thin_in), (wide_out, wide_in))[i]
        return pltpu.make_async_remote_copy(
            src_ref=source.at[goal], dst_ref=target.at[j], send_sem=far_send.at[i, j],
            recv_sem=far_recv.at[i, j], device_id=(dp, goal), device_id_type=MESH_ID,
        )

    for j in range(planes):
        for i in range(2):
            far(i, j).start()
    loads[3].wait()

    def to_rows(b, carry):
        rows = block_rows(b)
        perm = hot_matrix(place_col[rows, :] == iota((ROW_BLOCK, tok), 1))
        out[rows, :] = dot(perm, out_s[...]).astype(BF16)
        grad_hidden[rows, :] = dot(perm, high[...]) + dot(perm, lower[...])
        top, mid, last = split_three(d_logits[...])
        grad_gate[rows, :] = dot(perm, top) + (dot(perm, mid) + dot(perm, last))
        return carry

    lax.fori_loop(0, blocks, to_rows, 0)
    for j in range(planes):
        for i in range(2):
            far(i, j).wait_recv()
    thin = thin_out[z].astype(F32)
    wide = wide_out[z].astype(F32)
    for j in range(planes):
        thin = thin + thin_in[j].astype(F32)
        wide = wide + wide_in[j].astype(F32)
    own_ga_qkv[...] = thin[:a_count, :LANES]
    own_ga_out[...] = thin[:a_count, LANES:]
    for p, cols in enumerate(parts):
        own_gb_qkv[:, cols] = wide[p * b_count : (p + 1) * b_count]
    own_gb_out[...] = wide[3 * b_count : 4 * b_count]

    def sent(n, carry):
        for i in range(4):
            near(i, n).wait_send()
        return carry

    lax.fori_loop(0, others, sent, 0)
    for j in range(planes):
        for i in range(2):
            far(i, j).wait_send()


def split_three(values):
    top = values.astype(BF16)
    rest = values - top.astype(F32)
    mid = rest.astype(BF16)
    return top, mid, (rest - mid.astype(F32)).astype(BF16)


def post_attn_body(
    kinds, attn_low, hid_s, mask, small_s, w_out, a_out, b_out, router, gain,
    low_out, resid, act_two, gate,
):
    attn = attn_low[...]
    low = (dot(attn, a_out[...]) * mask[...].astype(F32)).astype(BF16)
    low_out[...] = low
    res = hid_s[...].astype(F32) + (dot(attn, w_out[...]) + dot(low, b_out[...]))
    resid[...] = res
    scale = lax.rsqrt(jnp.mean(res * res, axis=-1, keepdims=True) + EPSILON)
    act = (res * scale * gain[...]).astype(BF16)
    act_two[...] = act
    sm = small_s[...]
    carry = sm + (pltpu.roll(sm, LANES - 16, 1) + pltpu.roll(sm, LANES - 32, 1))
    logits = dot(act, router[...])
    lane = iota(logits.shape, 1)
    routed = jnp.where(lane < kinds, logits + carry, -1e30)
    top = jnp.max(routed, axis=1, keepdims=True)
    expo = jnp.exp(routed - top)
    prob = expo / jnp.sum(expo, axis=1, keepdims=True)
    gate[...] = jnp.where(lane < kinds, prob, logits)


def dispatch_body(experts, eids, small_s, gate, act_two, dy_s, mask, slot, sent, slot_rows):
    tok = act_two.shape[0]
    cap = sent.shape[1]
    step = pl.program_id(0)

    @pl.when(step == 0)
    def _():
        lane = iota((tok, LANES), 1)
        first = small_s[:, CHOICE_LANE : CHOICE_LANE + 1].astype(jnp.int32)
        second = small_s[:, CHOICE_LANE + 1 : CHOICE_LANE + 2].astype(jnp.int32)
        hot = ((first == lane) | (second == lane)) & (lane < experts)
        hot_low = hot_matrix(hot)
        for blk in range(tok // ROW_BLOCK):
            lo, hi = blk * ROW_BLOCK, (blk + 1) * ROW_BLOCK
            tri = hot_matrix(iota((ROW_BLOCK, hi), 1) < lo + iota((ROW_BLOCK, hi), 0))
            rank = dot(tri, hot_low[:hi, :])
            slot[lo:hi, :] = jnp.where(hot[lo:hi, :], rank, -1.0)
        slot_rows[...] = slot[...].T

    eid = eids[step]
    row = slot_rows[pl.ds(eid, 1), :].astype(jnp.int32)
    pick = hot_matrix(row == iota((cap, tok), 0))
    value = lane_value(gate[...], eid)
    scaled = (dy_s[...].astype(F32) * value).astype(BF16)
    sent[0, :, :MODEL_WIDTH] = dot(pick, act_two[...]).astype(BF16)
    sent[0, :, MODEL_WIDTH : 2 * MODEL_WIDTH] = dot(pick, scaled).astype(BF16)
    sent[0, :, 2 * MODEL_WIDTH :] = dot(pick, mask[...]).astype(BF16)


def ffn_math(
    rows, d_out, mask, w_gu, w_dn, a_gu, b_gu, a_dn, b_dn,
    ga_gu, gb_gu, ga_dn, gb_dn, acc_out, acc_dx, acc_low, acc_dlow,
):
    low_gu = (dot(rows, a_gu[...]) * mask).astype(BF16)
    dlow_dn = (dot_nt(d_out, b_dn[...]) * mask).astype(BF16)
    for ref in (acc_out, acc_dx, acc_low, acc_dlow):
        ref[...] = jnp.zeros_like(ref)

    def step(j, carry):
        lo = pl.multiple_of(j * HIDDEN_BLOCK, HIDDEN_BLOCK)
        g_cols = pl.ds(lo, HIDDEN_BLOCK)
        u_cols = pl.ds(pl.multiple_of(FEEDFWD_WIDTH + lo, HIDDEN_BLOCK), HIDDEN_BLOCK)
        gate = dot(rows, w_gu[:, g_cols]) + dot(low_gu, b_gu[:, g_cols])
        up = dot(rows, w_gu[:, u_cols]) + dot(low_gu, b_gu[:, u_cols])
        sig = 1.0 / (1.0 + jnp.exp(-gate))
        silu = gate * sig
        middle = (silu * up).astype(BF16)
        acc_out[...] += dot(middle, w_dn[g_cols, :])
        acc_low[...] += dot(middle, a_dn[g_cols, :])
        d_mid = dot_nt(d_out, w_dn[g_cols, :]) + dot_nt(dlow_dn, a_dn[g_cols, :])
        d_mid = d_mid.astype(BF16).astype(F32)
        d_gate = (d_mid * up * (sig * (1.0 + gate * (1.0 - sig)))).astype(BF16)
        d_up = (d_mid * silu).astype(BF16)
        acc_dx[...] += dot_nt(d_gate, w_gu[:, g_cols]) + dot_nt(d_up, w_gu[:, u_cols])
        acc_dlow[...] += dot_nt(d_gate, b_gu[:, g_cols]) + dot_nt(d_up, b_gu[:, u_cols])
        gb_gu[:, g_cols] += dot_tn(low_gu, d_gate)
        gb_gu[:, u_cols] += dot_tn(low_gu, d_up)
        ga_dn[g_cols, :] += dot_tn(middle, dlow_dn)
        return carry

    lax.fori_loop(0, FEEDFWD_WIDTH // HIDDEN_BLOCK, step, 0)
    low_dn = (acc_low[...] * mask).astype(BF16)
    result = (acc_out[...] + dot(low_dn, b_dn[...])).astype(BF16)
    gb_dn[...] += dot_tn(low_dn, d_out)
    dlow_gu = (acc_dlow[...] * mask).astype(BF16)
    d_rows = (acc_dx[...] + dot_nt(dlow_gu, a_gu[...])).astype(BF16)
    ga_gu[...] += dot_tn(rows, dlow_gu)
    return result, d_rows


def ffn_body(
    came, w_gu, w_dn, a_gu, b_gu, a_dn, b_dn,
    back, ga_gu, gb_gu, ga_dn, gb_dn, acc_out, acc_dx, acc_low, acc_dlow,
):
    @pl.when(pl.program_id(0) == 0)
    def _():
        for ref in (ga_gu, gb_gu, ga_dn, gb_dn):
            ref[...] = jnp.zeros_like(ref)

    back[0, :, :MODEL_WIDTH], back[0, :, MODEL_WIDTH:] = ffn_math(
        came[0, :, :MODEL_WIDTH], came[0, :, MODEL_WIDTH : 2 * MODEL_WIDTH],
        came[0, :, 2 * MODEL_WIDTH :].astype(F32), w_gu, w_dn, a_gu, b_gu, a_dn, b_dn,
        ga_gu, gb_gu, ga_dn, gb_dn, acc_out, acc_dx, acc_low, acc_dlow,
    )


def pair_ffn_body(
    sent, wide, mid, thin,
    returned, out_ga_gu, out_gb_gu, out_ga_dn, out_gb_dn,
    came, back, ga_gu, gb_gu, ga_dn, gb_dn, w_gu, w_dn, a_gu, b_gu, a_dn, b_dn, acc_out, acc_dx, acc_low, acc_dlow,
    load_sems, send_sems, came_sems, back_sems, done_sems,
):
    dp, z = lax.axis_index("dp"), lax.axis_index("expert")
    core, plane = dp % 2, z % 2

    def peer(k):
        return (dp + (k // 2) * (1 - 2 * core), z + (k % 2) * (1 - 2 * plane))

    barrier = pltpu.get_barrier_semaphore()
    for k in (1, 2, 3):
        pl.semaphore_signal(barrier, inc=1, device_id=peer(k), device_id_type=MESH_ID)
    pl.semaphore_wait(barrier, 3)

    def rows_out(k):
        return pltpu.make_async_remote_copy(
            src_ref=sent.at[k], dst_ref=came.at[k], send_sem=send_sems.at[k],
            recv_sem=came_sems.at[k], device_id=peer(k), device_id_type=MESH_ID,
        )

    def result_out(k):
        return pltpu.make_async_remote_copy(
            src_ref=back.at[k], dst_ref=returned.at[k], send_sem=back_sems.at[k],
            recv_sem=done_sems.at[k], device_id=peer(k), device_id_type=MESH_ID,
        )

    for k in (1, 2, 3):
        rows_out(k).start()
    own_in = pltpu.make_async_copy(sent.at[0], came.at[0], came_sems.at[0])
    own_in.start()

    gu_rows = w_gu.shape[0] // wide.shape[0]
    up_rows = b_gu.shape[0] // wide.shape[0]
    dn_rows = w_dn.shape[0] // wide.shape[0]
    plans = (
        (wide, 0, gu_rows, w_gu), (wide, gu_rows, up_rows, b_gu), (mid, 0, dn_rows, w_dn),
        (mid, dn_rows, up_rows, b_dn), (thin, 0, gu_rows, a_gu), (thin, gu_rows, dn_rows, a_dn),
    )

    def load(d, carry):
        for i, (source, at, count, target) in enumerate(plans):
            pltpu.make_async_copy(
                source.at[d, pl.ds(at, count)],
                target.at[pl.ds(pl.multiple_of(d * count, 16), count)],
                load_sems.at[i],
            ).start()
        return carry

    lax.fori_loop(0, wide.shape[0], load, 0)
    for ref in (ga_gu, gb_gu, ga_dn, gb_dn):
        ref[...] = jnp.zeros_like(ref)
    for i, (_, _, _, target) in enumerate(plans):
        pltpu.make_async_copy(target, target, load_sems.at[i]).wait()

    def source_step(s, carry):
        k = (s % 2) * 2 + s // 2

        @pl.when(s == 0)
        def _():
            own_in.wait()

        @pl.when(s > 0)
        def _():
            rows_out(k).wait_recv()

        back[k, :, :MODEL_WIDTH], back[k, :, MODEL_WIDTH:] = ffn_math(
            came[k, :, :MODEL_WIDTH], came[k, :, MODEL_WIDTH : 2 * MODEL_WIDTH],
            came[k, :, 2 * MODEL_WIDTH :].astype(F32), w_gu, w_dn, a_gu, b_gu, a_dn, b_dn,
            ga_gu, gb_gu, ga_dn, gb_dn, acc_out, acc_dx, acc_low, acc_dlow,
        )

        @pl.when(s > 0)
        def _():
            result_out(k).start()

        return carry

    lax.fori_loop(0, 4, source_step, 0)
    for out, total in (
        (out_ga_gu, ga_gu), (out_gb_gu, gb_gu), (out_ga_dn, ga_dn), (out_gb_dn, gb_dn),
    ):
        out[...] = total[...].astype(BF16)
    own_out = pltpu.make_async_copy(back.at[0], returned.at[0], done_sems.at[0])
    own_out.start()
    own_out.wait()
    for k in (1, 2, 3):
        rows_out(k).wait_send()
        result_out(k).wait_send()
        result_out(k).wait_recv()


def combine_body(
    experts, kinds, eids, resid, act_two, dy_s, gate, slot, small_s, low_out, attn_low, mask, came,
    w_out, a_out, b_out, router, const_value, gain,
    out_s, d_resid, d_attended, d_logits, ga_out, gb_out,
):
    @pl.when(pl.program_id(0) == 0)
    def _():
        ga_out[...] = jnp.zeros_like(ga_out)
        gb_out[...] = jnp.zeros_like(gb_out)

    rows = resid.shape[0]
    cap = came.shape[1]
    res = resid[...]
    act = act_two[...].astype(F32)
    dy = dy_s[...].astype(F32)
    prob = gate[...]
    lane = iota((rows, LANES), 1)
    out = res
    d_act = jnp.zeros((rows, MODEL_WIDTH), F32)
    d_gate = jnp.zeros((rows, LANES), F32)
    for k in range(came.shape[0]):
        eid = eids[k]
        place = lane_value(slot[...], eid).astype(jnp.int32)
        pick = hot_matrix(place == iota((rows, cap), 1))
        result = dot(pick, came[k, :, :MODEL_WIDTH])
        d_act = d_act + dot(pick, came[k, :, MODEL_WIDTH:])
        d_gate = jnp.where(lane == eid, jnp.sum(dy * result, axis=1, keepdims=True), d_gate)
        out = out + lane_value(prob, eid) * result
    sm = small_s[...]
    first = sm[:, CHOICE_LANE : CHOICE_LANE + 1]
    second = sm[:, CHOICE_LANE + 1 : CHOICE_LANE + 2]

    def chosen(kind):
        return jnp.where((first == kind) | (second == kind), 1.0, 0.0)

    has_copy, has_zero, has_one = chosen(experts + 1), chosen(experts + 2), chosen(experts + 3)
    g_copy = has_copy * prob[:, experts + 1 : experts + 2]
    g_zero = has_zero * prob[:, experts + 2 : experts + 3]
    g_one = has_one * prob[:, experts + 3 : experts + 4]

    def pair(at):
        left, right = prob[:, at : at + 1], prob[:, at + 1 : at + 2]
        top = jnp.maximum(left, right)
        e_left, e_right = jnp.exp(left - top), jnp.exp(right - top)
        return e_left / (e_left + e_right), e_right / (e_left + e_right)

    a00, a01 = pair(CONST_LANE)
    a10, a11 = pair(CONST_LANE + 2)
    v_zero, v_one = const_value[0:1, :], const_value[1:2, :]
    along_act = jnp.sum(dy * act, axis=1, keepdims=True)
    along_zero = jnp.sum(dy * v_zero, axis=1, keepdims=True)
    along_one = jnp.sum(dy * v_one, axis=1, keepdims=True)
    coef = g_copy + g_zero * a00 + g_one * a10
    out = out + coef * act + (g_zero * a01) * v_zero + (g_one * a11) * v_one
    out_s[...] = out.astype(BF16)
    d_gate = jnp.where(lane == experts + 1, has_copy * along_act, d_gate)
    d_gate = jnp.where(
        lane == experts + 2, has_zero * (a00 * along_act + a01 * along_zero), d_gate
    )
    d_gate = jnp.where(lane == experts + 3, has_one * (a10 * along_act + a11 * along_one), d_gate)
    prob = jnp.where(lane < kinds, prob, 0.0)
    d_logit = prob * (d_gate - jnp.sum(prob * d_gate, axis=1, keepdims=True))
    d_logits[...] = d_logit
    mix = d_logit
    for at, g_val, left, right, along in (
        (CONST_LANE, g_zero, a00, a01, along_zero),
        (CONST_LANE + 2, g_one, a10, a11, along_one),
    ):
        da_left, da_right = g_val * along_act, g_val * along
        level = left * da_left + right * da_right
        mix = jnp.where(lane == at, left * (da_left - level), mix)
        mix = jnp.where(lane == at + 1, right * (da_right - level), mix)
    mix_hi = mix.astype(BF16)
    mix_lo = (mix - mix_hi.astype(F32)).astype(BF16)
    d_act = d_act + coef * dy + (dot_nt(mix_hi, router[...]) + dot_nt(mix_lo, router[...]))
    scale = lax.rsqrt(jnp.mean(res * res, axis=-1, keepdims=True) + EPSILON)
    weighted = d_act * gain[...]
    d_res = dy + (
        scale * weighted
        - res * (scale * scale * scale) * jnp.mean(res * weighted, axis=-1, keepdims=True)
    )
    d_resid[...] = d_res
    d_attn = d_res.astype(BF16)
    dlow = (dot_nt(d_attn, b_out[...]) * mask[...].astype(F32)).astype(BF16)
    gb_out[...] += dot_tn(low_out[...], d_attn)
    ga_out[...] += dot_tn(attn_low[...], dlow)
    d_attended[...] = (dot_nt(d_attn, w_out[...]) + dot_nt(dlow, a_out[...])).astype(BF16)


def input_grad_body(
    d_query, d_key, d_value, low_qkv, act_one, mask, hid_s, d_resid, w_qkv, a_in, b_out, gain,
    high, lower, ga_qkv, gb_qkv,
):
    @pl.when(pl.program_id(0) == 0)
    def _():
        ga_qkv[...] = jnp.zeros_like(ga_qkv)
        gb_qkv[...] = jnp.zeros_like(gb_qkv)

    d_low = jnp.zeros((d_query.shape[0], LANES), F32)
    d_act = jnp.zeros((d_query.shape[0], MODEL_WIDTH), F32)
    for part, ref in enumerate((d_query, d_key, d_value)):
        cols = slice(part * MODEL_WIDTH, (part + 1) * MODEL_WIDTH)
        grad = ref[...]
        d_low = d_low + dot_nt(grad, b_out[:, cols])
        d_act = d_act + dot_nt(grad, w_qkv[:, cols])
        gb_qkv[:, cols] += dot_tn(low_qkv[...], grad)
    d_low = (d_low * mask[...].astype(F32)).astype(BF16)
    ga_qkv[...] += dot_tn(act_one[...], d_low)
    d_act = d_act + dot_nt(d_low, a_in[...])
    hid = hid_s[...].astype(F32)
    scale = lax.rsqrt(jnp.mean(hid * hid, axis=-1, keepdims=True) + EPSILON)
    weighted = d_act * gain[...]
    grad_hid = d_resid[...] + (
        scale * weighted
        - hid * (scale * scale * scale) * jnp.mean(hid * weighted, axis=-1, keepdims=True)
    )
    top = grad_hid.astype(BF16)
    high[...] = top
    lower[...] = (grad_hid - top.astype(F32)).astype(BF16)


def to_rows_body(place_col, out_s, d_logits, high, lower, out, grad_hidden, grad_gate):
    rows = out.shape[0]
    tok = out_s.shape[0]
    perm = hot_matrix(place_col[...] == iota((rows, tok), 1))
    out[...] = dot(perm, out_s[...]).astype(BF16)
    grad_hidden[...] = dot(perm, high[...]) + dot(perm, lower[...])
    logits = d_logits[...]
    top = logits.astype(BF16)
    rest = logits - top.astype(F32)
    mid = rest.astype(BF16)
    last = (rest - mid.astype(F32)).astype(BF16)
    grad_gate[...] = dot(perm, top) + (dot(perm, mid) + dot(perm, last))


class PairPlan:
    paired = True

    def __init__(self, dp, ex):
        self.ex = ex

    def expert_ids(self):
        own = lax.axis_index("expert") % 2 + 2 * (lax.axis_index("dp") % 2)
        return own ^ jnp.arange(self.ex, dtype=jnp.int32)


class AxisPlan:
    paired = False

    def __init__(self, dp, ex):
        self.dp, self.ex = dp, ex

    def gather(self, shard):
        return lax.all_gather(shard, "dp", axis=0)

    def expert_ids(self):
        return jnp.arange(self.ex, dtype=jnp.int32)

    def exchange(self, values):
        return lax.all_to_all(values, "expert", split_axis=0, concat_axis=0, tiled=True)

    def reduce(self, sums):
        return lax.psum_scatter(sums, "dp", scatter_dimension=0, tiled=True)[0].astype(F32)

    def reduce_all(self, sums):
        return lax.psum_scatter(
            sums, ("dp", "expert"), scatter_dimension=0, tiled=True
        )[0].astype(F32)


def shards(
    dp_size,
    expert_count,
    hidden_input,
    gate_carryover,
    sequence_length,
    token_stream_place,
    expert_choice_index,
    sequence_adapter,
    attention_gain,
    query_key_weight,
    output_weight,
    adapter_in_query,
    adapter_out_query,
    adapter_in_output,
    adapter_out_output,
    feedfwd_gain,
    router_weight,
    constant_gate,
    constant_value,
    gate_upward_weight,
    down_weight,
    adapter_in_gate,
    adapter_out_gate,
    adapter_in_down,
    adapter_out_down,
    output_gradient,
):
    tok = hidden_input.shape[0]
    width = MODEL_WIDTH
    kinds = expert_count + 4
    devices = dp_size * expert_count
    capacity = 5 * tok // (2 * kinds) // 8 * 8 + 8
    cap = -(-capacity // 16) * 16
    blocks = tok // ROW_BLOCK
    plan = (PairPlan if (dp_size, expert_count) == (8, 4) else AxisPlan)(dp_size, expert_count)

    a_rows, b_rows = query_key_weight.shape[0], adapter_out_query.shape[0]
    gu_rows, up_rows, dn_rows = (
        gate_upward_weight.shape[1], adapter_out_gate.shape[1], down_weight.shape[1],
    )
    pad_rows = -(a_rows + b_rows) % 16

    def pack(weight, adapter_in, adapter_out):
        lower = jnp.pad(adapter_out, ((0, pad_rows), (0, LANES)))
        return jnp.concatenate([jnp.concatenate([weight, adapter_in], axis=1), lower], axis=0)

    own_qkv = pack(query_key_weight, adapter_in_query, adapter_out_query)
    own_out = pack(output_weight, adapter_in_output, adapter_out_output)
    own_wide = jnp.concatenate([gate_upward_weight[0], adapter_out_gate[0]], axis=0)
    own_mid = jnp.concatenate([down_weight[0], adapter_out_down[0]], axis=0)
    own_thin = jnp.concatenate([adapter_in_gate[0], adapter_in_down[0]], axis=0)

    place = token_stream_place[0]
    ends = jnp.cumsum(sequence_length[0])
    begins = ends - sequence_length[0]
    stream = jnp.arange(tok, dtype=jnp.int32)
    seg = jnp.sum((stream[:, None] >= ends[None, :]).astype(jnp.int32), axis=1)
    seg_hot = seg[:, None] == jnp.arange(ends.shape[0], dtype=jnp.int32)[None, :]
    start = jnp.sum(jnp.where(seg_hot, begins[None, :], 0), axis=1)
    adapter = jnp.sum(jnp.where(seg_hot, sequence_adapter[0][None, :], 0), axis=1)
    half = HEAD_DIM // 2
    freq = jnp.exp(jnp.arange(half, dtype=F32) * (-math.log(10000.0) / half))
    angle = (stream - start).astype(F32)[:, None] * freq[None, :]
    cos, sin = jnp.cos(angle), jnp.sin(angle)
    cosine = jnp.concatenate([cos, cos, cos, cos], axis=1)
    sine = jnp.concatenate([-sin, sin, -sin, sin], axis=1)
    starts = start[:, None]
    mask = (jnp.arange(LANES)[None, :] // ADAPTER_RANK == adapter[:, None]).astype(BF16)
    top, middle, last = split_three(gate_carryover)
    gap = jnp.zeros((tok, 16 - kinds), BF16)
    small = jnp.concatenate(
        [top, gap, middle, gap, last, gap, expert_choice_index.astype(BF16),
         jnp.zeros((tok, LANES - CHOICE_LANE - 2), BF16)],
        axis=1,
    )
    gain_one = attention_gain.astype(F32)[None, :]
    gain_two = feedfwd_gain.astype(F32)[None, :]
    router = jnp.concatenate(
        [router_weight, jnp.zeros((width, CONST_LANE - kinds), BF16), constant_gate,
         jnp.zeros((width, LANES - CONST_LANE - 4), BF16)],
        axis=1,
    )
    const_value = constant_value.astype(F32)

    full = whole
    hbm = pl.BlockSpec(memory_space=pl.ANY)
    vmem = pl.BlockSpec(memory_space=pltpu.VMEM)
    pairs = HEAD_COUNT // 2
    if plan.paired:
        shapes = [
            sds((tok, width), BF16), sds((tok, width), BF16), sds((tok, LANES), F32),
            sds((tok, width), BF16), sds((tok, LANES), BF16), sds((tok, width), BF16),
            sds((tok, width), BF16), sds((tok, width), BF16), sds((width, 3 * width), BF16),
            sds((width, LANES), BF16), sds((LANES, 3 * width), BF16), sds((width, width), BF16),
            sds((width, LANES), BF16), sds((LANES, width), BF16), sds((tok, width), BF16),
            sds((tok, LANES), F32), sds((tok, LANES), BF16), sds((tok, width), F32),
            sds((tok, width), BF16), sds((tok, LANES), F32),
        ]
        (
            hid_s, dy_s, small_s, act_one, low_qkv, query, key, value, w_qkv, a_qkv, b_qkv,
            w_out, a_out, b_out, attn_low, lse, low_out, resid, act_two, gate, wide, mid, thin,
        ) = pl.pallas_call(
            functools.partial(pair_front_body, kinds, a_rows, b_rows),
            in_specs=[vmem] * 11 + [hbm] * 5,
            out_specs=[hbm] * 23,
            out_shape=shapes
            + [sds((dp_size,) + w.shape, BF16) for w in (own_wide, own_mid, own_thin)],
            scratch_shapes=[pltpu.VMEM(s.shape, s.dtype) for s in shapes]
            + [
                pltpu.VMEM((devices,) + own_qkv.shape, BF16),
                pltpu.VMEM((devices,) + own_out.shape, BF16),
                pltpu.SemaphoreType.DMA((2, 35)), pltpu.SemaphoreType.DMA((2, 35)),
                pltpu.SemaphoreType.DMA((4, 8)), pltpu.SemaphoreType.DMA((4, 8)),
                pltpu.SemaphoreType.DMA((20,)), pltpu.SemaphoreType.DMA((2,)),
            ],
            compiler_params=pltpu.CompilerParams(
                vmem_limit_bytes=VMEM_BYTES, collective_id=4, has_side_effects=True
            ),
            name="pair_front",
        )(place[None, :], hidden_input, output_gradient, small, cosine, sine, mask, starts,
          gain_one, gain_two, router, own_qkv, own_out, own_wide, own_mid, own_thin)
    else:
        all_qkv = lax.all_gather(own_qkv, ("dp", "expert"), axis=0)
        all_out = lax.all_gather(own_out, ("dp", "expert"), axis=0)
        upper = slice(a_rows, a_rows + b_rows)
        w_qkv = all_qkv[:, :a_rows, : 3 * width].reshape(width, 3 * width)
        a_qkv = all_qkv[:, :a_rows, 3 * width :].reshape(width, LANES)
        b_qkv = all_qkv[:, upper, : 3 * width].reshape(LANES, 3 * width)
        w_out = all_out[:, :a_rows, :width].reshape(width, width)
        a_out = all_out[:, :a_rows, width:].reshape(width, LANES)
        b_out = all_out[:, upper, :width].reshape(LANES, width)
        wide, mid, thin = (plan.gather(w) for w in (own_wide, own_mid, own_thin))
        hid_s, dy_s, small_s, act_one, low_qkv, query, key, value = call(
            proj_in_body,
            (blocks,),
            [full((1, tok)), full((tok, width)), full((tok, width)), full((tok, LANES)),
             row_spec(LANES), row_spec(LANES), row_spec(LANES), full((1, width)),
             full((width, 3 * width)), full((width, LANES)), full((LANES, 3 * width))],
            [row_spec(width), row_spec(width), row_spec(LANES), row_spec(width), row_spec(LANES),
             row_spec(width), row_spec(width), row_spec(width)],
            [sds((tok, width), BF16), sds((tok, width), BF16), sds((tok, LANES), F32),
             sds((tok, width), BF16), sds((tok, LANES), BF16), sds((tok, width), BF16),
             sds((tok, width), BF16), sds((tok, width), BF16)],
            name="proj_in",
        )(place[None, :], hidden_input, output_gradient, small, cosine, sine, mask, gain_one,
          w_qkv, a_qkv, b_qkv)

        attn_low, lse = call(
            attention_fwd_body,
            (pairs,),
            [col_spec(tok)] * 3 + [full((tok, 1))],
            [col_spec(tok), full((tok, LANES))],
            [sds((tok, width), BF16), sds((tok, LANES), F32)],
            name="attention_fwd",
        )(query, key, value, starts)

        low_out, resid, act_two, gate = call(
            functools.partial(post_attn_body, kinds),
            (blocks,),
            [row_spec(width), row_spec(width), row_spec(LANES), row_spec(LANES), full((width, width)),
             full((width, LANES)), full((LANES, width)), full((width, LANES)), full((1, width))],
            [row_spec(LANES), row_spec(width), row_spec(width), row_spec(LANES)],
            [sds((tok, LANES), BF16), sds((tok, width), F32), sds((tok, width), BF16),
             sds((tok, LANES), F32)],
            name="post_attn",
        )(attn_low, hid_s, mask, small_s, w_out, a_out, b_out, router, gain_two)

    eids = plan.expert_ids()
    smem = pl.BlockSpec(memory_space=pltpu.SMEM)
    sent_width = 2 * width + LANES
    slot, sent = call(
        functools.partial(dispatch_body, expert_count),
        (expert_count,),
        [smem, full((tok, LANES)), full((tok, LANES)), full((tok, width)), full((tok, width)),
         full((tok, LANES))],
        [full((tok, LANES)), pl.BlockSpec((1, cap, sent_width), lambda i: (i, 0, 0))],
        [sds((tok, LANES), F32), sds((expert_count, cap, sent_width), BF16)],
        scratch=[pltpu.VMEM((LANES, tok), F32)],
        name="dispatch",
    )(eids, small_s, gate, act_two, dy_s, mask)

    grad_shapes = [
        sds((width, LANES), F32), sds((LANES, 2 * FEEDFWD_WIDTH), F32),
        sds((FEEDFWD_WIDTH, LANES), F32), sds((LANES, width), F32),
    ]
    accumulators = [
        pltpu.VMEM((cap, width), F32), pltpu.VMEM((cap, width), F32),
        pltpu.VMEM((cap, LANES), F32), pltpu.VMEM((cap, LANES), F32),
    ]
    if plan.paired:
        returned, ga_gu, gb_gu, ga_dn, gb_dn = pl.pallas_call(
            pair_ffn_body,
            in_specs=[hbm] * 4,
            out_specs=[hbm] + [vmem] * 4,
            out_shape=[sds((expert_count, cap, 2 * width), BF16)]
            + [sds(g.shape, BF16) for g in grad_shapes],
            scratch_shapes=[
                pltpu.VMEM((expert_count, cap, sent_width), BF16),
                pltpu.VMEM((expert_count, cap, 2 * width), BF16),
                *[pltpu.VMEM(g.shape, F32) for g in grad_shapes],
                pltpu.VMEM((width, 2 * FEEDFWD_WIDTH), BF16), pltpu.VMEM((FEEDFWD_WIDTH, width), BF16),
                pltpu.VMEM((width, LANES), BF16), pltpu.VMEM((LANES, 2 * FEEDFWD_WIDTH), BF16),
                pltpu.VMEM((FEEDFWD_WIDTH, LANES), BF16), pltpu.VMEM((LANES, width), BF16),
                *accumulators,
                pltpu.SemaphoreType.DMA((6,)),
                *[pltpu.SemaphoreType.DMA((expert_count,)) for _ in range(4)],
            ],
            compiler_params=pltpu.CompilerParams(
                vmem_limit_bytes=VMEM_BYTES, collective_id=1, has_side_effects=True
            ),
            name="pair_ffn",
        )(sent, wide, mid, thin)
    else:
        w_gu = wide[:, :gu_rows].reshape(width, 2 * FEEDFWD_WIDTH)
        b_gu = wide[:, gu_rows:].reshape(LANES, 2 * FEEDFWD_WIDTH)
        w_dn = mid[:, :dn_rows].reshape(FEEDFWD_WIDTH, width)
        b_dn = mid[:, dn_rows:].reshape(LANES, width)
        a_gu = thin[:, :gu_rows].reshape(width, LANES)
        a_dn = thin[:, gu_rows:].reshape(FEEDFWD_WIDTH, LANES)
        came = plan.exchange(sent)
        back, ga_gu, gb_gu, ga_dn, gb_dn = call(
            ffn_body,
            (expert_count,),
            [pl.BlockSpec((1, cap, sent_width), lambda i: (i, 0, 0)),
             full((width, 2 * FEEDFWD_WIDTH)), full((FEEDFWD_WIDTH, width)), full((width, LANES)),
             full((LANES, 2 * FEEDFWD_WIDTH)), full((FEEDFWD_WIDTH, LANES)), full((LANES, width))],
            [pl.BlockSpec((1, cap, 2 * width), lambda i: (i, 0, 0)), full((width, LANES)),
             full((LANES, 2 * FEEDFWD_WIDTH)), full((FEEDFWD_WIDTH, LANES)), full((LANES, width))],
            [sds((expert_count, cap, 2 * width), BF16)] + grad_shapes,
            scratch=accumulators,
            name="ffn",
        )(came, w_gu, w_dn, a_gu, b_gu, a_dn, b_dn)
        returned = plan.exchange(back)

    out_s, d_resid, d_attended, d_logits, ga_out, gb_out = call(
        functools.partial(combine_body, expert_count, kinds),
        (blocks,),
        [smem, row_spec(width), row_spec(width), row_spec(width), row_spec(LANES), row_spec(LANES),
         row_spec(LANES), row_spec(LANES), row_spec(width), row_spec(LANES),
         full((expert_count, cap, 2 * width)), full((width, width)), full((width, LANES)),
         full((LANES, width)), full((width, LANES)), full((2, width)), full((1, width))],
        [row_spec(width), row_spec(width), row_spec(width), row_spec(LANES), full((width, LANES)),
         full((LANES, width))],
        [sds((tok, width), BF16), sds((tok, width), F32), sds((tok, width), BF16),
         sds((tok, LANES), F32), sds((width, LANES), F32), sds((LANES, width), F32)],
        name="combine",
    )(eids, resid, act_two, dy_s, gate, slot, small_s, low_out, attn_low, mask, returned,
      w_out, a_out, b_out, router, const_value, gain_two)

    if plan.paired:
        flow = dict(vmem_limit_bytes=VMEM_BYTES, has_side_effects=True)
        own_shapes = [
            sds((gu_rows, LANES), F32), sds((up_rows, 2 * FEEDFWD_WIDTH), F32),
            sds((dn_rows, LANES), F32), sds((up_rows, width), F32),
        ]
        d_query, d_key, d_value, *expert_owned = pl.pallas_call(
            pair_attention_bwd_body,
            grid=(pairs,),
            in_specs=[col_spec(tok)] * 5
            + [full((tok, LANES)), full((tok, 1)), full((tok, LANES)), full((tok, LANES))]
            + [hbm] * 4,
            out_specs=[col_spec(tok)] * 3 + [full(s.shape) for s in own_shapes],
            out_shape=[sds((tok, width), BF16)] * 3 + own_shapes,
            scratch_shapes=[pltpu.VMEM((tok, LANES), F32), pltpu.VMEM((tok, LANES), F32)]
            + [pltpu.VMEM((dp_size,) + s.shape, BF16) for s in own_shapes]
            + [pltpu.SemaphoreType.DMA((4, dp_size)), pltpu.SemaphoreType.DMA((4, dp_size))],
            compiler_params=pltpu.CompilerParams(collective_id=2, **flow),
            name="pair_attention_bwd",
        )(query, key, value, d_attended, attn_low, lse, starts, cosine, sine,
          ga_gu, gb_gu, ga_dn, gb_dn)
        sum_shapes = [(width, LANES), (LANES, 3 * width), (width, LANES), (LANES, width)]
        got_shapes = [(dp_size - 1, a // dp_size, b) for a, b in sum_shapes]
        thin_rows = -(-a_rows // 16) * 16
        output, grad_hidden, grad_gate, *attn_owned = pl.pallas_call(
            pair_tail_body,
            in_specs=[vmem] * 13 + [hbm] * 4,
            out_specs=[vmem] * 7,
            out_shape=[
                sds((tok, width), BF16), sds((tok, width), F32), sds((tok, LANES), F32),
                sds((a_rows, LANES), F32), sds((b_rows, 3 * width), F32),
                sds((a_rows, LANES), F32), sds((b_rows, width), F32),
            ],
            scratch_shapes=[
                pltpu.VMEM((tok, width), BF16), pltpu.VMEM((tok, width), F32),
                pltpu.VMEM((width, 3 * width), BF16), pltpu.VMEM((tok, width), BF16),
                pltpu.VMEM((tok, width), BF16), pltpu.VMEM((tok, width), BF16),
                pltpu.VMEM((tok, LANES), BF16),
                pltpu.VMEM((width, LANES), F32), pltpu.VMEM((LANES, 3 * width), F32),
                *[pltpu.VMEM(shape, BF16) for shape in sum_shapes + got_shapes],
                pltpu.VMEM((expert_count, thin_rows, 2 * LANES), BF16),
                pltpu.VMEM((expert_count, 4 * b_rows, width), BF16),
                pltpu.VMEM((expert_count - 1, thin_rows, 2 * LANES), BF16),
                pltpu.VMEM((expert_count - 1, 4 * b_rows, width), BF16),
                pltpu.SemaphoreType.DMA((4,)),
                pltpu.SemaphoreType.DMA((4, dp_size - 1)), pltpu.SemaphoreType.DMA((4, dp_size - 1)),
                pltpu.SemaphoreType.DMA((2, expert_count - 1)),
                pltpu.SemaphoreType.DMA((2, expert_count - 1)),
            ],
            compiler_params=pltpu.CompilerParams(collective_id=3, **flow),
            name="pair_tail",
        )(place[:, None], d_query, d_key, d_value, low_qkv, act_one, mask, a_qkv, b_qkv, gain_one,
          ga_out, gb_out, d_logits, hid_s, d_resid, w_qkv, out_s)
        return (
            output, grad_hidden, grad_gate[:, :kinds], *attn_owned,
            *[expert_owned[i][None] for i in range(4)],
        )

    owned_wide = plan.reduce(
        jnp.concatenate([gb_gu, gb_dn], axis=1).astype(BF16).reshape(dp_size, up_rows, -1)
    )
    owned_thin = plan.reduce(
        jnp.concatenate(
            [ga_gu.reshape(dp_size, gu_rows, LANES), ga_dn.reshape(dp_size, dn_rows, LANES)], axis=1
        ).astype(BF16)
    )

    d_query, d_key, d_value = call(
        attention_bwd_body,
        (pairs,),
        [col_spec(tok)] * 5
        + [full((tok, LANES)), full((tok, 1)), full((tok, LANES)), full((tok, LANES))],
        [col_spec(tok)] * 3,
        [sds((tok, width), BF16)] * 3,
        scratch=[pltpu.VMEM((tok, LANES), F32), pltpu.VMEM((tok, LANES), F32)],
        name="attention_bwd",
    )(query, key, value, d_attended, attn_low, lse, starts, cosine, sine)

    high, lower, ga_qkv, gb_qkv = call(
        input_grad_body,
        (blocks,),
        [row_spec(width)] * 3 + [row_spec(LANES), row_spec(width), row_spec(LANES), row_spec(width),
         row_spec(width), full((width, 3 * width)), full((width, LANES)), full((LANES, 3 * width)),
         full((1, width))],
        [row_spec(width), row_spec(width), full((width, LANES)), full((LANES, 3 * width))],
        [sds((tok, width), BF16), sds((tok, width), BF16), sds((width, LANES), F32),
         sds((LANES, 3 * width), F32)],
        name="input_grad",
    )(d_query, d_key, d_value, low_qkv, act_one, mask, hid_s, d_resid, w_qkv, a_qkv, b_qkv,
      gain_one)

    owned = plan.reduce_all(
        jnp.concatenate(
            [
                ga_qkv.reshape(devices, b_rows, -1),
                ga_out.reshape(devices, b_rows, -1),
                gb_qkv.reshape(devices, b_rows, -1),
                gb_out.reshape(devices, b_rows, -1),
            ],
            axis=2,
        ).astype(BF16)
    )

    output, grad_hidden, grad_gate = call(
        to_rows_body,
        (blocks,),
        [row_spec(1), full((tok, width)), full((tok, LANES)), full((tok, width)),
         full((tok, width))],
        [row_spec(width), row_spec(width), row_spec(LANES)],
        [sds((tok, width), BF16), sds((tok, width), F32), sds((tok, LANES), F32)],
        name="to_rows",
    )(place[:, None], out_s, d_logits, high, lower)

    return (
        output,
        grad_hidden,
        grad_gate[:, :kinds],
        owned[:, :width].reshape(a_rows, LANES),
        owned[:, 2 * width : 5 * width],
        owned[:, width : 2 * width].reshape(a_rows, LANES),
        owned[:, 5 * width :],
        owned_thin[None, :gu_rows],
        owned_wide[None, :, : 2 * FEEDFWD_WIDTH],
        owned_thin[None, gu_rows:],
        owned_wide[None, :, 2 * FEEDFWD_WIDTH :],
    )


def solution(mesh):
    rows = P(("dp", "expert"), None)
    expert_rows = P("expert", "dp", None)
    in_specs = (
        (rows,) * 6 + (P(),) + (rows,) * 6 + (P(),) * 4 + (expert_rows,) * 6 + (rows,)
    )
    out_specs = (rows,) * 7 + (expert_rows,) * 4
    body = functools.partial(shards, mesh.shape["dp"], mesh.shape["expert"])
    return jax.shard_map(body, mesh=mesh, in_specs=in_specs, out_specs=out_specs, check_vma=False)
```

```python
import functools
import math

import jax
import jax.numpy as jnp
from jax import lax
from jax.experimental import pallas as pl
from jax.experimental.pallas import tpu as pltpu
from jax.sharding import PartitionSpec as P

MODEL_WIDTH = 768
HEAD_COUNT = 12
HEAD_DIM = 64
FEEDFWD_WIDTH = 2048
ADAPTER_RANK = 16
ROW_BLOCK = 256
HIDDEN_BLOCK = 512
LANES = 128
CONST_LANE = 64
CHOICE_LANE = 48
EPSILON = 1e-06
VMEM_BYTES = 60 * 2**20
FRONT_KEPT = 26
MESH_ID = pl.DeviceIdType.MESH

F32 = jnp.float32
BF16 = jnp.bfloat16


def dot(a, b):
    return jnp.dot(a, b, preferred_element_type=F32)


def dot_nt(a, b):
    return lax.dot_general(a, b, (((1,), (1,)), ((), ())), preferred_element_type=F32)


def dot_tn(a, b):
    return lax.dot_general(a, b, (((0,), (0,)), ((), ())), preferred_element_type=F32)


def iota(shape, dim):
    return lax.broadcasted_iota(jnp.int32, shape, dim)


def hot_matrix(condition):
    return jnp.where(condition, 1.0, 0.0).astype(BF16)


def whole(shape):
    zeros = (0,) * len(shape)
    return pl.BlockSpec(shape, lambda *_: zeros)


def row_spec(width, rows=ROW_BLOCK):
    return pl.BlockSpec((rows, width), lambda i: (i, 0))


def col_spec(rows, width=LANES):
    return pl.BlockSpec((rows, width), lambda j: (0, j))


def sds(shape, dtype):
    return jax.ShapeDtypeStruct(shape, dtype)


def call(body, grid, in_specs, out_specs, out_shape, scratch=(), name=None):
    return pl.pallas_call(
        body,
        grid=grid,
        in_specs=in_specs,
        out_specs=out_specs,
        out_shape=out_shape,
        scratch_shapes=list(scratch),
        compiler_params=pltpu.CompilerParams(vmem_limit_bytes=VMEM_BYTES),
        name=name,
    )


def half_swap(values):
    lane = iota(values.shape, 1)
    up = pltpu.roll(values, 32, 1)
    down = pltpu.roll(values, LANES - 32, 1)
    return jnp.where(lane % HEAD_DIM < HEAD_DIM // 2, down, up)


def lane_value(values, lane_id):
    return jnp.sum(jnp.where(iota(values.shape, 1) == lane_id, values, 0.0), axis=1, keepdims=True)


def proj_in_body(
    place_row, hidden, upstream, small, cosine, sine, mask, gain, w_qkv, a_in, b_out,
    hid_s, dy_s, small_s, act_one, low_qkv, query, key, value,
):
    rows = hid_s.shape[0]
    base = pl.program_id(0) * rows
    perm = hot_matrix(place_row[...] == base + iota((rows, place_row.shape[1]), 0))
    hid = dot(perm, hidden[...])
    hid_s[...] = hid.astype(BF16)
    dy_s[...] = dot(perm, upstream[...]).astype(BF16)
    parts = dot(perm, small[...])
    small_s[...] = parts + (pltpu.roll(parts, LANES - 16, 1) + pltpu.roll(parts, LANES - 32, 1))
    act = normed(hid, gain)
    act_one[...] = act
    low, q_val, k_val, value[...] = project(
        act, mask[...], cosine[...], sine[...], w_qkv, a_in, b_out
    )
    low_qkv[...] = low
    query[...], key[...] = q_val, k_val


def normed(values, gain):
    scale = lax.rsqrt(jnp.mean(values * values, axis=-1, keepdims=True) + EPSILON)
    return (values * scale * gain[...].astype(F32)).astype(BF16)


def project(act, mask, cos, sin, w_qkv, a_in, b_out):
    low = (dot(act, a_in[...]) * mask.astype(F32)).astype(BF16)
    turned = []
    for start, factor in ((0, HEAD_DIM**-0.5), (MODEL_WIDTH, 1.0)):
        cols = slice(start, start + MODEL_WIDTH)
        vals = dot(act, w_qkv[:, cols]) + dot(low, b_out[:, cols])
        pieces = []
        for c in range(MODEL_WIDTH // LANES):
            piece = vals[:, c * LANES : (c + 1) * LANES]
            piece = (piece * cos + half_swap(piece) * sin).astype(BF16)
            pieces.append(piece if factor == 1.0 else piece * jnp.asarray(factor, BF16))
        turned.append(jnp.concatenate(pieces, axis=1))
    value = dot(act, w_qkv[:, 2 * MODEL_WIDTH :]) + dot(low, b_out[:, 2 * MODEL_WIDTH :])
    return low, turned[0], turned[1], value.astype(BF16)


def head_mask(shape, head):
    lane = iota(shape, 1)
    return (lane >= head * HEAD_DIM) & (lane < (head + 1) * HEAD_DIM)


def attention_fwd_body(query, key, value, starts, attended, lse):
    @pl.when(pl.program_id(0) == 0)
    def _():
        lse[...] = jnp.zeros_like(lse)

    attention_fwd_pair(pl.program_id(0), query, key, value, starts, attended, lse)


def attention_fwd_pair(pair, query, key, value, starts, attended, lse):
    tok = query.shape[0]
    size = ROW_BLOCK
    zero = jnp.zeros((), BF16)
    for blk in range(tok // size):
        lo, hi = blk * size, (blk + 1) * size
        q_blk = query[lo:hi, :]
        k_all = key[:hi, :]
        v_all = value[:hi, :]
        begin = starts[lo:hi, :]
        col = iota((size, hi), 1)
        allowed = (col <= lo + iota((size, hi), 0)) & (col >= begin)
        total = jnp.zeros((size, LANES), F32)
        stats = lse[lo:hi, :]
        lane = iota((size, LANES), 1)
        for head in range(2):
            mine = head_mask((size, LANES), head)
            scores = dot_nt(jnp.where(mine, q_blk, zero), k_all)
            scores = jnp.where(allowed, scores, -1000000000.0)
            top = jnp.max(scores, axis=1, keepdims=True)
            expo = jnp.exp(scores - top)
            norm = jnp.sum(expo, axis=1, keepdims=True)
            v_head = jnp.where(head_mask((hi, LANES), head), v_all, zero)
            total = total + dot(expo.astype(BF16), v_head) * (1.0 / norm)
            stats = jnp.where(lane == 2 * pair + head, top + jnp.log(norm), stats)
        attended[lo:hi, :] = total.astype(BF16)
        lse[lo:hi, :] = stats


def attention_bwd_body(
    query, key, value, dout, attended, lse, starts, cosine, sine, d_query, d_key, d_value, kacc, vacc
):
    tok = query.shape[0]
    size = ROW_BLOCK
    zero = jnp.zeros((), BF16)
    kacc[...] = jnp.zeros_like(kacc)
    vacc[...] = jnp.zeros_like(vacc)
    for blk in range(tok // size):
        lo, hi = blk * size, (blk + 1) * size
        q_blk = query[lo:hi, :]
        do_blk = dout[lo:hi, :]
        k_all = key[:hi, :]
        v_all = value[:hi, :]
        begin = starts[lo:hi, :]
        col = iota((size, hi), 1)
        allowed = (col <= lo + iota((size, hi), 0)) & (col >= begin)
        prod = do_blk.astype(F32) * attended[lo:hi, :].astype(F32)
        q_total = jnp.zeros((size, LANES), F32)
        for head in range(2):
            mine = head_mask((size, LANES), head)
            q_head = jnp.where(mine, q_blk, zero)
            do_head = jnp.where(mine, do_blk, zero)
            lse_head = lane_value(lse[lo:hi, :], 2 * pl.program_id(0) + head)
            delta = jnp.sum(jnp.where(mine, prod, 0.0), axis=1, keepdims=True)
            scores = dot_nt(q_head, k_all)
            prob = jnp.where(allowed, jnp.exp(jnp.minimum(scores - lse_head, 0.0)), 0.0)
            dprob = dot_nt(do_head, v_all)
            dscore = (prob * (dprob - delta)).astype(BF16)
            k_head = jnp.where(head_mask((hi, LANES), head), k_all, zero)
            q_total = q_total + dot(dscore, k_head)
            kacc[:hi, :] += dot_tn(dscore, q_head)
            vacc[:hi, :] += dot_tn(prob.astype(BF16), do_head)
        q_total = q_total * HEAD_DIM**-0.5
        d_query[lo:hi, :] = (
            q_total * cosine[lo:hi, :] - half_swap(q_total) * sine[lo:hi, :]
        ).astype(BF16)
    for blk in range(tok // size):
        lo, hi = blk * size, (blk + 1) * size
        k_total = kacc[lo:hi, :]
        d_key[lo:hi, :] = (
            k_total * cosine[lo:hi, :] - half_swap(k_total) * sine[lo:hi, :]
        ).astype(BF16)
    d_value[...] = vacc[...].astype(BF16)


def start_kernel(send_to, hear_from, count):
    barrier = pltpu.get_barrier_semaphore()
    for device, remote in hear_from:
        if remote is None:
            pl.semaphore_signal(barrier, inc=1, device_id=device, device_id_type=MESH_ID)
        else:

            @pl.when(remote)
            def _(device=device):
                pl.semaphore_signal(barrier, inc=1, device_id=device, device_id_type=MESH_ID)

    pl.semaphore_wait(barrier, count)


def pair_front_body(
    kinds, a_rows, b_rows,
    lengths, adapters, place_row, hidden, upstream, carry, choices, gain_one, gain_two,
    router_in, const_in, in_qkv, in_out, in_a_qkv, in_a_out, in_b_qkv, in_b_out,
    in_gu, in_b_gu, in_dn, in_b_dn, in_a_gu, in_a_dn, *rest,
):
    count = FRONT_KEPT
    outs, rest = rest[:count], rest[count:]
    (all_wide, all_mid, all_thin, came, last_sent), rest = rest[:5], rest[5:]
    kept, rest = rest[:count], rest[count:]
    (
        hid_s, dy_s, small_s, act_one, low_qkv, mask, starts, cosine, sine, router,
        query, key, value, w_qkv, a_qkv, b_qkv, w_out, a_out, b_out,
        attn_low, lse, low_out, resid, act_two, gate, slot,
    ) = kept
    (
        g_qkv, g_out, own_wide, own_mid, own_thin, sent, slot_rows,
        a_send, a_recv, e_send, e_recv, out_sems, own_sems, row_send, row_recv,
    ) = rest
    dp, z = lax.axis_index("dp"), lax.axis_index("expert")
    core, x_bit, y_bit = dp % 2, dp // 2 % 2, dp // 4
    across = dp + 1 - 2 * core
    x_dev, y_dev = dp + 2 - 4 * x_bit, dp + 4 - 8 * y_bit
    diag = x_dev + 4 - 8 * y_bit
    far = (z + 2) % 4
    home = z // 2
    columns = (dp, x_dev, y_dev, diag)
    tok = hidden.shape[0]
    blocks = tok // ROW_BLOCK

    def remote(source, target, send, recv, device):
        return pltpu.make_async_remote_copy(
            src_ref=source, dst_ref=target, send_sem=send, recv_sem=recv,
            device_id=device, device_id_type=MESH_ID,
        )

    packs = (g_qkv, g_out)

    def at(kind, back):
        return columns[kind] * 4 + (z + 4 - back) % 4

    def shard(p, kind, back, rows=None):
        view = packs[p].at[at(kind, back)]
        if rows is None:
            return view
        half = packs[p].shape[1] // 2
        return view.at[pl.ds(rows * half, half)]

    def along_z(p, j):
        return remote(
            shard(p, 0, 0), shard(p, 0, 0), a_send.at[p, j - 1], a_recv.at[p, j - 1],
            (dp, (z + j) % 4),
        )

    def z_arrival(p, j):
        return remote(
            shard(p, 0, j), shard(p, 0, j), a_send.at[p, j - 1], a_recv.at[p, j - 1],
            (dp, (z + j) % 4),
        )

    def to_x(p, back):
        return remote(
            shard(p, 0, back), shard(p, 0, back), a_send.at[p, 3 + back], a_recv.at[p, 3 + back],
            (x_dev, z),
        )

    def to_y(p, back):
        return remote(
            shard(p, 0, back), shard(p, 0, back), a_send.at[p, 7 + back], a_recv.at[p, 7 + back],
            (y_dev, z),
        )

    def relay_y(p, back):
        return remote(
            shard(p, 1, back, 0), shard(p, 1, back, 0), a_send.at[p, 11 + back],
            a_recv.at[p, 11 + back], (y_dev, z),
        )

    def relay_x(p, back):
        return remote(
            shard(p, 2, back, 1), shard(p, 2, back, 1), a_send.at[p, 15 + back],
            a_recv.at[p, 15 + back], (x_dev, z),
        )

    def to_core(p, kind, back):
        sem = 19 + 4 * kind + back
        return remote(
            shard(p, kind, back), shard(p, kind, back), a_send.at[p, sem], a_recv.at[p, sem],
            (across, z),
        )

    half_wide = own_wide.shape[1] // 2
    parts = []
    for own, everything, cols in (
        (own_mid, all_mid, None), (own_thin, all_thin, None),
        (own_wide, all_wide, (0, half_wide)), (own_wide, all_wide, (half_wide, half_wide)),
    ):
        if cols is None:
            parts.append((own, lambda d, ref=everything: ref.at[d]))
        else:
            parts.append(
                (own.at[:, pl.ds(*cols)], lambda d, ref=everything, c=cols: ref.at[d, :, pl.ds(*c)])
            )
    chunks = ((0, 1), (2,), (3,))

    def first_far(a):
        return remote(
            parts[a][0], parts[a][1](dp), e_send.at[a, 0], e_recv.at[a, core],
            (dp - core + home, far),
        )

    def first_across(a):
        return remote(
            parts[a][0], parts[a][1](dp), e_send.at[a, 1], e_recv.at[a, core], (across, z)
        )

    def first_keep(a):
        return pltpu.make_async_copy(parts[a][0], parts[a][1](dp), e_recv.at[a, core])

    def first_arrival(a, i):
        view = parts[a][1](dp - core + i)
        return remote(view, view, e_send.at[a, 0], e_recv.at[a, i], (dp, far))

    def expert_hop(a, column, i, sem, device):
        view = parts[a][1](column - core + i)
        return remote(view, view, e_send.at[a, sem], e_recv.at[a, sem], (device, z))

    def expert_x(a, i):
        return expert_hop(a, dp, i, 2 + i, x_dev)

    def expert_y(a, i):
        return expert_hop(a, dp, i, 4 + i, y_dev)

    def expert_relay_y(a):
        return expert_hop(a, x_dev, 0, 6, y_dev)

    def expert_relay_x(a):
        return expert_hop(a, y_dev, 1, 7, x_dev)

    def expert_first(c):
        for a in chunks[c]:
            first_far(a).start()

            @pl.when(core == home)
            def _(a=a):
                first_keep(a).start()

            @pl.when(core != home)
            def _(a=a):
                first_across(a).start()

    def expert_spread(c):
        for a in chunks[c]:

            @pl.when(core == home)
            def _(a=a):
                first_keep(a).wait()
                first_arrival(a, 1 - core).wait_recv()

            @pl.when(core != home)
            def _(a=a):
                for i in range(2):
                    first_arrival(a, i).wait_recv()

            for i in range(2):
                expert_x(a, i).start()
                expert_y(a, i).start()

    def expert_relay(c):
        for a in chunks[c]:
            for i in range(2):
                expert_hop(a, x_dev, i, 2 + i, x_dev).wait_recv()
            expert_relay_y(a).start()
            for i in range(2):
                expert_hop(a, y_dev, i, 4 + i, y_dev).wait_recv()
            expert_relay_x(a).start()

    def expert_finish(c):
        for a in chunks[c]:
            expert_hop(a, diag, 0, 6, y_dev).wait_recv()
            expert_hop(a, diag, 1, 7, x_dev).wait_recv()
            first_far(a).wait_send()

            @pl.when(core != home)
            def _(a=a):
                first_across(a).wait_send()

            for i in range(2):
                expert_x(a, i).wait_send()
                expert_y(a, i).wait_send()
            expert_relay_y(a).wait_send()
            expert_relay_x(a).wait_send()

    gu_rows, up_rows, dn_rows = in_gu.shape[1], in_b_gu.shape[1], in_dn.shape[1]
    own_loads = [
        pltpu.make_async_copy(source.at[0], target.at[pl.ds(at_row, rows)], own_sems.at[i])
        for i, (source, target, at_row, rows) in enumerate((
            (in_gu, own_wide, 0, gu_rows), (in_b_gu, own_wide, gu_rows, up_rows),
            (in_dn, own_mid, 0, dn_rows), (in_b_dn, own_mid, dn_rows, up_rows),
            (in_a_gu, own_thin, 0, gu_rows), (in_a_dn, own_thin, gu_rows, dn_rows),
        ))
    ]
    for load in own_loads:
        load.start()
    for gathered, weight, adapter_in, adapter_out in (
        (g_qkv, in_qkv, in_a_qkv, in_b_qkv), (g_out, in_out, in_a_out, in_b_out),
    ):
        spare = gathered.shape[1] - a_rows - b_rows
        wide_cols = weight.shape[1]
        gathered[at(0, 0), :, :wide_cols] = jnp.concatenate(
            [weight[...].astype(F32), adapter_out[...].astype(F32), jnp.zeros((spare, wide_cols), F32)],
            axis=0,
        ).astype(BF16)
        gathered[at(0, 0), :, wide_cols:] = jnp.concatenate(
            [adapter_in[...].astype(F32), jnp.zeros((spare + b_rows, LANES), F32)], axis=0
        ).astype(BF16)
    peers = [(x_dev, z), (y_dev, z), (across, z), (across, far)]
    peers += [(dp, (z + j) % 4) for j in (1, 2, 3)]
    next_z = z + 1 - 2 * (z % 2)
    start_kernel(None, [(device, None) for device in peers], len(peers))
    for p in range(2):
        for j in (1, 2, 3):
            along_z(p, jnp.where(z < 2, 4 - j, j)).start()
        to_x(p, 0).start()
        to_y(p, 0).start()
        to_core(p, 0, 0).start()
    router[...] = jnp.zeros_like(router)
    router[:, :kinds] = router_in[...]
    router[:, CONST_LANE : CONST_LANE + 4] = const_in[...]
    small_s[...] = jnp.zeros_like(small_s)
    carry_parts = split_three(carry[...])
    choices_low = choices[...].astype(F32).astype(BF16)
    half_dim = HEAD_DIM // 2
    freq = jnp.exp(
        (iota((1, LANES), 1) % half_dim).astype(F32) * (-math.log(10000.0) / half_dim)
    )
    sign = jnp.where(iota((1, LANES), 1) % HEAD_DIM < half_dim, -1.0, 1.0)

    def block_rows(b):
        return pl.ds(pl.multiple_of(b * ROW_BLOCK, ROW_BLOCK), ROW_BLOCK)

    def arrange(b, carry_on):
        rows = block_rows(b)
        perm = hot_matrix(place_row[...] == b * ROW_BLOCK + iota((ROW_BLOCK, tok), 0))
        hid = dot(perm, hidden[...])
        hid_s[rows, :] = hid.astype(BF16)
        act_one[rows, :] = normed(hid, gain_one)
        dy_s[rows, :] = dot(perm, upstream[...]).astype(BF16)
        top, mid, last = carry_parts
        small_s[rows, :kinds] = dot(perm, top) + (dot(perm, mid) + dot(perm, last))
        small_s[rows, CHOICE_LANE : CHOICE_LANE + 2] = dot(perm, choices_low)
        stream = b * ROW_BLOCK + iota((ROW_BLOCK, 1), 0)
        start = jnp.zeros((ROW_BLOCK, 1), jnp.int32)
        adapter = start + adapters[0, 0]
        begin = 0
        for n in range(1, lengths.shape[1]):
            begin = begin + lengths[0, n - 1]
            start = jnp.where(stream >= begin, begin, start)
            adapter = jnp.where(stream >= begin, adapters[0, n], adapter)
        starts[rows, :] = start
        mask[rows, :] = hot_matrix(iota((ROW_BLOCK, LANES), 1) // ADAPTER_RANK == adapter)
        angle = (stream - start).astype(F32) * freq
        cosine[rows, :] = jnp.cos(angle)
        sine[rows, :] = jnp.sin(angle) * sign
        return carry_on

    lax.fori_loop(0, blocks, arrange, 0)

    for p in range(2):

        def from_z(j, carry, p=p):
            z_arrival(p, j).wait_recv()
            to_x(p, j).start()
            to_y(p, j).start()
            to_core(p, 0, j).start()
            return carry

        lax.fori_loop(1, 4, from_z, 0)
    for p in range(2):

        def from_sides(back, carry, p=p):
            remote(
                shard(p, 1, back), shard(p, 1, back), a_send.at[p, 3 + back], a_recv.at[p, 3 + back],
                (x_dev, z),
            ).wait_recv()
            relay_y(p, back).start()
            to_core(p, 1, back).start()
            remote(
                shard(p, 2, back), shard(p, 2, back), a_send.at[p, 7 + back], a_recv.at[p, 7 + back],
                (y_dev, z),
            ).wait_recv()
            relay_x(p, back).start()
            to_core(p, 2, back).start()
            return carry

        lax.fori_loop(0, 4, from_sides, 0)
    for load in own_loads:
        load.wait()
    for c in range(len(chunks)):
        expert_first(c)
    for p in range(2):

        def from_diag(back, carry, p=p):
            remote(
                shard(p, 3, back, 0), shard(p, 3, back, 0), a_send.at[p, 11 + back],
                a_recv.at[p, 11 + back], (y_dev, z),
            ).wait_recv()
            remote(
                shard(p, 3, back, 1), shard(p, 3, back, 1), a_send.at[p, 15 + back],
                a_recv.at[p, 15 + back], (x_dev, z),
            ).wait_recv()
            to_core(p, 3, back).start()
            return carry

        lax.fori_loop(0, 4, from_diag, 0)
    core_columns = (across, x_dev + across - dp, y_dev + across - dp, diag + across - dp)

    def from_core(p):
        def body(back, carry):
            for kind in range(4):
                view = packs[p].at[core_columns[kind] * 4 + (z + 4 - back) % 4]
                sem = 19 + 4 * kind + back
                remote(view, view, a_send.at[p, sem], a_recv.at[p, sem], (across, z)).wait_recv()
            return carry

        lax.fori_loop(0, 4, body, 0)

    width = MODEL_WIDTH
    total = g_qkv.shape[0]

    def lay_rows(i, carry, gathered, targets):
        pair = [gathered[2 * i + n, :a_rows, :].astype(F32) for n in range(2)]
        both = jnp.concatenate(pair, axis=0).astype(BF16)
        rows = pl.ds(pl.multiple_of(i * 2 * a_rows, 16), 2 * a_rows)
        start = 0
        for target in targets:
            target[rows, :] = both[:, start : start + target.shape[1]]
            start += target.shape[1]
        return carry

    def lay_ups(i, carry, gathered, target):
        group = 16 // b_rows
        pieces = [
            gathered[group * i + n, a_rows : a_rows + b_rows, : target.shape[1]].astype(F32)
            for n in range(group)
        ]
        rows = pl.ds(pl.multiple_of(i * 16, 16), 16)
        target[rows, :] = jnp.concatenate(pieces, axis=0).astype(BF16)
        return carry

    def lay(gathered, targets, ups):
        lax.fori_loop(
            0, total // 2, functools.partial(lay_rows, gathered=gathered, targets=targets), 0
        )
        lax.fori_loop(
            0, total * b_rows // 16, functools.partial(lay_ups, gathered=gathered, target=ups), 0
        )

    def flush(first, last):
        return [
            pltpu.make_async_copy(kept[i], outs[i], out_sems.at[i]) for i in range(first, last)
        ]

    from_core(0)
    lay(g_qkv, (w_qkv, a_qkv), b_qkv)

    def projection(b, carry):
        rows = block_rows(b)
        low_qkv[rows, :], query[rows, :], key[rows, :], value[rows, :] = project(
            act_one[rows, :], mask[rows, :], cosine[rows, :], sine[rows, :], w_qkv, a_qkv, b_qkv
        )

        @pl.when(b == 1)
        def _():
            expert_spread(0)

        return carry

    lax.fori_loop(0, blocks, projection, 0)
    from_core(1)
    lay(g_out, (w_out, a_out), b_out)
    for copy in flush(0, 19):
        copy.start()
    lse[...] = jnp.zeros_like(lse)

    def attention(pair, carry):
        cols = pl.ds(pl.multiple_of(pair * LANES, LANES), LANES)
        attention_fwd_pair(
            pair, query.at[:, cols], key.at[:, cols], value.at[:, cols], starts,
            attn_low.at[:, cols], lse,
        )

        @pl.when(pair == 0)
        def _():
            expert_spread(1)

        @pl.when(pair == 1)
        def _():
            expert_relay(0)

        @pl.when(pair == 3)
        def _():
            expert_spread(2)

        @pl.when(pair == 5)
        def _():
            expert_relay(1)

        return carry

    lax.fori_loop(0, HEAD_COUNT // 2, attention, 0)
    for copy in flush(19, 21):
        copy.start()

    def after(b, carry):
        rows = block_rows(b)
        low_out[rows, :], resid[rows, :], act_two[rows, :], gate[rows, :] = post_attn(
            kinds, attn_low[rows, :], hid_s[rows, :], mask[rows, :], small_s[rows, :],
            w_out, a_out, b_out, router, gain_two,
        )
        return carry

    lax.fori_loop(0, blocks, after, 0)
    place_slots(4, small_s, slot, slot_rows)
    for copy in flush(21, FRONT_KEPT):
        copy.start()

    def rows_out(k):
        device = ((dp, next_z), (across, z))[k - 1]
        return remote(sent.at[k], came.at[k], row_send.at[k], row_recv.at[k], device)

    last_local = pltpu.make_async_copy(sent.at[0], last_sent, row_send.at[3])
    own_local = pltpu.make_async_copy(sent.at[0], came.at[0], row_send.at[0])

    def fill(n, carry):
        k = (n + 1) % 4
        eid = (z + k) % 2 + 2 * ((core + k // 2) % 2)
        fill_slots(eid, gate, act_two, dy_s, mask, slot_rows, sent.at[k % 3])

        @pl.when(n == 0)
        def _():
            rows_out(1).start()

        @pl.when(n == 1)
        def _():
            rows_out(2).start()

        @pl.when(n == 2)
        def _():
            last_local.start()
            last_local.wait()

        return carry

    lax.fori_loop(0, 4, fill, 0)
    own_local.start()
    expert_relay(2)
    for c in range(len(chunks)):
        expert_finish(c)
    for k in (1, 2):
        rows_out(k).wait_recv()
        rows_out(k).wait_send()
    own_local.wait()

    def attn_sent(n, carry):
        for p in range(2):
            to_x(p, n).wait_send()
            to_y(p, n).wait_send()
            relay_x(p, n).wait_send()
            relay_y(p, n).wait_send()
            for kind in range(4):
                to_core(p, kind, n).wait_send()
        return carry

    lax.fori_loop(0, 4, attn_sent, 0)
    for p in range(2):
        for j in (1, 2, 3):
            along_z(p, j).wait_send()
    for copy in flush(0, FRONT_KEPT):
        copy.wait()


def pair_attention_bwd_body(
    query, key, value, dout, attended, lse, starts, cosine, sine, ga_gu, gb_gu, ga_dn, gb_dn,
    d_query, d_key, d_value, own_ga_gu, own_gb_gu, own_ga_dn, own_gb_dn,
    kacc, vacc, r_ga_gu, r_gb_gu, r_ga_dn, r_gb_dn, send_sems, recv_sems,
):
    dp, z = lax.axis_index("dp"), lax.axis_index("expert")
    core, spot, half = dp % 2, dp // 2, z // 2
    own = z % 2 + 2 * core
    far = (z + 2) % 4
    at_home = core == half
    away = 1 - (core * half + (1 - core) * (1 - half))
    slot = 2 * spot + away
    groups = (
        (ga_gu, r_ga_gu, own_ga_gu), (gb_gu, r_gb_gu, own_gb_gu),
        (ga_dn, r_ga_dn, own_ga_dn), (gb_dn, r_gb_dn, own_gb_dn),
    )
    owners = 8

    def piece(i, d):
        source, target, _ = groups[i]
        count = target.shape[1]
        return source.at[pl.ds(pl.multiple_of(d * count, 16), count)]

    def push(i, d):
        return pltpu.make_async_remote_copy(
            src_ref=piece(i, d), dst_ref=groups[i][1].at[slot], send_sem=send_sems.at[i, d],
            recv_sem=recv_sems.at[i, slot], device_id=(d, own), device_id_type=MESH_ID,
        )

    def keep(i):
        return pltpu.make_async_copy(
            piece(i, dp), groups[i][1].at[2 * spot], recv_sems.at[i, 2 * spot]
        )

    def arrival(i, s):
        return pltpu.make_async_remote_copy(
            src_ref=piece(i, 0), dst_ref=groups[i][1].at[s], send_sem=send_sems.at[i, 0],
            recv_sem=recv_sems.at[i, s], device_id=(0, own), device_id_type=MESH_ID,
        )

    @pl.when(pl.program_id(0) == 0)
    def _():
        senders = []
        for m in range(owners // 2):
            device = 2 * m + half
            senders.append(((device, z), device != dp))
            senders.append(((device, far), None))
        start_kernel(None, senders, owners - 1 + away)

        def send(d, carry):
            mine = at_home & (d == dp)

            @pl.when(mine)
            def _():
                for i in range(4):
                    keep(i).start()

            @pl.when(jnp.logical_not(mine))
            def _():
                for i in range(4):
                    push(i, d).start()

            return carry

        lax.fori_loop(0, owners, send, 0)

    attention_bwd_body(
        query, key, value, dout, attended, lse, starts, cosine, sine, d_query, d_key, d_value,
        kacc, vacc,
    )

    @pl.when(pl.program_id(0) == pl.num_programs(0) - 1)
    def _():
        def finish(s, carry):
            mine = at_home & (s == 2 * spot)

            @pl.when(mine)
            def _():
                for i in range(4):
                    keep(i).wait()

            @pl.when(jnp.logical_not(mine))
            def _():
                for i in range(4):
                    arrival(i, s).wait_recv()

            @pl.when(jnp.logical_not(at_home & (s == dp)))
            def _():
                for i in range(4):
                    push(i, s).wait_send()

            return carry

        lax.fori_loop(0, owners, finish, 0)
        for _, target, out in groups:
            total = target[0].astype(F32)
            for s in range(1, owners):
                total = total + target[s].astype(F32)
            out[...] = total


def pair_tail_body(
    place_col, d_query, d_key, d_value, low_qkv, act_one, mask, a_in, b_out, gain, ga_out, gb_out,
    d_logits, hid_hbm, resid_hbm, w_hbm, out_hbm,
    out, grad_hidden, grad_gate, own_ga_qkv, own_gb_qkv, own_ga_out, own_gb_out,
    hid_s, d_resid, w_qkv, out_s, high, lower, d_low_all, ga_sum, gb_sum,
    s_ga_qkv, s_gb_qkv, s_ga_out, s_gb_out, r_ga_qkv, r_gb_qkv, r_ga_out, r_gb_out,
    thin_out, wide_out, thin_in, wide_in, load_sems, send_sems, recv_sems, far_send, far_recv,
):
    dp, z = lax.axis_index("dp"), lax.axis_index("expert")
    others, planes = 7, 3
    tok = place_col.shape[0]
    blocks = tok // ROW_BLOCK
    loads = [
        pltpu.make_async_copy(source, target, load_sems.at[i])
        for i, (source, target) in enumerate(
            ((w_hbm, w_qkv), (hid_hbm, hid_s), (resid_hbm, d_resid), (out_hbm, out_s))
        )
    ]
    for load in loads:
        load.start()
    start_kernel(
        None,
        [(((dp + i) % 8, z), None) for i in range(1, 8)] + [((dp, (z + j) % 4), None) for j in (1, 2, 3)],
        others + planes,
    )
    ga_sum[...] = jnp.zeros_like(ga_sum)
    gb_sum[...] = jnp.zeros_like(gb_sum)
    parts = [slice(p * MODEL_WIDTH, (p + 1) * MODEL_WIDTH) for p in range(3)]
    d_refs = (d_query, d_key, d_value)

    def block_rows(b):
        return pl.ds(pl.multiple_of(b * ROW_BLOCK, ROW_BLOCK), ROW_BLOCK)

    def sums(b, carry):
        rows = block_rows(b)
        low = low_qkv[rows, :]
        d_low = jnp.zeros((ROW_BLOCK, LANES), F32)
        for cols, ref in zip(parts, d_refs):
            grad = ref[rows, :]
            d_low = d_low + dot_nt(grad, b_out[:, cols])
            gb_sum[:, cols] += dot_tn(low, grad)
        d_low = (d_low * mask[rows, :].astype(F32)).astype(BF16)
        d_low_all[rows, :] = d_low
        ga_sum[...] += dot_tn(act_one[rows, :], d_low)
        return carry

    lax.fori_loop(0, blocks, sums, 0)
    s_ga_qkv[...] = ga_sum[...].astype(BF16)
    s_gb_qkv[...] = gb_sum[...].astype(BF16)
    s_ga_out[...] = ga_out[...].astype(BF16)
    s_gb_out[...] = gb_out[...].astype(BF16)
    groups = (
        (s_ga_qkv, r_ga_qkv), (s_gb_qkv, r_gb_qkv), (s_ga_out, r_ga_out), (s_gb_out, r_gb_out),
    )

    def share(i, d):
        count = groups[i][1].shape[1]
        return groups[i][0].at[pl.ds(pl.multiple_of(d * count, 16), count)]

    def near(i, n):
        goal = (dp + n + 1) % 8
        return pltpu.make_async_remote_copy(
            src_ref=share(i, goal), dst_ref=groups[i][1].at[n], send_sem=send_sems.at[i, n],
            recv_sem=recv_sems.at[i, n], device_id=(goal, z), device_id_type=MESH_ID,
        )

    def send_near(n, carry):
        for i in range(4):
            near(i, n).start()
        return carry

    lax.fori_loop(0, others, send_near, 0)

    for load in loads[:3]:
        load.wait()

    def back(b, carry):
        rows = block_rows(b)
        d_act = dot_nt(d_low_all[rows, :], a_in[...])
        for cols, ref in zip(parts, d_refs):
            d_act = d_act + dot_nt(ref[rows, :], w_qkv[:, cols])
        hid = hid_s[rows, :].astype(F32)
        scale = lax.rsqrt(jnp.mean(hid * hid, axis=-1, keepdims=True) + EPSILON)
        weighted = d_act * gain[...].astype(F32)
        grad_hid = d_resid[rows, :] + (
            scale * weighted
            - hid * (scale * scale * scale) * jnp.mean(hid * weighted, axis=-1, keepdims=True)
        )
        top = grad_hid.astype(BF16)
        high[rows, :] = top
        lower[rows, :] = (grad_hid - top.astype(F32)).astype(BF16)
        return carry

    lax.fori_loop(0, blocks, back, 0)

    def near_done(n, carry):
        for i in range(4):
            near(i, n).wait_recv()
        return carry

    lax.fori_loop(0, others, near_done, 0)
    totals = []
    for i in range(4):
        total = share(i, dp)[...].astype(F32)
        for n in range(others):
            total = total + groups[i][1][n].astype(F32)
        totals.append(total)
    a_qkv, b_qkv, a_o, b_o = totals
    a_count, b_count = a_qkv.shape[0] // 4, b_qkv.shape[0] // 4
    for p in range(4):
        a_rows, b_rows = slice(p * a_count, (p + 1) * a_count), slice(p * b_count, (p + 1) * b_count)
        thin_out[p, :a_count, :LANES] = a_qkv[a_rows].astype(BF16)
        thin_out[p, :a_count, LANES:] = a_o[a_rows].astype(BF16)
        thin_out[p, a_count:, :] = jnp.zeros((thin_out.shape[1] - a_count, 2 * LANES), BF16)
        wide_out[p] = jnp.concatenate(
            [b_qkv[b_rows, cols] for cols in parts] + [b_o[b_rows]], axis=0
        ).astype(BF16)

    def far(i, j):
        goal = (z + j + 1) % 4
        source, target = ((thin_out, thin_in), (wide_out, wide_in))[i]
        return pltpu.make_async_remote_copy(
            src_ref=source.at[goal], dst_ref=target.at[j], send_sem=far_send.at[i, j],
            recv_sem=far_recv.at[i, j], device_id=(dp, goal), device_id_type=MESH_ID,
        )

    for j in range(planes):
        for i in range(2):
            far(i, j).start()
    loads[3].wait()

    top, mid, last = (jnp.where(iota((tok, LANES), 1) < 16, v.astype(F32), 0.0) for v in split_three(d_logits[...]))
    logit_parts = (top + pltpu.roll(mid, 16, 1) + pltpu.roll(last, 32, 1)).astype(BF16)

    def to_rows(b, carry):
        rows = block_rows(b)
        perm = hot_matrix(place_col[rows, :] == iota((ROW_BLOCK, tok), 1))
        out[rows, :] = dot(perm, out_s[...]).astype(BF16)
        grad_hidden[rows, :] = dot(perm, high[...]) + dot(perm, lower[...])
        moved = dot(perm, logit_parts)
        grad_gate[rows, :] = moved + (
            pltpu.roll(moved, LANES - 16, 1) + pltpu.roll(moved, LANES - 32, 1)
        )
        return carry

    lax.fori_loop(0, blocks, to_rows, 0)
    for j in range(planes):
        for i in range(2):
            far(i, j).wait_recv()
    thin = thin_out[z].astype(F32)
    wide = wide_out[z].astype(F32)
    for j in range(planes):
        thin = thin + thin_in[j].astype(F32)
        wide = wide + wide_in[j].astype(F32)
    own_ga_qkv[...] = thin[:a_count, :LANES]
    own_ga_out[...] = thin[:a_count, LANES:]
    for p, cols in enumerate(parts):
        own_gb_qkv[:, cols] = wide[p * b_count : (p + 1) * b_count]
    own_gb_out[...] = wide[3 * b_count : 4 * b_count]

    def sent(n, carry):
        for i in range(4):
            near(i, n).wait_send()
        return carry

    lax.fori_loop(0, others, sent, 0)
    for j in range(planes):
        for i in range(2):
            far(i, j).wait_send()


def split_three(values):
    top = values.astype(BF16)
    rest = values - top.astype(F32)
    mid = rest.astype(BF16)
    return top, mid, (rest - mid.astype(F32)).astype(BF16)


def post_attn_body(
    kinds, attn_low, hid_s, mask, small_s, w_out, a_out, b_out, router, gain,
    low_out, resid, act_two, gate,
):
    low_out[...], resid[...], act_two[...], gate[...] = post_attn(
        kinds, attn_low[...], hid_s[...], mask[...], small_s[...], w_out, a_out, b_out, router, gain
    )


def post_attn(kinds, attn, hid, mask, sm, w_out, a_out, b_out, router, gain):
    low = (dot(attn, a_out[...]) * mask.astype(F32)).astype(BF16)
    res = hid.astype(F32) + (dot(attn, w_out[...]) + dot(low, b_out[...]))
    act = normed(res, gain)
    logits = dot(act, router[...])
    lane = iota(logits.shape, 1)
    routed = jnp.where(lane < kinds, logits + sm, -1e30)
    top = jnp.max(routed, axis=1, keepdims=True)
    expo = jnp.exp(routed - top)
    prob = expo / jnp.sum(expo, axis=1, keepdims=True)
    return low, res, act, jnp.where(lane < kinds, prob, logits)


def start_kernel(send_to, hear_from, count):
    barrier = pltpu.get_barrier_semaphore()
    for device, remote in hear_from:
        if remote is None:
            pl.semaphore_signal(barrier, inc=1, device_id=device, device_id_type=MESH_ID)
        else:

            @pl.when(remote)
            def _(device=device):
                pl.semaphore_signal(barrier, inc=1, device_id=device, device_id_type=MESH_ID)

    pl.semaphore_wait(barrier, count)


def pair_attention_bwd_body(
    query, key, value, dout, attended, lse, starts, cosine, sine, ga_gu, gb_gu, ga_dn, gb_dn,
    d_query, d_key, d_value, own_ga_gu, own_gb_gu, own_ga_dn, own_gb_dn,
    kacc, vacc, r_ga_gu, r_gb_gu, r_ga_dn, r_gb_dn, send_sems, recv_sems,
):
    dp, z = lax.axis_index("dp"), lax.axis_index("expert")
    core, spot, half = dp % 2, dp // 2, z // 2
    own = z % 2 + 2 * core
    far = (z + 2) % 4
    at_home = core == half
    away = 1 - (core * half + (1 - core) * (1 - half))
    slot = 2 * spot + away
    groups = (
        (ga_gu, r_ga_gu, own_ga_gu), (gb_gu, r_gb_gu, own_gb_gu),
        (ga_dn, r_ga_dn, own_ga_dn), (gb_dn, r_gb_dn, own_gb_dn),
    )
    owners = 8

    def piece(i, d):
        source, target, _ = groups[i]
        count = target.shape[1]
        return source.at[pl.ds(pl.multiple_of(d * count, 16), count)]

    def push(i, d):
        return pltpu.make_async_remote_copy(
            src_ref=piece(i, d), dst_ref=groups[i][1].at[slot], send_sem=send_sems.at[i, d],
            recv_sem=recv_sems.at[i, slot], device_id=(d, own), device_id_type=MESH_ID,
        )

    def keep(i):
        return pltpu.make_async_copy(
            piece(i, dp), groups[i][1].at[2 * spot], recv_sems.at[i, 2 * spot]
        )

    def arrival(i, s):
        return pltpu.make_async_remote_copy(
            src_ref=piece(i, 0), dst_ref=groups[i][1].at[s], send_sem=send_sems.at[i, 0],
            recv_sem=recv_sems.at[i, s], device_id=(0, own), device_id_type=MESH_ID,
        )

    @pl.when(pl.program_id(0) == 0)
    def _():
        senders = []
        for m in range(owners // 2):
            device = 2 * m + half
            senders.append(((device, z), device != dp))
            senders.append(((device, far), None))
        start_kernel(None, senders, owners - 1 + away)

        def send(d, carry):
            mine = at_home & (d == dp)

            @pl.when(mine)
            def _():
                for i in range(4):
                    keep(i).start()

            @pl.when(jnp.logical_not(mine))
            def _():
                for i in range(4):
                    push(i, d).start()

            return carry

        lax.fori_loop(0, owners, send, 0)

    attention_bwd_body(
        query, key, value, dout, attended, lse, starts, cosine, sine, d_query, d_key, d_value,
        kacc, vacc,
    )

    @pl.when(pl.program_id(0) == pl.num_programs(0) - 1)
    def _():
        def finish(s, carry):
            mine = at_home & (s == 2 * spot)

            @pl.when(mine)
            def _():
                for i in range(4):
                    keep(i).wait()

            @pl.when(jnp.logical_not(mine))
            def _():
                for i in range(4):
                    arrival(i, s).wait_recv()

            @pl.when(jnp.logical_not(at_home & (s == dp)))
            def _():
                for i in range(4):
                    push(i, s).wait_send()

            return carry

        lax.fori_loop(0, owners, finish, 0)
        for _, target, out in groups:
            total = target[0].astype(F32)
            for s in range(1, owners):
                total = total + target[s].astype(F32)
            out[...] = total


def pair_tail_body(
    place_col, d_query, d_key, d_value, low_qkv, act_one, mask, a_in, b_out, gain, ga_out, gb_out,
    d_logits, hid_hbm, resid_hbm, w_hbm, out_hbm,
    out, grad_hidden, grad_gate, own_ga_qkv, own_gb_qkv, own_ga_out, own_gb_out,
    hid_s, d_resid, w_qkv, out_s, high, lower, d_low_all, ga_sum, gb_sum,
    s_ga_qkv, s_gb_qkv, s_ga_out, s_gb_out, r_ga_qkv, r_gb_qkv, r_ga_out, r_gb_out,
    thin_out, wide_out, thin_in, wide_in, load_sems, send_sems, recv_sems, far_send, far_recv,
):
    dp, z = lax.axis_index("dp"), lax.axis_index("expert")
    others, planes = 7, 3
    tok = place_col.shape[0]
    blocks = tok // ROW_BLOCK
    loads = [
        pltpu.make_async_copy(source, target, load_sems.at[i])
        for i, (source, target) in enumerate(
            ((w_hbm, w_qkv), (hid_hbm, hid_s), (resid_hbm, d_resid), (out_hbm, out_s))
        )
    ]
    for load in loads:
        load.start()
    start_kernel(
        None,
        [(((dp + i) % 8, z), None) for i in range(1, 8)] + [((dp, (z + j) % 4), None) for j in (1, 2, 3)],
        others + planes,
    )
    ga_sum[...] = jnp.zeros_like(ga_sum)
    gb_sum[...] = jnp.zeros_like(gb_sum)
    parts = [slice(p * MODEL_WIDTH, (p + 1) * MODEL_WIDTH) for p in range(3)]
    d_refs = (d_query, d_key, d_value)

    def block_rows(b):
        return pl.ds(pl.multiple_of(b * ROW_BLOCK, ROW_BLOCK), ROW_BLOCK)

    def sums(b, carry):
        rows = block_rows(b)
        low = low_qkv[rows, :]
        d_low = jnp.zeros((ROW_BLOCK, LANES), F32)
        for cols, ref in zip(parts, d_refs):
            grad = ref[rows, :]
            d_low = d_low + dot_nt(grad, b_out[:, cols])
            gb_sum[:, cols] += dot_tn(low, grad)
        d_low = (d_low * mask[rows, :].astype(F32)).astype(BF16)
        d_low_all[rows, :] = d_low
        ga_sum[...] += dot_tn(act_one[rows, :], d_low)
        return carry

    lax.fori_loop(0, blocks, sums, 0)
    s_ga_qkv[...] = ga_sum[...].astype(BF16)
    s_gb_qkv[...] = gb_sum[...].astype(BF16)
    s_ga_out[...] = ga_out[...].astype(BF16)
    s_gb_out[...] = gb_out[...].astype(BF16)
    groups = (
        (s_ga_qkv, r_ga_qkv), (s_gb_qkv, r_gb_qkv), (s_ga_out, r_ga_out), (s_gb_out, r_gb_out),
    )

    def share(i, d):
        count = groups[i][1].shape[1]
        return groups[i][0].at[pl.ds(pl.multiple_of(d * count, 16), count)]

    def near(i, n):
        goal = (dp + n + 1) % 8
        return pltpu.make_async_remote_copy(
            src_ref=share(i, goal), dst_ref=groups[i][1].at[n], send_sem=send_sems.at[i, n],
            recv_sem=recv_sems.at[i, n], device_id=(goal, z), device_id_type=MESH_ID,
        )

    def send_near(n, carry):
        for i in range(4):
            near(i, n).start()
        return carry

    lax.fori_loop(0, others, send_near, 0)

    for load in loads[:3]:
        load.wait()

    def back(b, carry):
        rows = block_rows(b)
        d_act = dot_nt(d_low_all[rows, :], a_in[...])
        for cols, ref in zip(parts, d_refs):
            d_act = d_act + dot_nt(ref[rows, :], w_qkv[:, cols])
        hid = hid_s[rows, :].astype(F32)
        scale = lax.rsqrt(jnp.mean(hid * hid, axis=-1, keepdims=True) + EPSILON)
        weighted = d_act * gain[...].astype(F32)
        grad_hid = d_resid[rows, :] + (
            scale * weighted
            - hid * (scale * scale * scale) * jnp.mean(hid * weighted, axis=-1, keepdims=True)
        )
        top = grad_hid.astype(BF16)
        high[rows, :] = top
        lower[rows, :] = (grad_hid - top.astype(F32)).astype(BF16)
        return carry

    lax.fori_loop(0, blocks, back, 0)

    def near_done(n, carry):
        for i in range(4):
            near(i, n).wait_recv()
        return carry

    lax.fori_loop(0, others, near_done, 0)
    totals = []
    for i in range(4):
        total = share(i, dp)[...].astype(F32)
        for n in range(others):
            total = total + groups[i][1][n].astype(F32)
        totals.append(total)
    a_qkv, b_qkv, a_o, b_o = totals
    a_count, b_count = a_qkv.shape[0] // 4, b_qkv.shape[0] // 4
    for p in range(4):
        a_rows, b_rows = slice(p * a_count, (p + 1) * a_count), slice(p * b_count, (p + 1) * b_count)
        thin_out[p, :a_count, :LANES] = a_qkv[a_rows].astype(BF16)
        thin_out[p, :a_count, LANES:] = a_o[a_rows].astype(BF16)
        thin_out[p, a_count:, :] = jnp.zeros((thin_out.shape[1] - a_count, 2 * LANES), BF16)
        wide_out[p] = jnp.concatenate(
            [b_qkv[b_rows, cols] for cols in parts] + [b_o[b_rows]], axis=0
        ).astype(BF16)

    def far(i, j):
        goal = (z + j + 1) % 4
        source, target = ((thin_out, thin_in), (wide_out, wide_in))[i]
        return pltpu.make_async_remote_copy(
            src_ref=source.at[goal], dst_ref=target.at[j], send_sem=far_send.at[i, j],
            recv_sem=far_recv.at[i, j], device_id=(dp, goal), device_id_type=MESH_ID,
        )

    for j in range(planes):
        for i in range(2):
            far(i, j).start()
    loads[3].wait()

    def to_rows(b, carry):
        rows = block_rows(b)
        perm = hot_matrix(place_col[rows, :] == iota((ROW_BLOCK, tok), 1))
        out[rows, :] = dot(perm, out_s[...]).astype(BF16)
        grad_hidden[rows, :] = dot(perm, high[...]) + dot(perm, lower[...])
        top, mid, last = split_three(d_logits[...])
        grad_gate[rows, :] = dot(perm, top) + (dot(perm, mid) + dot(perm, last))
        return carry

    lax.fori_loop(0, blocks, to_rows, 0)
    for j in range(planes):
        for i in range(2):
            far(i, j).wait_recv()
    thin = thin_out[z].astype(F32)
    wide = wide_out[z].astype(F32)
    for j in range(planes):
        thin = thin + thin_in[j].astype(F32)
        wide = wide + wide_in[j].astype(F32)
    own_ga_qkv[...] = thin[:a_count, :LANES]
    own_ga_out[...] = thin[:a_count, LANES:]
    for p, cols in enumerate(parts):
        own_gb_qkv[:, cols] = wide[p * b_count : (p + 1) * b_count]
    own_gb_out[...] = wide[3 * b_count : 4 * b_count]

    def sent(n, carry):
        for i in range(4):
            near(i, n).wait_send()
        return carry

    lax.fori_loop(0, others, sent, 0)
    for j in range(planes):
        for i in range(2):
            far(i, j).wait_send()


def split_three(values):
    top = values.astype(BF16)
    rest = values - top.astype(F32)
    mid = rest.astype(BF16)
    return top, mid, (rest - mid.astype(F32)).astype(BF16)


def post_attn_body(
    kinds, attn_low, hid_s, mask, small_s, w_out, a_out, b_out, router, gain,
    low_out, resid, act_two, gate,
):
    attn = attn_low[...]
    low = (dot(attn, a_out[...]) * mask[...].astype(F32)).astype(BF16)
    low_out[...] = low
    res = hid_s[...].astype(F32) + (dot(attn, w_out[...]) + dot(low, b_out[...]))
    resid[...] = res
    scale = lax.rsqrt(jnp.mean(res * res, axis=-1, keepdims=True) + EPSILON)
    act = (res * scale * gain[...]).astype(BF16)
    act_two[...] = act
    sm = small_s[...]
    logits = dot(act, router[...])
    lane = iota(logits.shape, 1)
    routed = jnp.where(lane < kinds, logits + sm, -1e30)
    top = jnp.max(routed, axis=1, keepdims=True)
    expo = jnp.exp(routed - top)
    prob = expo / jnp.sum(expo, axis=1, keepdims=True)
    gate[...] = jnp.where(lane < kinds, prob, logits)


def place_slots(experts, small_s, slot, slot_rows):
    tok = slot.shape[0]
    lane = iota((tok, LANES), 1)
    first = small_s[:, CHOICE_LANE : CHOICE_LANE + 1].astype(jnp.int32)
    second = small_s[:, CHOICE_LANE + 1 : CHOICE_LANE + 2].astype(jnp.int32)
    hot = ((first == lane) | (second == lane)) & (lane < experts)
    hot_low = hot_matrix(hot)
    for blk in range(tok // ROW_BLOCK):
        lo, hi = blk * ROW_BLOCK, (blk + 1) * ROW_BLOCK
        tri = hot_matrix(iota((ROW_BLOCK, hi), 1) < lo + iota((ROW_BLOCK, hi), 0))
        rank = dot(tri, hot_low[:hi, :])
        slot[lo:hi, :] = jnp.where(hot[lo:hi, :], rank, -1.0)
    slot_rows[...] = slot[...].T


def fill_slots(eid, gate, act_two, dy_s, mask, slot_rows, target):
    row = slot_rows[pl.ds(eid, 1), :].astype(jnp.int32)
    pick = hot_matrix(row == iota((target.shape[0], row.shape[1]), 0))
    value = lane_value(gate[...], eid)
    scaled = (dy_s[...].astype(F32) * value).astype(BF16)
    target[:, :MODEL_WIDTH] = dot(pick, act_two[...]).astype(BF16)
    target[:, MODEL_WIDTH : 2 * MODEL_WIDTH] = dot(pick, scaled).astype(BF16)
    target[:, 2 * MODEL_WIDTH :] = dot(pick, mask[...]).astype(BF16)


def dispatch_body(experts, eids, small_s, gate, act_two, dy_s, mask, slot, sent, slot_rows):
    step = pl.program_id(0)

    @pl.when(step == 0)
    def _():
        place_slots(experts, small_s, slot, slot_rows)

    fill_slots(eids[step], gate, act_two, dy_s, mask, slot_rows, sent.at[0])


def ffn_math(
    rows, d_out, mask, w_gu, w_dn, a_gu, b_gu, a_dn, b_dn,
    ga_gu, gb_gu, ga_dn, gb_dn, acc_out, acc_dx, acc_low, acc_dlow,
):
    low_gu = (dot(rows, a_gu[...]) * mask).astype(BF16)
    dlow_dn = (dot_nt(d_out, b_dn[...]) * mask).astype(BF16)
    for ref in (acc_out, acc_dx, acc_low, acc_dlow):
        ref[...] = jnp.zeros_like(ref)

    def step(j, carry):
        lo = pl.multiple_of(j * HIDDEN_BLOCK, HIDDEN_BLOCK)
        g_cols = pl.ds(lo, HIDDEN_BLOCK)
        u_cols = pl.ds(pl.multiple_of(FEEDFWD_WIDTH + lo, HIDDEN_BLOCK), HIDDEN_BLOCK)
        gate = dot(rows, w_gu[:, g_cols]) + dot(low_gu, b_gu[:, g_cols])
        up = dot(rows, w_gu[:, u_cols]) + dot(low_gu, b_gu[:, u_cols])
        sig = 1.0 / (1.0 + jnp.exp(-gate))
        silu = gate * sig
        middle = (silu * up).astype(BF16)
        acc_out[...] += dot(middle, w_dn[g_cols, :])
        acc_low[...] += dot(middle, a_dn[g_cols, :])
        d_mid = dot_nt(d_out, w_dn[g_cols, :]) + dot_nt(dlow_dn, a_dn[g_cols, :])
        d_mid = d_mid.astype(BF16).astype(F32)
        d_gate = (d_mid * up * (sig * (1.0 + gate * (1.0 - sig)))).astype(BF16)
        d_up = (d_mid * silu).astype(BF16)
        acc_dx[...] += dot_nt(d_gate, w_gu[:, g_cols]) + dot_nt(d_up, w_gu[:, u_cols])
        acc_dlow[...] += dot_nt(d_gate, b_gu[:, g_cols]) + dot_nt(d_up, b_gu[:, u_cols])
        gb_gu[:, g_cols] += dot_tn(low_gu, d_gate)
        gb_gu[:, u_cols] += dot_tn(low_gu, d_up)
        ga_dn[g_cols, :] += dot_tn(middle, dlow_dn)
        return carry

    lax.fori_loop(0, FEEDFWD_WIDTH // HIDDEN_BLOCK, step, 0)
    low_dn = (acc_low[...] * mask).astype(BF16)
    result = (acc_out[...] + dot(low_dn, b_dn[...])).astype(BF16)
    gb_dn[...] += dot_tn(low_dn, d_out)
    dlow_gu = (acc_dlow[...] * mask).astype(BF16)
    d_rows = (acc_dx[...] + dot_nt(dlow_gu, a_gu[...])).astype(BF16)
    ga_gu[...] += dot_tn(rows, dlow_gu)
    return result, d_rows


def ffn_body(
    came, w_gu, w_dn, a_gu, b_gu, a_dn, b_dn,
    back, ga_gu, gb_gu, ga_dn, gb_dn, acc_out, acc_dx, acc_low, acc_dlow,
):
    @pl.when(pl.program_id(0) == 0)
    def _():
        for ref in (ga_gu, gb_gu, ga_dn, gb_dn):
            ref[...] = jnp.zeros_like(ref)

    back[0, :, :MODEL_WIDTH], back[0, :, MODEL_WIDTH:] = ffn_math(
        came[0, :, :MODEL_WIDTH], came[0, :, MODEL_WIDTH : 2 * MODEL_WIDTH],
        came[0, :, 2 * MODEL_WIDTH :].astype(F32), w_gu, w_dn, a_gu, b_gu, a_dn, b_dn,
        ga_gu, gb_gu, ga_dn, gb_dn, acc_out, acc_dx, acc_low, acc_dlow,
    )


def pair_ffn_body(
    had, last_sent, wide, mid, thin,
    returned, out_ga_gu, out_gb_gu, out_ga_dn, out_gb_dn,
    came, back, ga_gu, gb_gu, ga_dn, gb_dn, w_gu, w_dn, a_gu, b_gu, a_dn, b_dn, acc_out, acc_dx, acc_low, acc_dlow,
    load_sems, came_sems, back_sems, done_sems, last_sem,
):
    dp, z = lax.axis_index("dp"), lax.axis_index("expert")
    core, plane = dp % 2, z % 2

    def peer(k):
        return (dp + (k // 2) * (1 - 2 * core), z + (k % 2) * (1 - 2 * plane))

    start_kernel(None, [(peer(k), None) for k in (1, 2, 3)], 3)

    def had_in(k):
        return pltpu.make_async_copy(had.at[k], came.at[k], came_sems.at[k])

    last_out = pltpu.make_async_remote_copy(
        src_ref=last_sent, dst_ref=came.at[3], send_sem=last_sem, recv_sem=came_sems.at[3],
        device_id=peer(3), device_id_type=MESH_ID,
    )

    def result_out(k):
        return pltpu.make_async_remote_copy(
            src_ref=back.at[k], dst_ref=returned.at[k], send_sem=back_sems.at[k],
            recv_sem=done_sems.at[k], device_id=peer(k), device_id_type=MESH_ID,
        )

    last_out.start()
    for k in (1, 0, 2):
        had_in(k).start()

    gu_rows = w_gu.shape[0] // wide.shape[0]
    up_rows = b_gu.shape[0] // wide.shape[0]
    dn_rows = w_dn.shape[0] // wide.shape[0]
    plans = (
        (wide, 0, gu_rows, w_gu), (wide, gu_rows, up_rows, b_gu), (mid, 0, dn_rows, w_dn),
        (mid, dn_rows, up_rows, b_dn), (thin, 0, gu_rows, a_gu), (thin, gu_rows, dn_rows, a_dn),
    )

    def load(d, carry):
        for i, (source, at, count, target) in enumerate(plans):
            pltpu.make_async_copy(
                source.at[d, pl.ds(at, count)],
                target.at[pl.ds(pl.multiple_of(d * count, 16), count)],
                load_sems.at[i],
            ).start()
        return carry

    lax.fori_loop(0, wide.shape[0], load, 0)
    for ref in (ga_gu, gb_gu, ga_dn, gb_dn):
        ref[...] = jnp.zeros_like(ref)
    for i, (_, _, _, target) in enumerate(plans):
        pltpu.make_async_copy(target, target, load_sems.at[i]).wait()

    def source_step(s, carry):
        k = s + 1 - 2 * (s % 2)

        @pl.when(k != 3)
        def _():
            had_in(k).wait()

        @pl.when(k == 3)
        def _():
            last_out.wait_recv()

        back[k, :, :MODEL_WIDTH], back[k, :, MODEL_WIDTH:] = ffn_math(
            came[k, :, :MODEL_WIDTH], came[k, :, MODEL_WIDTH : 2 * MODEL_WIDTH],
            came[k, :, 2 * MODEL_WIDTH :].astype(F32), w_gu, w_dn, a_gu, b_gu, a_dn, b_dn,
            ga_gu, gb_gu, ga_dn, gb_dn, acc_out, acc_dx, acc_low, acc_dlow,
        )

        @pl.when(k != 0)
        def _():
            result_out(k).start()

        return carry

    lax.fori_loop(0, 4, source_step, 0)
    for out, total in (
        (out_ga_gu, ga_gu), (out_gb_gu, gb_gu), (out_ga_dn, ga_dn), (out_gb_dn, gb_dn),
    ):
        out[...] = total[...].astype(BF16)
    own_out = pltpu.make_async_copy(back.at[0], returned.at[0], done_sems.at[0])
    own_out.start()
    own_out.wait()
    last_out.wait_send()
    for k in (1, 2, 3):
        result_out(k).wait_send()
        result_out(k).wait_recv()


def combine_body(
    experts, kinds, eids, resid, act_two, dy_s, gate, slot, small_s, low_out, attn_low, mask, came,
    w_out, a_out, b_out, router, const_value, gain,
    out_s, d_resid, d_attended, d_logits, ga_out, gb_out,
):
    @pl.when(pl.program_id(0) == 0)
    def _():
        ga_out[...] = jnp.zeros_like(ga_out)
        gb_out[...] = jnp.zeros_like(gb_out)

    rows = resid.shape[0]
    cap = came.shape[1]
    res = resid[...]
    act = act_two[...].astype(F32)
    dy = dy_s[...].astype(F32)
    prob = gate[...]
    lane = iota((rows, LANES), 1)
    out = res
    d_act = jnp.zeros((rows, MODEL_WIDTH), F32)
    d_gate = jnp.zeros((rows, LANES), F32)
    for k in range(came.shape[0]):
        eid = eids[k]
        place = lane_value(slot[...], eid).astype(jnp.int32)
        pick = hot_matrix(place == iota((rows, cap), 1))
        result = dot(pick, came[k, :, :MODEL_WIDTH])
        d_act = d_act + dot(pick, came[k, :, MODEL_WIDTH:])
        d_gate = jnp.where(lane == eid, jnp.sum(dy * result, axis=1, keepdims=True), d_gate)
        out = out + lane_value(prob, eid) * result
    sm = small_s[...]
    first = sm[:, CHOICE_LANE : CHOICE_LANE + 1]
    second = sm[:, CHOICE_LANE + 1 : CHOICE_LANE + 2]

    def chosen(kind):
        return jnp.where((first == kind) | (second == kind), 1.0, 0.0)

    has_copy, has_zero, has_one = chosen(experts + 1), chosen(experts + 2), chosen(experts + 3)
    g_copy = has_copy * prob[:, experts + 1 : experts + 2]
    g_zero = has_zero * prob[:, experts + 2 : experts + 3]
    g_one = has_one * prob[:, experts + 3 : experts + 4]

    def pair(at):
        left, right = prob[:, at : at + 1], prob[:, at + 1 : at + 2]
        top = jnp.maximum(left, right)
        e_left, e_right = jnp.exp(left - top), jnp.exp(right - top)
        return e_left / (e_left + e_right), e_right / (e_left + e_right)

    a00, a01 = pair(CONST_LANE)
    a10, a11 = pair(CONST_LANE + 2)
    v_zero, v_one = const_value[0:1, :], const_value[1:2, :]
    along_act = jnp.sum(dy * act, axis=1, keepdims=True)
    along_zero = jnp.sum(dy * v_zero, axis=1, keepdims=True)
    along_one = jnp.sum(dy * v_one, axis=1, keepdims=True)
    coef = g_copy + g_zero * a00 + g_one * a10
    out = out + coef * act + (g_zero * a01) * v_zero + (g_one * a11) * v_one
    out_s[...] = out.astype(BF16)
    d_gate = jnp.where(lane == experts + 1, has_copy * along_act, d_gate)
    d_gate = jnp.where(
        lane == experts + 2, has_zero * (a00 * along_act + a01 * along_zero), d_gate
    )
    d_gate = jnp.where(lane == experts + 3, has_one * (a10 * along_act + a11 * along_one), d_gate)
    prob = jnp.where(lane < kinds, prob, 0.0)
    d_logit = prob * (d_gate - jnp.sum(prob * d_gate, axis=1, keepdims=True))
    d_logits[...] = d_logit
    mix = d_logit
    for at, g_val, left, right, along in (
        (CONST_LANE, g_zero, a00, a01, along_zero),
        (CONST_LANE + 2, g_one, a10, a11, along_one),
    ):
        da_left, da_right = g_val * along_act, g_val * along
        level = left * da_left + right * da_right
        mix = jnp.where(lane == at, left * (da_left - level), mix)
        mix = jnp.where(lane == at + 1, right * (da_right - level), mix)
    mix_hi = mix.astype(BF16)
    mix_lo = (mix - mix_hi.astype(F32)).astype(BF16)
    d_act = d_act + coef * dy + (dot_nt(mix_hi, router[...]) + dot_nt(mix_lo, router[...]))
    scale = lax.rsqrt(jnp.mean(res * res, axis=-1, keepdims=True) + EPSILON)
    weighted = d_act * gain[...].astype(F32)
    d_res = dy + (
        scale * weighted
        - res * (scale * scale * scale) * jnp.mean(res * weighted, axis=-1, keepdims=True)
    )
    d_resid[...] = d_res
    d_attn = d_res.astype(BF16)
    dlow = (dot_nt(d_attn, b_out[...]) * mask[...].astype(F32)).astype(BF16)
    gb_out[...] += dot_tn(low_out[...], d_attn)
    ga_out[...] += dot_tn(attn_low[...], dlow)
    d_attended[...] = (dot_nt(d_attn, w_out[...]) + dot_nt(dlow, a_out[...])).astype(BF16)


def input_grad_body(
    d_query, d_key, d_value, low_qkv, act_one, mask, hid_s, d_resid, w_qkv, a_in, b_out, gain,
    high, lower, ga_qkv, gb_qkv,
):
    @pl.when(pl.program_id(0) == 0)
    def _():
        ga_qkv[...] = jnp.zeros_like(ga_qkv)
        gb_qkv[...] = jnp.zeros_like(gb_qkv)

    d_low = jnp.zeros((d_query.shape[0], LANES), F32)
    d_act = jnp.zeros((d_query.shape[0], MODEL_WIDTH), F32)
    for part, ref in enumerate((d_query, d_key, d_value)):
        cols = slice(part * MODEL_WIDTH, (part + 1) * MODEL_WIDTH)
        grad = ref[...]
        d_low = d_low + dot_nt(grad, b_out[:, cols])
        d_act = d_act + dot_nt(grad, w_qkv[:, cols])
        gb_qkv[:, cols] += dot_tn(low_qkv[...], grad)
    d_low = (d_low * mask[...].astype(F32)).astype(BF16)
    ga_qkv[...] += dot_tn(act_one[...], d_low)
    d_act = d_act + dot_nt(d_low, a_in[...])
    hid = hid_s[...].astype(F32)
    scale = lax.rsqrt(jnp.mean(hid * hid, axis=-1, keepdims=True) + EPSILON)
    weighted = d_act * gain[...].astype(F32)
    grad_hid = d_resid[...] + (
        scale * weighted
        - hid * (scale * scale * scale) * jnp.mean(hid * weighted, axis=-1, keepdims=True)
    )
    top = grad_hid.astype(BF16)
    high[...] = top
    lower[...] = (grad_hid - top.astype(F32)).astype(BF16)


def to_rows_body(place_col, out_s, d_logits, high, lower, out, grad_hidden, grad_gate):
    rows = out.shape[0]
    tok = out_s.shape[0]
    perm = hot_matrix(place_col[...] == iota((rows, tok), 1))
    out[...] = dot(perm, out_s[...]).astype(BF16)
    grad_hidden[...] = dot(perm, high[...]) + dot(perm, lower[...])
    logits = d_logits[...]
    top = logits.astype(BF16)
    rest = logits - top.astype(F32)
    mid = rest.astype(BF16)
    last = (rest - mid.astype(F32)).astype(BF16)
    grad_gate[...] = dot(perm, top) + (dot(perm, mid) + dot(perm, last))


class PairPlan:
    paired = True

    def __init__(self, dp, ex):
        self.ex = ex

    def expert_ids(self):
        own = lax.axis_index("expert") % 2 + 2 * (lax.axis_index("dp") % 2)
        return own ^ jnp.arange(self.ex, dtype=jnp.int32)


class AxisPlan:
    paired = False

    def __init__(self, dp, ex):
        self.dp, self.ex = dp, ex

    def gather(self, shard):
        return lax.all_gather(shard, "dp", axis=0)

    def expert_ids(self):
        return jnp.arange(self.ex, dtype=jnp.int32)

    def exchange(self, values):
        return lax.all_to_all(values, "expert", split_axis=0, concat_axis=0, tiled=True)

    def reduce(self, sums):
        return lax.psum_scatter(sums, "dp", scatter_dimension=0, tiled=True)[0].astype(F32)

    def reduce_all(self, sums):
        return lax.psum_scatter(
            sums, ("dp", "expert"), scatter_dimension=0, tiled=True
        )[0].astype(F32)


def shards(
    dp_size,
    expert_count,
    hidden_input,
    gate_carryover,
    sequence_length,
    token_stream_place,
    expert_choice_index,
    sequence_adapter,
    attention_gain,
    query_key_weight,
    output_weight,
    adapter_in_query,
    adapter_out_query,
    adapter_in_output,
    adapter_out_output,
    feedfwd_gain,
    router_weight,
    constant_gate,
    constant_value,
    gate_upward_weight,
    down_weight,
    adapter_in_gate,
    adapter_out_gate,
    adapter_in_down,
    adapter_out_down,
    output_gradient,
):
    tok = hidden_input.shape[0]
    width = MODEL_WIDTH
    kinds = expert_count + 4
    devices = dp_size * expert_count
    capacity = 5 * tok // (2 * kinds) // 8 * 8 + 8
    cap = -(-capacity // 16) * 16
    blocks = tok // ROW_BLOCK
    plan = (PairPlan if (dp_size, expert_count) == (8, 4) else AxisPlan)(dp_size, expert_count)

    a_rows, b_rows = query_key_weight.shape[0], adapter_out_query.shape[0]
    gu_rows, up_rows, dn_rows = (
        gate_upward_weight.shape[1], adapter_out_gate.shape[1], down_weight.shape[1],
    )
    gain_one, gain_two = attention_gain[None, :], feedfwd_gain[None, :]
    const_value = constant_value.astype(F32)
    sent_width = 2 * width + LANES
    full = whole
    hbm = pl.BlockSpec(memory_space=pl.ANY)
    vmem = pl.BlockSpec(memory_space=pltpu.VMEM)
    pairs = HEAD_COUNT // 2
    smem = pl.BlockSpec(memory_space=pltpu.SMEM)
    eids = plan.expert_ids()
    if plan.paired:
        shapes = [
            sds((tok, width), BF16), sds((tok, width), BF16), sds((tok, LANES), F32),
            sds((tok, width), BF16), sds((tok, LANES), BF16), sds((tok, LANES), BF16),
            sds((tok, 1), jnp.int32), sds((tok, LANES), F32), sds((tok, LANES), F32),
            sds((width, LANES), BF16),
            sds((tok, width), BF16), sds((tok, width), BF16), sds((tok, width), BF16),
            sds((width, 3 * width), BF16), sds((width, LANES), BF16), sds((LANES, 3 * width), BF16),
            sds((width, width), BF16), sds((width, LANES), BF16), sds((LANES, width), BF16),
            sds((tok, width), BF16), sds((tok, LANES), F32), sds((tok, LANES), BF16),
            sds((tok, width), F32), sds((tok, width), BF16), sds((tok, LANES), F32),
            sds((tok, LANES), F32),
        ]
        shard_rows = -(-(a_rows + b_rows) // 16) * 16
        packed = [
            (gu_rows + up_rows, 2 * FEEDFWD_WIDTH), (dn_rows + up_rows, width),
            (gu_rows + dn_rows, LANES),
        ]
        row_shape = (expert_count, cap, sent_width)
        (
            hid_s, dy_s, small_s, act_one, low_qkv, mask, starts, cosine, sine, router,
            query, key, value, w_qkv, a_qkv, b_qkv, w_out, a_out, b_out,
            attn_low, lse, low_out, resid, act_two, gate, slot,
            wide, mid, thin, came, last_sent,
        ) = pl.pallas_call(
            functools.partial(pair_front_body, kinds, a_rows, b_rows),
            in_specs=[smem] * 2 + [vmem] * 15 + [hbm] * 6,
            out_specs=[hbm] * (FRONT_KEPT + 5),
            out_shape=shapes
            + [sds((dp_size,) + shape, BF16) for shape in packed]
            + [sds(row_shape, BF16), sds(row_shape[1:], BF16)],
            scratch_shapes=[pltpu.VMEM(s.shape, s.dtype) for s in shapes]
            + [
                pltpu.VMEM((devices, shard_rows, 3 * width + LANES), BF16),
                pltpu.VMEM((devices, shard_rows, width + LANES), BF16),
                *[pltpu.VMEM(shape, BF16) for shape in packed],
                pltpu.VMEM((3,) + row_shape[1:], BF16),
                pltpu.VMEM((LANES, tok), F32),
                pltpu.SemaphoreType.DMA((2, 35)), pltpu.SemaphoreType.DMA((2, 35)),
                pltpu.SemaphoreType.DMA((4, 8)), pltpu.SemaphoreType.DMA((4, 8)),
                pltpu.SemaphoreType.DMA((FRONT_KEPT,)), pltpu.SemaphoreType.DMA((6,)),
                pltpu.SemaphoreType.DMA((4,)), pltpu.SemaphoreType.DMA((4,)),
            ],
            compiler_params=pltpu.CompilerParams(
                vmem_limit_bytes=VMEM_BYTES, collective_id=4, has_side_effects=True
            ),
            name="pair_front",
        )(sequence_length, sequence_adapter, token_stream_place, hidden_input, output_gradient,
          gate_carryover, expert_choice_index, gain_one, gain_two, router_weight, constant_gate,
          query_key_weight, output_weight, adapter_in_query, adapter_in_output, adapter_out_query,
          adapter_out_output, gate_upward_weight, adapter_out_gate, down_weight, adapter_out_down,
          adapter_in_gate, adapter_in_down)
        place = token_stream_place[0]
    else:
        pad_rows = -(a_rows + b_rows) % 16

        def pack(weight, adapter_in, adapter_out):
            lower = jnp.pad(adapter_out, ((0, pad_rows), (0, LANES)))
            return jnp.concatenate([jnp.concatenate([weight, adapter_in], axis=1), lower], axis=0)

        own_qkv = pack(query_key_weight, adapter_in_query, adapter_out_query)
        own_out = pack(output_weight, adapter_in_output, adapter_out_output)
        own_wide = jnp.concatenate([gate_upward_weight[0], adapter_out_gate[0]], axis=0)
        own_mid = jnp.concatenate([down_weight[0], adapter_out_down[0]], axis=0)
        own_thin = jnp.concatenate([adapter_in_gate[0], adapter_in_down[0]], axis=0)

        place = token_stream_place[0]
        ends = jnp.cumsum(sequence_length[0])
        begins = ends - sequence_length[0]
        stream = jnp.arange(tok, dtype=jnp.int32)
        seg = jnp.sum((stream[:, None] >= ends[None, :]).astype(jnp.int32), axis=1)
        seg_hot = seg[:, None] == jnp.arange(ends.shape[0], dtype=jnp.int32)[None, :]
        start = jnp.sum(jnp.where(seg_hot, begins[None, :], 0), axis=1)
        adapter = jnp.sum(jnp.where(seg_hot, sequence_adapter[0][None, :], 0), axis=1)
        half = HEAD_DIM // 2
        freq = jnp.exp(jnp.arange(half, dtype=F32) * (-math.log(10000.0) / half))
        angle = (stream - start).astype(F32)[:, None] * freq[None, :]
        cos, sin = jnp.cos(angle), jnp.sin(angle)
        cosine = jnp.concatenate([cos, cos, cos, cos], axis=1)
        sine = jnp.concatenate([-sin, sin, -sin, sin], axis=1)
        starts = start[:, None]
        mask = (jnp.arange(LANES)[None, :] // ADAPTER_RANK == adapter[:, None]).astype(BF16)
        top, middle, last = split_three(gate_carryover)
        gap = jnp.zeros((tok, 16 - kinds), BF16)
        small = jnp.concatenate(
            [top, gap, middle, gap, last, gap, expert_choice_index.astype(BF16),
             jnp.zeros((tok, LANES - CHOICE_LANE - 2), BF16)],
            axis=1,
        )
        router = jnp.concatenate(
            [router_weight, jnp.zeros((width, CONST_LANE - kinds), BF16), constant_gate,
             jnp.zeros((width, LANES - CONST_LANE - 4), BF16)],
            axis=1,
        )

        all_qkv = lax.all_gather(own_qkv, ("dp", "expert"), axis=0)
        all_out = lax.all_gather(own_out, ("dp", "expert"), axis=0)
        upper = slice(a_rows, a_rows + b_rows)
        w_qkv = all_qkv[:, :a_rows, : 3 * width].reshape(width, 3 * width)
        a_qkv = all_qkv[:, :a_rows, 3 * width :].reshape(width, LANES)
        b_qkv = all_qkv[:, upper, : 3 * width].reshape(LANES, 3 * width)
        w_out = all_out[:, :a_rows, :width].reshape(width, width)
        a_out = all_out[:, :a_rows, width:].reshape(width, LANES)
        b_out = all_out[:, upper, :width].reshape(LANES, width)
        wide, mid, thin = (plan.gather(w) for w in (own_wide, own_mid, own_thin))
        hid_s, dy_s, small_s, act_one, low_qkv, query, key, value = call(
            proj_in_body,
            (blocks,),
            [full((1, tok)), full((tok, width)), full((tok, width)), full((tok, LANES)),
             row_spec(LANES), row_spec(LANES), row_spec(LANES), full((1, width)),
             full((width, 3 * width)), full((width, LANES)), full((LANES, 3 * width))],
            [row_spec(width), row_spec(width), row_spec(LANES), row_spec(width), row_spec(LANES),
             row_spec(width), row_spec(width), row_spec(width)],
            [sds((tok, width), BF16), sds((tok, width), BF16), sds((tok, LANES), F32),
             sds((tok, width), BF16), sds((tok, LANES), BF16), sds((tok, width), BF16),
             sds((tok, width), BF16), sds((tok, width), BF16)],
            name="proj_in",
        )(place[None, :], hidden_input, output_gradient, small, cosine, sine, mask, gain_one,
          w_qkv, a_qkv, b_qkv)

        attn_low, lse = call(
            attention_fwd_body,
            (pairs,),
            [col_spec(tok)] * 3 + [full((tok, 1))],
            [col_spec(tok), full((tok, LANES))],
            [sds((tok, width), BF16), sds((tok, LANES), F32)],
            name="attention_fwd",
        )(query, key, value, starts)

        low_out, resid, act_two, gate = call(
            functools.partial(post_attn_body, kinds),
            (blocks,),
            [row_spec(width), row_spec(width), row_spec(LANES), row_spec(LANES), full((width, width)),
             full((width, LANES)), full((LANES, width)), full((width, LANES)), full((1, width))],
            [row_spec(LANES), row_spec(width), row_spec(width), row_spec(LANES)],
            [sds((tok, LANES), BF16), sds((tok, width), F32), sds((tok, width), BF16),
             sds((tok, LANES), F32)],
            name="post_attn",
        )(attn_low, hid_s, mask, small_s, w_out, a_out, b_out, router, gain_two)

        slot, sent = call(
            functools.partial(dispatch_body, expert_count),
            (expert_count,),
            [smem, full((tok, LANES)), full((tok, LANES)), full((tok, width)), full((tok, width)),
             full((tok, LANES))],
            [full((tok, LANES)), pl.BlockSpec((1, cap, sent_width), lambda i: (i, 0, 0))],
            [sds((tok, LANES), F32), sds((expert_count, cap, sent_width), BF16)],
            scratch=[pltpu.VMEM((LANES, tok), F32)],
            name="dispatch",
        )(eids, small_s, gate, act_two, dy_s, mask)

    grad_shapes = [
        sds((width, LANES), F32), sds((LANES, 2 * FEEDFWD_WIDTH), F32),
        sds((FEEDFWD_WIDTH, LANES), F32), sds((LANES, width), F32),
    ]
    accumulators = [
        pltpu.VMEM((cap, width), F32), pltpu.VMEM((cap, width), F32),
        pltpu.VMEM((cap, LANES), F32), pltpu.VMEM((cap, LANES), F32),
    ]
    if plan.paired:
        returned, ga_gu, gb_gu, ga_dn, gb_dn = pl.pallas_call(
            pair_ffn_body,
            in_specs=[hbm] * 5,
            out_specs=[hbm] + [vmem] * 4,
            out_shape=[sds((expert_count, cap, 2 * width), BF16)]
            + [sds(g.shape, BF16) for g in grad_shapes],
            scratch_shapes=[
                pltpu.VMEM((expert_count, cap, sent_width), BF16),
                pltpu.VMEM((expert_count, cap, 2 * width), BF16),
                *[pltpu.VMEM(g.shape, F32) for g in grad_shapes],
                pltpu.VMEM((width, 2 * FEEDFWD_WIDTH), BF16), pltpu.VMEM((FEEDFWD_WIDTH, width), BF16),
                pltpu.VMEM((width, LANES), BF16), pltpu.VMEM((LANES, 2 * FEEDFWD_WIDTH), BF16),
                pltpu.VMEM((FEEDFWD_WIDTH, LANES), BF16), pltpu.VMEM((LANES, width), BF16),
                *accumulators,
                pltpu.SemaphoreType.DMA((6,)),
                *[pltpu.SemaphoreType.DMA((expert_count,)) for _ in range(3)],
                pltpu.SemaphoreType.DMA,
            ],
            compiler_params=pltpu.CompilerParams(
                vmem_limit_bytes=VMEM_BYTES, collective_id=1, has_side_effects=True
            ),
            name="pair_ffn",
        )(came, last_sent, wide, mid, thin)
    else:
        w_gu = wide[:, :gu_rows].reshape(width, 2 * FEEDFWD_WIDTH)
        b_gu = wide[:, gu_rows:].reshape(LANES, 2 * FEEDFWD_WIDTH)
        w_dn = mid[:, :dn_rows].reshape(FEEDFWD_WIDTH, width)
        b_dn = mid[:, dn_rows:].reshape(LANES, width)
        a_gu = thin[:, :gu_rows].reshape(width, LANES)
        a_dn = thin[:, gu_rows:].reshape(FEEDFWD_WIDTH, LANES)
        came = plan.exchange(sent)
        back, ga_gu, gb_gu, ga_dn, gb_dn = call(
            ffn_body,
            (expert_count,),
            [pl.BlockSpec((1, cap, sent_width), lambda i: (i, 0, 0)),
             full((width, 2 * FEEDFWD_WIDTH)), full((FEEDFWD_WIDTH, width)), full((width, LANES)),
             full((LANES, 2 * FEEDFWD_WIDTH)), full((FEEDFWD_WIDTH, LANES)), full((LANES, width))],
            [pl.BlockSpec((1, cap, 2 * width), lambda i: (i, 0, 0)), full((width, LANES)),
             full((LANES, 2 * FEEDFWD_WIDTH)), full((FEEDFWD_WIDTH, LANES)), full((LANES, width))],
            [sds((expert_count, cap, 2 * width), BF16)] + grad_shapes,
            scratch=accumulators,
            name="ffn",
        )(came, w_gu, w_dn, a_gu, b_gu, a_dn, b_dn)
        returned = plan.exchange(back)

    out_s, d_resid, d_attended, d_logits, ga_out, gb_out = call(
        functools.partial(combine_body, expert_count, kinds),
        (tok // ROW_BLOCK,),
        [smem, row_spec(width, ROW_BLOCK), row_spec(width, ROW_BLOCK), row_spec(width, ROW_BLOCK), row_spec(LANES, ROW_BLOCK), row_spec(LANES, ROW_BLOCK),
         row_spec(LANES, ROW_BLOCK), row_spec(LANES, ROW_BLOCK), row_spec(width, ROW_BLOCK), row_spec(LANES, ROW_BLOCK),
         full((expert_count, cap, 2 * width)), full((width, width)), full((width, LANES)),
         full((LANES, width)), full((width, LANES)), full((2, width)), full((1, width))],
        [row_spec(width, ROW_BLOCK), row_spec(width, ROW_BLOCK), row_spec(width, ROW_BLOCK), row_spec(LANES, ROW_BLOCK), full((width, LANES)),
         full((LANES, width))],
        [sds((tok, width), BF16), sds((tok, width), F32), sds((tok, width), BF16),
         sds((tok, LANES), F32), sds((width, LANES), F32), sds((LANES, width), F32)],
        name="combine",
    )(eids, resid, act_two, dy_s, gate, slot, small_s, low_out, attn_low, mask, returned,
      w_out, a_out, b_out, router, const_value, gain_two)

    if plan.paired:
        flow = dict(vmem_limit_bytes=VMEM_BYTES, has_side_effects=True)
        own_shapes = [
            sds((gu_rows, LANES), F32), sds((up_rows, 2 * FEEDFWD_WIDTH), F32),
            sds((dn_rows, LANES), F32), sds((up_rows, width), F32),
        ]
        d_query, d_key, d_value, *expert_owned = pl.pallas_call(
            pair_attention_bwd_body,
            grid=(pairs,),
            in_specs=[col_spec(tok)] * 5
            + [full((tok, LANES)), full((tok, 1)), full((tok, LANES)), full((tok, LANES))]
            + [hbm] * 4,
            out_specs=[col_spec(tok)] * 3 + [full(s.shape) for s in own_shapes],
            out_shape=[sds((tok, width), BF16)] * 3 + own_shapes,
            scratch_shapes=[pltpu.VMEM((tok, LANES), F32), pltpu.VMEM((tok, LANES), F32)]
            + [pltpu.VMEM((dp_size,) + s.shape, BF16) for s in own_shapes]
            + [pltpu.SemaphoreType.DMA((4, dp_size)), pltpu.SemaphoreType.DMA((4, dp_size))],
            compiler_params=pltpu.CompilerParams(collective_id=2, **flow),
            name="pair_attention_bwd",
        )(query, key, value, d_attended, attn_low, lse, starts, cosine, sine,
          ga_gu, gb_gu, ga_dn, gb_dn)
        sum_shapes = [(width, LANES), (LANES, 3 * width), (width, LANES), (LANES, width)]
        got_shapes = [(dp_size - 1, a // dp_size, b) for a, b in sum_shapes]
        thin_rows = -(-a_rows // 16) * 16
        output, grad_hidden, grad_gate, *attn_owned = pl.pallas_call(
            pair_tail_body,
            in_specs=[vmem] * 13 + [hbm] * 4,
            out_specs=[vmem] * 7,
            out_shape=[
                sds((tok, width), BF16), sds((tok, width), F32), sds((tok, LANES), F32),
                sds((a_rows, LANES), F32), sds((b_rows, 3 * width), F32),
                sds((a_rows, LANES), F32), sds((b_rows, width), F32),
            ],
            scratch_shapes=[
                pltpu.VMEM((tok, width), BF16), pltpu.VMEM((tok, width), F32),
                pltpu.VMEM((width, 3 * width), BF16), pltpu.VMEM((tok, width), BF16),
                pltpu.VMEM((tok, width), BF16), pltpu.VMEM((tok, width), BF16),
                pltpu.VMEM((tok, LANES), BF16),
                pltpu.VMEM((width, LANES), F32), pltpu.VMEM((LANES, 3 * width), F32),
                *[pltpu.VMEM(shape, BF16) for shape in sum_shapes + got_shapes],
                pltpu.VMEM((expert_count, thin_rows, 2 * LANES), BF16),
                pltpu.VMEM((expert_count, 4 * b_rows, width), BF16),
                pltpu.VMEM((expert_count - 1, thin_rows, 2 * LANES), BF16),
                pltpu.VMEM((expert_count - 1, 4 * b_rows, width), BF16),
                pltpu.SemaphoreType.DMA((4,)),
                pltpu.SemaphoreType.DMA((4, dp_size - 1)), pltpu.SemaphoreType.DMA((4, dp_size - 1)),
                pltpu.SemaphoreType.DMA((2, expert_count - 1)),
                pltpu.SemaphoreType.DMA((2, expert_count - 1)),
            ],
            compiler_params=pltpu.CompilerParams(collective_id=3, **flow),
            name="pair_tail",
        )(place[:, None], d_query, d_key, d_value, low_qkv, act_one, mask, a_qkv, b_qkv, gain_one,
          ga_out, gb_out, d_logits, hid_s, d_resid, w_qkv, out_s)
        return (
            output, grad_hidden, grad_gate[:, :kinds], *attn_owned,
            *[expert_owned[i][None] for i in range(4)],
        )

    owned_wide = plan.reduce(
        jnp.concatenate([gb_gu, gb_dn], axis=1).astype(BF16).reshape(dp_size, up_rows, -1)
    )
    owned_thin = plan.reduce(
        jnp.concatenate(
            [ga_gu.reshape(dp_size, gu_rows, LANES), ga_dn.reshape(dp_size, dn_rows, LANES)], axis=1
        ).astype(BF16)
    )

    d_query, d_key, d_value = call(
        attention_bwd_body,
        (pairs,),
        [col_spec(tok)] * 5
        + [full((tok, LANES)), full((tok, 1)), full((tok, LANES)), full((tok, LANES))],
        [col_spec(tok)] * 3,
        [sds((tok, width), BF16)] * 3,
        scratch=[pltpu.VMEM((tok, LANES), F32), pltpu.VMEM((tok, LANES), F32)],
        name="attention_bwd",
    )(query, key, value, d_attended, attn_low, lse, starts, cosine, sine)

    high, lower, ga_qkv, gb_qkv = call(
        input_grad_body,
        (blocks,),
        [row_spec(width)] * 3 + [row_spec(LANES), row_spec(width), row_spec(LANES), row_spec(width),
         row_spec(width), full((width, 3 * width)), full((width, LANES)), full((LANES, 3 * width)),
         full((1, width))],
        [row_spec(width), row_spec(width), full((width, LANES)), full((LANES, 3 * width))],
        [sds((tok, width), BF16), sds((tok, width), BF16), sds((width, LANES), F32),
         sds((LANES, 3 * width), F32)],
        name="input_grad",
    )(d_query, d_key, d_value, low_qkv, act_one, mask, hid_s, d_resid, w_qkv, a_qkv, b_qkv,
      gain_one)

    owned = plan.reduce_all(
        jnp.concatenate(
            [
                ga_qkv.reshape(devices, b_rows, -1),
                ga_out.reshape(devices, b_rows, -1),
                gb_qkv.reshape(devices, b_rows, -1),
                gb_out.reshape(devices, b_rows, -1),
            ],
            axis=2,
        ).astype(BF16)
    )

    output, grad_hidden, grad_gate = call(
        to_rows_body,
        (blocks,),
        [row_spec(1), full((tok, width)), full((tok, LANES)), full((tok, width)),
         full((tok, width))],
        [row_spec(width), row_spec(width), row_spec(LANES)],
        [sds((tok, width), BF16), sds((tok, width), F32), sds((tok, LANES), F32)],
        name="to_rows",
    )(place[:, None], out_s, d_logits, high, lower)

    return (
        output,
        grad_hidden,
        grad_gate[:, :kinds],
        owned[:, :width].reshape(a_rows, LANES),
        owned[:, 2 * width : 5 * width],
        owned[:, width : 2 * width].reshape(a_rows, LANES),
        owned[:, 5 * width :],
        owned_thin[None, :gu_rows],
        owned_wide[None, :, : 2 * FEEDFWD_WIDTH],
        owned_thin[None, gu_rows:],
        owned_wide[None, :, 2 * FEEDFWD_WIDTH :],
    )


def solution(mesh):
    rows = P(("dp", "expert"), None)
    expert_rows = P("expert", "dp", None)
    in_specs = (
        (rows,) * 6 + (P(),) + (rows,) * 6 + (P(),) * 4 + (expert_rows,) * 6 + (rows,)
    )
    out_specs = (rows,) * 7 + (expert_rows,) * 4
    body = functools.partial(shards, mesh.shape["dp"], mesh.shape["expert"])
    return jax.shard_map(body, mesh=mesh, in_specs=in_specs, out_specs=out_specs, check_vma=False)
```

```python
import functools
import math

import jax
import jax.numpy as jnp
from jax import lax
from jax.experimental import pallas as pl
from jax.experimental.pallas import tpu as pltpu
from jax.sharding import PartitionSpec as P

MODEL_WIDTH = 768
HEAD_COUNT = 12
HEAD_DIM = 64
FEEDFWD_WIDTH = 2048
ADAPTER_RANK = 16
ROW_BLOCK = 256
HIDDEN_BLOCK = 1024
LANES = 128
CONST_LANE = 64
CHOICE_LANE = 48
CHOICE_ROWS = 16
EPSILON = 1e-06
VMEM_BYTES = 60 * 2**20
FRONT_KEPT = 26
MESH_ID = pl.DeviceIdType.MESH

F32 = jnp.float32
BF16 = jnp.bfloat16


def dot(a, b):
    return jnp.dot(a, b, preferred_element_type=F32)


def dot_nt(a, b):
    return lax.dot_general(a, b, (((1,), (1,)), ((), ())), preferred_element_type=F32)


def dot_tn(a, b):
    return lax.dot_general(a, b, (((0,), (0,)), ((), ())), preferred_element_type=F32)


def iota(shape, dim):
    return lax.broadcasted_iota(jnp.int32, shape, dim)


def hot_matrix(condition):
    return jnp.where(condition, 1.0, 0.0).astype(BF16)


def whole(shape):
    zeros = (0,) * len(shape)
    return pl.BlockSpec(shape, lambda *_: zeros)


def row_spec(width, rows=ROW_BLOCK):
    return pl.BlockSpec((rows, width), lambda i: (i, 0))


def col_spec(rows, width=LANES):
    return pl.BlockSpec((rows, width), lambda j: (0, j))


def sds(shape, dtype):
    return jax.ShapeDtypeStruct(shape, dtype)


def call(body, grid, in_specs, out_specs, out_shape, scratch=(), name=None):
    return pl.pallas_call(
        body,
        grid=grid,
        in_specs=in_specs,
        out_specs=out_specs,
        out_shape=out_shape,
        scratch_shapes=list(scratch),
        compiler_params=pltpu.CompilerParams(vmem_limit_bytes=VMEM_BYTES),
        name=name,
    )


def half_swap(values):
    lane = iota(values.shape, 1)
    up = pltpu.roll(values, 32, 1)
    down = pltpu.roll(values, LANES - 32, 1)
    return jnp.where(lane % HEAD_DIM < HEAD_DIM // 2, down, up)


def lane_value(values, lane_id):
    return jnp.sum(jnp.where(iota(values.shape, 1) == lane_id, values, 0.0), axis=1, keepdims=True)


def proj_in_body(
    place_row, hidden, upstream, small, cosine, sine, mask, gain, w_qkv, a_in, b_out,
    hid_s, dy_s, small_s, act_one, low_qkv, query, key, value,
):
    rows = hid_s.shape[0]
    base = pl.program_id(0) * rows
    perm = hot_matrix(place_row[...] == base + iota((rows, place_row.shape[1]), 0))
    hid = dot(perm, hidden[...])
    hid_s[...] = hid.astype(BF16)
    dy_s[...] = dot(perm, upstream[...]).astype(BF16)
    parts = dot(perm, small[...])
    small_s[...] = parts + (pltpu.roll(parts, LANES - 16, 1) + pltpu.roll(parts, LANES - 32, 1))
    act = normed(hid, gain)
    act_one[...] = act
    low, q_val, k_val, value[...] = project(
        act, mask[...], cosine[...], sine[...], w_qkv, a_in, b_out
    )
    low_qkv[...] = low
    query[...], key[...] = q_val, k_val


def normed(values, gain):
    scale = lax.rsqrt(jnp.mean(values * values, axis=-1, keepdims=True) + EPSILON)
    return (values * scale * gain[...].astype(F32)).astype(BF16)


def project(act, mask, cos, sin, w_qkv, a_in, b_out):
    low = (dot(act, a_in[...]) * mask.astype(F32)).astype(BF16)
    turned = []
    for start, factor in ((0, HEAD_DIM**-0.5), (MODEL_WIDTH, 1.0)):
        cols = slice(start, start + MODEL_WIDTH)
        vals = dot(act, w_qkv[:, cols]) + dot(low, b_out[:, cols])
        pieces = []
        for c in range(MODEL_WIDTH // LANES):
            piece = vals[:, c * LANES : (c + 1) * LANES]
            piece = (piece * cos + half_swap(piece) * sin).astype(BF16)
            pieces.append(piece if factor == 1.0 else piece * jnp.asarray(factor, BF16))
        turned.append(jnp.concatenate(pieces, axis=1))
    value = dot(act, w_qkv[:, 2 * MODEL_WIDTH :]) + dot(low, b_out[:, 2 * MODEL_WIDTH :])
    return low, turned[0], turned[1], value.astype(BF16)


def head_mask(shape, head):
    lane = iota(shape, 1)
    return (lane >= head * HEAD_DIM) & (lane < (head + 1) * HEAD_DIM)


def attention_fwd_body(query, key, value, starts, attended, lse):
    attention_fwd_pair(pl.program_id(0), query, key, value, starts, attended, lse)


def visible(lo, hi, starts):
    rows = iota((hi, hi - lo), 0)
    return (rows <= lo + iota((hi, hi - lo), 1)) & (rows >= starts[:, lo:hi])


def attention_fwd_pair(pair, query, key, value, starts, attended, lse):
    size = ROW_BLOCK
    zero = jnp.zeros((), BF16)
    for blk in range(query.shape[0] // size):
        lo, hi = blk * size, (blk + 1) * size
        q_blk = query[lo:hi, :]
        k_all = key[:hi, :]
        v_all = value[:hi, :]
        allowed = visible(lo, hi, starts)
        total = jnp.zeros((size, LANES), F32)
        for head in range(2):
            mine = head_mask((size, LANES), head)
            scores = dot_nt(k_all, jnp.where(mine, q_blk, zero))
            scores = jnp.where(allowed, scores, -1000000000.0)
            top = jnp.max(scores, axis=0, keepdims=True)
            expo = jnp.exp(scores - top)
            norm = jnp.sum(expo, axis=0, keepdims=True)
            prob = (expo * (1.0 / norm)).astype(BF16)
            total = jnp.where(mine, dot_tn(prob, v_all), total)
            lse[pl.ds(2 * pair + head, 1), lo:hi] = top + jnp.log(norm)
        attended[lo:hi, :] = total.astype(BF16)


def attention_bwd_body(
    query, key, value, dout, attended, lse, starts, cosine, sine, d_query, d_key, d_value, kacc, vacc
):
    pair = pl.program_id(0)
    tok = query.shape[0]
    size = ROW_BLOCK
    zero = jnp.zeros((), BF16)
    kacc[...] = jnp.zeros_like(kacc)
    vacc[...] = jnp.zeros_like(vacc)
    for blk in range(tok // size):
        lo, hi = blk * size, (blk + 1) * size
        q_blk = query[lo:hi, :]
        do_blk = dout[lo:hi, :]
        k_all = key[:hi, :]
        v_all = value[:hi, :]
        allowed = visible(lo, hi, starts)
        prod = (do_blk.astype(F32) * attended[lo:hi, :].astype(F32)).T
        probs, dscores, q_heads, do_heads = [], [], [], []
        q_total = jnp.zeros((size, LANES), F32)
        for head in range(2):
            mine = head_mask((size, LANES), head)
            q_heads.append(jnp.where(mine, q_blk, zero))
            do_heads.append(jnp.where(mine, do_blk, zero))
            lse_head = lse[pl.ds(2 * pair + head, 1), lo:hi]
            delta = jnp.sum(
                prod[head * HEAD_DIM : (head + 1) * HEAD_DIM], axis=0, keepdims=True
            )
            scores = dot_nt(k_all, q_heads[head])
            prob = jnp.where(allowed, jnp.exp(scores - lse_head), 0.0)
            dprob = dot_nt(v_all, do_heads[head])
            dscores.append((prob * (dprob - delta)).astype(BF16))
            probs.append(prob.astype(BF16))
            k_head = jnp.where(head_mask((hi, LANES), head), k_all, zero)
            q_total = q_total + dot_tn(dscores[head], k_head)
        kacc[:hi, :] += dot(jnp.concatenate(dscores, axis=1), jnp.concatenate(q_heads, axis=0))
        vacc[:hi, :] += dot(jnp.concatenate(probs, axis=1), jnp.concatenate(do_heads, axis=0))
        q_total = q_total * HEAD_DIM**-0.5
        d_query[lo:hi, :] = (
            q_total * cosine[lo:hi, :] - half_swap(q_total) * sine[lo:hi, :]
        ).astype(BF16)
    for blk in range(tok // size):
        lo, hi = blk * size, (blk + 1) * size
        k_total = kacc[lo:hi, :]
        d_key[lo:hi, :] = (
            k_total * cosine[lo:hi, :] - half_swap(k_total) * sine[lo:hi, :]
        ).astype(BF16)
    d_value[...] = vacc[...].astype(BF16)


def start_kernel(send_to, hear_from, count):
    barrier = pltpu.get_barrier_semaphore()
    for device, remote in hear_from:
        if remote is None:
            pl.semaphore_signal(barrier, inc=1, device_id=device, device_id_type=MESH_ID)
        else:

            @pl.when(remote)
            def _(device=device):
                pl.semaphore_signal(barrier, inc=1, device_id=device, device_id_type=MESH_ID)

    pl.semaphore_wait(barrier, count)


def pair_front_body(
    kinds, a_rows, b_rows,
    lengths, adapters, place_row, hidden, upstream, carry, choices, gain_one, gain_two,
    router_in, const_in, in_qkv, in_out, in_a_qkv, in_a_out, in_b_qkv, in_b_out,
    in_gu, in_b_gu, in_dn, in_b_dn, in_a_gu, in_a_dn, *rest,
):
    count = FRONT_KEPT
    outs, rest = rest[:count], rest[count:]
    (all_wide, all_mid, all_thin, came, last_sent), rest = rest[:5], rest[5:]
    kept, rest = rest[:count], rest[count:]
    (
        hid_s, dy_s, small_s, act_one, low_qkv, mask, starts, cosine, sine, router,
        query, key, value, w_qkv, a_qkv, b_qkv, w_out, a_out, b_out,
        attn_low, lse, low_out, resid, act_two, gate, slot,
    ) = kept
    (
        g_qkv, g_out, own_wide, own_mid, own_thin, sent, slot_rows,
        a_send, a_recv, z_send, e_send, e_recv, out_sems, own_sems, row_send, row_recv,
    ) = rest
    dp, z = lax.axis_index("dp"), lax.axis_index("expert")
    core, x_bit, y_bit = dp % 2, dp // 2 % 2, dp // 4
    across = dp + 1 - 2 * core
    x_dev, y_dev = dp + 2 - 4 * x_bit, dp + 4 - 8 * y_bit
    diag = x_dev + 4 - 8 * y_bit
    far = (z + 2) % 4
    home = z // 2
    columns = (dp, x_dev, y_dev, diag)
    tok = hidden.shape[0]
    blocks = tok // ROW_BLOCK

    def remote(source, target, send, recv, device):
        return pltpu.make_async_remote_copy(
            src_ref=source, dst_ref=target, send_sem=send, recv_sem=recv,
            device_id=device, device_id_type=MESH_ID,
        )

    packs = (g_qkv, g_out)

    def at(kind, back):
        return columns[kind] * 4 + (z + 4 - back) % 4

    def shard(p, kind, back, rows=None):
        view = packs[p].at[at(kind, back)]
        if rows is None:
            return view
        half = packs[p].shape[1] // 2
        return view.at[pl.ds(rows * half, half)]

    def z_up(p, t):
        view = shard(p, 0, t)
        return remote(view, view, z_send.at[p, t], a_recv.at[p, t], (dp, z + 1))

    def z_down(p, t):
        view = shard(p, 0, (4 - t) % 4)
        return remote(view, view, z_send.at[p, 3 + t], a_recv.at[p, 2 - t], (dp, z - 1))

    def z_sends(p, t, act):
        @pl.when((z < 3) & (z >= t))
        def _():
            act(z_up(p, t))

        @pl.when((z > 0) & (z + t <= 3))
        def _():
            act(z_down(p, t))

    def to_x(p, back):
        return remote(
            shard(p, 0, back), shard(p, 0, back), a_send.at[p, 3 + back], a_recv.at[p, 3 + back],
            (x_dev, z),
        )

    def to_y(p, back):
        return remote(
            shard(p, 0, back), shard(p, 0, back), a_send.at[p, 7 + back], a_recv.at[p, 7 + back],
            (y_dev, z),
        )

    def relay_y(p, back):
        return remote(
            shard(p, 1, back, 0), shard(p, 1, back, 0), a_send.at[p, 11 + back],
            a_recv.at[p, 11 + back], (y_dev, z),
        )

    def relay_x(p, back):
        return remote(
            shard(p, 2, back, 1), shard(p, 2, back, 1), a_send.at[p, 15 + back],
            a_recv.at[p, 15 + back], (x_dev, z),
        )

    def to_core(p, kind, back):
        sem = 19 + 4 * kind + back
        return remote(
            shard(p, kind, back), shard(p, kind, back), a_send.at[p, sem], a_recv.at[p, sem],
            (across, z),
        )

    half_wide = own_wide.shape[1] // 2
    parts = []
    for own, everything, cols in (
        (own_mid, all_mid, None), (own_thin, all_thin, None),
        (own_wide, all_wide, (0, half_wide)), (own_wide, all_wide, (half_wide, half_wide)),
    ):
        if cols is None:
            parts.append((own, lambda d, ref=everything: ref.at[d]))
        else:
            parts.append(
                (own.at[:, pl.ds(*cols)], lambda d, ref=everything, c=cols: ref.at[d, :, pl.ds(*c)])
            )
    chunks = ((0, 1), (2,), (3,))

    def first_far(a):
        return remote(
            parts[a][0], parts[a][1](dp), e_send.at[a, 0], e_recv.at[a, core],
            (dp - core + home, far),
        )

    def first_across(a):
        return remote(
            parts[a][0], parts[a][1](dp), e_send.at[a, 1], e_recv.at[a, core], (across, z)
        )

    def first_keep(a):
        return pltpu.make_async_copy(parts[a][0], parts[a][1](dp), e_recv.at[a, core])

    def first_arrival(a, i):
        view = parts[a][1](dp - core + i)
        return remote(view, view, e_send.at[a, 0], e_recv.at[a, i], (dp, far))

    def expert_hop(a, column, i, sem, device):
        view = parts[a][1](column - core + i)
        return remote(view, view, e_send.at[a, sem], e_recv.at[a, sem], (device, z))

    def expert_x(a, i):
        return expert_hop(a, dp, i, 2 + i, x_dev)

    def expert_y(a, i):
        return expert_hop(a, dp, i, 4 + i, y_dev)

    def expert_relay_y(a):
        return expert_hop(a, x_dev, 0, 6, y_dev)

    def expert_relay_x(a):
        return expert_hop(a, y_dev, 1, 7, x_dev)

    def expert_first(c):
        for a in chunks[c]:
            first_far(a).start()

            @pl.when(core == home)
            def _(a=a):
                first_keep(a).start()

            @pl.when(core != home)
            def _(a=a):
                first_across(a).start()

    def at_home(step, *args):
        @pl.when(core == home)
        def _():
            step(*args)

    def abroad(step, *args):
        @pl.when(core != home)
        def _():
            step(*args)

    def send_sides(a):
        for i in range(2):
            expert_x(a, i).start()
            expert_y(a, i).start()

    def spread_home(c):
        for a in chunks[c]:
            first_keep(a).wait()
            first_arrival(a, 1 - core).wait_recv()
            send_sides(a)

    def spread_far(c):
        for a in chunks[c]:
            for i in range(2):
                first_arrival(a, i).wait_recv()
            send_sides(a)

    def expert_relay(c):
        for a in chunks[c]:
            for i in range(2):
                expert_hop(a, x_dev, i, 2 + i, x_dev).wait_recv()
            expert_relay_y(a).start()
            for i in range(2):
                expert_hop(a, y_dev, i, 4 + i, y_dev).wait_recv()
            expert_relay_x(a).start()

    def expert_finish(c):
        for a in chunks[c]:
            expert_hop(a, diag, 0, 6, y_dev).wait_recv()
            expert_hop(a, diag, 1, 7, x_dev).wait_recv()
            first_far(a).wait_send()

            @pl.when(core != home)
            def _(a=a):
                first_across(a).wait_send()

            for i in range(2):
                expert_x(a, i).wait_send()
                expert_y(a, i).wait_send()
            expert_relay_y(a).wait_send()
            expert_relay_x(a).wait_send()

    gu_rows, up_rows, dn_rows = in_gu.shape[1], in_b_gu.shape[1], in_dn.shape[1]
    own_loads = [
        pltpu.make_async_copy(source.at[0], target.at[pl.ds(at_row, rows)], own_sems.at[i])
        for i, (source, target, at_row, rows) in enumerate((
            (in_gu, own_wide, 0, gu_rows), (in_b_gu, own_wide, gu_rows, up_rows),
            (in_dn, own_mid, 0, dn_rows), (in_b_dn, own_mid, dn_rows, up_rows),
            (in_a_gu, own_thin, 0, gu_rows), (in_a_dn, own_thin, gu_rows, dn_rows),
        ))
    ]
    for load in own_loads:
        load.start()
    for gathered, weight, adapter_in, adapter_out in (
        (g_qkv, in_qkv, in_a_qkv, in_b_qkv), (g_out, in_out, in_a_out, in_b_out),
    ):
        spare = gathered.shape[1] - a_rows - b_rows
        wide_cols = weight.shape[1]
        gathered[at(0, 0), :, :wide_cols] = jnp.concatenate(
            [weight[...].astype(F32), adapter_out[...].astype(F32), jnp.zeros((spare, wide_cols), F32)],
            axis=0,
        ).astype(BF16)
        gathered[at(0, 0), :, wide_cols:] = jnp.concatenate(
            [adapter_in[...].astype(F32), jnp.zeros((spare + b_rows, LANES), F32)], axis=0
        ).astype(BF16)
    next_z = z + 1 - 2 * (z % 2)
    peers = [(x_dev, z), (y_dev, z), (across, z), (across, far), (across, next_z)]
    peers += [(dp, (z + j) % 4) for j in (1, 2, 3)]
    start_kernel(None, [(device, None) for device in peers], len(peers))
    def send_own(p):
        z_sends(p, 0, lambda copy: copy.start())
        to_x(p, 0).start()
        to_y(p, 0).start()
        to_core(p, 0, 0).start()

    send_own(0)
    router[...] = jnp.concatenate(
        [router_in[...].astype(F32), jnp.zeros((CONST_LANE - kinds, MODEL_WIDTH), F32),
         const_in[...].astype(F32), jnp.zeros((LANES - CONST_LANE - 4, MODEL_WIDTH), F32)],
        axis=0,
    ).astype(BF16)
    small_s[...] = jnp.zeros_like(small_s)
    carry_parts = split_three(carry[...])
    choices_low = choices[...].astype(F32).astype(BF16)
    half_dim = HEAD_DIM // 2
    freq = jnp.exp(
        (iota((1, LANES), 1) % half_dim).astype(F32) * (-math.log(10000.0) / half_dim)
    )
    sign = jnp.where(iota((1, LANES), 1) % HEAD_DIM < half_dim, -1.0, 1.0)

    def block_rows(b):
        return pl.ds(pl.multiple_of(b * ROW_BLOCK, ROW_BLOCK), ROW_BLOCK)

    def arrange(b, carry_on):
        rows = block_rows(b)
        perm = hot_matrix(place_row[...] == b * ROW_BLOCK + iota((ROW_BLOCK, tok), 0))
        hid = dot(perm, hidden[...])
        hid_s[rows, :] = hid.astype(BF16)
        act_one[rows, :] = normed(hid, gain_one)
        return carry_on

    def arrange_rest(b, carry_on):
        rows = block_rows(b)
        perm = hot_matrix(place_row[...] == b * ROW_BLOCK + iota((ROW_BLOCK, tok), 0))
        dy_s[rows, :] = dot(perm, upstream[...]).astype(BF16)
        top, mid, last = carry_parts
        small_s[rows, :kinds] = dot_nt(perm, top) + (dot_nt(perm, mid) + dot_nt(perm, last))
        small_s[rows, CHOICE_LANE : CHOICE_LANE + 2] = dot_nt(perm, choices_low)
        return carry_on

    place = iota((1, tok), 1)
    begin_row = jnp.zeros((1, tok), jnp.int32)
    begin = 0
    for n in range(1, lengths.shape[1]):
        begin = begin + lengths[0, n - 1]
        begin_row = jnp.where(place >= begin, begin, begin_row)
    starts[...] = begin_row

    def positions(b, carry_on):
        rows = block_rows(b)
        stream = b * ROW_BLOCK + iota((ROW_BLOCK, 1), 0)
        start = jnp.zeros((ROW_BLOCK, 1), jnp.int32)
        adapter = start + adapters[0, 0]
        begin = 0
        for n in range(1, lengths.shape[1]):
            begin = begin + lengths[0, n - 1]
            start = jnp.where(stream >= begin, begin, start)
            adapter = jnp.where(stream >= begin, adapters[0, n], adapter)
        mask[rows, :] = hot_matrix(iota((ROW_BLOCK, LANES), 1) // ADAPTER_RANK == adapter)
        angle = (stream - start).astype(F32) * freq
        cosine[rows, :] = jnp.cos(angle)
        sine[rows, :] = jnp.sin(angle) * sign
        return carry_on

    lax.fori_loop(0, blocks, arrange, 0)

    at_end = (z == 0) | (z == 3)
    order = (
        jnp.where(z == 0, 3, 1), jnp.where(at_end, 2, 3),
        jnp.where(z == 0, 1, jnp.where(z == 3, 3, 2)),
    )

    def spread_shard(p, back):
        view = shard(p, 0, back)
        remote(view, view, z_send.at[p, 0], a_recv.at[p, back - 1], (dp, z)).wait_recv()
        to_x(p, back).start()
        to_y(p, back).start()
        to_core(p, 0, back).start()

    def from_z(p, t):
        @pl.when(z > t)
        def _():
            spread_shard(p, 1 + t)

        @pl.when(z + t < 3)
        def _():
            spread_shard(p, 3 - t)

        if t < 2:
            z_sends(p, t + 1, lambda copy: copy.start())

    def from_sides(p, back):
        view = shard(p, 1, back)
        remote(view, view, a_send.at[p, 3 + back], a_recv.at[p, 3 + back], (x_dev, z)).wait_recv()
        relay_y(p, back).start()
        to_core(p, 1, back).start()
        view = shard(p, 2, back)
        remote(view, view, a_send.at[p, 7 + back], a_recv.at[p, 7 + back], (y_dev, z)).wait_recv()
        relay_x(p, back).start()
        to_core(p, 2, back).start()

    def from_diag(p, back):
        view = shard(p, 3, back, 0)
        remote(view, view, a_send.at[p, 11 + back], a_recv.at[p, 11 + back], (y_dev, z)).wait_recv()
        view = shard(p, 3, back, 1)
        remote(view, view, a_send.at[p, 15 + back], a_recv.at[p, 15 + back], (x_dev, z)).wait_recv()
        to_core(p, 3, back).start()

    for t in range(3):
        from_z(0, t)
    send_own(1)
    from_sides(0, 0)
    lax.fori_loop(0, 2, arrange_rest, 0)
    from_sides(0, order[0])
    lax.fori_loop(2, 4, arrange_rest, 0)
    from_sides(0, order[1])
    lax.fori_loop(4, blocks, arrange_rest, 0)
    from_sides(0, order[2])
    for t in range(3):
        from_z(1, t)
    for load in own_loads:
        load.wait()
    for c in range(len(chunks)):
        expert_first(c)
    for back in (0,) + order[:2]:
        from_diag(0, back)
    lax.fori_loop(0, blocks, positions, 0)
    from_diag(0, order[2])
    core_columns = (across, x_dev + across - dp, y_dev + across - dp, diag + across - dp)

    def from_core(p):
        def body(back, carry):
            for kind in range(4):
                view = packs[p].at[core_columns[kind] * 4 + (z + 4 - back) % 4]
                sem = 19 + 4 * kind + back
                remote(view, view, a_send.at[p, sem], a_recv.at[p, sem], (across, z)).wait_recv()
            return carry

        lax.fori_loop(0, 4, body, 0)

    width = MODEL_WIDTH
    total = g_qkv.shape[0]

    def lay_rows(i, carry, gathered, targets):
        pair = [gathered[2 * i + n, :a_rows, :].astype(F32) for n in range(2)]
        both = jnp.concatenate(pair, axis=0).astype(BF16)
        rows = pl.ds(pl.multiple_of(i * 2 * a_rows, 16), 2 * a_rows)
        start = 0
        for target in targets:
            target[rows, :] = both[:, start : start + target.shape[1]]
            start += target.shape[1]
        return carry

    def lay_ups(i, carry, gathered, target):
        group = 16 // b_rows
        pieces = [
            gathered[group * i + n, a_rows : a_rows + b_rows, : target.shape[1]].astype(F32)
            for n in range(group)
        ]
        rows = pl.ds(pl.multiple_of(i * 16, 16), 16)
        target[rows, :] = jnp.concatenate(pieces, axis=0).astype(BF16)
        return carry

    def lay(gathered, targets, ups):
        lax.fori_loop(
            0, total // 2, functools.partial(lay_rows, gathered=gathered, targets=targets), 0
        )
        lax.fori_loop(
            0, total * b_rows // 16, functools.partial(lay_ups, gathered=gathered, target=ups), 0
        )

    def flush(first, last):
        return [
            pltpu.make_async_copy(kept[i], outs[i], out_sems.at[i]) for i in range(first, last)
        ]

    for back in (0,) + order:
        from_sides(1, back)
    for c in range(len(chunks)):
        at_home(spread_home, c)
    from_core(0)
    lay(g_qkv, (w_qkv, a_qkv), b_qkv)

    def projection(b, carry):
        rows = block_rows(b)
        low_qkv[rows, :], query[rows, :], key[rows, :], value[rows, :] = project(
            act_one[rows, :], mask[rows, :], cosine[rows, :], sine[rows, :], w_qkv, a_qkv, b_qkv
        )

        return carry

    lax.fori_loop(0, blocks, projection, 0)
    abroad(spread_far, 0)
    for copy in flush(0, 16):
        copy.start()
    lse[...] = jnp.zeros_like(lse)

    def attention(pair, carry):
        cols = pl.ds(pl.multiple_of(pair * LANES, LANES), LANES)
        attention_fwd_pair(
            pair, query.at[:, cols], key.at[:, cols], value.at[:, cols], starts,
            attn_low.at[:, cols], lse,
        )

        @pl.when(pair == 0)
        def _():
            for back in (0,) + order:
                from_diag(1, back)
            at_home(expert_relay, 0)

        @pl.when(pair == 2)
        def _():
            at_home(expert_relay, 1)

        @pl.when(pair == 3)
        def _():
            abroad(spread_far, 1)
            abroad(expert_relay, 0)

        @pl.when(pair == 4)
        def _():
            at_home(expert_relay, 2)

        return carry

    lax.fori_loop(0, HEAD_COUNT // 2, attention, 0)
    from_core(1)
    lay(g_out, (w_out, a_out), b_out)
    for copy in flush(16, 21):
        copy.start()

    def after(b, carry):
        rows = block_rows(b)
        low_out[rows, :], resid[rows, :], act_two[rows, :], gate[rows, :] = post_attn(
            kinds, attn_low[rows, :], hid_s[rows, :], mask[rows, :], small_s[rows, :],
            w_out, a_out, b_out, router, gain_two,
        )
        return carry

    lax.fori_loop(0, blocks, after, 0)
    abroad(spread_far, 2)
    abroad(expert_relay, 1)
    place_slots(4, small_s, slot, slot_rows)
    for copy in flush(21, FRONT_KEPT):
        copy.start()

    def rows_out(k):
        device = ((dp, next_z), (across, z))[k - 1]
        return remote(sent.at[k], came.at[k], row_send.at[k], row_recv.at[k], device)

    last_local = pltpu.make_async_copy(sent.at[0], last_sent, row_send.at[3])
    own_local = pltpu.make_async_copy(sent.at[0], came.at[0], row_send.at[0])
    def fill(n, carry):
        k = (n + 1) % 4
        eid = (z + k) % 2 + 2 * ((core + k // 2) % 2)
        fill_slots(eid, gate, act_two, dy_s, mask, slot_rows, sent.at[k % 3])

        @pl.when(n == 0)
        def _():
            rows_out(1).start()

        @pl.when(n == 1)
        def _():
            rows_out(2).start()

        @pl.when(n == 2)
        def _():
            last_local.start()
            last_local.wait()

        return carry

    lax.fori_loop(0, 4, fill, 0)
    own_local.start()
    abroad(expert_relay, 2)
    for c in range(len(chunks)):
        expert_finish(c)
    for k in (1, 2):
        rows_out(k).wait_recv()
        rows_out(k).wait_send()
    own_local.wait()

    def attn_sent(n, carry):
        for p in range(2):
            to_x(p, n).wait_send()
            to_y(p, n).wait_send()
            relay_x(p, n).wait_send()
            relay_y(p, n).wait_send()
            for kind in range(4):
                to_core(p, kind, n).wait_send()
        return carry

    lax.fori_loop(0, 4, attn_sent, 0)
    for p in range(2):
        for t in range(3):
            z_sends(p, t, lambda copy: copy.wait_send())
    for copy in flush(0, FRONT_KEPT):
        copy.wait()


def pair_attention_bwd_body(
    query, key, value, dout, attended, lse, starts, cosine, sine, ga_gu, gb_gu, ga_dn, gb_dn,
    d_query, d_key, d_value, own_ga_gu, own_gb_gu, own_ga_dn, own_gb_dn,
    kacc, vacc, r_ga_gu, r_gb_gu, r_ga_dn, r_gb_dn, send_sems, recv_sems,
):
    dp, z = lax.axis_index("dp"), lax.axis_index("expert")
    core, spot, half = dp % 2, dp // 2, z // 2
    own = z % 2 + 2 * core
    far = (z + 2) % 4
    at_home = core == half
    away = 1 - (core * half + (1 - core) * (1 - half))
    slot = 2 * spot + away
    groups = (
        (ga_gu, r_ga_gu, own_ga_gu), (gb_gu, r_gb_gu, own_gb_gu),
        (ga_dn, r_ga_dn, own_ga_dn), (gb_dn, r_gb_dn, own_gb_dn),
    )
    owners = 8

    def piece(i, d):
        source, target, _ = groups[i]
        count = target.shape[1]
        return source.at[pl.ds(pl.multiple_of(d * count, 16), count)]

    def push(i, d):
        return pltpu.make_async_remote_copy(
            src_ref=piece(i, d), dst_ref=groups[i][1].at[slot], send_sem=send_sems.at[i, d],
            recv_sem=recv_sems.at[i, slot], device_id=(d, own), device_id_type=MESH_ID,
        )

    def keep(i):
        return pltpu.make_async_copy(
            piece(i, dp), groups[i][1].at[2 * spot], recv_sems.at[i, 2 * spot]
        )

    def arrival(i, s):
        return pltpu.make_async_remote_copy(
            src_ref=piece(i, 0), dst_ref=groups[i][1].at[s], send_sem=send_sems.at[i, 0],
            recv_sem=recv_sems.at[i, s], device_id=(0, own), device_id_type=MESH_ID,
        )

    @pl.when(pl.program_id(0) == 0)
    def _():
        senders = []
        for m in range(owners // 2):
            device = 2 * m + half
            senders.append(((device, z), device != dp))
            senders.append(((device, far), None))
        start_kernel(None, senders, owners - 1 + away)

        def send(d, carry):
            mine = at_home & (d == dp)

            @pl.when(mine)
            def _():
                for i in range(4):
                    keep(i).start()

            @pl.when(jnp.logical_not(mine))
            def _():
                for i in range(4):
                    push(i, d).start()

            return carry

        lax.fori_loop(0, owners, send, 0)

    attention_bwd_body(
        query, key, value, dout, attended, lse, starts, cosine, sine, d_query, d_key, d_value,
        kacc, vacc,
    )

    @pl.when(pl.program_id(0) == pl.num_programs(0) - 1)
    def _():
        def finish(s, carry):
            mine = at_home & (s == 2 * spot)

            @pl.when(mine)
            def _():
                for i in range(4):
                    keep(i).wait()

            @pl.when(jnp.logical_not(mine))
            def _():
                for i in range(4):
                    arrival(i, s).wait_recv()

            @pl.when(jnp.logical_not(at_home & (s == dp)))
            def _():
                for i in range(4):
                    push(i, s).wait_send()

            return carry

        lax.fori_loop(0, owners, finish, 0)
        for _, target, out in groups:
            total = target[0].astype(F32)
            for s in range(1, owners):
                total = total + target[s].astype(F32)
            out[...] = total


def pair_tail_body(
    place_col, d_query, d_key, d_value, low_qkv, act_one, mask, a_in, b_out, gain, ga_out, gb_out,
    d_logits, hid_hbm, resid_hbm, w_hbm, out_hbm,
    out, grad_hidden, grad_gate, own_ga_qkv, own_gb_qkv, own_ga_out, own_gb_out,
    hid_s, d_resid, w_qkv, out_s, high, lower, d_low_all, ga_sum, gb_sum,
    s_ga_qkv, s_gb_qkv, s_ga_out, s_gb_out, r_ga_qkv, r_gb_qkv, r_ga_out, r_gb_out,
    thin_out, wide_out, thin_in, wide_in, load_sems, send_sems, recv_sems, far_send, far_recv,
):
    dp, z = lax.axis_index("dp"), lax.axis_index("expert")
    others, planes = 7, 3
    tok = place_col.shape[0]
    blocks = tok // ROW_BLOCK
    loads = [
        pltpu.make_async_copy(source, target, load_sems.at[i])
        for i, (source, target) in enumerate(
            ((w_hbm, w_qkv), (hid_hbm, hid_s), (resid_hbm, d_resid), (out_hbm, out_s))
        )
    ]
    for load in loads:
        load.start()
    start_kernel(
        None,
        [(((dp + i) % 8, z), None) for i in range(1, 8)] + [((dp, (z + j) % 4), None) for j in (1, 2, 3)],
        others + planes,
    )
    ga_sum[...] = jnp.zeros_like(ga_sum)
    gb_sum[...] = jnp.zeros_like(gb_sum)
    parts = [slice(p * MODEL_WIDTH, (p + 1) * MODEL_WIDTH) for p in range(3)]
    d_refs = (d_query, d_key, d_value)

    def block_rows(b):
        return pl.ds(pl.multiple_of(b * ROW_BLOCK, ROW_BLOCK), ROW_BLOCK)

    def sums(b, carry):
        rows = block_rows(b)
        low = low_qkv[rows, :]
        d_low = jnp.zeros((ROW_BLOCK, LANES), F32)
        for cols, ref in zip(parts, d_refs):
            grad = ref[rows, :]
            d_low = d_low + dot_nt(grad, b_out[:, cols])
            gb_sum[:, cols] += dot_tn(low, grad)
        d_low = (d_low * mask[rows, :].astype(F32)).astype(BF16)
        d_low_all[rows, :] = d_low
        ga_sum[...] += dot_tn(act_one[rows, :], d_low)
        return carry

    lax.fori_loop(0, blocks, sums, 0)
    s_ga_qkv[...] = ga_sum[...].astype(BF16)
    s_gb_qkv[...] = gb_sum[...].astype(BF16)
    s_ga_out[...] = ga_out[...].astype(BF16)
    s_gb_out[...] = gb_out[...].astype(BF16)
    groups = (
        (s_ga_qkv, r_ga_qkv), (s_gb_qkv, r_gb_qkv), (s_ga_out, r_ga_out), (s_gb_out, r_gb_out),
    )

    def share(i, d):
        count = groups[i][1].shape[1]
        return groups[i][0].at[pl.ds(pl.multiple_of(d * count, 16), count)]

    def near(i, n):
        goal = (dp + n + 1) % 8
        return pltpu.make_async_remote_copy(
            src_ref=share(i, goal), dst_ref=groups[i][1].at[n], send_sem=send_sems.at[i, n],
            recv_sem=recv_sems.at[i, n], device_id=(goal, z), device_id_type=MESH_ID,
        )

    def send_near(n, carry):
        for i in range(4):
            near(i, n).start()
        return carry

    lax.fori_loop(0, others, send_near, 0)

    for load in loads[:3]:
        load.wait()

    def back(b, carry):
        rows = block_rows(b)
        d_act = dot_nt(d_low_all[rows, :], a_in[...])
        for cols, ref in zip(parts, d_refs):
            d_act = d_act + dot_nt(ref[rows, :], w_qkv[:, cols])
        hid = hid_s[rows, :].astype(F32)
        scale = lax.rsqrt(jnp.mean(hid * hid, axis=-1, keepdims=True) + EPSILON)
        weighted = d_act * gain[...].astype(F32)
        grad_hid = d_resid[rows, :] + (
            scale * weighted
            - hid * (scale * scale * scale) * jnp.mean(hid * weighted, axis=-1, keepdims=True)
        )
        top = grad_hid.astype(BF16)
        high[rows, :] = top
        lower[rows, :] = (grad_hid - top.astype(F32)).astype(BF16)
        return carry

    lax.fori_loop(0, blocks, back, 0)

    def near_done(n, carry):
        for i in range(4):
            near(i, n).wait_recv()
        return carry

    lax.fori_loop(0, others, near_done, 0)
    totals = []
    for i in range(4):
        total = share(i, dp)[...].astype(F32)
        for n in range(others):
            total = total + groups[i][1][n].astype(F32)
        totals.append(total)
    a_qkv, b_qkv, a_o, b_o = totals
    a_count, b_count = a_qkv.shape[0] // 4, b_qkv.shape[0] // 4
    for p in range(4):
        a_rows, b_rows = slice(p * a_count, (p + 1) * a_count), slice(p * b_count, (p + 1) * b_count)
        thin_out[p, :a_count, :LANES] = a_qkv[a_rows].astype(BF16)
        thin_out[p, :a_count, LANES:] = a_o[a_rows].astype(BF16)
        thin_out[p, a_count:, :] = jnp.zeros((thin_out.shape[1] - a_count, 2 * LANES), BF16)
        wide_out[p] = jnp.concatenate(
            [b_qkv[b_rows, cols] for cols in parts] + [b_o[b_rows]], axis=0
        ).astype(BF16)

    def far(i, j):
        goal = (z + j + 1) % 4
        source, target = ((thin_out, thin_in), (wide_out, wide_in))[i]
        return pltpu.make_async_remote_copy(
            src_ref=source.at[goal], dst_ref=target.at[j], send_sem=far_send.at[i, j],
            recv_sem=far_recv.at[i, j], device_id=(dp, goal), device_id_type=MESH_ID,
        )

    for j in range(planes):
        for i in range(2):
            far(i, j).start()
    loads[3].wait()

    top, mid, last = (jnp.where(iota((tok, LANES), 1) < 16, v.astype(F32), 0.0) for v in split_three(d_logits[...]))
    logit_parts = (top + pltpu.roll(mid, 16, 1) + pltpu.roll(last, 32, 1)).astype(BF16)

    def to_rows(b, carry):
        rows = block_rows(b)
        perm = hot_matrix(place_col[rows, :] == iota((ROW_BLOCK, tok), 1))
        out[rows, :] = dot(perm, out_s[...]).astype(BF16)
        grad_hidden[rows, :] = dot(perm, high[...]) + dot(perm, lower[...])
        moved = dot(perm, logit_parts)
        grad_gate[rows, :] = moved + (
            pltpu.roll(moved, LANES - 16, 1) + pltpu.roll(moved, LANES - 32, 1)
        )
        return carry

    lax.fori_loop(0, blocks, to_rows, 0)
    for j in range(planes):
        for i in range(2):
            far(i, j).wait_recv()
    thin = thin_out[z].astype(F32)
    wide = wide_out[z].astype(F32)
    for j in range(planes):
        thin = thin + thin_in[j].astype(F32)
        wide = wide + wide_in[j].astype(F32)
    own_ga_qkv[...] = thin[:a_count, :LANES]
    own_ga_out[...] = thin[:a_count, LANES:]
    for p, cols in enumerate(parts):
        own_gb_qkv[:, cols] = wide[p * b_count : (p + 1) * b_count]
    own_gb_out[...] = wide[3 * b_count : 4 * b_count]

    def sent(n, carry):
        for i in range(4):
            near(i, n).wait_send()
        return carry

    lax.fori_loop(0, others, sent, 0)
    for j in range(planes):
        for i in range(2):
            far(i, j).wait_send()


def split_three(values):
    top = values.astype(BF16)
    rest = values - top.astype(F32)
    mid = rest.astype(BF16)
    return top, mid, (rest - mid.astype(F32)).astype(BF16)


def post_attn_body(
    kinds, attn_low, hid_s, mask, small_s, w_out, a_out, b_out, router, gain,
    low_out, resid, act_two, gate,
):
    low_out[...], resid[...], act_two[...], gate[...] = post_attn(
        kinds, attn_low[...], hid_s[...], mask[...], small_s[...], w_out, a_out, b_out, router, gain
    )


def post_attn(kinds, attn, hid, mask, sm, w_out, a_out, b_out, router, gain):
    low = (dot(attn, a_out[...]) * mask.astype(F32)).astype(BF16)
    res = hid.astype(F32) + (dot(attn, w_out[...]) + dot(low, b_out[...]))
    act = normed(res, gain)
    logits = dot_nt(act, router[...])
    lane = iota(logits.shape, 1)
    routed = jnp.where(lane < kinds, logits + sm, -1e30)
    top = jnp.max(routed, axis=1, keepdims=True)
    expo = jnp.exp(routed - top)
    prob = expo / jnp.sum(expo, axis=1, keepdims=True)
    return low, res, act, jnp.where(lane < kinds, prob, logits)


def place_slots(experts, small_s, slot, slot_rows):
    tok = slot.shape[0]
    lane = iota((tok, LANES), 1)
    first = small_s[:, CHOICE_LANE : CHOICE_LANE + 1].astype(jnp.int32)
    second = small_s[:, CHOICE_LANE + 1 : CHOICE_LANE + 2].astype(jnp.int32)
    hot = ((first == lane) | (second == lane)) & (lane < experts)
    hot_low = hot_matrix(hot)
    for blk in range(tok // ROW_BLOCK):
        lo, hi = blk * ROW_BLOCK, (blk + 1) * ROW_BLOCK
        tri = hot_matrix(iota((ROW_BLOCK, hi), 1) < lo + iota((ROW_BLOCK, hi), 0))
        rank = dot(tri, hot_low[:hi, :])
        slot[lo:hi, :] = jnp.where(hot[lo:hi, :], rank, -1.0)
    slot_rows[...] = slot[...].T


def fill_slots(eid, gate, act_two, dy_s, mask, slot_rows, target):
    row = slot_rows[pl.ds(eid, 1), :].astype(jnp.int32)
    pick = hot_matrix(row == iota((target.shape[0], row.shape[1]), 0))
    value = lane_value(gate[...], eid)
    scaled = (dy_s[...].astype(F32) * value).astype(BF16)
    target[:, :MODEL_WIDTH] = dot(pick, act_two[...]).astype(BF16)
    target[:, MODEL_WIDTH : 2 * MODEL_WIDTH] = dot(pick, scaled).astype(BF16)
    target[:, 2 * MODEL_WIDTH :] = dot(pick, mask[...]).astype(BF16)


def dispatch_body(experts, eids, small_s, gate, act_two, dy_s, mask, slot, sent, slot_rows):
    step = pl.program_id(0)

    @pl.when(step == 0)
    def _():
        place_slots(experts, small_s, slot, slot_rows)

    fill_slots(eids[step], gate, act_two, dy_s, mask, slot_rows, sent.at[0])


def ffn_math(
    rows, d_out, mask, w_gu, w_dn, a_gu, b_gu, a_dn, b_dn,
    ga_gu, gb_gu, ga_dn, gb_dn, acc_out, acc_dx, acc_low, acc_dlow,
):
    low_gu = (dot(rows, a_gu[...]) * mask).astype(BF16)
    dlow_dn = (dot_nt(d_out, b_dn[...]) * mask).astype(BF16)
    for ref in (acc_out, acc_dx, acc_low, acc_dlow):
        ref[...] = jnp.zeros_like(ref)

    def step(j, carry):
        lo = pl.multiple_of(j * HIDDEN_BLOCK, HIDDEN_BLOCK)
        g_cols = pl.ds(lo, HIDDEN_BLOCK)
        u_cols = pl.ds(pl.multiple_of(FEEDFWD_WIDTH + lo, HIDDEN_BLOCK), HIDDEN_BLOCK)
        gate = dot(rows, w_gu[:, g_cols]) + dot(low_gu, b_gu[:, g_cols])
        up = dot(rows, w_gu[:, u_cols]) + dot(low_gu, b_gu[:, u_cols])
        sig = 1.0 / (1.0 + jnp.exp(-gate))
        silu = gate * sig
        middle = (silu * up).astype(BF16)
        acc_out[...] += dot(middle, w_dn[g_cols, :])
        acc_low[...] += dot(middle, a_dn[g_cols, :])
        d_mid = dot_nt(d_out, w_dn[g_cols, :]) + dot_nt(dlow_dn, a_dn[g_cols, :])
        d_mid = d_mid.astype(BF16).astype(F32)
        d_gate = (d_mid * up * (sig * (1.0 + gate * (1.0 - sig)))).astype(BF16)
        d_up = (d_mid * silu).astype(BF16)
        acc_dx[...] += dot_nt(d_gate, w_gu[:, g_cols]) + dot_nt(d_up, w_gu[:, u_cols])
        acc_dlow[...] += dot_nt(d_gate, b_gu[:, g_cols]) + dot_nt(d_up, b_gu[:, u_cols])
        gb_gu[:, g_cols] += dot_tn(low_gu, d_gate)
        gb_gu[:, u_cols] += dot_tn(low_gu, d_up)
        ga_dn[g_cols, :] += dot_tn(middle, dlow_dn)
        return carry

    lax.fori_loop(0, FEEDFWD_WIDTH // HIDDEN_BLOCK, step, 0)
    low_dn = (acc_low[...] * mask).astype(BF16)
    result = (acc_out[...] + dot(low_dn, b_dn[...])).astype(BF16)
    gb_dn[...] += dot_tn(low_dn, d_out)
    dlow_gu = (acc_dlow[...] * mask).astype(BF16)
    d_rows = (acc_dx[...] + dot_nt(dlow_gu, a_gu[...])).astype(BF16)
    ga_gu[...] += dot_tn(rows, dlow_gu)
    return result, d_rows


def ffn_body(
    came, w_gu, w_dn, a_gu, b_gu, a_dn, b_dn,
    back, ga_gu, gb_gu, ga_dn, gb_dn, acc_out, acc_dx, acc_low, acc_dlow,
):
    @pl.when(pl.program_id(0) == 0)
    def _():
        for ref in (ga_gu, gb_gu, ga_dn, gb_dn):
            ref[...] = jnp.zeros_like(ref)

    back[0, :, :MODEL_WIDTH], back[0, :, MODEL_WIDTH:] = ffn_math(
        came[0, :, :MODEL_WIDTH], came[0, :, MODEL_WIDTH : 2 * MODEL_WIDTH],
        came[0, :, 2 * MODEL_WIDTH :].astype(F32), w_gu, w_dn, a_gu, b_gu, a_dn, b_dn,
        ga_gu, gb_gu, ga_dn, gb_dn, acc_out, acc_dx, acc_low, acc_dlow,
    )


def pair_ffn_body(
    had, last_sent, wide, mid, thin,
    returned, out_ga_gu, out_gb_gu, out_ga_dn, out_gb_dn,
    came, back, ga_gu, gb_gu, ga_dn, gb_dn, w_gu, w_dn, a_gu, b_gu, a_dn, b_dn, acc_out, acc_dx, acc_low, acc_dlow,
    load_sems, came_sems, back_sems, done_sems, last_sems,
):
    dp, z = lax.axis_index("dp"), lax.axis_index("expert")
    core, plane = dp % 2, z % 2

    def peer(k):
        return (dp + (k // 2) * (1 - 2 * core), z + (k % 2) * (1 - 2 * plane))

    start_kernel(None, [(peer(k), None) for k in (1, 2, 3)], 3)

    half = last_sent.shape[0] // 2
    late = pl.ds(0, 2 * half)

    def had_in(k):
        return pltpu.make_async_copy(had.at[k], came.at[k], came_sems.at[k])

    last_out = pltpu.make_async_remote_copy(
        src_ref=last_sent.at[late], dst_ref=came.at[3, late], send_sem=last_sems.at[0],
        recv_sem=last_sems.at[1], device_id=peer(3), device_id_type=MESH_ID,
    )

    def result_out(k):
        return pltpu.make_async_remote_copy(
            src_ref=back.at[k], dst_ref=returned.at[k], send_sem=back_sems.at[k],
            recv_sem=done_sems.at[k], device_id=peer(k), device_id_type=MESH_ID,
        )

    last_out.start()
    for k in (1, 0, 2):
        had_in(k).start()

    gu_rows = w_gu.shape[0] // wide.shape[0]
    up_rows = b_gu.shape[0] // wide.shape[0]
    dn_rows = w_dn.shape[0] // wide.shape[0]
    plans = (
        (wide, 0, gu_rows, w_gu), (wide, gu_rows, up_rows, b_gu), (mid, 0, dn_rows, w_dn),
        (mid, dn_rows, up_rows, b_dn), (thin, 0, gu_rows, a_gu), (thin, gu_rows, dn_rows, a_dn),
    )

    def load(d, carry):
        for i, (source, at, count, target) in enumerate(plans):
            pltpu.make_async_copy(
                source.at[d, pl.ds(at, count)],
                target.at[pl.ds(pl.multiple_of(d * count, 16), count)],
                load_sems.at[i],
            ).start()
        return carry

    lax.fori_loop(0, wide.shape[0], load, 0)
    for ref in (ga_gu, gb_gu, ga_dn, gb_dn):
        ref[...] = jnp.zeros_like(ref)
    for i, (_, _, _, target) in enumerate(plans):
        pltpu.make_async_copy(target, target, load_sems.at[i]).wait()

    def source_step(s, carry):
        k = s + 1 - 2 * (s % 2)

        @pl.when(k != 3)
        def _():
            had_in(k).wait()

        @pl.when(k == 3)
        def _():
            last_out.wait_recv()

        back[k, :, :MODEL_WIDTH], back[k, :, MODEL_WIDTH:] = ffn_math(
            came[k, :, :MODEL_WIDTH], came[k, :, MODEL_WIDTH : 2 * MODEL_WIDTH],
            came[k, :, 2 * MODEL_WIDTH :].astype(F32), w_gu, w_dn, a_gu, b_gu, a_dn, b_dn,
            ga_gu, gb_gu, ga_dn, gb_dn, acc_out, acc_dx, acc_low, acc_dlow,
        )

        @pl.when(k != 0)
        def _():
            result_out(k).start()

        return carry

    lax.fori_loop(0, 4, source_step, 0)
    for out, total in (
        (out_ga_gu, ga_gu), (out_gb_gu, gb_gu), (out_ga_dn, ga_dn), (out_gb_dn, gb_dn),
    ):
        out[...] = total[...].astype(BF16)
    own_out = pltpu.make_async_copy(back.at[0], returned.at[0], done_sems.at[0])
    own_out.start()
    own_out.wait()
    last_out.wait_send()
    for k in (1, 2, 3):
        result_out(k).wait_send()
        result_out(k).wait_recv()


def combine_body(
    experts, kinds, eids, resid, act_two, dy_s, gate, slot, small_s, low_out, attn_low, mask, came,
    w_out, a_out, b_out, router, const_value, gain,
    out_s, d_resid, d_attended, d_logits, ga_out, gb_out,
):
    @pl.when(pl.program_id(0) == 0)
    def _():
        ga_out[...] = jnp.zeros_like(ga_out)
        gb_out[...] = jnp.zeros_like(gb_out)

    rows = resid.shape[0]
    cap = came.shape[1]
    res = resid[...]
    act = act_two[...].astype(F32)
    dy_low = dy_s[...]
    dy = dy_low.astype(F32)
    lane = iota((rows, LANES), 1)
    levels = gate[...].T
    top = iota((CHOICE_ROWS, rows), 0)
    prob = jnp.where(top < kinds, levels[:CHOICE_ROWS], 0.0)

    def row(values, index):
        return jnp.sum(jnp.where(top == index, values, 0.0), axis=0, keepdims=True)

    picked = small_s[...].T
    first = picked[CHOICE_LANE : CHOICE_LANE + 1]
    second = picked[CHOICE_LANE + 1 : CHOICE_LANE + 2]

    def chosen(kind):
        return jnp.where((first == kind) | (second == kind), 1.0, 0.0)

    has_copy, has_zero, has_one = chosen(experts + 1), chosen(experts + 2), chosen(experts + 3)
    g_copy = has_copy * row(prob, experts + 1)
    g_zero = has_zero * row(prob, experts + 2)
    g_one = has_one * row(prob, experts + 3)

    def pair(at):
        left, right = levels[at : at + 1], levels[at + 1 : at + 2]
        high = jnp.maximum(left, right)
        e_left, e_right = jnp.exp(left - high), jnp.exp(right - high)
        scale = 1.0 / (e_left + e_right)
        return e_left * scale, e_right * scale

    a00, a01 = pair(CONST_LANE)
    a10, a11 = pair(CONST_LANE + 2)
    coef = g_copy + g_zero * a00 + g_one * a10
    factors = [coef, g_zero * a01, g_one * a11]
    factors += [row(prob, eids[k]) for k in range(came.shape[0])]
    spot = iota((LANES, rows), 0)
    columns = jnp.zeros((LANES, rows), F32)
    for n, factor in enumerate(factors):
        columns = jnp.where(spot == n, factor, columns)
    columns = columns.T
    v_zero, v_one = const_value[0:1, :], const_value[1:2, :]
    out = res + columns[:, 0:1] * act + columns[:, 1:2] * v_zero + columns[:, 2:3] * v_one
    d_act = columns[:, 0:1] * dy
    met = jnp.where(lane == 0, jnp.sum(dy * act, axis=1, keepdims=True), 0.0)
    met = jnp.where(lane == 1, jnp.sum(dy * v_zero, axis=1, keepdims=True), met)
    met = jnp.where(lane == 2, jnp.sum(dy * v_one, axis=1, keepdims=True), met)
    for k in range(came.shape[0]):
        place = lane_value(slot[...], eids[k]).astype(jnp.int32)
        pick = hot_matrix(place == iota((rows, cap), 1))
        result = dot(pick, came[k, :, :MODEL_WIDTH])
        d_act = d_act + dot(pick, came[k, :, MODEL_WIDTH:])
        met = jnp.where(lane == 3 + k, jnp.sum(dy * result, axis=1, keepdims=True), met)
        out = out + columns[:, 3 + k : 4 + k] * result
    out_s[...] = out.astype(BF16)
    met = met.T
    along_act, along_zero, along_one = met[0:1], met[1:2], met[2:3]
    d_gate = jnp.zeros((CHOICE_ROWS, rows), F32)
    for k in range(came.shape[0]):
        d_gate = jnp.where(top == eids[k], met[3 + k : 4 + k], d_gate)
    d_gate = jnp.where(top == experts + 1, has_copy * along_act, d_gate)
    d_gate = jnp.where(top == experts + 2, has_zero * (a00 * along_act + a01 * along_zero), d_gate)
    d_gate = jnp.where(top == experts + 3, has_one * (a10 * along_act + a11 * along_one), d_gate)
    d_logit = prob * (d_gate - jnp.sum(prob * d_gate, axis=0, keepdims=True))
    tail = iota((8, rows), 0)
    d_pair = jnp.zeros((8, rows), F32)
    for n, (g_val, left, right, along) in enumerate(
        ((g_zero, a00, a01, along_zero), (g_one, a10, a11, along_one))
    ):
        da_left, da_right = g_val * along_act, g_val * along
        level = left * da_left + right * da_right
        d_pair = jnp.where(tail == 2 * n, left * (da_left - level), d_pair)
        d_pair = jnp.where(tail == 2 * n + 1, right * (da_right - level), d_pair)
    mix = jnp.concatenate(
        [d_logit, jnp.zeros((CONST_LANE - CHOICE_ROWS, rows), F32), d_pair,
         jnp.zeros((LANES - CONST_LANE - 8, rows), F32)],
        axis=0,
    ).T
    d_logits[...] = mix
    mix_hi = mix.astype(BF16)
    mix_lo = (mix - mix_hi.astype(F32)).astype(BF16)
    d_act = d_act + (dot(mix_hi, router[...]) + dot(mix_lo, router[...]))
    scale = lax.rsqrt(jnp.mean(res * res, axis=-1, keepdims=True) + EPSILON)
    weighted = d_act * gain[...].astype(F32)
    d_res = dy + (
        scale * weighted
        - res * (scale * scale * scale) * jnp.mean(res * weighted, axis=-1, keepdims=True)
    )
    d_resid[...] = d_res
    d_attn = d_res.astype(BF16)
    dlow = (dot_nt(d_attn, b_out[...]) * mask[...].astype(F32)).astype(BF16)
    gb_out[...] += dot_tn(low_out[...], d_attn)
    ga_out[...] += dot_tn(attn_low[...], dlow)
    d_attended[...] = (dot_nt(d_attn, w_out[...]) + dot_nt(dlow, a_out[...])).astype(BF16)


def input_grad_body(
    d_query, d_key, d_value, low_qkv, act_one, mask, hid_s, d_resid, w_qkv, a_in, b_out, gain,
    high, lower, ga_qkv, gb_qkv,
):
    @pl.when(pl.program_id(0) == 0)
    def _():
        ga_qkv[...] = jnp.zeros_like(ga_qkv)
        gb_qkv[...] = jnp.zeros_like(gb_qkv)

    d_low = jnp.zeros((d_query.shape[0], LANES), F32)
    d_act = jnp.zeros((d_query.shape[0], MODEL_WIDTH), F32)
    for part, ref in enumerate((d_query, d_key, d_value)):
        cols = slice(part * MODEL_WIDTH, (part + 1) * MODEL_WIDTH)
        grad = ref[...]
        d_low = d_low + dot_nt(grad, b_out[:, cols])
        d_act = d_act + dot_nt(grad, w_qkv[:, cols])
        gb_qkv[:, cols] += dot_tn(low_qkv[...], grad)
    d_low = (d_low * mask[...].astype(F32)).astype(BF16)
    ga_qkv[...] += dot_tn(act_one[...], d_low)
    d_act = d_act + dot_nt(d_low, a_in[...])
    hid = hid_s[...].astype(F32)
    scale = lax.rsqrt(jnp.mean(hid * hid, axis=-1, keepdims=True) + EPSILON)
    weighted = d_act * gain[...].astype(F32)
    grad_hid = d_resid[...] + (
        scale * weighted
        - hid * (scale * scale * scale) * jnp.mean(hid * weighted, axis=-1, keepdims=True)
    )
    top = grad_hid.astype(BF16)
    high[...] = top
    lower[...] = (grad_hid - top.astype(F32)).astype(BF16)


def to_rows_body(place_col, out_s, d_logits, high, lower, out, grad_hidden, grad_gate):
    rows = out.shape[0]
    tok = out_s.shape[0]
    perm = hot_matrix(place_col[...] == iota((rows, tok), 1))
    out[...] = dot(perm, out_s[...]).astype(BF16)
    grad_hidden[...] = dot(perm, high[...]) + dot(perm, lower[...])
    logits = d_logits[...]
    top = logits.astype(BF16)
    rest = logits - top.astype(F32)
    mid = rest.astype(BF16)
    last = (rest - mid.astype(F32)).astype(BF16)
    grad_gate[...] = dot(perm, top) + (dot(perm, mid) + dot(perm, last))


class PairPlan:
    paired = True

    def __init__(self, dp, ex):
        self.ex = ex

    def expert_ids(self):
        own = lax.axis_index("expert") % 2 + 2 * (lax.axis_index("dp") % 2)
        return own ^ jnp.arange(self.ex, dtype=jnp.int32)


class AxisPlan:
    paired = False

    def __init__(self, dp, ex):
        self.dp, self.ex = dp, ex

    def gather(self, shard):
        return lax.all_gather(shard, "dp", axis=0)

    def expert_ids(self):
        return jnp.arange(self.ex, dtype=jnp.int32)

    def exchange(self, values):
        return lax.all_to_all(values, "expert", split_axis=0, concat_axis=0, tiled=True)

    def reduce(self, sums):
        return lax.psum_scatter(sums, "dp", scatter_dimension=0, tiled=True)[0].astype(F32)

    def reduce_all(self, sums):
        return lax.psum_scatter(
            sums, ("dp", "expert"), scatter_dimension=0, tiled=True
        )[0].astype(F32)


def shards(
    dp_size,
    expert_count,
    hidden_input,
    gate_carryover,
    sequence_length,
    token_stream_place,
    expert_choice_index,
    sequence_adapter,
    attention_gain,
    query_key_weight,
    output_weight,
    adapter_in_query,
    adapter_out_query,
    adapter_in_output,
    adapter_out_output,
    feedfwd_gain,
    router_weight,
    constant_gate,
    constant_value,
    gate_upward_weight,
    down_weight,
    adapter_in_gate,
    adapter_out_gate,
    adapter_in_down,
    adapter_out_down,
    output_gradient,
):
    tok = hidden_input.shape[0]
    width = MODEL_WIDTH
    kinds = expert_count + 4
    devices = dp_size * expert_count
    capacity = 5 * tok // (2 * kinds) // 8 * 8 + 8
    cap = -(-capacity // 16) * 16
    blocks = tok // ROW_BLOCK
    plan = (PairPlan if (dp_size, expert_count) == (8, 4) else AxisPlan)(dp_size, expert_count)

    a_rows, b_rows = query_key_weight.shape[0], adapter_out_query.shape[0]
    gu_rows, up_rows, dn_rows = (
        gate_upward_weight.shape[1], adapter_out_gate.shape[1], down_weight.shape[1],
    )
    gain_one, gain_two = attention_gain[None, :], feedfwd_gain[None, :]
    const_value = constant_value.astype(F32)
    sent_width = 2 * width + LANES
    full = whole
    hbm = pl.BlockSpec(memory_space=pl.ANY)
    vmem = pl.BlockSpec(memory_space=pltpu.VMEM)
    pairs = HEAD_COUNT // 2
    lse_rows = -(-HEAD_COUNT // 8) * 8
    smem = pl.BlockSpec(memory_space=pltpu.SMEM)
    eids = plan.expert_ids()
    if plan.paired:
        shapes = [
            sds((tok, width), BF16), sds((tok, width), BF16), sds((tok, LANES), F32),
            sds((tok, width), BF16), sds((tok, LANES), BF16), sds((tok, LANES), BF16),
            sds((1, tok), jnp.int32), sds((tok, LANES), F32), sds((tok, LANES), F32),
            sds((LANES, width), BF16),
            sds((tok, width), BF16), sds((tok, width), BF16), sds((tok, width), BF16),
            sds((width, 3 * width), BF16), sds((width, LANES), BF16), sds((LANES, 3 * width), BF16),
            sds((width, width), BF16), sds((width, LANES), BF16), sds((LANES, width), BF16),
            sds((tok, width), BF16), sds((lse_rows, tok), F32), sds((tok, LANES), BF16),
            sds((tok, width), F32), sds((tok, width), BF16), sds((tok, LANES), F32),
            sds((tok, LANES), F32),
        ]
        shard_rows = -(-(a_rows + b_rows) // 16) * 16
        packed = [
            (gu_rows + up_rows, 2 * FEEDFWD_WIDTH), (dn_rows + up_rows, width),
            (gu_rows + dn_rows, LANES),
        ]
        row_shape = (expert_count, cap, sent_width)
        (
            hid_s, dy_s, small_s, act_one, low_qkv, mask, starts, cosine, sine, router,
            query, key, value, w_qkv, a_qkv, b_qkv, w_out, a_out, b_out,
            attn_low, lse, low_out, resid, act_two, gate, slot,
            wide, mid, thin, came, last_sent,
        ) = pl.pallas_call(
            functools.partial(pair_front_body, kinds, a_rows, b_rows),
            in_specs=[smem] * 2 + [vmem] * 15 + [hbm] * 6,
            out_specs=[hbm] * (FRONT_KEPT + 5),
            out_shape=shapes
            + [sds((dp_size,) + shape, BF16) for shape in packed]
            + [sds(row_shape, BF16), sds(row_shape[1:], BF16)],
            scratch_shapes=[pltpu.VMEM(s.shape, s.dtype) for s in shapes]
            + [
                pltpu.VMEM((devices, shard_rows, 3 * width + LANES), BF16),
                pltpu.VMEM((devices, shard_rows, width + LANES), BF16),
                *[pltpu.VMEM(shape, BF16) for shape in packed],
                pltpu.VMEM((3,) + row_shape[1:], BF16),
                pltpu.VMEM((LANES, tok), F32),
                pltpu.SemaphoreType.DMA((2, 35)), pltpu.SemaphoreType.DMA((2, 35)),
                pltpu.SemaphoreType.DMA((2, 6)),
                pltpu.SemaphoreType.DMA((4, 8)), pltpu.SemaphoreType.DMA((4, 8)),
                pltpu.SemaphoreType.DMA((FRONT_KEPT,)), pltpu.SemaphoreType.DMA((6,)),
                pltpu.SemaphoreType.DMA((5,)), pltpu.SemaphoreType.DMA((4,)),
            ],
            compiler_params=pltpu.CompilerParams(
                vmem_limit_bytes=VMEM_BYTES, collective_id=4, has_side_effects=True
            ),
            name="pair_front",
        )(sequence_length, sequence_adapter, token_stream_place, hidden_input, output_gradient,
          gate_carryover.T, expert_choice_index.T, gain_one, gain_two, router_weight.T,
          constant_gate.T,
          query_key_weight, output_weight, adapter_in_query, adapter_in_output, adapter_out_query,
          adapter_out_output, gate_upward_weight, adapter_out_gate, down_weight, adapter_out_down,
          adapter_in_gate, adapter_in_down)
        place = token_stream_place[0]
    else:
        pad_rows = -(a_rows + b_rows) % 16

        def pack(weight, adapter_in, adapter_out):
            lower = jnp.pad(adapter_out, ((0, pad_rows), (0, LANES)))
            return jnp.concatenate([jnp.concatenate([weight, adapter_in], axis=1), lower], axis=0)

        own_qkv = pack(query_key_weight, adapter_in_query, adapter_out_query)
        own_out = pack(output_weight, adapter_in_output, adapter_out_output)
        own_wide = jnp.concatenate([gate_upward_weight[0], adapter_out_gate[0]], axis=0)
        own_mid = jnp.concatenate([down_weight[0], adapter_out_down[0]], axis=0)
        own_thin = jnp.concatenate([adapter_in_gate[0], adapter_in_down[0]], axis=0)

        place = token_stream_place[0]
        ends = jnp.cumsum(sequence_length[0])
        begins = ends - sequence_length[0]
        stream = jnp.arange(tok, dtype=jnp.int32)
        seg = jnp.sum((stream[:, None] >= ends[None, :]).astype(jnp.int32), axis=1)
        seg_hot = seg[:, None] == jnp.arange(ends.shape[0], dtype=jnp.int32)[None, :]
        start = jnp.sum(jnp.where(seg_hot, begins[None, :], 0), axis=1)
        adapter = jnp.sum(jnp.where(seg_hot, sequence_adapter[0][None, :], 0), axis=1)
        half = HEAD_DIM // 2
        freq = jnp.exp(jnp.arange(half, dtype=F32) * (-math.log(10000.0) / half))
        angle = (stream - start).astype(F32)[:, None] * freq[None, :]
        cos, sin = jnp.cos(angle), jnp.sin(angle)
        cosine = jnp.concatenate([cos, cos, cos, cos], axis=1)
        sine = jnp.concatenate([-sin, sin, -sin, sin], axis=1)
        starts = start[None, :]
        mask = (jnp.arange(LANES)[None, :] // ADAPTER_RANK == adapter[:, None]).astype(BF16)
        top, middle, last = split_three(gate_carryover)
        gap = jnp.zeros((tok, 16 - kinds), BF16)
        small = jnp.concatenate(
            [top, gap, middle, gap, last, gap, expert_choice_index.astype(BF16),
             jnp.zeros((tok, LANES - CHOICE_LANE - 2), BF16)],
            axis=1,
        )
        router = jnp.concatenate(
            [router_weight.T, jnp.zeros((CONST_LANE - kinds, width), BF16), constant_gate.T,
             jnp.zeros((LANES - CONST_LANE - 4, width), BF16)],
            axis=0,
        )

        all_qkv = lax.all_gather(own_qkv, ("dp", "expert"), axis=0)
        all_out = lax.all_gather(own_out, ("dp", "expert"), axis=0)
        upper = slice(a_rows, a_rows + b_rows)
        w_qkv = all_qkv[:, :a_rows, : 3 * width].reshape(width, 3 * width)
        a_qkv = all_qkv[:, :a_rows, 3 * width :].reshape(width, LANES)
        b_qkv = all_qkv[:, upper, : 3 * width].reshape(LANES, 3 * width)
        w_out = all_out[:, :a_rows, :width].reshape(width, width)
        a_out = all_out[:, :a_rows, width:].reshape(width, LANES)
        b_out = all_out[:, upper, :width].reshape(LANES, width)
        wide, mid, thin = (plan.gather(w) for w in (own_wide, own_mid, own_thin))
        hid_s, dy_s, small_s, act_one, low_qkv, query, key, value = call(
            proj_in_body,
            (blocks,),
            [full((1, tok)), full((tok, width)), full((tok, width)), full((tok, LANES)),
             row_spec(LANES), row_spec(LANES), row_spec(LANES), full((1, width)),
             full((width, 3 * width)), full((width, LANES)), full((LANES, 3 * width))],
            [row_spec(width), row_spec(width), row_spec(LANES), row_spec(width), row_spec(LANES),
             row_spec(width), row_spec(width), row_spec(width)],
            [sds((tok, width), BF16), sds((tok, width), BF16), sds((tok, LANES), F32),
             sds((tok, width), BF16), sds((tok, LANES), BF16), sds((tok, width), BF16),
             sds((tok, width), BF16), sds((tok, width), BF16)],
            name="proj_in",
        )(place[None, :], hidden_input, output_gradient, small, cosine, sine, mask, gain_one,
          w_qkv, a_qkv, b_qkv)

        attn_low, lse = call(
            attention_fwd_body,
            (pairs,),
            [col_spec(tok)] * 3 + [full((1, tok))],
            [col_spec(tok), full((lse_rows, tok))],
            [sds((tok, width), BF16), sds((lse_rows, tok), F32)],
            name="attention_fwd",
        )(query, key, value, starts)

        low_out, resid, act_two, gate = call(
            functools.partial(post_attn_body, kinds),
            (blocks,),
            [row_spec(width), row_spec(width), row_spec(LANES), row_spec(LANES), full((width, width)),
             full((width, LANES)), full((LANES, width)), full((LANES, width)), full((1, width))],
            [row_spec(LANES), row_spec(width), row_spec(width), row_spec(LANES)],
            [sds((tok, LANES), BF16), sds((tok, width), F32), sds((tok, width), BF16),
             sds((tok, LANES), F32)],
            name="post_attn",
        )(attn_low, hid_s, mask, small_s, w_out, a_out, b_out, router, gain_two)

        slot, sent = call(
            functools.partial(dispatch_body, expert_count),
            (expert_count,),
            [smem, full((tok, LANES)), full((tok, LANES)), full((tok, width)), full((tok, width)),
             full((tok, LANES))],
            [full((tok, LANES)), pl.BlockSpec((1, cap, sent_width), lambda i: (i, 0, 0))],
            [sds((tok, LANES), F32), sds((expert_count, cap, sent_width), BF16)],
            scratch=[pltpu.VMEM((LANES, tok), F32)],
            name="dispatch",
        )(eids, small_s, gate, act_two, dy_s, mask)

    grad_shapes = [
        sds((width, LANES), F32), sds((LANES, 2 * FEEDFWD_WIDTH), F32),
        sds((FEEDFWD_WIDTH, LANES), F32), sds((LANES, width), F32),
    ]
    accumulators = [
        pltpu.VMEM((cap, width), F32), pltpu.VMEM((cap, width), F32),
        pltpu.VMEM((cap, LANES), F32), pltpu.VMEM((cap, LANES), F32),
    ]
    if plan.paired:
        returned, ga_gu, gb_gu, ga_dn, gb_dn = pl.pallas_call(
            pair_ffn_body,
            in_specs=[hbm] * 5,
            out_specs=[hbm] + [vmem] * 4,
            out_shape=[sds((expert_count, cap, 2 * width), BF16)]
            + [sds(g.shape, BF16) for g in grad_shapes],
            scratch_shapes=[
                pltpu.VMEM((expert_count, cap, sent_width), BF16),
                pltpu.VMEM((expert_count, cap, 2 * width), BF16),
                *[pltpu.VMEM(g.shape, F32) for g in grad_shapes],
                pltpu.VMEM((width, 2 * FEEDFWD_WIDTH), BF16), pltpu.VMEM((FEEDFWD_WIDTH, width), BF16),
                pltpu.VMEM((width, LANES), BF16), pltpu.VMEM((LANES, 2 * FEEDFWD_WIDTH), BF16),
                pltpu.VMEM((FEEDFWD_WIDTH, LANES), BF16), pltpu.VMEM((LANES, width), BF16),
                *accumulators,
                pltpu.SemaphoreType.DMA((6,)),
                *[pltpu.SemaphoreType.DMA((expert_count,)) for _ in range(3)],
                pltpu.SemaphoreType.DMA((2,)),
            ],
            compiler_params=pltpu.CompilerParams(
                vmem_limit_bytes=VMEM_BYTES, collective_id=1, has_side_effects=True
            ),
            name="pair_ffn",
        )(came, last_sent, wide, mid, thin)
    else:
        w_gu = wide[:, :gu_rows].reshape(width, 2 * FEEDFWD_WIDTH)
        b_gu = wide[:, gu_rows:].reshape(LANES, 2 * FEEDFWD_WIDTH)
        w_dn = mid[:, :dn_rows].reshape(FEEDFWD_WIDTH, width)
        b_dn = mid[:, dn_rows:].reshape(LANES, width)
        a_gu = thin[:, :gu_rows].reshape(width, LANES)
        a_dn = thin[:, gu_rows:].reshape(FEEDFWD_WIDTH, LANES)
        came = plan.exchange(sent)
        back, ga_gu, gb_gu, ga_dn, gb_dn = call(
            ffn_body,
            (expert_count,),
            [pl.BlockSpec((1, cap, sent_width), lambda i: (i, 0, 0)),
             full((width, 2 * FEEDFWD_WIDTH)), full((FEEDFWD_WIDTH, width)), full((width, LANES)),
             full((LANES, 2 * FEEDFWD_WIDTH)), full((FEEDFWD_WIDTH, LANES)), full((LANES, width))],
            [pl.BlockSpec((1, cap, 2 * width), lambda i: (i, 0, 0)), full((width, LANES)),
             full((LANES, 2 * FEEDFWD_WIDTH)), full((FEEDFWD_WIDTH, LANES)), full((LANES, width))],
            [sds((expert_count, cap, 2 * width), BF16)] + grad_shapes,
            scratch=accumulators,
            name="ffn",
        )(came, w_gu, w_dn, a_gu, b_gu, a_dn, b_dn)
        returned = plan.exchange(back)

    out_s, d_resid, d_attended, d_logits, ga_out, gb_out = call(
        functools.partial(combine_body, expert_count, kinds),
        (tok // ROW_BLOCK,),
        [smem, row_spec(width, ROW_BLOCK), row_spec(width, ROW_BLOCK), row_spec(width, ROW_BLOCK), row_spec(LANES, ROW_BLOCK), row_spec(LANES, ROW_BLOCK),
         row_spec(LANES, ROW_BLOCK), row_spec(LANES, ROW_BLOCK), row_spec(width, ROW_BLOCK), row_spec(LANES, ROW_BLOCK),
         full((expert_count, cap, 2 * width)), full((width, width)), full((width, LANES)),
         full((LANES, width)), full((LANES, width)), full((2, width)), full((1, width))],
        [row_spec(width, ROW_BLOCK), row_spec(width, ROW_BLOCK), row_spec(width, ROW_BLOCK), row_spec(LANES, ROW_BLOCK), full((width, LANES)),
         full((LANES, width))],
        [sds((tok, width), BF16), sds((tok, width), F32), sds((tok, width), BF16),
         sds((tok, LANES), F32), sds((width, LANES), F32), sds((LANES, width), F32)],
        name="combine",
    )(eids, resid, act_two, dy_s, gate, slot, small_s, low_out, attn_low, mask, returned,
      w_out, a_out, b_out, router, const_value, gain_two)

    if plan.paired:
        flow = dict(vmem_limit_bytes=VMEM_BYTES, has_side_effects=True)
        own_shapes = [
            sds((gu_rows, LANES), F32), sds((up_rows, 2 * FEEDFWD_WIDTH), F32),
            sds((dn_rows, LANES), F32), sds((up_rows, width), F32),
        ]
        d_query, d_key, d_value, *expert_owned = pl.pallas_call(
            pair_attention_bwd_body,
            grid=(pairs,),
            in_specs=[col_spec(tok)] * 5
            + [full((lse_rows, tok)), full((1, tok)), full((tok, LANES)), full((tok, LANES))]
            + [hbm] * 4,
            out_specs=[col_spec(tok)] * 3 + [full(s.shape) for s in own_shapes],
            out_shape=[sds((tok, width), BF16)] * 3 + own_shapes,
            scratch_shapes=[pltpu.VMEM((tok, LANES), F32), pltpu.VMEM((tok, LANES), F32)]
            + [pltpu.VMEM((dp_size,) + s.shape, BF16) for s in own_shapes]
            + [pltpu.SemaphoreType.DMA((4, dp_size)), pltpu.SemaphoreType.DMA((4, dp_size))],
            compiler_params=pltpu.CompilerParams(collective_id=2, **flow),
            name="pair_attention_bwd",
        )(query, key, value, d_attended, attn_low, lse, starts, cosine, sine,
          ga_gu, gb_gu, ga_dn, gb_dn)
        sum_shapes = [(width, LANES), (LANES, 3 * width), (width, LANES), (LANES, width)]
        got_shapes = [(dp_size - 1, a // dp_size, b) for a, b in sum_shapes]
        thin_rows = -(-a_rows // 16) * 16
        output, grad_hidden, grad_gate, *attn_owned = pl.pallas_call(
            pair_tail_body,
            in_specs=[vmem] * 13 + [hbm] * 4,
            out_specs=[vmem] * 7,
            out_shape=[
                sds((tok, width), BF16), sds((tok, width), F32), sds((tok, LANES), F32),
                sds((a_rows, LANES), F32), sds((b_rows, 3 * width), F32),
                sds((a_rows, LANES), F32), sds((b_rows, width), F32),
            ],
            scratch_shapes=[
                pltpu.VMEM((tok, width), BF16), pltpu.VMEM((tok, width), F32),
                pltpu.VMEM((width, 3 * width), BF16), pltpu.VMEM((tok, width), BF16),
                pltpu.VMEM((tok, width), BF16), pltpu.VMEM((tok, width), BF16),
                pltpu.VMEM((tok, LANES), BF16),
                pltpu.VMEM((width, LANES), F32), pltpu.VMEM((LANES, 3 * width), F32),
                *[pltpu.VMEM(shape, BF16) for shape in sum_shapes + got_shapes],
                pltpu.VMEM((expert_count, thin_rows, 2 * LANES), BF16),
                pltpu.VMEM((expert_count, 4 * b_rows, width), BF16),
                pltpu.VMEM((expert_count - 1, thin_rows, 2 * LANES), BF16),
                pltpu.VMEM((expert_count - 1, 4 * b_rows, width), BF16),
                pltpu.SemaphoreType.DMA((4,)),
                pltpu.SemaphoreType.DMA((4, dp_size - 1)), pltpu.SemaphoreType.DMA((4, dp_size - 1)),
                pltpu.SemaphoreType.DMA((2, expert_count - 1)),
                pltpu.SemaphoreType.DMA((2, expert_count - 1)),
            ],
            compiler_params=pltpu.CompilerParams(collective_id=3, **flow),
            name="pair_tail",
        )(place[:, None], d_query, d_key, d_value, low_qkv, act_one, mask, a_qkv, b_qkv, gain_one,
          ga_out, gb_out, d_logits, hid_s, d_resid, w_qkv, out_s)
        return (
            output, grad_hidden, grad_gate[:, :kinds], *attn_owned,
            *[expert_owned[i][None] for i in range(4)],
        )

    owned_wide = plan.reduce(
        jnp.concatenate([gb_gu, gb_dn], axis=1).astype(BF16).reshape(dp_size, up_rows, -1)
    )
    owned_thin = plan.reduce(
        jnp.concatenate(
            [ga_gu.reshape(dp_size, gu_rows, LANES), ga_dn.reshape(dp_size, dn_rows, LANES)], axis=1
        ).astype(BF16)
    )

    d_query, d_key, d_value = call(
        attention_bwd_body,
        (pairs,),
        [col_spec(tok)] * 5
        + [full((lse_rows, tok)), full((1, tok)), full((tok, LANES)), full((tok, LANES))],
        [col_spec(tok)] * 3,
        [sds((tok, width), BF16)] * 3,
        scratch=[pltpu.VMEM((tok, LANES), F32), pltpu.VMEM((tok, LANES), F32)],
        name="attention_bwd",
    )(query, key, value, d_attended, attn_low, lse, starts, cosine, sine)

    high, lower, ga_qkv, gb_qkv = call(
        input_grad_body,
        (blocks,),
        [row_spec(width)] * 3 + [row_spec(LANES), row_spec(width), row_spec(LANES), row_spec(width),
         row_spec(width), full((width, 3 * width)), full((width, LANES)), full((LANES, 3 * width)),
         full((1, width))],
        [row_spec(width), row_spec(width), full((width, LANES)), full((LANES, 3 * width))],
        [sds((tok, width), BF16), sds((tok, width), BF16), sds((width, LANES), F32),
         sds((LANES, 3 * width), F32)],
        name="input_grad",
    )(d_query, d_key, d_value, low_qkv, act_one, mask, hid_s, d_resid, w_qkv, a_qkv, b_qkv,
      gain_one)

    owned = plan.reduce_all(
        jnp.concatenate(
            [
                ga_qkv.reshape(devices, b_rows, -1),
                ga_out.reshape(devices, b_rows, -1),
                gb_qkv.reshape(devices, b_rows, -1),
                gb_out.reshape(devices, b_rows, -1),
            ],
            axis=2,
        ).astype(BF16)
    )

    output, grad_hidden, grad_gate = call(
        to_rows_body,
        (blocks,),
        [row_spec(1), full((tok, width)), full((tok, LANES)), full((tok, width)),
         full((tok, width))],
        [row_spec(width), row_spec(width), row_spec(LANES)],
        [sds((tok, width), BF16), sds((tok, width), F32), sds((tok, LANES), F32)],
        name="to_rows",
    )(place[:, None], out_s, d_logits, high, lower)

    return (
        output,
        grad_hidden,
        grad_gate[:, :kinds],
        owned[:, :width].reshape(a_rows, LANES),
        owned[:, 2 * width : 5 * width],
        owned[:, width : 2 * width].reshape(a_rows, LANES),
        owned[:, 5 * width :],
        owned_thin[None, :gu_rows],
        owned_wide[None, :, : 2 * FEEDFWD_WIDTH],
        owned_thin[None, gu_rows:],
        owned_wide[None, :, 2 * FEEDFWD_WIDTH :],
    )


def solution(mesh):
    rows = P(("dp", "expert"), None)
    expert_rows = P("expert", "dp", None)
    in_specs = (
        (rows,) * 6 + (P(),) + (rows,) * 6 + (P(),) * 4 + (expert_rows,) * 6 + (rows,)
    )
    out_specs = (rows,) * 7 + (expert_rows,) * 4
    body = functools.partial(shards, mesh.shape["dp"], mesh.shape["expert"])
    return jax.shard_map(body, mesh=mesh, in_specs=in_specs, out_specs=out_specs, check_vma=False)
```

```python
import functools
import math

import jax
import jax.numpy as jnp
from jax import lax
from jax.experimental import pallas as pl
from jax.experimental.pallas import tpu as pltpu
from jax.sharding import PartitionSpec as P

MODEL_WIDTH = 768
HEAD_COUNT = 12
HEAD_DIM = 64
FEEDFWD_WIDTH = 2048
ADAPTER_RANK = 16
ROW_BLOCK = 256
HIDDEN_BLOCK = 1024
LANES = 128
CONST_LANE = 64
CHOICE_LANE = 48
CHOICE_ROWS = 16
EPSILON = 1e-06
VMEM_BYTES = 60 * 2**20
FRONT_KEPT = 26
MESH_ID = pl.DeviceIdType.MESH

F32 = jnp.float32
BF16 = jnp.bfloat16


def dot(a, b):
    return jnp.dot(a, b, preferred_element_type=F32)


def dot_nt(a, b):
    return lax.dot_general(a, b, (((1,), (1,)), ((), ())), preferred_element_type=F32)


def dot_tn(a, b):
    return lax.dot_general(a, b, (((0,), (0,)), ((), ())), preferred_element_type=F32)


def iota(shape, dim):
    return lax.broadcasted_iota(jnp.int32, shape, dim)


def hot_matrix(condition):
    return jnp.where(condition, 1.0, 0.0).astype(BF16)


def whole(shape):
    zeros = (0,) * len(shape)
    return pl.BlockSpec(shape, lambda *_: zeros)


def row_spec(width, rows=ROW_BLOCK):
    return pl.BlockSpec((rows, width), lambda i: (i, 0))


def col_spec(rows, width=LANES):
    return pl.BlockSpec((rows, width), lambda j: (0, j))


def sds(shape, dtype):
    return jax.ShapeDtypeStruct(shape, dtype)


def call(body, grid, in_specs, out_specs, out_shape, scratch=(), name=None):
    return pl.pallas_call(
        body,
        grid=grid,
        in_specs=in_specs,
        out_specs=out_specs,
        out_shape=out_shape,
        scratch_shapes=list(scratch),
        compiler_params=pltpu.CompilerParams(vmem_limit_bytes=VMEM_BYTES),
        name=name,
    )


def half_swap(values):
    lane = iota(values.shape, 1)
    up = pltpu.roll(values, 32, 1)
    down = pltpu.roll(values, LANES - 32, 1)
    return jnp.where(lane % HEAD_DIM < HEAD_DIM // 2, down, up)


def lane_value(values, lane_id):
    return jnp.sum(jnp.where(iota(values.shape, 1) == lane_id, values, 0.0), axis=1, keepdims=True)


def proj_in_body(
    place_row, hidden, upstream, small, cosine, sine, mask, gain, w_qkv, a_in, b_out,
    hid_s, dy_s, small_s, act_one, low_qkv, query, key, value,
):
    rows = hid_s.shape[0]
    base = pl.program_id(0) * rows
    perm = hot_matrix(place_row[...] == base + iota((rows, place_row.shape[1]), 0))
    hid = dot(perm, hidden[...])
    hid_s[...] = hid.astype(BF16)
    dy_s[...] = dot(perm, upstream[...]).astype(BF16)
    parts = dot(perm, small[...])
    small_s[...] = parts + (pltpu.roll(parts, LANES - 16, 1) + pltpu.roll(parts, LANES - 32, 1))
    act = normed(hid, gain)
    act_one[...] = act
    low, q_val, k_val, value[...] = project(
        act, mask[...], cosine[...], sine[...], w_qkv, a_in, b_out
    )
    low_qkv[...] = low
    query[...], key[...] = q_val, k_val


def normed(values, gain):
    scale = lax.rsqrt(jnp.mean(values * values, axis=-1, keepdims=True) + EPSILON)
    return (values * scale * gain[...].astype(F32)).astype(BF16)


def project(act, mask, cos, sin, w_qkv, a_in, b_out):
    low = (dot(act, a_in[...]) * mask.astype(F32)).astype(BF16)
    turned = []
    for start, factor in ((0, HEAD_DIM**-0.5), (MODEL_WIDTH, 1.0)):
        cols = slice(start, start + MODEL_WIDTH)
        vals = dot(act, w_qkv[:, cols]) + dot(low, b_out[:, cols])
        pieces = []
        for c in range(MODEL_WIDTH // LANES):
            piece = vals[:, c * LANES : (c + 1) * LANES]
            piece = (piece * cos + half_swap(piece) * sin).astype(BF16)
            pieces.append(piece if factor == 1.0 else piece * jnp.asarray(factor, BF16))
        turned.append(jnp.concatenate(pieces, axis=1))
    value = dot(act, w_qkv[:, 2 * MODEL_WIDTH :]) + dot(low, b_out[:, 2 * MODEL_WIDTH :])
    return low, turned[0], turned[1], value.astype(BF16)


def head_mask(shape, head):
    lane = iota(shape, 1)
    return (lane >= head * HEAD_DIM) & (lane < (head + 1) * HEAD_DIM)


def attention_fwd_body(query, key, value, starts, attended, lse):
    attention_fwd_pair(pl.program_id(0), query, key, value, starts, attended, lse)


def visible(lo, hi, starts):
    rows = iota((hi, hi - lo), 0)
    return (rows <= lo + iota((hi, hi - lo), 1)) & (rows >= starts[:, lo:hi])


def attention_fwd_pair(pair, query, key, value, starts, attended, lse):
    size = ROW_BLOCK
    zero = jnp.zeros((), BF16)
    for blk in range(query.shape[0] // size):
        lo, hi = blk * size, (blk + 1) * size
        q_blk = query[lo:hi, :]
        k_all = key[:hi, :]
        v_all = value[:hi, :]
        allowed = visible(lo, hi, starts)
        total = jnp.zeros((size, LANES), F32)
        for head in range(2):
            mine = head_mask((size, LANES), head)
            scores = dot_nt(k_all, jnp.where(mine, q_blk, zero))
            scores = jnp.where(allowed, scores, -1000000000.0)
            top = jnp.max(scores, axis=0, keepdims=True)
            expo = jnp.exp(scores - top)
            norm = jnp.sum(expo, axis=0, keepdims=True)
            prob = (expo * (1.0 / norm)).astype(BF16)
            total = jnp.where(mine, dot_tn(prob, v_all), total)
            lse[pl.ds(2 * pair + head, 1), lo:hi] = top + jnp.log(norm)
        attended[lo:hi, :] = total.astype(BF16)


def attention_bwd_body(
    query, key, value, dout, attended, lse, starts, cosine, sine, d_query, d_key, d_value, kacc, vacc
):
    pair = pl.program_id(0)
    tok = query.shape[0]
    size = ROW_BLOCK
    zero = jnp.zeros((), BF16)
    kacc[...] = jnp.zeros_like(kacc)
    vacc[...] = jnp.zeros_like(vacc)
    for blk in range(tok // size):
        lo, hi = blk * size, (blk + 1) * size
        q_blk = query[lo:hi, :]
        do_blk = dout[lo:hi, :]
        k_all = key[:hi, :]
        v_all = value[:hi, :]
        allowed = visible(lo, hi, starts)
        prod = (do_blk.astype(F32) * attended[lo:hi, :].astype(F32)).T
        probs, dscores, q_heads, do_heads = [], [], [], []
        q_total = jnp.zeros((size, LANES), F32)
        for head in range(2):
            mine = head_mask((size, LANES), head)
            q_heads.append(jnp.where(mine, q_blk, zero))
            do_heads.append(jnp.where(mine, do_blk, zero))
            lse_head = lse[pl.ds(2 * pair + head, 1), lo:hi]
            delta = jnp.sum(
                prod[head * HEAD_DIM : (head + 1) * HEAD_DIM], axis=0, keepdims=True
            )
            scores = dot_nt(k_all, q_heads[head])
            prob = jnp.where(allowed, jnp.exp(scores - lse_head), 0.0)
            dprob = dot_nt(v_all, do_heads[head])
            dscores.append((prob * (dprob - delta)).astype(BF16))
            probs.append(prob.astype(BF16))
            k_head = jnp.where(head_mask((hi, LANES), head), k_all, zero)
            q_total = q_total + dot_tn(dscores[head], k_head)
        kacc[:hi, :] += dot(jnp.concatenate(dscores, axis=1), jnp.concatenate(q_heads, axis=0))
        vacc[:hi, :] += dot(jnp.concatenate(probs, axis=1), jnp.concatenate(do_heads, axis=0))
        q_total = q_total * HEAD_DIM**-0.5
        d_query[lo:hi, :] = (
            q_total * cosine[lo:hi, :] - half_swap(q_total) * sine[lo:hi, :]
        ).astype(BF16)
    for blk in range(tok // size):
        lo, hi = blk * size, (blk + 1) * size
        k_total = kacc[lo:hi, :]
        d_key[lo:hi, :] = (
            k_total * cosine[lo:hi, :] - half_swap(k_total) * sine[lo:hi, :]
        ).astype(BF16)
    d_value[...] = vacc[...].astype(BF16)


def start_kernel(send_to, hear_from, count):
    barrier = pltpu.get_barrier_semaphore()
    for device, remote in hear_from:
        if remote is None:
            pl.semaphore_signal(barrier, inc=1, device_id=device, device_id_type=MESH_ID)
        else:

            @pl.when(remote)
            def _(device=device):
                pl.semaphore_signal(barrier, inc=1, device_id=device, device_id_type=MESH_ID)

    pl.semaphore_wait(barrier, count)


def pair_front_body(
    kinds, a_rows, b_rows,
    lengths, adapters, place_row, hidden, upstream, carry, choices, gains,
    router_in, const_in, in_qkv, in_out, in_a_qkv, in_a_out, in_b_qkv, in_b_out,
    in_gu, in_b_gu, in_dn, in_b_dn, in_a_gu, in_a_dn, *rest,
):
    count = FRONT_KEPT
    outs, rest = rest[:count], rest[count:]
    (all_wide, all_mid, all_thin, came, last_sent), rest = rest[:5], rest[5:]
    kept, rest = rest[:count], rest[count:]
    (
        hid_s, dy_s, small_s, act_one, low_qkv, mask, starts, cosine, sine, router,
        query, key, value, w_qkv, a_qkv, b_qkv, w_out, a_out, b_out,
        attn_low, lse, low_out, resid, act_two, gate, slot,
    ) = kept
    (
        g_qkv, g_out, own_wide, own_mid, own_thin, sent, slot_rows,
        a_send, a_recv, z_send, e_send, e_recv, out_sems, own_sems, row_send, row_recv,
    ) = rest
    gain_one, gain_two = gains[0:1, :], gains[1:2, :]
    dp, z = lax.axis_index("dp"), lax.axis_index("expert")
    core, x_bit, y_bit = dp % 2, dp // 2 % 2, dp // 4
    across = dp + 1 - 2 * core
    x_dev, y_dev = dp + 2 - 4 * x_bit, dp + 4 - 8 * y_bit
    diag = x_dev + 4 - 8 * y_bit
    far = (z + 2) % 4
    home = z // 2
    columns = (dp, x_dev, y_dev, diag)
    tok = hidden.shape[0]
    blocks = tok // ROW_BLOCK

    def remote(source, target, send, recv, device):
        return pltpu.make_async_remote_copy(
            src_ref=source, dst_ref=target, send_sem=send, recv_sem=recv,
            device_id=device, device_id_type=MESH_ID,
        )

    packs = (g_qkv, g_out)

    def at(kind, back):
        return columns[kind] * 4 + (z + 4 - back) % 4

    def shard(p, kind, back, rows=None):
        view = packs[p].at[at(kind, back)]
        if rows is None:
            return view
        half = packs[p].shape[1] // 2
        return view.at[pl.ds(rows * half, half)]

    def z_up(p, t):
        view = shard(p, 0, t)
        return remote(view, view, z_send.at[p, t], a_recv.at[p, t], (dp, z + 1))

    def z_down(p, t):
        view = shard(p, 0, (4 - t) % 4)
        return remote(view, view, z_send.at[p, 3 + t], a_recv.at[p, 2 - t], (dp, z - 1))

    def z_sends(p, t, act):
        @pl.when((z < 3) & (z >= t))
        def _():
            act(z_up(p, t))

        @pl.when((z > 0) & (z + t <= 3))
        def _():
            act(z_down(p, t))

    def to_x(p, back):
        return remote(
            shard(p, 0, back), shard(p, 0, back), a_send.at[p, 3 + back], a_recv.at[p, 3 + back],
            (x_dev, z),
        )

    def to_y(p, back):
        return remote(
            shard(p, 0, back), shard(p, 0, back), a_send.at[p, 7 + back], a_recv.at[p, 7 + back],
            (y_dev, z),
        )

    def relay_y(p, back):
        return remote(
            shard(p, 1, back, 0), shard(p, 1, back, 0), a_send.at[p, 11 + back],
            a_recv.at[p, 11 + back], (y_dev, z),
        )

    def relay_x(p, back):
        return remote(
            shard(p, 2, back, 1), shard(p, 2, back, 1), a_send.at[p, 15 + back],
            a_recv.at[p, 15 + back], (x_dev, z),
        )

    def to_core(p, kind, back):
        sem = 19 + 4 * kind + back
        return remote(
            shard(p, kind, back), shard(p, kind, back), a_send.at[p, sem], a_recv.at[p, sem],
            (across, z),
        )

    half_wide = own_wide.shape[1] // 2
    parts = []
    for own, everything, cols in (
        (own_mid, all_mid, None), (own_thin, all_thin, None),
        (own_wide, all_wide, (0, half_wide)), (own_wide, all_wide, (half_wide, half_wide)),
    ):
        if cols is None:
            parts.append((own, lambda d, ref=everything: ref.at[d]))
        else:
            parts.append(
                (own.at[:, pl.ds(*cols)], lambda d, ref=everything, c=cols: ref.at[d, :, pl.ds(*c)])
            )
    chunks = ((0, 1), (2,), (3,))

    def first_far(a):
        return remote(
            parts[a][0], parts[a][1](dp), e_send.at[a, 0], e_recv.at[a, core],
            (dp - core + home, far),
        )

    def first_across(a):
        return remote(
            parts[a][0], parts[a][1](dp), e_send.at[a, 1], e_recv.at[a, core], (across, z)
        )

    def first_keep(a):
        return pltpu.make_async_copy(parts[a][0], parts[a][1](dp), e_recv.at[a, core])

    def first_arrival(a, i):
        view = parts[a][1](dp - core + i)
        return remote(view, view, e_send.at[a, 0], e_recv.at[a, i], (dp, far))

    def expert_hop(a, column, i, sem, device):
        view = parts[a][1](column - core + i)
        return remote(view, view, e_send.at[a, sem], e_recv.at[a, sem], (device, z))

    def expert_x(a, i):
        return expert_hop(a, dp, i, 2 + i, x_dev)

    def expert_y(a, i):
        return expert_hop(a, dp, i, 4 + i, y_dev)

    def expert_relay_y(a):
        return expert_hop(a, x_dev, 0, 6, y_dev)

    def expert_relay_x(a):
        return expert_hop(a, y_dev, 1, 7, x_dev)

    def expert_first(c):
        for a in chunks[c]:
            first_far(a).start()

            @pl.when(core == home)
            def _(a=a):
                first_keep(a).start()

            @pl.when(core != home)
            def _(a=a):
                first_across(a).start()

    def at_home(step, *args):
        @pl.when(core == home)
        def _():
            step(*args)

    def abroad(step, *args):
        @pl.when(core != home)
        def _():
            step(*args)

    def send_sides(a):
        for i in range(2):
            expert_x(a, i).start()
            expert_y(a, i).start()

    def spread_home(c):
        for a in chunks[c]:
            first_keep(a).wait()
            first_arrival(a, 1 - core).wait_recv()
            send_sides(a)

    def spread_far(c):
        for a in chunks[c]:
            for i in range(2):
                first_arrival(a, i).wait_recv()
            send_sides(a)

    def expert_relay(c):
        for a in chunks[c]:
            for i in range(2):
                expert_hop(a, x_dev, i, 2 + i, x_dev).wait_recv()
            expert_relay_y(a).start()
            for i in range(2):
                expert_hop(a, y_dev, i, 4 + i, y_dev).wait_recv()
            expert_relay_x(a).start()

    def expert_finish(c):
        for a in chunks[c]:
            expert_hop(a, diag, 0, 6, y_dev).wait_recv()
            expert_hop(a, diag, 1, 7, x_dev).wait_recv()
            first_far(a).wait_send()

            @pl.when(core != home)
            def _(a=a):
                first_across(a).wait_send()

            for i in range(2):
                expert_x(a, i).wait_send()
                expert_y(a, i).wait_send()
            expert_relay_y(a).wait_send()
            expert_relay_x(a).wait_send()

    gu_rows, up_rows, dn_rows = in_gu.shape[1], in_b_gu.shape[1], in_dn.shape[1]
    own_loads = [
        pltpu.make_async_copy(source.at[0], target.at[pl.ds(at_row, rows)], own_sems.at[i])
        for i, (source, target, at_row, rows) in enumerate((
            (in_gu, own_wide, 0, gu_rows), (in_b_gu, own_wide, gu_rows, up_rows),
            (in_dn, own_mid, 0, dn_rows), (in_b_dn, own_mid, dn_rows, up_rows),
            (in_a_gu, own_thin, 0, gu_rows), (in_a_dn, own_thin, gu_rows, dn_rows),
        ))
    ]
    for load in own_loads:
        load.start()
    for gathered, weight, adapter_in, adapter_out in (
        (g_qkv, in_qkv, in_a_qkv, in_b_qkv), (g_out, in_out, in_a_out, in_b_out),
    ):
        spare = gathered.shape[1] - a_rows - b_rows
        wide_cols = weight.shape[1]
        gathered[at(0, 0), :, :wide_cols] = jnp.concatenate(
            [weight[...].astype(F32), adapter_out[...].astype(F32), jnp.zeros((spare, wide_cols), F32)],
            axis=0,
        ).astype(BF16)
        gathered[at(0, 0), :, wide_cols:] = jnp.concatenate(
            [adapter_in[...].astype(F32), jnp.zeros((spare + b_rows, LANES), F32)], axis=0
        ).astype(BF16)
    next_z = z + 1 - 2 * (z % 2)
    peers = [(x_dev, z), (y_dev, z), (across, z), (across, far), (across, next_z)]
    peers += [(dp, (z + j) % 4) for j in (1, 2, 3)]
    start_kernel(None, [(device, None) for device in peers], len(peers))
    def send_own(p):
        z_sends(p, 0, lambda copy: copy.start())
        to_x(p, 0).start()
        to_y(p, 0).start()
        to_core(p, 0, 0).start()

    send_own(0)
    router[...] = jnp.concatenate(
        [router_in[...].astype(F32), jnp.zeros((CONST_LANE - kinds, MODEL_WIDTH), F32),
         const_in[...].astype(F32), jnp.zeros((LANES - CONST_LANE - 4, MODEL_WIDTH), F32)],
        axis=0,
    ).astype(BF16)
    small_s[...] = jnp.zeros_like(small_s)
    carry_parts = split_three(carry[...])
    choices_low = choices[...].astype(F32).astype(BF16)
    half_dim = HEAD_DIM // 2
    freq = jnp.exp(
        (iota((1, LANES), 1) % half_dim).astype(F32) * (-math.log(10000.0) / half_dim)
    )
    sign = jnp.where(iota((1, LANES), 1) % HEAD_DIM < half_dim, -1.0, 1.0)

    def block_rows(b):
        return pl.ds(pl.multiple_of(b * ROW_BLOCK, ROW_BLOCK), ROW_BLOCK)

    def arrange(b, carry_on):
        rows = block_rows(b)
        perm = hot_matrix(place_row[...] == b * ROW_BLOCK + iota((ROW_BLOCK, tok), 0))
        hid = dot(perm, hidden[...])
        hid_s[rows, :] = hid.astype(BF16)
        act_one[rows, :] = normed(hid, gain_one)
        return carry_on

    def arrange_rest(b, carry_on):
        rows = block_rows(b)
        perm = hot_matrix(place_row[...] == b * ROW_BLOCK + iota((ROW_BLOCK, tok), 0))
        dy_s[rows, :] = dot(perm, upstream[...]).astype(BF16)
        top, mid, last = carry_parts
        small_s[rows, :kinds] = dot_nt(perm, top) + (dot_nt(perm, mid) + dot_nt(perm, last))
        small_s[rows, CHOICE_LANE : CHOICE_LANE + 2] = dot_nt(perm, choices_low)
        return carry_on

    place = iota((1, tok), 1)
    begin_row = jnp.zeros((1, tok), jnp.int32)
    begin = 0
    for n in range(1, lengths.shape[1]):
        begin = begin + lengths[0, n - 1]
        begin_row = jnp.where(place >= begin, begin, begin_row)
    starts[...] = begin_row

    def positions(b, carry_on):
        rows = block_rows(b)
        stream = b * ROW_BLOCK + iota((ROW_BLOCK, 1), 0)
        start = jnp.zeros((ROW_BLOCK, 1), jnp.int32)
        adapter = start + adapters[0, 0]
        begin = 0
        for n in range(1, lengths.shape[1]):
            begin = begin + lengths[0, n - 1]
            start = jnp.where(stream >= begin, begin, start)
            adapter = jnp.where(stream >= begin, adapters[0, n], adapter)
        mask[rows, :] = hot_matrix(iota((ROW_BLOCK, LANES), 1) // ADAPTER_RANK == adapter)
        angle = (stream - start).astype(F32) * freq
        cosine[rows, :] = jnp.cos(angle)
        sine[rows, :] = jnp.sin(angle) * sign
        return carry_on

    lax.fori_loop(0, blocks, arrange, 0)

    at_end = (z == 0) | (z == 3)
    order = (
        jnp.where(z == 0, 3, 1), jnp.where(at_end, 2, 3),
        jnp.where(z == 0, 1, jnp.where(z == 3, 3, 2)),
    )

    def spread_shard(p, back):
        view = shard(p, 0, back)
        remote(view, view, z_send.at[p, 0], a_recv.at[p, back - 1], (dp, z)).wait_recv()
        to_x(p, back).start()
        to_y(p, back).start()
        to_core(p, 0, back).start()

    def from_z(p, t):
        @pl.when(z > t)
        def _():
            spread_shard(p, 1 + t)

        @pl.when(z + t < 3)
        def _():
            spread_shard(p, 3 - t)

        if t < 2:
            z_sends(p, t + 1, lambda copy: copy.start())

    def from_sides(p, back):
        view = shard(p, 1, back)
        remote(view, view, a_send.at[p, 3 + back], a_recv.at[p, 3 + back], (x_dev, z)).wait_recv()
        relay_y(p, back).start()
        to_core(p, 1, back).start()
        view = shard(p, 2, back)
        remote(view, view, a_send.at[p, 7 + back], a_recv.at[p, 7 + back], (y_dev, z)).wait_recv()
        relay_x(p, back).start()
        to_core(p, 2, back).start()

    def from_diag(p, back):
        view = shard(p, 3, back, 0)
        remote(view, view, a_send.at[p, 11 + back], a_recv.at[p, 11 + back], (y_dev, z)).wait_recv()
        view = shard(p, 3, back, 1)
        remote(view, view, a_send.at[p, 15 + back], a_recv.at[p, 15 + back], (x_dev, z)).wait_recv()
        to_core(p, 3, back).start()

    for t in range(3):
        from_z(0, t)
    send_own(1)
    from_sides(0, 0)
    lax.fori_loop(0, 2, arrange_rest, 0)
    from_sides(0, order[0])
    lax.fori_loop(2, 4, arrange_rest, 0)
    from_sides(0, order[1])
    lax.fori_loop(4, blocks, arrange_rest, 0)
    from_sides(0, order[2])
    for t in range(3):
        from_z(1, t)
    for load in own_loads:
        load.wait()
    for c in range(len(chunks)):
        expert_first(c)
    for back in (0,) + order[:2]:
        from_diag(0, back)
    lax.fori_loop(0, blocks, positions, 0)
    from_diag(0, order[2])
    core_columns = (across, x_dev + across - dp, y_dev + across - dp, diag + across - dp)

    def from_core(p):
        def body(back, carry):
            for kind in range(4):
                view = packs[p].at[core_columns[kind] * 4 + (z + 4 - back) % 4]
                sem = 19 + 4 * kind + back
                remote(view, view, a_send.at[p, sem], a_recv.at[p, sem], (across, z)).wait_recv()
            return carry

        lax.fori_loop(0, 4, body, 0)

    width = MODEL_WIDTH
    total = g_qkv.shape[0]

    def lay_rows(i, carry, gathered, targets):
        pair = [gathered[2 * i + n, :a_rows, :].astype(F32) for n in range(2)]
        both = jnp.concatenate(pair, axis=0).astype(BF16)
        rows = pl.ds(pl.multiple_of(i * 2 * a_rows, 16), 2 * a_rows)
        start = 0
        for target in targets:
            target[rows, :] = both[:, start : start + target.shape[1]]
            start += target.shape[1]
        return carry

    def lay_ups(i, carry, gathered, target):
        group = 16 // b_rows
        pieces = [
            gathered[group * i + n, a_rows : a_rows + b_rows, : target.shape[1]].astype(F32)
            for n in range(group)
        ]
        rows = pl.ds(pl.multiple_of(i * 16, 16), 16)
        target[rows, :] = jnp.concatenate(pieces, axis=0).astype(BF16)
        return carry

    def lay(gathered, targets, ups):
        lax.fori_loop(
            0, total // 2, functools.partial(lay_rows, gathered=gathered, targets=targets), 0
        )
        lax.fori_loop(
            0, total * b_rows // 16, functools.partial(lay_ups, gathered=gathered, target=ups), 0
        )

    def flush(first, last):
        return [
            pltpu.make_async_copy(kept[i], outs[i], out_sems.at[i]) for i in range(first, last)
        ]

    for back in (0,) + order:
        from_sides(1, back)
    for c in range(len(chunks)):
        at_home(spread_home, c)
    from_core(0)
    lay(g_qkv, (w_qkv, a_qkv), b_qkv)

    def projection(b, carry):
        rows = block_rows(b)
        low_qkv[rows, :], query[rows, :], key[rows, :], value[rows, :] = project(
            act_one[rows, :], mask[rows, :], cosine[rows, :], sine[rows, :], w_qkv, a_qkv, b_qkv
        )

        return carry

    lax.fori_loop(0, blocks, projection, 0)
    abroad(spread_far, 0)
    for copy in flush(0, 16):
        copy.start()
    lse[...] = jnp.zeros_like(lse)

    def attention(pair, carry):
        cols = pl.ds(pl.multiple_of(pair * LANES, LANES), LANES)
        attention_fwd_pair(
            pair, query.at[:, cols], key.at[:, cols], value.at[:, cols], starts,
            attn_low.at[:, cols], lse,
        )

        @pl.when(pair == 0)
        def _():
            for back in (0,) + order:
                from_diag(1, back)
            at_home(expert_relay, 0)

        @pl.when(pair == 2)
        def _():
            at_home(expert_relay, 1)

        @pl.when(pair == 3)
        def _():
            abroad(spread_far, 1)
            abroad(expert_relay, 0)

        @pl.when(pair == 4)
        def _():
            at_home(expert_relay, 2)

        return carry

    lax.fori_loop(0, HEAD_COUNT // 2, attention, 0)
    from_core(1)
    lay(g_out, (w_out, a_out), b_out)
    for copy in flush(16, 21):
        copy.start()

    def after(b, carry):
        rows = block_rows(b)
        low_out[rows, :], resid[rows, :], act_two[rows, :], gate[rows, :] = post_attn(
            kinds, attn_low[rows, :], hid_s[rows, :], mask[rows, :], small_s[rows, :],
            w_out, a_out, b_out, router, gain_two,
        )
        return carry

    lax.fori_loop(0, blocks, after, 0)
    abroad(spread_far, 2)
    abroad(expert_relay, 1)
    place_slots(4, small_s, slot, slot_rows)
    for copy in flush(21, FRONT_KEPT):
        copy.start()

    def rows_out(k):
        device = ((dp, next_z), (across, z))[k - 1]
        return remote(sent.at[k], came.at[k], row_send.at[k], row_recv.at[k], device)

    last_local = pltpu.make_async_copy(sent.at[0], last_sent, row_send.at[3])
    own_local = pltpu.make_async_copy(sent.at[0], came.at[0], row_send.at[0])
    some = pl.ds(0, last_sent.shape[0] // 2)
    last_half = remote(
        last_sent.at[some], came.at[3, some], row_send.at[4], row_recv.at[3], (across, next_z)
    )
    def fill(n, carry):
        k = (n + 1) % 4
        eid = (z + k) % 2 + 2 * ((core + k // 2) % 2)
        fill_slots(eid, gate, act_two, dy_s, mask, slot_rows, sent.at[k % 3])

        @pl.when(n == 0)
        def _():
            rows_out(1).start()

        @pl.when(n == 1)
        def _():
            rows_out(2).start()

        @pl.when(n == 2)
        def _():
            last_local.start()
            last_local.wait()
            last_half.start()

        return carry

    lax.fori_loop(0, 4, fill, 0)
    own_local.start()
    abroad(expert_relay, 2)
    for c in range(len(chunks)):
        expert_finish(c)
    for k in (1, 2):
        rows_out(k).wait_recv()
        rows_out(k).wait_send()
    last_half.wait_recv()
    last_half.wait_send()
    own_local.wait()

    def attn_sent(n, carry):
        for p in range(2):
            to_x(p, n).wait_send()
            to_y(p, n).wait_send()
            relay_x(p, n).wait_send()
            relay_y(p, n).wait_send()
            for kind in range(4):
                to_core(p, kind, n).wait_send()
        return carry

    lax.fori_loop(0, 4, attn_sent, 0)
    for p in range(2):
        for t in range(3):
            z_sends(p, t, lambda copy: copy.wait_send())
    for copy in flush(0, FRONT_KEPT):
        copy.wait()


def pair_attention_bwd_body(
    query, key, value, dout, attended, lse, starts, cosine, sine, ga_out, gb_out,
    ga_gu, gb_gu, ga_dn, gb_dn,
    d_query, d_key, d_value, own_ga_gu, own_gb_gu, own_ga_dn, own_gb_dn, plane_ga_out, plane_gb_out,
    kacc, vacc, r_ga_gu, r_gb_gu, r_ga_dn, r_gb_dn, s_ga_out, s_gb_out, r_ga_out, r_gb_out,
    send_sems, recv_sems, near_send, near_recv,
):
    dp, z = lax.axis_index("dp"), lax.axis_index("expert")
    core, spot, half = dp % 2, dp // 2, z // 2
    own = z % 2 + 2 * core
    far = (z + 2) % 4
    at_home = core == half
    away = 1 - (core * half + (1 - core) * (1 - half))
    slot = 2 * spot + away
    groups = (
        (ga_gu, r_ga_gu, own_ga_gu), (gb_gu, r_gb_gu, own_gb_gu),
        (ga_dn, r_ga_dn, own_ga_dn), (gb_dn, r_gb_dn, own_gb_dn),
    )
    owners = 8
    plane_groups = (
        (s_ga_out, r_ga_out, plane_ga_out), (s_gb_out, r_gb_out, plane_gb_out),
    )

    def share(i, d):
        count = plane_groups[i][1].shape[1]
        return plane_groups[i][0].at[pl.ds(pl.multiple_of(d * count, 16), count)]

    def near(i, n):
        goal = (dp + n + 1) % owners
        return pltpu.make_async_remote_copy(
            src_ref=share(i, goal), dst_ref=plane_groups[i][1].at[n], send_sem=near_send.at[i, n],
            recv_sem=near_recv.at[i, n], device_id=(goal, z), device_id_type=MESH_ID,
        )

    def piece(i, d):
        source, target, _ = groups[i]
        count = target.shape[1]
        return source.at[pl.ds(pl.multiple_of(d * count, 16), count)]

    def push(i, d):
        return pltpu.make_async_remote_copy(
            src_ref=piece(i, d), dst_ref=groups[i][1].at[slot], send_sem=send_sems.at[i, d],
            recv_sem=recv_sems.at[i, slot], device_id=(d, own), device_id_type=MESH_ID,
        )

    def keep(i):
        return pltpu.make_async_copy(
            piece(i, dp), groups[i][1].at[2 * spot], recv_sems.at[i, 2 * spot]
        )

    def arrival(i, s):
        return pltpu.make_async_remote_copy(
            src_ref=piece(i, 0), dst_ref=groups[i][1].at[s], send_sem=send_sems.at[i, 0],
            recv_sem=recv_sems.at[i, s], device_id=(0, own), device_id_type=MESH_ID,
        )

    @pl.when(pl.program_id(0) == 0)
    def _():
        s_ga_out[...] = ga_out[...].astype(BF16)
        s_gb_out[...] = gb_out[...].astype(BF16)
        senders = [((2 * m + half, far), None) for m in range(owners // 2)]
        senders += [(((dp + n) % owners, z), None) for n in range(1, owners)]
        start_kernel(None, senders, owners - 1 + owners * away)

        def send_near(n, carry):
            for i in range(2):
                near(i, n).start()
            return carry

        lax.fori_loop(0, owners - 1, send_near, 0)

        def send(d, carry):
            mine = at_home & (d == dp)

            @pl.when(mine)
            def _():
                for i in range(4):
                    keep(i).start()

            @pl.when(jnp.logical_not(mine))
            def _():
                for i in range(4):
                    push(i, d).start()

            return carry

        lax.fori_loop(0, owners, send, 0)

    attention_bwd_body(
        query, key, value, dout, attended, lse, starts, cosine, sine, d_query, d_key, d_value,
        kacc, vacc,
    )

    @pl.when(pl.program_id(0) == pl.num_programs(0) - 1)
    def _():
        def finish(s, carry):
            mine = at_home & (s == 2 * spot)

            @pl.when(mine)
            def _():
                for i in range(4):
                    keep(i).wait()

            @pl.when(jnp.logical_not(mine))
            def _():
                for i in range(4):
                    arrival(i, s).wait_recv()

            @pl.when(jnp.logical_not(at_home & (s == dp)))
            def _():
                for i in range(4):
                    push(i, s).wait_send()

            return carry

        lax.fori_loop(0, owners, finish, 0)
        for _, target, out in groups:
            total = target[0].astype(F32)
            for s in range(1, owners):
                total = total + target[s].astype(F32)
            out[...] = total

        def finish_near(n, carry):
            for i in range(2):
                near(i, n).wait_recv()
                near(i, n).wait_send()
            return carry

        lax.fori_loop(0, owners - 1, finish_near, 0)
        for i, (_, target, out) in enumerate(plane_groups):
            total = share(i, dp)[...].astype(F32)
            for n in range(owners - 1):
                total = total + target[n].astype(F32)
            out[...] = total


def pair_tail_body(
    place_row, mask, a_in, b_out, gain, a_o, b_o, d_logits,
    q_hbm, k_hbm, v_hbm, low_hbm, act_hbm, hid_hbm, resid_hbm, w_hbm, out_hbm,
    out, grad_hidden, grad_gate, own_ga_qkv, own_gb_qkv, own_ga_out, own_gb_out,
    d_query, d_key, d_value, low_qkv, act_one,
    hid_s, d_resid, w_qkv, out_s, place_col, high, lower, d_low_all, ga_sum, gb_sum,
    s_ga_qkv, s_gb_qkv, r_ga_qkv, r_gb_qkv,
    thin_out, wide_out, thin_in, wide_in, load_sems, send_sems, recv_sems, far_send, far_recv,
):
    dp, z = lax.axis_index("dp"), lax.axis_index("expert")
    others, planes = 7, 3
    tok = place_row.shape[1]
    blocks = tok // ROW_BLOCK
    loads = [
        pltpu.make_async_copy(source, target, load_sems.at[i])
        for i, (source, target) in enumerate(
            ((q_hbm, d_query), (k_hbm, d_key), (v_hbm, d_value), (low_hbm, low_qkv),
             (act_hbm, act_one), (w_hbm, w_qkv), (hid_hbm, hid_s), (resid_hbm, d_resid),
             (out_hbm, out_s))
        )
    ]
    for load in loads:
        load.start()
    start_kernel(
        None,
        [(((dp + i) % 8, z), None) for i in range(1, 8)] + [((dp, (z + j) % 4), None) for j in (1, 2, 3)],
        others + planes,
    )
    ga_sum[...] = jnp.zeros_like(ga_sum)
    gb_sum[...] = jnp.zeros_like(gb_sum)
    parts = [slice(p * MODEL_WIDTH, (p + 1) * MODEL_WIDTH) for p in range(3)]
    d_refs = (d_query, d_key, d_value)

    def block_rows(b):
        return pl.ds(pl.multiple_of(b * ROW_BLOCK, ROW_BLOCK), ROW_BLOCK)

    def sums(b, carry):
        rows = block_rows(b)
        low = low_qkv[rows, :]
        d_low = jnp.zeros((ROW_BLOCK, LANES), F32)
        for cols, ref in zip(parts, d_refs):
            grad = ref[rows, :]
            d_low = d_low + dot_nt(grad, b_out[:, cols])
            gb_sum[:, cols] += dot_tn(low, grad)
        d_low = (d_low * mask[rows, :].astype(F32)).astype(BF16)
        d_low_all[rows, :] = d_low
        ga_sum[...] += dot_tn(act_one[rows, :], d_low)
        return carry

    for load in loads[:5]:
        load.wait()
    lax.fori_loop(0, blocks, sums, 0)
    s_ga_qkv[...] = ga_sum[...].astype(BF16)
    s_gb_qkv[...] = gb_sum[...].astype(BF16)
    groups = ((s_ga_qkv, r_ga_qkv), (s_gb_qkv, r_gb_qkv))

    def share(i, d):
        count = groups[i][1].shape[1]
        return groups[i][0].at[pl.ds(pl.multiple_of(d * count, 16), count)]

    def near(i, n):
        goal = (dp + n + 1) % 8
        return pltpu.make_async_remote_copy(
            src_ref=share(i, goal), dst_ref=groups[i][1].at[n], send_sem=send_sems.at[i, n],
            recv_sem=recv_sems.at[i, n], device_id=(goal, z), device_id_type=MESH_ID,
        )

    def send_near(n, carry):
        for i in range(2):
            near(i, n).start()
        return carry

    lax.fori_loop(0, others, send_near, 0)

    for load in loads[5:8]:
        load.wait()

    def back(b, carry):
        rows = block_rows(b)
        d_act = dot_nt(d_low_all[rows, :], a_in[...])
        for cols, ref in zip(parts, d_refs):
            d_act = d_act + dot_nt(ref[rows, :], w_qkv[:, cols])
        hid = hid_s[rows, :].astype(F32)
        scale = lax.rsqrt(jnp.mean(hid * hid, axis=-1, keepdims=True) + EPSILON)
        weighted = d_act * gain[...].astype(F32)
        grad_hid = d_resid[rows, :] + (
            scale * weighted
            - hid * (scale * scale * scale) * jnp.mean(hid * weighted, axis=-1, keepdims=True)
        )
        top = grad_hid.astype(BF16)
        high[rows, :] = top
        lower[rows, :] = (grad_hid - top.astype(F32)).astype(BF16)
        return carry

    lax.fori_loop(0, blocks, back, 0)
    place_col[...] = jnp.broadcast_to(place_row[...].astype(F32), (LANES, tok)).T

    def near_done(n, carry):
        for i in range(2):
            near(i, n).wait_recv()
        return carry

    lax.fori_loop(0, others, near_done, 0)
    totals = []
    for i in range(2):
        total = share(i, dp)[...].astype(F32)
        for n in range(others):
            total = total + groups[i][1][n].astype(F32)
        totals.append(total)
    a_qkv, b_qkv = totals
    a_count, b_count = a_qkv.shape[0] // 4, b_qkv.shape[0] // 4
    for p in range(4):
        a_rows, b_rows = slice(p * a_count, (p + 1) * a_count), slice(p * b_count, (p + 1) * b_count)
        thin_out[p, :a_count, :LANES] = a_qkv[a_rows].astype(BF16)
        thin_out[p, :a_count, LANES:] = a_o[a_rows, :].astype(BF16)
        thin_out[p, a_count:, :] = jnp.zeros((thin_out.shape[1] - a_count, 2 * LANES), BF16)
        wide_out[p] = jnp.concatenate(
            [b_qkv[b_rows, cols] for cols in parts] + [b_o[b_rows, :]], axis=0
        ).astype(BF16)

    def far(i, j):
        goal = (z + j + 1) % 4
        source, target = ((thin_out, thin_in), (wide_out, wide_in))[i]
        return pltpu.make_async_remote_copy(
            src_ref=source.at[goal], dst_ref=target.at[j], send_sem=far_send.at[i, j],
            recv_sem=far_recv.at[i, j], device_id=(dp, goal), device_id_type=MESH_ID,
        )

    for j in range(planes):
        for i in range(2):
            far(i, j).start()
    loads[8].wait()

    top, mid, last = (jnp.where(iota((tok, LANES), 1) < 16, v.astype(F32), 0.0) for v in split_three(d_logits[...]))
    logit_parts = (top + pltpu.roll(mid, 16, 1) + pltpu.roll(last, 32, 1)).astype(BF16)

    def to_rows(b, carry):
        rows = block_rows(b)
        perm = hot_matrix(place_col[rows, 0:1].astype(jnp.int32) == iota((ROW_BLOCK, tok), 1))
        out[rows, :] = dot(perm, out_s[...]).astype(BF16)
        grad_hidden[rows, :] = dot(perm, high[...]) + dot(perm, lower[...])
        moved = dot(perm, logit_parts)
        grad_gate[rows, :] = moved + (
            pltpu.roll(moved, LANES - 16, 1) + pltpu.roll(moved, LANES - 32, 1)
        )
        return carry

    lax.fori_loop(0, blocks, to_rows, 0)
    for j in range(planes):
        for i in range(2):
            far(i, j).wait_recv()
    thin = thin_out[z].astype(F32)
    wide = wide_out[z].astype(F32)
    for j in range(planes):
        thin = thin + thin_in[j].astype(F32)
        wide = wide + wide_in[j].astype(F32)
    own_ga_qkv[...] = thin[:a_count, :LANES]
    own_ga_out[...] = thin[:a_count, LANES:]
    for p, cols in enumerate(parts):
        own_gb_qkv[:, cols] = wide[p * b_count : (p + 1) * b_count]
    own_gb_out[...] = wide[3 * b_count : 4 * b_count]

    def sent(n, carry):
        for i in range(2):
            near(i, n).wait_send()
        return carry

    lax.fori_loop(0, others, sent, 0)
    for j in range(planes):
        for i in range(2):
            far(i, j).wait_send()


def settle_body(*refs):
    count = len(refs) // 2
    for n, (source, target) in enumerate(zip(refs[:count], refs[count:])):
        target[...] = source[...].T[: target.shape[0]] if n == 0 else source[...]


def split_three(values):
    top = values.astype(BF16)
    rest = values - top.astype(F32)
    mid = rest.astype(BF16)
    return top, mid, (rest - mid.astype(F32)).astype(BF16)


def post_attn_body(
    kinds, attn_low, hid_s, mask, small_s, w_out, a_out, b_out, router, gain,
    low_out, resid, act_two, gate,
):
    low_out[...], resid[...], act_two[...], gate[...] = post_attn(
        kinds, attn_low[...], hid_s[...], mask[...], small_s[...], w_out, a_out, b_out, router, gain
    )


def post_attn(kinds, attn, hid, mask, sm, w_out, a_out, b_out, router, gain):
    low = (dot(attn, a_out[...]) * mask.astype(F32)).astype(BF16)
    res = hid.astype(F32) + (dot(attn, w_out[...]) + dot(low, b_out[...]))
    act = normed(res, gain)
    logits = dot_nt(act, router[...])
    lane = iota(logits.shape, 1)
    routed = jnp.where(lane < kinds, logits + sm, -1e30)
    top = jnp.max(routed, axis=1, keepdims=True)
    expo = jnp.exp(routed - top)
    prob = expo / jnp.sum(expo, axis=1, keepdims=True)
    return low, res, act, jnp.where(lane < kinds, prob, logits)


def place_slots(experts, small_s, slot, slot_rows):
    tok = slot.shape[0]
    lane = iota((tok, LANES), 1)
    first = small_s[:, CHOICE_LANE : CHOICE_LANE + 1].astype(jnp.int32)
    second = small_s[:, CHOICE_LANE + 1 : CHOICE_LANE + 2].astype(jnp.int32)
    hot = ((first == lane) | (second == lane)) & (lane < experts)
    hot_low = hot_matrix(hot)
    for blk in range(tok // ROW_BLOCK):
        lo, hi = blk * ROW_BLOCK, (blk + 1) * ROW_BLOCK
        tri = hot_matrix(iota((ROW_BLOCK, hi), 1) < lo + iota((ROW_BLOCK, hi), 0))
        rank = dot(tri, hot_low[:hi, :])
        slot[lo:hi, :] = jnp.where(hot[lo:hi, :], rank, -1.0)
    slot_rows[...] = slot[...].T


def fill_slots(eid, gate, act_two, dy_s, mask, slot_rows, target):
    row = slot_rows[pl.ds(eid, 1), :].astype(jnp.int32)
    pick = hot_matrix(row == iota((target.shape[0], row.shape[1]), 0))
    value = lane_value(gate[...], eid)
    scaled = (dy_s[...].astype(F32) * value).astype(BF16)
    target[:, :MODEL_WIDTH] = dot(pick, act_two[...]).astype(BF16)
    target[:, MODEL_WIDTH : 2 * MODEL_WIDTH] = dot(pick, scaled).astype(BF16)
    target[:, 2 * MODEL_WIDTH :] = dot(pick, mask[...]).astype(BF16)


def dispatch_body(experts, eids, small_s, gate, act_two, dy_s, mask, slot, sent, slot_rows):
    step = pl.program_id(0)

    @pl.when(step == 0)
    def _():
        place_slots(experts, small_s, slot, slot_rows)

    fill_slots(eids[step], gate, act_two, dy_s, mask, slot_rows, sent.at[0])


def ffn_math(
    rows, d_out, mask, w_gu, w_dn, a_gu, b_gu, a_dn, b_dn,
    ga_gu, gb_gu, ga_dn, gb_dn, acc_out, acc_dx, acc_low, acc_dlow,
):
    low_gu = (dot(rows, a_gu[...]) * mask).astype(BF16)
    dlow_dn = (dot_nt(d_out, b_dn[...]) * mask).astype(BF16)
    for ref in (acc_out, acc_dx, acc_low, acc_dlow):
        ref[...] = jnp.zeros_like(ref)

    def step(j, carry):
        lo = pl.multiple_of(j * HIDDEN_BLOCK, HIDDEN_BLOCK)
        g_cols = pl.ds(lo, HIDDEN_BLOCK)
        u_cols = pl.ds(pl.multiple_of(FEEDFWD_WIDTH + lo, HIDDEN_BLOCK), HIDDEN_BLOCK)
        gate = dot(rows, w_gu[:, g_cols]) + dot(low_gu, b_gu[:, g_cols])
        up = dot(rows, w_gu[:, u_cols]) + dot(low_gu, b_gu[:, u_cols])
        sig = 1.0 / (1.0 + jnp.exp(-gate))
        silu = gate * sig
        middle = (silu * up).astype(BF16)
        acc_out[...] += dot(middle, w_dn[g_cols, :])
        acc_low[...] += dot(middle, a_dn[g_cols, :])
        d_mid = dot_nt(d_out, w_dn[g_cols, :]) + dot_nt(dlow_dn, a_dn[g_cols, :])
        d_mid = d_mid.astype(BF16).astype(F32)
        d_gate = (d_mid * up * (sig * (1.0 + gate * (1.0 - sig)))).astype(BF16)
        d_up = (d_mid * silu).astype(BF16)
        acc_dx[...] += dot_nt(d_gate, w_gu[:, g_cols]) + dot_nt(d_up, w_gu[:, u_cols])
        acc_dlow[...] += dot_nt(d_gate, b_gu[:, g_cols]) + dot_nt(d_up, b_gu[:, u_cols])
        gb_gu[:, g_cols] += dot_tn(low_gu, d_gate)
        gb_gu[:, u_cols] += dot_tn(low_gu, d_up)
        ga_dn[g_cols, :] += dot_tn(middle, dlow_dn)
        return carry

    lax.fori_loop(0, FEEDFWD_WIDTH // HIDDEN_BLOCK, step, 0)
    low_dn = (acc_low[...] * mask).astype(BF16)
    result = (acc_out[...] + dot(low_dn, b_dn[...])).astype(BF16)
    gb_dn[...] += dot_tn(low_dn, d_out)
    dlow_gu = (acc_dlow[...] * mask).astype(BF16)
    d_rows = (acc_dx[...] + dot_nt(dlow_gu, a_gu[...])).astype(BF16)
    ga_gu[...] += dot_tn(rows, dlow_gu)
    return result, d_rows


def ffn_body(
    came, w_gu, w_dn, a_gu, b_gu, a_dn, b_dn,
    back, ga_gu, gb_gu, ga_dn, gb_dn, acc_out, acc_dx, acc_low, acc_dlow,
):
    @pl.when(pl.program_id(0) == 0)
    def _():
        for ref in (ga_gu, gb_gu, ga_dn, gb_dn):
            ref[...] = jnp.zeros_like(ref)

    back[0, :, :MODEL_WIDTH], back[0, :, MODEL_WIDTH:] = ffn_math(
        came[0, :, :MODEL_WIDTH], came[0, :, MODEL_WIDTH : 2 * MODEL_WIDTH],
        came[0, :, 2 * MODEL_WIDTH :].astype(F32), w_gu, w_dn, a_gu, b_gu, a_dn, b_dn,
        ga_gu, gb_gu, ga_dn, gb_dn, acc_out, acc_dx, acc_low, acc_dlow,
    )


def pair_ffn_body(
    had, last_sent, wide, mid, thin,
    returned, out_ga_gu, out_gb_gu, out_ga_dn, out_gb_dn,
    came, back, ga_gu, gb_gu, ga_dn, gb_dn, w_gu, w_dn, a_gu, b_gu, a_dn, b_dn, acc_out, acc_dx, acc_low, acc_dlow,
    load_sems, came_sems, back_sems, done_sems, last_sems,
):
    dp, z = lax.axis_index("dp"), lax.axis_index("expert")
    core, plane = dp % 2, z % 2

    def peer(k):
        return (dp + (k // 2) * (1 - 2 * core), z + (k % 2) * (1 - 2 * plane))

    start_kernel(None, [(peer(k), None) for k in (1, 2, 3)], 3)

    half = last_sent.shape[0] // 2
    early, late = pl.ds(0, half), pl.ds(half, half)

    def had_in(k):
        return pltpu.make_async_copy(had.at[k], came.at[k], came_sems.at[k])

    early_in = pltpu.make_async_copy(had.at[3, early], came.at[3, early], came_sems.at[3])
    last_out = pltpu.make_async_remote_copy(
        src_ref=last_sent.at[late], dst_ref=came.at[3, late], send_sem=last_sems.at[0],
        recv_sem=last_sems.at[1], device_id=peer(3), device_id_type=MESH_ID,
    )

    def result_out(k):
        return pltpu.make_async_remote_copy(
            src_ref=back.at[k], dst_ref=returned.at[k], send_sem=back_sems.at[k],
            recv_sem=done_sems.at[k], device_id=peer(k), device_id_type=MESH_ID,
        )

    last_out.start()
    for k in (1, 0, 2):
        had_in(k).start()
    early_in.start()

    gu_rows = w_gu.shape[0] // wide.shape[0]
    up_rows = b_gu.shape[0] // wide.shape[0]
    dn_rows = w_dn.shape[0] // wide.shape[0]
    plans = (
        (wide, 0, gu_rows, w_gu), (wide, gu_rows, up_rows, b_gu), (mid, 0, dn_rows, w_dn),
        (mid, dn_rows, up_rows, b_dn), (thin, 0, gu_rows, a_gu), (thin, gu_rows, dn_rows, a_dn),
    )

    def load(d, carry):
        for i, (source, at, count, target) in enumerate(plans):
            pltpu.make_async_copy(
                source.at[d, pl.ds(at, count)],
                target.at[pl.ds(pl.multiple_of(d * count, 16), count)],
                load_sems.at[i],
            ).start()
        return carry

    lax.fori_loop(0, wide.shape[0], load, 0)
    for ref in (ga_gu, gb_gu, ga_dn, gb_dn):
        ref[...] = jnp.zeros_like(ref)
    for i, (_, _, _, target) in enumerate(plans):
        pltpu.make_async_copy(target, target, load_sems.at[i]).wait()

    def source_step(s, carry):
        k = jnp.where(s < 2, 1 + 2 * s, 2 * s - 4)

        @pl.when(k != 3)
        def _():
            had_in(k).wait()

        @pl.when(k == 3)
        def _():
            early_in.wait()
            last_out.wait_recv()

        back[k, :, :MODEL_WIDTH], back[k, :, MODEL_WIDTH:] = ffn_math(
            came[k, :, :MODEL_WIDTH], came[k, :, MODEL_WIDTH : 2 * MODEL_WIDTH],
            came[k, :, 2 * MODEL_WIDTH :].astype(F32), w_gu, w_dn, a_gu, b_gu, a_dn, b_dn,
            ga_gu, gb_gu, ga_dn, gb_dn, acc_out, acc_dx, acc_low, acc_dlow,
        )

        @pl.when(k != 0)
        def _():
            result_out(k).start()

        return carry

    lax.fori_loop(0, 4, source_step, 0)
    for out, total in (
        (out_ga_gu, ga_gu), (out_gb_gu, gb_gu), (out_ga_dn, ga_dn), (out_gb_dn, gb_dn),
    ):
        out[...] = total[...].astype(BF16)
    own_out = pltpu.make_async_copy(back.at[0], returned.at[0], done_sems.at[0])
    own_out.start()
    own_out.wait()
    last_out.wait_send()
    for k in (1, 2, 3):
        result_out(k).wait_send()
        result_out(k).wait_recv()


def combine_body(
    experts, kinds, eids, resid, act_two, dy_s, gate, slot, small_s, low_out, attn_low, mask, came,
    w_out, a_out, b_out, router, const_value, gain,
    out_s, d_resid, d_attended, d_logits, ga_out, gb_out,
):
    @pl.when(pl.program_id(0) == 0)
    def _():
        ga_out[...] = jnp.zeros_like(ga_out)
        gb_out[...] = jnp.zeros_like(gb_out)

    rows = resid.shape[0]
    cap = came.shape[1]
    res = resid[...]
    act = act_two[...].astype(F32)
    dy_low = dy_s[...]
    dy = dy_low.astype(F32)
    lane = iota((rows, LANES), 1)
    levels = gate[...].T
    top = iota((CHOICE_ROWS, rows), 0)
    prob = jnp.where(top < kinds, levels[:CHOICE_ROWS], 0.0)

    def row(values, index):
        return jnp.sum(jnp.where(top == index, values, 0.0), axis=0, keepdims=True)

    picked = small_s[...].T
    first = picked[CHOICE_LANE : CHOICE_LANE + 1]
    second = picked[CHOICE_LANE + 1 : CHOICE_LANE + 2]

    def chosen(kind):
        return jnp.where((first == kind) | (second == kind), 1.0, 0.0)

    has_copy, has_zero, has_one = chosen(experts + 1), chosen(experts + 2), chosen(experts + 3)
    g_copy = has_copy * row(prob, experts + 1)
    g_zero = has_zero * row(prob, experts + 2)
    g_one = has_one * row(prob, experts + 3)

    def pair(at):
        left, right = levels[at : at + 1], levels[at + 1 : at + 2]
        high = jnp.maximum(left, right)
        e_left, e_right = jnp.exp(left - high), jnp.exp(right - high)
        scale = 1.0 / (e_left + e_right)
        return e_left * scale, e_right * scale

    a00, a01 = pair(CONST_LANE)
    a10, a11 = pair(CONST_LANE + 2)
    coef = g_copy + g_zero * a00 + g_one * a10
    factors = [coef, g_zero * a01, g_one * a11]
    factors += [row(prob, eids[k]) for k in range(came.shape[0])]
    spot = iota((LANES, rows), 0)
    columns = jnp.zeros((LANES, rows), F32)
    for n, factor in enumerate(factors):
        columns = jnp.where(spot == n, factor, columns)
    columns = columns.T
    v_zero, v_one = const_value[0:1, :], const_value[1:2, :]
    out = res + columns[:, 0:1] * act + columns[:, 1:2] * v_zero + columns[:, 2:3] * v_one
    d_act = columns[:, 0:1] * dy
    met = jnp.where(lane == 0, jnp.sum(dy * act, axis=1, keepdims=True), 0.0)
    met = jnp.where(lane == 1, jnp.sum(dy * v_zero, axis=1, keepdims=True), met)
    met = jnp.where(lane == 2, jnp.sum(dy * v_one, axis=1, keepdims=True), met)
    for k in range(came.shape[0]):
        place = lane_value(slot[...], eids[k]).astype(jnp.int32)
        pick = hot_matrix(place == iota((rows, cap), 1))
        result = dot(pick, came[k, :, :MODEL_WIDTH])
        d_act = d_act + dot(pick, came[k, :, MODEL_WIDTH:])
        met = jnp.where(lane == 3 + k, jnp.sum(dy * result, axis=1, keepdims=True), met)
        out = out + columns[:, 3 + k : 4 + k] * result
    out_s[...] = out.astype(BF16)
    met = met.T
    along_act, along_zero, along_one = met[0:1], met[1:2], met[2:3]
    d_gate = jnp.zeros((CHOICE_ROWS, rows), F32)
    for k in range(came.shape[0]):
        d_gate = jnp.where(top == eids[k], met[3 + k : 4 + k], d_gate)
    d_gate = jnp.where(top == experts + 1, has_copy * along_act, d_gate)
    d_gate = jnp.where(top == experts + 2, has_zero * (a00 * along_act + a01 * along_zero), d_gate)
    d_gate = jnp.where(top == experts + 3, has_one * (a10 * along_act + a11 * along_one), d_gate)
    d_logit = prob * (d_gate - jnp.sum(prob * d_gate, axis=0, keepdims=True))
    tail = iota((8, rows), 0)
    d_pair = jnp.zeros((8, rows), F32)
    for n, (g_val, left, right, along) in enumerate(
        ((g_zero, a00, a01, along_zero), (g_one, a10, a11, along_one))
    ):
        da_left, da_right = g_val * along_act, g_val * along
        level = left * da_left + right * da_right
        d_pair = jnp.where(tail == 2 * n, left * (da_left - level), d_pair)
        d_pair = jnp.where(tail == 2 * n + 1, right * (da_right - level), d_pair)
    mix = jnp.concatenate(
        [d_logit, jnp.zeros((CONST_LANE - CHOICE_ROWS, rows), F32), d_pair,
         jnp.zeros((LANES - CONST_LANE - 8, rows), F32)],
        axis=0,
    ).T
    d_logits[...] = mix
    mix_hi = mix.astype(BF16)
    mix_lo = (mix - mix_hi.astype(F32)).astype(BF16)
    d_act = d_act + (dot(mix_hi, router[...]) + dot(mix_lo, router[...]))
    scale = lax.rsqrt(jnp.mean(res * res, axis=-1, keepdims=True) + EPSILON)
    weighted = d_act * gain[...].astype(F32)
    d_res = dy + (
        scale * weighted
        - res * (scale * scale * scale) * jnp.mean(res * weighted, axis=-1, keepdims=True)
    )
    d_resid[...] = d_res
    d_attn = d_res.astype(BF16)
    dlow = (dot_nt(d_attn, b_out[...]) * mask[...].astype(F32)).astype(BF16)
    gb_out[...] += dot_tn(low_out[...], d_attn)
    ga_out[...] += dot_tn(attn_low[...], dlow)
    d_attended[...] = (dot_nt(d_attn, w_out[...]) + dot_nt(dlow, a_out[...])).astype(BF16)


def input_grad_body(
    d_query, d_key, d_value, low_qkv, act_one, mask, hid_s, d_resid, w_qkv, a_in, b_out, gain,
    high, lower, ga_qkv, gb_qkv,
):
    @pl.when(pl.program_id(0) == 0)
    def _():
        ga_qkv[...] = jnp.zeros_like(ga_qkv)
        gb_qkv[...] = jnp.zeros_like(gb_qkv)

    d_low = jnp.zeros((d_query.shape[0], LANES), F32)
    d_act = jnp.zeros((d_query.shape[0], MODEL_WIDTH), F32)
    for part, ref in enumerate((d_query, d_key, d_value)):
        cols = slice(part * MODEL_WIDTH, (part + 1) * MODEL_WIDTH)
        grad = ref[...]
        d_low = d_low + dot_nt(grad, b_out[:, cols])
        d_act = d_act + dot_nt(grad, w_qkv[:, cols])
        gb_qkv[:, cols] += dot_tn(low_qkv[...], grad)
    d_low = (d_low * mask[...].astype(F32)).astype(BF16)
    ga_qkv[...] += dot_tn(act_one[...], d_low)
    d_act = d_act + dot_nt(d_low, a_in[...])
    hid = hid_s[...].astype(F32)
    scale = lax.rsqrt(jnp.mean(hid * hid, axis=-1, keepdims=True) + EPSILON)
    weighted = d_act * gain[...].astype(F32)
    grad_hid = d_resid[...] + (
        scale * weighted
        - hid * (scale * scale * scale) * jnp.mean(hid * weighted, axis=-1, keepdims=True)
    )
    top = grad_hid.astype(BF16)
    high[...] = top
    lower[...] = (grad_hid - top.astype(F32)).astype(BF16)


def to_rows_body(place_col, out_s, d_logits, high, lower, out, grad_hidden, grad_gate):
    rows = out.shape[0]
    tok = out_s.shape[0]
    perm = hot_matrix(place_col[...] == iota((rows, tok), 1))
    out[...] = dot(perm, out_s[...]).astype(BF16)
    grad_hidden[...] = dot(perm, high[...]) + dot(perm, lower[...])
    logits = d_logits[...]
    top = logits.astype(BF16)
    rest = logits - top.astype(F32)
    mid = rest.astype(BF16)
    last = (rest - mid.astype(F32)).astype(BF16)
    grad_gate[...] = dot(perm, top) + (dot(perm, mid) + dot(perm, last))


class PairPlan:
    paired = True

    def __init__(self, dp, ex):
        self.ex = ex

    def expert_ids(self):
        own = lax.axis_index("expert") % 2 + 2 * (lax.axis_index("dp") % 2)
        return own ^ jnp.arange(self.ex, dtype=jnp.int32)


class AxisPlan:
    paired = False

    def __init__(self, dp, ex):
        self.dp, self.ex = dp, ex

    def gather(self, shard):
        return lax.all_gather(shard, "dp", axis=0)

    def expert_ids(self):
        return jnp.arange(self.ex, dtype=jnp.int32)

    def exchange(self, values):
        return lax.all_to_all(values, "expert", split_axis=0, concat_axis=0, tiled=True)

    def reduce(self, sums):
        return lax.psum_scatter(sums, "dp", scatter_dimension=0, tiled=True)[0].astype(F32)

    def reduce_all(self, sums):
        return lax.psum_scatter(
            sums, ("dp", "expert"), scatter_dimension=0, tiled=True
        )[0].astype(F32)


def shards(
    dp_size,
    expert_count,
    hidden_input,
    gate_carryover,
    sequence_length,
    token_stream_place,
    expert_choice_index,
    sequence_adapter,
    attention_gain,
    query_key_weight,
    output_weight,
    adapter_in_query,
    adapter_out_query,
    adapter_in_output,
    adapter_out_output,
    feedfwd_gain,
    router_weight,
    constant_gate,
    constant_value,
    gate_upward_weight,
    down_weight,
    adapter_in_gate,
    adapter_out_gate,
    adapter_in_down,
    adapter_out_down,
    output_gradient,
):
    tok = hidden_input.shape[0]
    width = MODEL_WIDTH
    kinds = expert_count + 4
    devices = dp_size * expert_count
    capacity = 5 * tok // (2 * kinds) // 8 * 8 + 8
    cap = -(-capacity // 16) * 16
    blocks = tok // ROW_BLOCK
    plan = (PairPlan if (dp_size, expert_count) == (8, 4) else AxisPlan)(dp_size, expert_count)

    a_rows, b_rows = query_key_weight.shape[0], adapter_out_query.shape[0]
    gu_rows, up_rows, dn_rows = (
        gate_upward_weight.shape[1], adapter_out_gate.shape[1], down_weight.shape[1],
    )
    gains = jnp.stack([attention_gain, feedfwd_gain])
    gain_one, gain_two = gains[0:1], gains[1:2]
    const_value = constant_value.astype(F32)
    sent_width = 2 * width + LANES
    full = whole
    hbm = pl.BlockSpec(memory_space=pl.ANY)
    vmem = pl.BlockSpec(memory_space=pltpu.VMEM)
    pairs = HEAD_COUNT // 2
    lse_rows = -(-HEAD_COUNT // 8) * 8
    smem = pl.BlockSpec(memory_space=pltpu.SMEM)
    eids = plan.expert_ids()
    if plan.paired:
        shapes = [
            sds((tok, width), BF16), sds((tok, width), BF16), sds((tok, LANES), F32),
            sds((tok, width), BF16), sds((tok, LANES), BF16), sds((tok, LANES), BF16),
            sds((1, tok), jnp.int32), sds((tok, LANES), F32), sds((tok, LANES), F32),
            sds((LANES, width), BF16),
            sds((tok, width), BF16), sds((tok, width), BF16), sds((tok, width), BF16),
            sds((width, 3 * width), BF16), sds((width, LANES), BF16), sds((LANES, 3 * width), BF16),
            sds((width, width), BF16), sds((width, LANES), BF16), sds((LANES, width), BF16),
            sds((tok, width), BF16), sds((lse_rows, tok), F32), sds((tok, LANES), BF16),
            sds((tok, width), F32), sds((tok, width), BF16), sds((tok, LANES), F32),
            sds((tok, LANES), F32),
        ]
        shard_rows = -(-(a_rows + b_rows) // 16) * 16
        packed = [
            (gu_rows + up_rows, 2 * FEEDFWD_WIDTH), (dn_rows + up_rows, width),
            (gu_rows + dn_rows, LANES),
        ]
        row_shape = (expert_count, cap, sent_width)
        (
            hid_s, dy_s, small_s, act_one, low_qkv, mask, starts, cosine, sine, router,
            query, key, value, w_qkv, a_qkv, b_qkv, w_out, a_out, b_out,
            attn_low, lse, low_out, resid, act_two, gate, slot,
            wide, mid, thin, came, last_sent,
        ) = pl.pallas_call(
            functools.partial(pair_front_body, kinds, a_rows, b_rows),
            in_specs=[smem] * 2 + [vmem] * 14 + [hbm] * 6,
            out_specs=[hbm] * (FRONT_KEPT + 5),
            out_shape=shapes
            + [sds((dp_size,) + shape, BF16) for shape in packed]
            + [sds(row_shape, BF16), sds(row_shape[1:], BF16)],
            scratch_shapes=[pltpu.VMEM(s.shape, s.dtype) for s in shapes]
            + [
                pltpu.VMEM((devices, shard_rows, 3 * width + LANES), BF16),
                pltpu.VMEM((devices, shard_rows, width + LANES), BF16),
                *[pltpu.VMEM(shape, BF16) for shape in packed],
                pltpu.VMEM((3,) + row_shape[1:], BF16),
                pltpu.VMEM((LANES, tok), F32),
                pltpu.SemaphoreType.DMA((2, 35)), pltpu.SemaphoreType.DMA((2, 35)),
                pltpu.SemaphoreType.DMA((2, 6)),
                pltpu.SemaphoreType.DMA((4, 8)), pltpu.SemaphoreType.DMA((4, 8)),
                pltpu.SemaphoreType.DMA((FRONT_KEPT,)), pltpu.SemaphoreType.DMA((6,)),
                pltpu.SemaphoreType.DMA((5,)), pltpu.SemaphoreType.DMA((4,)),
            ],
            compiler_params=pltpu.CompilerParams(
                vmem_limit_bytes=VMEM_BYTES, collective_id=4, has_side_effects=True
            ),
            name="pair_front",
        )(sequence_length, sequence_adapter, token_stream_place, hidden_input, output_gradient,
          gate_carryover.T, expert_choice_index.T, gains, router_weight.T,
          constant_gate.T,
          query_key_weight, output_weight, adapter_in_query, adapter_in_output, adapter_out_query,
          adapter_out_output, gate_upward_weight, adapter_out_gate, down_weight, adapter_out_down,
          adapter_in_gate, adapter_in_down)
        place = token_stream_place[0]
    else:
        pad_rows = -(a_rows + b_rows) % 16

        def pack(weight, adapter_in, adapter_out):
            lower = jnp.pad(adapter_out, ((0, pad_rows), (0, LANES)))
            return jnp.concatenate([jnp.concatenate([weight, adapter_in], axis=1), lower], axis=0)

        own_qkv = pack(query_key_weight, adapter_in_query, adapter_out_query)
        own_out = pack(output_weight, adapter_in_output, adapter_out_output)
        own_wide = jnp.concatenate([gate_upward_weight[0], adapter_out_gate[0]], axis=0)
        own_mid = jnp.concatenate([down_weight[0], adapter_out_down[0]], axis=0)
        own_thin = jnp.concatenate([adapter_in_gate[0], adapter_in_down[0]], axis=0)

        place = token_stream_place[0]
        ends = jnp.cumsum(sequence_length[0])
        begins = ends - sequence_length[0]
        stream = jnp.arange(tok, dtype=jnp.int32)
        seg = jnp.sum((stream[:, None] >= ends[None, :]).astype(jnp.int32), axis=1)
        seg_hot = seg[:, None] == jnp.arange(ends.shape[0], dtype=jnp.int32)[None, :]
        start = jnp.sum(jnp.where(seg_hot, begins[None, :], 0), axis=1)
        adapter = jnp.sum(jnp.where(seg_hot, sequence_adapter[0][None, :], 0), axis=1)
        half = HEAD_DIM // 2
        freq = jnp.exp(jnp.arange(half, dtype=F32) * (-math.log(10000.0) / half))
        angle = (stream - start).astype(F32)[:, None] * freq[None, :]
        cos, sin = jnp.cos(angle), jnp.sin(angle)
        cosine = jnp.concatenate([cos, cos, cos, cos], axis=1)
        sine = jnp.concatenate([-sin, sin, -sin, sin], axis=1)
        starts = start[None, :]
        mask = (jnp.arange(LANES)[None, :] // ADAPTER_RANK == adapter[:, None]).astype(BF16)
        top, middle, last = split_three(gate_carryover)
        gap = jnp.zeros((tok, 16 - kinds), BF16)
        small = jnp.concatenate(
            [top, gap, middle, gap, last, gap, expert_choice_index.astype(BF16),
             jnp.zeros((tok, LANES - CHOICE_LANE - 2), BF16)],
            axis=1,
        )
        router = jnp.concatenate(
            [router_weight.T, jnp.zeros((CONST_LANE - kinds, width), BF16), constant_gate.T,
             jnp.zeros((LANES - CONST_LANE - 4, width), BF16)],
            axis=0,
        )

        all_qkv = lax.all_gather(own_qkv, ("dp", "expert"), axis=0)
        all_out = lax.all_gather(own_out, ("dp", "expert"), axis=0)
        upper = slice(a_rows, a_rows + b_rows)
        w_qkv = all_qkv[:, :a_rows, : 3 * width].reshape(width, 3 * width)
        a_qkv = all_qkv[:, :a_rows, 3 * width :].reshape(width, LANES)
        b_qkv = all_qkv[:, upper, : 3 * width].reshape(LANES, 3 * width)
        w_out = all_out[:, :a_rows, :width].reshape(width, width)
        a_out = all_out[:, :a_rows, width:].reshape(width, LANES)
        b_out = all_out[:, upper, :width].reshape(LANES, width)
        wide, mid, thin = (plan.gather(w) for w in (own_wide, own_mid, own_thin))
        hid_s, dy_s, small_s, act_one, low_qkv, query, key, value = call(
            proj_in_body,
            (blocks,),
            [full((1, tok)), full((tok, width)), full((tok, width)), full((tok, LANES)),
             row_spec(LANES), row_spec(LANES), row_spec(LANES), full((1, width)),
             full((width, 3 * width)), full((width, LANES)), full((LANES, 3 * width))],
            [row_spec(width), row_spec(width), row_spec(LANES), row_spec(width), row_spec(LANES),
             row_spec(width), row_spec(width), row_spec(width)],
            [sds((tok, width), BF16), sds((tok, width), BF16), sds((tok, LANES), F32),
             sds((tok, width), BF16), sds((tok, LANES), BF16), sds((tok, width), BF16),
             sds((tok, width), BF16), sds((tok, width), BF16)],
            name="proj_in",
        )(place[None, :], hidden_input, output_gradient, small, cosine, sine, mask, gain_one,
          w_qkv, a_qkv, b_qkv)

        attn_low, lse = call(
            attention_fwd_body,
            (pairs,),
            [col_spec(tok)] * 3 + [full((1, tok))],
            [col_spec(tok), full((lse_rows, tok))],
            [sds((tok, width), BF16), sds((lse_rows, tok), F32)],
            name="attention_fwd",
        )(query, key, value, starts)

        low_out, resid, act_two, gate = call(
            functools.partial(post_attn_body, kinds),
            (blocks,),
            [row_spec(width), row_spec(width), row_spec(LANES), row_spec(LANES), full((width, width)),
             full((width, LANES)), full((LANES, width)), full((LANES, width)), full((1, width))],
            [row_spec(LANES), row_spec(width), row_spec(width), row_spec(LANES)],
            [sds((tok, LANES), BF16), sds((tok, width), F32), sds((tok, width), BF16),
             sds((tok, LANES), F32)],
            name="post_attn",
        )(attn_low, hid_s, mask, small_s, w_out, a_out, b_out, router, gain_two)

        slot, sent = call(
            functools.partial(dispatch_body, expert_count),
            (expert_count,),
            [smem, full((tok, LANES)), full((tok, LANES)), full((tok, width)), full((tok, width)),
             full((tok, LANES))],
            [full((tok, LANES)), pl.BlockSpec((1, cap, sent_width), lambda i: (i, 0, 0))],
            [sds((tok, LANES), F32), sds((expert_count, cap, sent_width), BF16)],
            scratch=[pltpu.VMEM((LANES, tok), F32)],
            name="dispatch",
        )(eids, small_s, gate, act_two, dy_s, mask)

    grad_shapes = [
        sds((width, LANES), F32), sds((LANES, 2 * FEEDFWD_WIDTH), F32),
        sds((FEEDFWD_WIDTH, LANES), F32), sds((LANES, width), F32),
    ]
    accumulators = [
        pltpu.VMEM((cap, width), F32), pltpu.VMEM((cap, width), F32),
        pltpu.VMEM((cap, LANES), F32), pltpu.VMEM((cap, LANES), F32),
    ]
    if plan.paired:
        returned, ga_gu, gb_gu, ga_dn, gb_dn = pl.pallas_call(
            pair_ffn_body,
            in_specs=[hbm] * 5,
            out_specs=[hbm] + [vmem] * 4,
            out_shape=[sds((expert_count, cap, 2 * width), BF16)]
            + [sds(g.shape, BF16) for g in grad_shapes],
            scratch_shapes=[
                pltpu.VMEM((expert_count, cap, sent_width), BF16),
                pltpu.VMEM((expert_count, cap, 2 * width), BF16),
                *[pltpu.VMEM(g.shape, F32) for g in grad_shapes],
                pltpu.VMEM((width, 2 * FEEDFWD_WIDTH), BF16), pltpu.VMEM((FEEDFWD_WIDTH, width), BF16),
                pltpu.VMEM((width, LANES), BF16), pltpu.VMEM((LANES, 2 * FEEDFWD_WIDTH), BF16),
                pltpu.VMEM((FEEDFWD_WIDTH, LANES), BF16), pltpu.VMEM((LANES, width), BF16),
                *accumulators,
                pltpu.SemaphoreType.DMA((6,)),
                *[pltpu.SemaphoreType.DMA((expert_count,)) for _ in range(3)],
                pltpu.SemaphoreType.DMA((2,)),
            ],
            compiler_params=pltpu.CompilerParams(
                vmem_limit_bytes=VMEM_BYTES, collective_id=1, has_side_effects=True
            ),
            name="pair_ffn",
        )(came, last_sent, wide, mid, thin)
    else:
        w_gu = wide[:, :gu_rows].reshape(width, 2 * FEEDFWD_WIDTH)
        b_gu = wide[:, gu_rows:].reshape(LANES, 2 * FEEDFWD_WIDTH)
        w_dn = mid[:, :dn_rows].reshape(FEEDFWD_WIDTH, width)
        b_dn = mid[:, dn_rows:].reshape(LANES, width)
        a_gu = thin[:, :gu_rows].reshape(width, LANES)
        a_dn = thin[:, gu_rows:].reshape(FEEDFWD_WIDTH, LANES)
        came = plan.exchange(sent)
        back, ga_gu, gb_gu, ga_dn, gb_dn = call(
            ffn_body,
            (expert_count,),
            [pl.BlockSpec((1, cap, sent_width), lambda i: (i, 0, 0)),
             full((width, 2 * FEEDFWD_WIDTH)), full((FEEDFWD_WIDTH, width)), full((width, LANES)),
             full((LANES, 2 * FEEDFWD_WIDTH)), full((FEEDFWD_WIDTH, LANES)), full((LANES, width))],
            [pl.BlockSpec((1, cap, 2 * width), lambda i: (i, 0, 0)), full((width, LANES)),
             full((LANES, 2 * FEEDFWD_WIDTH)), full((FEEDFWD_WIDTH, LANES)), full((LANES, width))],
            [sds((expert_count, cap, 2 * width), BF16)] + grad_shapes,
            scratch=accumulators,
            name="ffn",
        )(came, w_gu, w_dn, a_gu, b_gu, a_dn, b_dn)
        returned = plan.exchange(back)

    out_s, d_resid, d_attended, d_logits, ga_out, gb_out = call(
        functools.partial(combine_body, expert_count, kinds),
        (tok // ROW_BLOCK,),
        [smem, row_spec(width, ROW_BLOCK), row_spec(width, ROW_BLOCK), row_spec(width, ROW_BLOCK), row_spec(LANES, ROW_BLOCK), row_spec(LANES, ROW_BLOCK),
         row_spec(LANES, ROW_BLOCK), row_spec(LANES, ROW_BLOCK), row_spec(width, ROW_BLOCK), row_spec(LANES, ROW_BLOCK),
         full((expert_count, cap, 2 * width)), full((width, width)), full((width, LANES)),
         full((LANES, width)), full((LANES, width)), full((2, width)), full((1, width))],
        [row_spec(width, ROW_BLOCK), row_spec(width, ROW_BLOCK), row_spec(width, ROW_BLOCK), row_spec(LANES, ROW_BLOCK), full((width, LANES)),
         full((LANES, width))],
        [sds((tok, width), BF16), sds((tok, width), F32), sds((tok, width), BF16),
         sds((tok, LANES), F32), sds((width, LANES), F32), sds((LANES, width), F32)],
        name="combine",
    )(eids, resid, act_two, dy_s, gate, slot, small_s, low_out, attn_low, mask, returned,
      w_out, a_out, b_out, router, const_value, gain_two)

    if plan.paired:
        flow = dict(vmem_limit_bytes=VMEM_BYTES, has_side_effects=True)
        own_shapes = [
            sds((gu_rows, LANES), F32), sds((up_rows, 2 * FEEDFWD_WIDTH), F32),
            sds((dn_rows, LANES), F32), sds((up_rows, width), F32),
        ]
        plane_shapes = [
            sds((width // dp_size, LANES), F32), sds((LANES // dp_size, width), F32),
        ]
        d_query, d_key, d_value, *expert_owned, plane_ga, plane_gb = pl.pallas_call(
            pair_attention_bwd_body,
            grid=(pairs,),
            in_specs=[col_spec(tok)] * 5
            + [full((lse_rows, tok)), full((1, tok)), full((tok, LANES)), full((tok, LANES)),
               full((width, LANES)), full((LANES, width))]
            + [hbm] * 4,
            out_specs=[col_spec(tok)] * 3 + [full(s.shape) for s in own_shapes + plane_shapes],
            out_shape=[sds((tok, width), BF16)] * 3 + own_shapes + plane_shapes,
            scratch_shapes=[pltpu.VMEM((tok, LANES), F32), pltpu.VMEM((tok, LANES), F32)]
            + [pltpu.VMEM((dp_size,) + s.shape, BF16) for s in own_shapes]
            + [pltpu.VMEM((width, LANES), BF16), pltpu.VMEM((LANES, width), BF16)]
            + [pltpu.VMEM((dp_size - 1,) + s.shape, BF16) for s in plane_shapes]
            + [pltpu.SemaphoreType.DMA((4, dp_size)), pltpu.SemaphoreType.DMA((4, dp_size)),
               pltpu.SemaphoreType.DMA((2, dp_size)), pltpu.SemaphoreType.DMA((2, dp_size))],
            compiler_params=pltpu.CompilerParams(collective_id=2, **flow),
            name="pair_attention_bwd",
        )(query, key, value, d_attended, attn_low, lse, starts, cosine, sine, ga_out, gb_out,
          ga_gu, gb_gu, ga_dn, gb_dn)
        sum_shapes = [(width, LANES), (LANES, 3 * width)]
        got_shapes = [(dp_size - 1, a // dp_size, b) for a, b in sum_shapes]
        thin_rows = -(-a_rows // 16) * 16
        tail_shapes = [
            sds((tok, width), BF16), sds((tok, width), F32), sds((tok, LANES), F32),
            sds((a_rows, LANES), F32), sds((b_rows, 3 * width), F32),
            sds((a_rows, LANES), F32), sds((b_rows, width), F32),
        ]
        tail = pl.pallas_call(
            pair_tail_body,
            in_specs=[vmem] * 8 + [hbm] * 9,
            out_specs=[vmem] * 7,
            out_shape=tail_shapes,
            scratch_shapes=[
                *[pltpu.VMEM((tok, width), BF16) for _ in range(3)],
                pltpu.VMEM((tok, LANES), BF16), pltpu.VMEM((tok, width), BF16),
                pltpu.VMEM((tok, width), BF16), pltpu.VMEM((tok, width), F32),
                pltpu.VMEM((width, 3 * width), BF16), pltpu.VMEM((tok, width), BF16),
                pltpu.VMEM((tok, LANES), F32),
                pltpu.VMEM((tok, width), BF16), pltpu.VMEM((tok, width), BF16),
                pltpu.VMEM((tok, LANES), BF16),
                pltpu.VMEM((width, LANES), F32), pltpu.VMEM((LANES, 3 * width), F32),
                *[pltpu.VMEM(shape, BF16) for shape in sum_shapes + got_shapes],
                pltpu.VMEM((expert_count, thin_rows, 2 * LANES), BF16),
                pltpu.VMEM((expert_count, 4 * b_rows, width), BF16),
                pltpu.VMEM((expert_count - 1, thin_rows, 2 * LANES), BF16),
                pltpu.VMEM((expert_count - 1, 4 * b_rows, width), BF16),
                pltpu.SemaphoreType.DMA((9,)),
                pltpu.SemaphoreType.DMA((2, dp_size - 1)), pltpu.SemaphoreType.DMA((2, dp_size - 1)),
                pltpu.SemaphoreType.DMA((2, expert_count - 1)),
                pltpu.SemaphoreType.DMA((2, expert_count - 1)),
            ],
            compiler_params=pltpu.CompilerParams(collective_id=3, **flow),
            name="pair_tail",
        )(token_stream_place, mask, a_qkv, b_qkv, gain_one, plane_ga, plane_gb, d_logits,
          d_query, d_key, d_value, low_qkv, act_one, hid_s, d_resid, w_qkv, out_s)
        output, grad_hidden, grad_gate, *attn_owned = tail
        small_owned = [*attn_owned, *expert_owned]
        small_specs = [full(v.shape) for v in small_owned]
        grad_gate, output, grad_hidden, *owned = call(
            settle_body,
            (blocks,),
            [row_spec(LANES), row_spec(width), row_spec(width)] + small_specs,
            [pl.BlockSpec((kinds, ROW_BLOCK), lambda i: (0, i)), row_spec(width), row_spec(width)]
            + small_specs,
            [sds((kinds, tok), F32), sds((tok, width), BF16), sds((tok, width), F32)]
            + [sds(v.shape, F32) for v in small_owned],
            name="settle",
        )(grad_gate, output, grad_hidden, *small_owned)
        attn_owned, expert_owned = owned[:4], owned[4:]
        grad_gate = grad_gate.T
        return (
            output, grad_hidden, grad_gate[:, :kinds], *attn_owned,
            *[expert_owned[i][None] for i in range(4)],
        )

    owned_wide = plan.reduce(
        jnp.concatenate([gb_gu, gb_dn], axis=1).astype(BF16).reshape(dp_size, up_rows, -1)
    )
    owned_thin = plan.reduce(
        jnp.concatenate(
            [ga_gu.reshape(dp_size, gu_rows, LANES), ga_dn.reshape(dp_size, dn_rows, LANES)], axis=1
        ).astype(BF16)
    )

    d_query, d_key, d_value = call(
        attention_bwd_body,
        (pairs,),
        [col_spec(tok)] * 5
        + [full((lse_rows, tok)), full((1, tok)), full((tok, LANES)), full((tok, LANES))],
        [col_spec(tok)] * 3,
        [sds((tok, width), BF16)] * 3,
        scratch=[pltpu.VMEM((tok, LANES), F32), pltpu.VMEM((tok, LANES), F32)],
        name="attention_bwd",
    )(query, key, value, d_attended, attn_low, lse, starts, cosine, sine)

    high, lower, ga_qkv, gb_qkv = call(
        input_grad_body,
        (blocks,),
        [row_spec(width)] * 3 + [row_spec(LANES), row_spec(width), row_spec(LANES), row_spec(width),
         row_spec(width), full((width, 3 * width)), full((width, LANES)), full((LANES, 3 * width)),
         full((1, width))],
        [row_spec(width), row_spec(width), full((width, LANES)), full((LANES, 3 * width))],
        [sds((tok, width), BF16), sds((tok, width), BF16), sds((width, LANES), F32),
         sds((LANES, 3 * width), F32)],
        name="input_grad",
    )(d_query, d_key, d_value, low_qkv, act_one, mask, hid_s, d_resid, w_qkv, a_qkv, b_qkv,
      gain_one)

    owned = plan.reduce_all(
        jnp.concatenate(
            [
                ga_qkv.reshape(devices, b_rows, -1),
                ga_out.reshape(devices, b_rows, -1),
                gb_qkv.reshape(devices, b_rows, -1),
                gb_out.reshape(devices, b_rows, -1),
            ],
            axis=2,
        ).astype(BF16)
    )

    output, grad_hidden, grad_gate = call(
        to_rows_body,
        (blocks,),
        [row_spec(1), full((tok, width)), full((tok, LANES)), full((tok, width)),
         full((tok, width))],
        [row_spec(width), row_spec(width), row_spec(LANES)],
        [sds((tok, width), BF16), sds((tok, width), F32), sds((tok, LANES), F32)],
        name="to_rows",
    )(place[:, None], out_s, d_logits, high, lower)

    return (
        output,
        grad_hidden,
        grad_gate[:, :kinds],
        owned[:, :width].reshape(a_rows, LANES),
        owned[:, 2 * width : 5 * width],
        owned[:, width : 2 * width].reshape(a_rows, LANES),
        owned[:, 5 * width :],
        owned_thin[None, :gu_rows],
        owned_wide[None, :, : 2 * FEEDFWD_WIDTH],
        owned_thin[None, gu_rows:],
        owned_wide[None, :, 2 * FEEDFWD_WIDTH :],
    )


def solution(mesh):
    rows = P(("dp", "expert"), None)
    expert_rows = P("expert", "dp", None)
    in_specs = (
        (rows,) * 6 + (P(),) + (rows,) * 6 + (P(),) * 4 + (expert_rows,) * 6 + (rows,)
    )
    out_specs = (rows,) * 7 + (expert_rows,) * 4
    body = functools.partial(shards, mesh.shape["dp"], mesh.shape["expert"])
    return jax.shard_map(body, mesh=mesh, in_specs=in_specs, out_specs=out_specs, check_vma=False)
```

```python
import functools
import math

import jax
import jax.numpy as jnp
from jax import lax
from jax.experimental import pallas as pl
from jax.experimental.pallas import tpu as pltpu
from jax.sharding import PartitionSpec as P

MODEL_WIDTH = 768
HEAD_COUNT = 12
HEAD_DIM = 64
FEEDFWD_WIDTH = 2048
ADAPTER_RANK = 16
ROW_BLOCK = 256
HIDDEN_BLOCK = 1024
LANES = 128
CONST_LANE = 64
CHOICE_LANE = 48
CHOICE_ROWS = 16
EPSILON = 1e-06
VMEM_BYTES = 60 * 2**20
FRONT_KEPT = 26
MESH_ID = pl.DeviceIdType.MESH

F32 = jnp.float32
BF16 = jnp.bfloat16


def dot(a, b):
    return jnp.dot(a, b, preferred_element_type=F32)


def dot_nt(a, b):
    return lax.dot_general(a, b, (((1,), (1,)), ((), ())), preferred_element_type=F32)


def dot_tn(a, b):
    return lax.dot_general(a, b, (((0,), (0,)), ((), ())), preferred_element_type=F32)


def iota(shape, dim):
    return lax.broadcasted_iota(jnp.int32, shape, dim)


def hot_matrix(condition):
    return jnp.where(condition, 1.0, 0.0).astype(BF16)


def whole(shape):
    zeros = (0,) * len(shape)
    return pl.BlockSpec(shape, lambda *_: zeros)


def row_spec(width, rows=ROW_BLOCK):
    return pl.BlockSpec((rows, width), lambda i: (i, 0))


def col_spec(rows, width=LANES):
    return pl.BlockSpec((rows, width), lambda j: (0, j))


def sds(shape, dtype):
    return jax.ShapeDtypeStruct(shape, dtype)


def call(body, grid, in_specs, out_specs, out_shape, scratch=(), name=None):
    return pl.pallas_call(
        body,
        grid=grid,
        in_specs=in_specs,
        out_specs=out_specs,
        out_shape=out_shape,
        scratch_shapes=list(scratch),
        compiler_params=pltpu.CompilerParams(vmem_limit_bytes=VMEM_BYTES),
        name=name,
    )


def half_swap(values):
    lane = iota(values.shape, 1)
    up = pltpu.roll(values, 32, 1)
    down = pltpu.roll(values, LANES - 32, 1)
    return jnp.where(lane % HEAD_DIM < HEAD_DIM // 2, down, up)


def lane_value(values, lane_id):
    return jnp.sum(jnp.where(iota(values.shape, 1) == lane_id, values, 0.0), axis=1, keepdims=True)


def proj_in_body(
    place_row, hidden, upstream, small, cosine, sine, mask, gain, w_qkv, a_in, b_out,
    hid_s, dy_s, small_s, act_one, low_qkv, query, key, value,
):
    rows = hid_s.shape[0]
    base = pl.program_id(0) * rows
    perm = hot_matrix(place_row[...] == base + iota((rows, place_row.shape[1]), 0))
    hid = dot(perm, hidden[...])
    hid_s[...] = hid.astype(BF16)
    dy_s[...] = dot(perm, upstream[...]).astype(BF16)
    parts = dot(perm, small[...])
    small_s[...] = parts + (pltpu.roll(parts, LANES - 16, 1) + pltpu.roll(parts, LANES - 32, 1))
    act = normed(hid, gain)
    act_one[...] = act
    low, q_val, k_val, value[...] = project(
        act, mask[...], cosine[...], sine[...], w_qkv, a_in, b_out
    )
    low_qkv[...] = low
    query[...], key[...] = q_val, k_val


def normed(values, gain):
    scale = lax.rsqrt(jnp.mean(values * values, axis=-1, keepdims=True) + EPSILON)
    return (values * scale * gain[...].astype(F32)).astype(BF16)


def project(act, mask, cos, sin, w_qkv, a_in, b_out):
    low = (dot(act, a_in[...]) * mask.astype(F32)).astype(BF16)
    turned = []
    for start, factor in ((0, HEAD_DIM**-0.5), (MODEL_WIDTH, 1.0)):
        cols = slice(start, start + MODEL_WIDTH)
        vals = dot(act, w_qkv[:, cols]) + dot(low, b_out[:, cols])
        pieces = []
        for c in range(MODEL_WIDTH // LANES):
            piece = vals[:, c * LANES : (c + 1) * LANES]
            piece = (piece * cos + half_swap(piece) * sin).astype(BF16)
            pieces.append(piece if factor == 1.0 else piece * jnp.asarray(factor, BF16))
        turned.append(jnp.concatenate(pieces, axis=1))
    value = dot(act, w_qkv[:, 2 * MODEL_WIDTH :]) + dot(low, b_out[:, 2 * MODEL_WIDTH :])
    return low, turned[0], turned[1], value.astype(BF16)


def head_mask(shape, head):
    lane = iota(shape, 1)
    return (lane >= head * HEAD_DIM) & (lane < (head + 1) * HEAD_DIM)


def attention_fwd_body(query, key, value, starts, attended, lse):
    attention_fwd_pair(pl.program_id(0), query, key, value, starts, attended, lse)


def visible(lo, hi, starts):
    rows = iota((hi, hi - lo), 0)
    return (rows <= lo + iota((hi, hi - lo), 1)) & (rows >= starts[:, lo:hi])


def attention_fwd_pair(pair, query, key, value, starts, attended, lse):
    size = ROW_BLOCK
    zero = jnp.zeros((), BF16)
    for blk in range(query.shape[0] // size):
        lo, hi = blk * size, (blk + 1) * size
        q_blk = query[lo:hi, :]
        k_all = key[:hi, :]
        v_all = value[:hi, :]
        allowed = visible(lo, hi, starts)
        total = jnp.zeros((size, LANES), F32)
        for head in range(2):
            mine = head_mask((size, LANES), head)
            scores = dot_nt(k_all, jnp.where(mine, q_blk, zero))
            scores = jnp.where(allowed, scores, -1000000000.0)
            top = jnp.max(scores, axis=0, keepdims=True)
            expo = jnp.exp(scores - top)
            norm = jnp.sum(expo, axis=0, keepdims=True)
            prob = (expo * (1.0 / norm)).astype(BF16)
            total = jnp.where(mine, dot_tn(prob, v_all), total)
            lse[pl.ds(2 * pair + head, 1), lo:hi] = top + jnp.log(norm)
        attended[lo:hi, :] = total.astype(BF16)


def attention_bwd_body(
    query, key, value, dout, attended, lse, starts, cosine, sine, d_query, d_key, d_value, kacc, vacc
):
    pair = pl.program_id(0)
    tok = query.shape[0]
    size = ROW_BLOCK
    zero = jnp.zeros((), BF16)
    kacc[...] = jnp.zeros_like(kacc)
    vacc[...] = jnp.zeros_like(vacc)
    for blk in range(tok // size):
        lo, hi = blk * size, (blk + 1) * size
        q_blk = query[lo:hi, :]
        do_blk = dout[lo:hi, :]
        k_all = key[:hi, :]
        v_all = value[:hi, :]
        allowed = visible(lo, hi, starts)
        prod = (do_blk.astype(F32) * attended[lo:hi, :].astype(F32)).T
        probs, dscores, q_heads, do_heads = [], [], [], []
        q_total = jnp.zeros((size, LANES), F32)
        for head in range(2):
            mine = head_mask((size, LANES), head)
            q_heads.append(jnp.where(mine, q_blk, zero))
            do_heads.append(jnp.where(mine, do_blk, zero))
            lse_head = lse[pl.ds(2 * pair + head, 1), lo:hi]
            delta = jnp.sum(
                prod[head * HEAD_DIM : (head + 1) * HEAD_DIM], axis=0, keepdims=True
            )
            scores = dot_nt(k_all, q_heads[head])
            prob = jnp.where(allowed, jnp.exp(scores - lse_head), 0.0)
            dprob = dot_nt(v_all, do_heads[head])
            dscores.append((prob * (dprob - delta)).astype(BF16))
            probs.append(prob.astype(BF16))
            k_head = jnp.where(head_mask((hi, LANES), head), k_all, zero)
            q_total = q_total + dot_tn(dscores[head], k_head)
        kacc[:hi, :] += dot(jnp.concatenate(dscores, axis=1), jnp.concatenate(q_heads, axis=0))
        vacc[:hi, :] += dot(jnp.concatenate(probs, axis=1), jnp.concatenate(do_heads, axis=0))
        q_total = q_total * HEAD_DIM**-0.5
        d_query[lo:hi, :] = (
            q_total * cosine[lo:hi, :] - half_swap(q_total) * sine[lo:hi, :]
        ).astype(BF16)
    for blk in range(tok // size):
        lo, hi = blk * size, (blk + 1) * size
        k_total = kacc[lo:hi, :]
        d_key[lo:hi, :] = (
            k_total * cosine[lo:hi, :] - half_swap(k_total) * sine[lo:hi, :]
        ).astype(BF16)
    d_value[...] = vacc[...].astype(BF16)


def start_kernel(send_to, hear_from, count):
    barrier = pltpu.get_barrier_semaphore()
    for device, remote in hear_from:
        if remote is None:
            pl.semaphore_signal(barrier, inc=1, device_id=device, device_id_type=MESH_ID)
        else:

            @pl.when(remote)
            def _(device=device):
                pl.semaphore_signal(barrier, inc=1, device_id=device, device_id_type=MESH_ID)

    pl.semaphore_wait(barrier, count)


def pair_front_body(
    kinds, a_rows, b_rows,
    lengths, adapters, place_row, hidden, upstream, carry, choices, gains,
    router_in, const_in, in_qkv, in_out, in_a_qkv, in_a_out, in_b_qkv, in_b_out,
    in_gu, in_b_gu, in_dn, in_b_dn, in_a_gu, in_a_dn, *rest,
):
    count = FRONT_KEPT
    outs, rest = rest[:count], rest[count:]
    (all_wide, all_mid, all_thin, came, last_sent), rest = rest[:5], rest[5:]
    kept, rest = rest[:count], rest[count:]
    (
        hid_s, dy_s, small_s, act_one, low_qkv, mask, starts, cosine, sine, router,
        query, key, value, w_qkv, a_qkv, b_qkv, w_out, a_out, b_out,
        attn_low, lse, low_out, resid, act_two, gate, slot,
    ) = kept
    (
        g_qkv, g_out, own_wide, own_mid, own_thin, sent, slot_rows,
        a_send, a_recv, z_send, e_send, e_recv, out_sems, own_sems, row_send, row_recv,
    ) = rest
    gain_one, gain_two = gains[0:1, :], gains[1:2, :]
    dp, z = lax.axis_index("dp"), lax.axis_index("expert")
    core, x_bit, y_bit = dp % 2, dp // 2 % 2, dp // 4
    across = dp + 1 - 2 * core
    x_dev, y_dev = dp + 2 - 4 * x_bit, dp + 4 - 8 * y_bit
    diag = x_dev + 4 - 8 * y_bit
    far = (z + 2) % 4
    home = z // 2
    columns = (dp, x_dev, y_dev, diag)
    tok = hidden.shape[0]
    blocks = tok // ROW_BLOCK

    def remote(source, target, send, recv, device):
        return pltpu.make_async_remote_copy(
            src_ref=source, dst_ref=target, send_sem=send, recv_sem=recv,
            device_id=device, device_id_type=MESH_ID,
        )

    packs = (g_qkv, g_out)

    def at(kind, back):
        return columns[kind] * 4 + (z + 4 - back) % 4

    def shard(p, kind, back, rows=None):
        view = packs[p].at[at(kind, back)]
        if rows is None:
            return view
        half = packs[p].shape[1] // 2
        return view.at[pl.ds(rows * half, half)]

    def z_up(p, t):
        view = shard(p, 0, t)
        return remote(view, view, z_send.at[p, t], a_recv.at[p, t], (dp, z + 1))

    def z_down(p, t):
        view = shard(p, 0, (4 - t) % 4)
        return remote(view, view, z_send.at[p, 3 + t], a_recv.at[p, 2 - t], (dp, z - 1))

    def z_sends(p, t, act):
        @pl.when((z < 3) & (z >= t))
        def _():
            act(z_up(p, t))

        @pl.when((z > 0) & (z + t <= 3))
        def _():
            act(z_down(p, t))

    def to_x(p, back):
        return remote(
            shard(p, 0, back), shard(p, 0, back), a_send.at[p, 3 + back], a_recv.at[p, 3 + back],
            (x_dev, z),
        )

    def to_y(p, back):
        return remote(
            shard(p, 0, back), shard(p, 0, back), a_send.at[p, 7 + back], a_recv.at[p, 7 + back],
            (y_dev, z),
        )

    def relay_y(p, back):
        return remote(
            shard(p, 1, back, 0), shard(p, 1, back, 0), a_send.at[p, 11 + back],
            a_recv.at[p, 11 + back], (y_dev, z),
        )

    def relay_x(p, back):
        return remote(
            shard(p, 2, back, 1), shard(p, 2, back, 1), a_send.at[p, 15 + back],
            a_recv.at[p, 15 + back], (x_dev, z),
        )

    def to_core(p, kind, back):
        sem = 19 + 4 * kind + back
        return remote(
            shard(p, kind, back), shard(p, kind, back), a_send.at[p, sem], a_recv.at[p, sem],
            (across, z),
        )

    half_wide = own_wide.shape[1] // 2
    parts = []
    for own, everything, cols in (
        (own_mid, all_mid, None), (own_thin, all_thin, None),
        (own_wide, all_wide, (0, half_wide)), (own_wide, all_wide, (half_wide, half_wide)),
    ):
        if cols is None:
            parts.append((own, lambda d, ref=everything: ref.at[d]))
        else:
            parts.append(
                (own.at[:, pl.ds(*cols)], lambda d, ref=everything, c=cols: ref.at[d, :, pl.ds(*c)])
            )
    chunks = ((0, 1), (2,), (3,))

    def first_far(a):
        return remote(
            parts[a][0], parts[a][1](dp), e_send.at[a, 0], e_recv.at[a, core],
            (dp - core + home, far),
        )

    def first_across(a):
        return remote(
            parts[a][0], parts[a][1](dp), e_send.at[a, 1], e_recv.at[a, core], (across, z)
        )

    def first_keep(a):
        return pltpu.make_async_copy(parts[a][0], parts[a][1](dp), e_recv.at[a, core])

    def first_arrival(a, i):
        view = parts[a][1](dp - core + i)
        return remote(view, view, e_send.at[a, 0], e_recv.at[a, i], (dp, far))

    def expert_hop(a, column, i, sem, device):
        view = parts[a][1](column - core + i)
        return remote(view, view, e_send.at[a, sem], e_recv.at[a, sem], (device, z))

    def expert_x(a, i):
        return expert_hop(a, dp, i, 2 + i, x_dev)

    def expert_y(a, i):
        return expert_hop(a, dp, i, 4 + i, y_dev)

    def expert_relay_y(a):
        return expert_hop(a, x_dev, 0, 6, y_dev)

    def expert_relay_x(a):
        return expert_hop(a, y_dev, 1, 7, x_dev)

    def expert_first(c):
        for a in chunks[c]:
            first_far(a).start()

            @pl.when(core == home)
            def _(a=a):
                first_keep(a).start()

            @pl.when(core != home)
            def _(a=a):
                first_across(a).start()

    def at_home(step, *args):
        @pl.when(core == home)
        def _():
            step(*args)

    def abroad(step, *args):
        @pl.when(core != home)
        def _():
            step(*args)

    def send_sides(a):
        for i in range(2):
            expert_x(a, i).start()
            expert_y(a, i).start()

    def spread_home(c):
        for a in chunks[c]:
            first_keep(a).wait()
            first_arrival(a, 1 - core).wait_recv()
            send_sides(a)

    def spread_far(c):
        for a in chunks[c]:
            for i in range(2):
                first_arrival(a, i).wait_recv()
            send_sides(a)

    def expert_relay(c):
        for a in chunks[c]:
            for i in range(2):
                expert_hop(a, x_dev, i, 2 + i, x_dev).wait_recv()
            expert_relay_y(a).start()
            for i in range(2):
                expert_hop(a, y_dev, i, 4 + i, y_dev).wait_recv()
            expert_relay_x(a).start()

    def expert_finish(c):
        for a in chunks[c]:
            expert_hop(a, diag, 0, 6, y_dev).wait_recv()
            expert_hop(a, diag, 1, 7, x_dev).wait_recv()
            first_far(a).wait_send()

            @pl.when(core != home)
            def _(a=a):
                first_across(a).wait_send()

            for i in range(2):
                expert_x(a, i).wait_send()
                expert_y(a, i).wait_send()
            expert_relay_y(a).wait_send()
            expert_relay_x(a).wait_send()

    gu_rows, up_rows, dn_rows = in_gu.shape[1], in_b_gu.shape[1], in_dn.shape[1]
    own_loads = [
        pltpu.make_async_copy(source.at[0], target.at[pl.ds(at_row, rows)], own_sems.at[i])
        for i, (source, target, at_row, rows) in enumerate((
            (in_gu, own_wide, 0, gu_rows), (in_b_gu, own_wide, gu_rows, up_rows),
            (in_dn, own_mid, 0, dn_rows), (in_b_dn, own_mid, dn_rows, up_rows),
            (in_a_gu, own_thin, 0, gu_rows), (in_a_dn, own_thin, gu_rows, dn_rows),
        ))
    ]
    for load in own_loads:
        load.start()
    for gathered, weight, adapter_in, adapter_out in (
        (g_qkv, in_qkv, in_a_qkv, in_b_qkv), (g_out, in_out, in_a_out, in_b_out),
    ):
        spare = gathered.shape[1] - a_rows - b_rows
        wide_cols = weight.shape[1]
        gathered[at(0, 0), :, :wide_cols] = jnp.concatenate(
            [weight[...].astype(F32), adapter_out[...].astype(F32), jnp.zeros((spare, wide_cols), F32)],
            axis=0,
        ).astype(BF16)
        gathered[at(0, 0), :, wide_cols:] = jnp.concatenate(
            [adapter_in[...].astype(F32), jnp.zeros((spare + b_rows, LANES), F32)], axis=0
        ).astype(BF16)
    next_z = z + 1 - 2 * (z % 2)
    peers = [(x_dev, z), (y_dev, z), (across, z), (across, far), (across, next_z)]
    peers += [(dp, (z + j) % 4) for j in (1, 2, 3)]
    start_kernel(None, [(device, None) for device in peers], len(peers))
    def send_own(p):
        z_sends(p, 0, lambda copy: copy.start())
        to_x(p, 0).start()
        to_y(p, 0).start()
        to_core(p, 0, 0).start()

    send_own(0)
    router[...] = jnp.concatenate(
        [router_in[...].astype(F32), jnp.zeros((CONST_LANE - kinds, MODEL_WIDTH), F32),
         const_in[...].astype(F32), jnp.zeros((LANES - CONST_LANE - 4, MODEL_WIDTH), F32)],
        axis=0,
    ).astype(BF16)
    small_s[...] = jnp.zeros_like(small_s)
    carry_parts = split_three(carry[...])
    choices_low = choices[...].astype(F32).astype(BF16)
    half_dim = HEAD_DIM // 2
    freq = jnp.exp(
        (iota((1, LANES), 1) % half_dim).astype(F32) * (-math.log(10000.0) / half_dim)
    )
    sign = jnp.where(iota((1, LANES), 1) % HEAD_DIM < half_dim, -1.0, 1.0)

    def block_rows(b):
        return pl.ds(pl.multiple_of(b * ROW_BLOCK, ROW_BLOCK), ROW_BLOCK)

    def arrange(b, carry_on):
        rows = block_rows(b)
        perm = hot_matrix(place_row[...] == b * ROW_BLOCK + iota((ROW_BLOCK, tok), 0))
        hid = dot(perm, hidden[...])
        hid_s[rows, :] = hid.astype(BF16)
        act_one[rows, :] = normed(hid, gain_one)
        return carry_on

    def arrange_rest(b, carry_on):
        rows = block_rows(b)
        perm = hot_matrix(place_row[...] == b * ROW_BLOCK + iota((ROW_BLOCK, tok), 0))
        dy_s[rows, :] = dot(perm, upstream[...]).astype(BF16)
        top, mid, last = carry_parts
        small_s[rows, :kinds] = dot_nt(perm, top) + (dot_nt(perm, mid) + dot_nt(perm, last))
        small_s[rows, CHOICE_LANE : CHOICE_LANE + 2] = dot_nt(perm, choices_low)
        return carry_on

    place = iota((1, tok), 1)
    begin_row = jnp.zeros((1, tok), jnp.int32)
    begin = 0
    for n in range(1, lengths.shape[1]):
        begin = begin + lengths[0, n - 1]
        begin_row = jnp.where(place >= begin, begin, begin_row)
    starts[...] = begin_row

    def positions(b, carry_on):
        rows = block_rows(b)
        stream = b * ROW_BLOCK + iota((ROW_BLOCK, 1), 0)
        start = jnp.zeros((ROW_BLOCK, 1), jnp.int32)
        adapter = start + adapters[0, 0]
        begin = 0
        for n in range(1, lengths.shape[1]):
            begin = begin + lengths[0, n - 1]
            start = jnp.where(stream >= begin, begin, start)
            adapter = jnp.where(stream >= begin, adapters[0, n], adapter)
        mask[rows, :] = hot_matrix(iota((ROW_BLOCK, LANES), 1) // ADAPTER_RANK == adapter)
        angle = (stream - start).astype(F32) * freq
        cosine[rows, :] = jnp.cos(angle)
        sine[rows, :] = jnp.sin(angle) * sign
        return carry_on

    lax.fori_loop(0, blocks, arrange, 0)

    at_end = (z == 0) | (z == 3)
    order = (
        jnp.where(z == 0, 3, 1), jnp.where(at_end, 2, 3),
        jnp.where(z == 0, 1, jnp.where(z == 3, 3, 2)),
    )

    def spread_shard(p, back):
        view = shard(p, 0, back)
        remote(view, view, z_send.at[p, 0], a_recv.at[p, back - 1], (dp, z)).wait_recv()
        to_x(p, back).start()
        to_y(p, back).start()
        to_core(p, 0, back).start()

    def from_z(p, t):
        @pl.when(z > t)
        def _():
            spread_shard(p, 1 + t)

        @pl.when(z + t < 3)
        def _():
            spread_shard(p, 3 - t)

        if t < 2:
            z_sends(p, t + 1, lambda copy: copy.start())

    def from_sides(p, back):
        view = shard(p, 1, back)
        remote(view, view, a_send.at[p, 3 + back], a_recv.at[p, 3 + back], (x_dev, z)).wait_recv()
        relay_y(p, back).start()
        to_core(p, 1, back).start()
        view = shard(p, 2, back)
        remote(view, view, a_send.at[p, 7 + back], a_recv.at[p, 7 + back], (y_dev, z)).wait_recv()
        relay_x(p, back).start()
        to_core(p, 2, back).start()

    def from_diag(p, back):
        view = shard(p, 3, back, 0)
        remote(view, view, a_send.at[p, 11 + back], a_recv.at[p, 11 + back], (y_dev, z)).wait_recv()
        view = shard(p, 3, back, 1)
        remote(view, view, a_send.at[p, 15 + back], a_recv.at[p, 15 + back], (x_dev, z)).wait_recv()
        to_core(p, 3, back).start()

    for t in range(3):
        from_z(0, t)
    send_own(1)
    from_sides(0, 0)
    lax.fori_loop(0, 2, arrange_rest, 0)
    from_sides(0, order[0])
    lax.fori_loop(2, 4, arrange_rest, 0)
    from_sides(0, order[1])
    lax.fori_loop(4, blocks, arrange_rest, 0)
    from_sides(0, order[2])
    for t in range(3):
        from_z(1, t)
    for load in own_loads:
        load.wait()
    for c in range(len(chunks)):
        expert_first(c)
    for back in (0,) + order[:2]:
        from_diag(0, back)
    lax.fori_loop(0, blocks, positions, 0)
    from_diag(0, order[2])
    core_columns = (across, x_dev + across - dp, y_dev + across - dp, diag + across - dp)

    def from_core(p):
        def body(back, carry):
            for kind in range(4):
                view = packs[p].at[core_columns[kind] * 4 + (z + 4 - back) % 4]
                sem = 19 + 4 * kind + back
                remote(view, view, a_send.at[p, sem], a_recv.at[p, sem], (across, z)).wait_recv()
            return carry

        lax.fori_loop(0, 4, body, 0)

    width = MODEL_WIDTH
    total = g_qkv.shape[0]

    def lay_rows(i, carry, gathered, targets):
        pair = [gathered[2 * i + n, :a_rows, :].astype(F32) for n in range(2)]
        both = jnp.concatenate(pair, axis=0).astype(BF16)
        rows = pl.ds(pl.multiple_of(i * 2 * a_rows, 16), 2 * a_rows)
        start = 0
        for target in targets:
            target[rows, :] = both[:, start : start + target.shape[1]]
            start += target.shape[1]
        return carry

    def lay_ups(i, carry, gathered, target):
        group = 16 // b_rows
        pieces = [
            gathered[group * i + n, a_rows : a_rows + b_rows, : target.shape[1]].astype(F32)
            for n in range(group)
        ]
        rows = pl.ds(pl.multiple_of(i * 16, 16), 16)
        target[rows, :] = jnp.concatenate(pieces, axis=0).astype(BF16)
        return carry

    def lay(gathered, targets, ups):
        lax.fori_loop(
            0, total // 2, functools.partial(lay_rows, gathered=gathered, targets=targets), 0
        )
        lax.fori_loop(
            0, total * b_rows // 16, functools.partial(lay_ups, gathered=gathered, target=ups), 0
        )

    def flush(first, last):
        return [
            pltpu.make_async_copy(kept[i], outs[i], out_sems.at[i]) for i in range(first, last)
        ]

    for back in (0,) + order:
        from_sides(1, back)
    for c in range(len(chunks)):
        at_home(spread_home, c)
    from_core(0)
    lay(g_qkv, (w_qkv, a_qkv), b_qkv)

    def projection(b, carry):
        rows = block_rows(b)
        low_qkv[rows, :], query[rows, :], key[rows, :], value[rows, :] = project(
            act_one[rows, :], mask[rows, :], cosine[rows, :], sine[rows, :], w_qkv, a_qkv, b_qkv
        )

        return carry

    lax.fori_loop(0, blocks, projection, 0)
    abroad(spread_far, 0)
    for copy in flush(0, 16):
        copy.start()
    lse[...] = jnp.zeros_like(lse)

    def attention(pair, carry):
        cols = pl.ds(pl.multiple_of(pair * LANES, LANES), LANES)
        attention_fwd_pair(
            pair, query.at[:, cols], key.at[:, cols], value.at[:, cols], starts,
            attn_low.at[:, cols], lse,
        )

        @pl.when(pair == 0)
        def _():
            for back in (0,) + order:
                from_diag(1, back)
            at_home(expert_relay, 0)

        @pl.when(pair == 2)
        def _():
            at_home(expert_relay, 1)

        @pl.when(pair == 3)
        def _():
            abroad(spread_far, 1)
            abroad(expert_relay, 0)

        @pl.when(pair == 4)
        def _():
            at_home(expert_relay, 2)

        return carry

    lax.fori_loop(0, HEAD_COUNT // 2, attention, 0)
    from_core(1)
    lay(g_out, (w_out, a_out), b_out)
    for copy in flush(16, 21):
        copy.start()

    def after(b, carry):
        rows = block_rows(b)
        low_out[rows, :], resid[rows, :], act_two[rows, :], gate[rows, :] = post_attn(
            kinds, attn_low[rows, :], hid_s[rows, :], mask[rows, :], small_s[rows, :],
            w_out, a_out, b_out, router, gain_two,
        )
        return carry

    lax.fori_loop(0, blocks, after, 0)
    abroad(spread_far, 2)
    abroad(expert_relay, 1)
    place_slots(4, small_s, slot, slot_rows)
    for copy in flush(21, FRONT_KEPT):
        copy.start()

    def rows_out(k):
        device = ((dp, next_z), (across, z))[k - 1]
        return remote(sent.at[k], came.at[k], row_send.at[k], row_recv.at[k], device)

    last_local = pltpu.make_async_copy(sent.at[0], last_sent, row_send.at[3])
    own_local = pltpu.make_async_copy(sent.at[0], came.at[0], row_send.at[0])
    some = pl.ds(0, last_sent.shape[0] // 2)
    last_half = remote(
        last_sent.at[some], came.at[3, some], row_send.at[4], row_recv.at[3], (across, next_z)
    )
    def fill(n, carry):
        k = (n + 1) % 4
        eid = (z + k) % 2 + 2 * ((core + k // 2) % 2)
        fill_slots(eid, gate, act_two, dy_s, mask, slot_rows, sent.at[k % 3])

        @pl.when(n == 0)
        def _():
            rows_out(1).start()

        @pl.when(n == 1)
        def _():
            rows_out(2).start()

        @pl.when(n == 2)
        def _():
            last_local.start()
            last_local.wait()
            last_half.start()

        return carry

    lax.fori_loop(0, 4, fill, 0)
    own_local.start()
    abroad(expert_relay, 2)
    for c in range(len(chunks)):
        expert_finish(c)
    for k in (1, 2):
        rows_out(k).wait_recv()
        rows_out(k).wait_send()
    last_half.wait_recv()
    last_half.wait_send()
    own_local.wait()

    def attn_sent(n, carry):
        for p in range(2):
            to_x(p, n).wait_send()
            to_y(p, n).wait_send()
            relay_x(p, n).wait_send()
            relay_y(p, n).wait_send()
            for kind in range(4):
                to_core(p, kind, n).wait_send()
        return carry

    lax.fori_loop(0, 4, attn_sent, 0)
    for p in range(2):
        for t in range(3):
            z_sends(p, t, lambda copy: copy.wait_send())
    for copy in flush(0, FRONT_KEPT):
        copy.wait()


def pair_attention_bwd_body(
    query, key, value, dout, attended, lse, starts, cosine, sine, ga_out, gb_out,
    ga_gu, gb_gu, ga_dn, gb_dn,
    d_query, d_key, d_value, own_ga_gu, own_gb_gu, own_ga_dn, own_gb_dn, plane_ga_out, plane_gb_out,
    kacc, vacc, *rest,
):
    mine, got, halves, final = (rest[4 * n : 4 * n + 4] for n in range(4))
    (
        s_ga_out, s_gb_out, r_ga_out, r_gb_out,
        own_sems, side_send, side_recv, end_send, end_recv, near_send, near_recv,
    ) = rest[16:]
    dp, z = lax.axis_index("dp"), lax.axis_index("expert")
    core, spot, half = dp % 2, dp // 2, z // 2
    far = (z + 2) % 4
    across = dp + 1 - 2 * core
    home = core == half
    away = core + half - 2 * core * half
    owners, spots = 8, 4
    sources = (ga_gu, gb_gu, ga_dn, gb_dn)
    outs = (own_ga_gu, own_gb_gu, own_ga_dn, own_gb_dn)
    plane_groups = (
        (s_ga_out, r_ga_out, plane_ga_out), (s_gb_out, r_gb_out, plane_gb_out),
    )

    def remote(source, target, send, recv, device):
        return pltpu.make_async_remote_copy(
            src_ref=source, dst_ref=target, send_sem=send, recv_sem=recv,
            device_id=device, device_id_type=MESH_ID,
        )

    def share(i, d):
        count = plane_groups[i][1].shape[1]
        return plane_groups[i][0].at[pl.ds(pl.multiple_of(d * count, 16), count)]

    def near(i, n):
        goal = (dp + n + 1) % owners
        return remote(
            share(i, goal), plane_groups[i][1].at[n], near_send.at[i, n], near_recv.at[i, n], (goal, z)
        )

    def quarter(i, m):
        count = mine[i].shape[0]
        return sources[i].at[pl.ds(pl.multiple_of(m * count, 16), count)]

    def keep(i):
        return pltpu.make_async_copy(quarter(i, spot), mine[i], own_sems.at[i])

    def side(i, n):
        goal = (spot + n + 1) % spots
        return remote(
            quarter(i, goal), got[i].at[n], side_send.at[i, n], side_recv.at[i, n],
            (2 * goal + core, z),
        )

    def to_across(i):
        return remote(
            halves[i].at[1 - core], final[i].at[0], end_send.at[i, 0], end_recv.at[i, 0], (across, z)
        )

    def to_far(i, h):
        return remote(
            halves[i].at[h], final[i].at[1], end_send.at[i, h], end_recv.at[i, 1],
            (dp - core + h, far),
        )

    step = pl.program_id(0)

    @pl.when(step == 0)
    def _():
        s_ga_out[...] = ga_out[...].astype(BF16)
        s_gb_out[...] = gb_out[...].astype(BF16)
        senders = [((dp - core + half, far), None)]
        senders += [(((dp + n) % owners, z), None) for n in range(1, owners)]
        start_kernel(None, senders, owners - 1 + 2 * away)
        for i in range(4):
            keep(i).start()

        def send_side(n, carry):
            for i in range(4):
                side(i, n).start()
            return carry

        lax.fori_loop(0, spots - 1, send_side, 0)

        def send_near(n, carry):
            for i in range(2):
                near(i, n).start()
            return carry

        lax.fori_loop(0, owners - 1, send_near, 0)

    @pl.when(step == pl.num_programs(0) - 2)
    def _():
        for i in range(4):
            keep(i).wait()
            total = mine[i][...].astype(F32)
            for n in range(spots - 1):
                side(i, n).wait_recv()
                total = total + got[i][n].astype(F32)
            count = halves[i].shape[1]
            for h in range(2):
                halves[i][h] = total[h * count : (h + 1) * count].astype(BF16)

            @pl.when(home)
            def _(i=i):
                to_across(i).start()

            @pl.when(jnp.logical_not(home))
            def _(i=i):
                for h in range(2):
                    to_far(i, h).start()

    attention_bwd_body(
        query, key, value, dout, attended, lse, starts, cosine, sine, d_query, d_key, d_value,
        kacc, vacc,
    )

    @pl.when(step == pl.num_programs(0) - 1)
    def _():
        for i in range(4):
            to_far(i, 0).wait_recv()

            @pl.when(home)
            def _(i=i):
                outs[i][...] = halves[i][core].astype(F32) + final[i][1].astype(F32)
                to_across(i).wait_send()

            @pl.when(jnp.logical_not(home))
            def _(i=i):
                to_across(i).wait_recv()
                outs[i][...] = final[i][0].astype(F32) + final[i][1].astype(F32)
                for h in range(2):
                    to_far(i, h).wait_send()

        def sent_side(n, carry):
            for i in range(4):
                side(i, n).wait_send()
            return carry

        lax.fori_loop(0, spots - 1, sent_side, 0)

        def finish_near(n, carry):
            for i in range(2):
                near(i, n).wait_recv()
                near(i, n).wait_send()
            return carry

        lax.fori_loop(0, owners - 1, finish_near, 0)
        for i, (_, target, out) in enumerate(plane_groups):
            total = share(i, dp)[...].astype(F32)
            for n in range(owners - 1):
                total = total + target[n].astype(F32)
            out[...] = total


def pair_tail_body(
    place_row, mask, a_in, b_out, gain, a_o, b_o, d_logits,
    q_hbm, k_hbm, v_hbm, low_hbm, act_hbm, hid_hbm, resid_hbm, w_hbm, out_hbm,
    out, grad_hidden, grad_gate, own_ga_qkv, own_gb_qkv, own_ga_out, own_gb_out,
    d_query, d_key, d_value, low_qkv, act_one,
    hid_s, d_resid, w_qkv, out_s, place_col, high, lower, d_low_all, ga_sum, gb_sum,
    s_ga_qkv, s_gb_qkv, r_ga_qkv, r_gb_qkv,
    thin_out, wide_out, thin_in, wide_in, load_sems, send_sems, recv_sems, far_send, far_recv,
):
    dp, z = lax.axis_index("dp"), lax.axis_index("expert")
    others, planes = 7, 3
    tok = place_row.shape[1]
    blocks = tok // ROW_BLOCK
    loads = [
        pltpu.make_async_copy(source, target, load_sems.at[i])
        for i, (source, target) in enumerate(
            ((q_hbm, d_query), (k_hbm, d_key), (v_hbm, d_value), (low_hbm, low_qkv),
             (act_hbm, act_one), (w_hbm, w_qkv), (hid_hbm, hid_s), (resid_hbm, d_resid),
             (out_hbm, out_s))
        )
    ]
    for load in loads:
        load.start()
    start_kernel(
        None,
        [(((dp + i) % 8, z), None) for i in range(1, 8)] + [((dp, (z + j) % 4), None) for j in (1, 2, 3)],
        others + planes,
    )
    ga_sum[...] = jnp.zeros_like(ga_sum)
    gb_sum[...] = jnp.zeros_like(gb_sum)
    parts = [slice(p * MODEL_WIDTH, (p + 1) * MODEL_WIDTH) for p in range(3)]
    d_refs = (d_query, d_key, d_value)

    def block_rows(b):
        return pl.ds(pl.multiple_of(b * ROW_BLOCK, ROW_BLOCK), ROW_BLOCK)

    def sums(b, carry):
        rows = block_rows(b)
        low = low_qkv[rows, :]
        d_low = jnp.zeros((ROW_BLOCK, LANES), F32)
        for cols, ref in zip(parts, d_refs):
            grad = ref[rows, :]
            d_low = d_low + dot_nt(grad, b_out[:, cols])
            gb_sum[:, cols] += dot_tn(low, grad)
        d_low = (d_low * mask[rows, :].astype(F32)).astype(BF16)
        d_low_all[rows, :] = d_low
        ga_sum[...] += dot_tn(act_one[rows, :], d_low)
        return carry

    for load in loads[:5]:
        load.wait()
    lax.fori_loop(0, blocks, sums, 0)
    s_ga_qkv[...] = ga_sum[...].astype(BF16)
    s_gb_qkv[...] = gb_sum[...].astype(BF16)
    groups = ((s_ga_qkv, r_ga_qkv), (s_gb_qkv, r_gb_qkv))

    def share(i, d):
        count = groups[i][1].shape[1]
        return groups[i][0].at[pl.ds(pl.multiple_of(d * count, 16), count)]

    def near(i, n):
        goal = (dp + n + 1) % 8
        return pltpu.make_async_remote_copy(
            src_ref=share(i, goal), dst_ref=groups[i][1].at[n], send_sem=send_sems.at[i, n],
            recv_sem=recv_sems.at[i, n], device_id=(goal, z), device_id_type=MESH_ID,
        )

    def send_near(n, carry):
        for i in range(2):
            near(i, n).start()
        return carry

    lax.fori_loop(0, others, send_near, 0)

    for load in loads[5:8]:
        load.wait()

    def back(b, carry):
        rows = block_rows(b)
        d_act = dot_nt(d_low_all[rows, :], a_in[...])
        for cols, ref in zip(parts, d_refs):
            d_act = d_act + dot_nt(ref[rows, :], w_qkv[:, cols])
        hid = hid_s[rows, :].astype(F32)
        scale = lax.rsqrt(jnp.mean(hid * hid, axis=-1, keepdims=True) + EPSILON)
        weighted = d_act * gain[...].astype(F32)
        grad_hid = d_resid[rows, :] + (
            scale * weighted
            - hid * (scale * scale * scale) * jnp.mean(hid * weighted, axis=-1, keepdims=True)
        )
        top = grad_hid.astype(BF16)
        high[rows, :] = top
        lower[rows, :] = (grad_hid - top.astype(F32)).astype(BF16)
        return carry

    lax.fori_loop(0, blocks, back, 0)
    place_col[...] = jnp.broadcast_to(place_row[...].astype(F32), (LANES, tok)).T

    def near_done(n, carry):
        for i in range(2):
            near(i, n).wait_recv()
        return carry

    lax.fori_loop(0, others, near_done, 0)
    totals = []
    for i in range(2):
        total = share(i, dp)[...].astype(F32)
        for n in range(others):
            total = total + groups[i][1][n].astype(F32)
        totals.append(total)
    a_qkv, b_qkv = totals
    a_count, b_count = a_qkv.shape[0] // 4, b_qkv.shape[0] // 4
    for p in range(4):
        a_rows, b_rows = slice(p * a_count, (p + 1) * a_count), slice(p * b_count, (p + 1) * b_count)
        thin_out[p, :a_count, :LANES] = a_qkv[a_rows].astype(BF16)
        thin_out[p, :a_count, LANES:] = a_o[a_rows, :].astype(BF16)
        thin_out[p, a_count:, :] = jnp.zeros((thin_out.shape[1] - a_count, 2 * LANES), BF16)
        wide_out[p] = jnp.concatenate(
            [b_qkv[b_rows, cols] for cols in parts] + [b_o[b_rows, :]], axis=0
        ).astype(BF16)

    def far(i, j):
        goal = (z + j + 1) % 4
        source, target = ((thin_out, thin_in), (wide_out, wide_in))[i]
        return pltpu.make_async_remote_copy(
            src_ref=source.at[goal], dst_ref=target.at[j], send_sem=far_send.at[i, j],
            recv_sem=far_recv.at[i, j], device_id=(dp, goal), device_id_type=MESH_ID,
        )

    for j in range(planes):
        for i in range(2):
            far(i, j).start()
    loads[8].wait()

    top, mid, last = (jnp.where(iota((tok, LANES), 1) < 16, v.astype(F32), 0.0) for v in split_three(d_logits[...]))
    logit_parts = (top + pltpu.roll(mid, 16, 1) + pltpu.roll(last, 32, 1)).astype(BF16)

    def to_rows(b, carry):
        rows = block_rows(b)
        perm = hot_matrix(place_col[rows, 0:1].astype(jnp.int32) == iota((ROW_BLOCK, tok), 1))
        out[rows, :] = dot(perm, out_s[...]).astype(BF16)
        grad_hidden[rows, :] = dot(perm, high[...]) + dot(perm, lower[...])
        moved = dot(perm, logit_parts)
        grad_gate[rows, :] = moved + (
            pltpu.roll(moved, LANES - 16, 1) + pltpu.roll(moved, LANES - 32, 1)
        )
        return carry

    lax.fori_loop(0, blocks, to_rows, 0)
    for j in range(planes):
        for i in range(2):
            far(i, j).wait_recv()
    thin = thin_out[z].astype(F32)
    wide = wide_out[z].astype(F32)
    for j in range(planes):
        thin = thin + thin_in[j].astype(F32)
        wide = wide + wide_in[j].astype(F32)
    own_ga_qkv[...] = thin[:a_count, :LANES]
    own_ga_out[...] = thin[:a_count, LANES:]
    for p, cols in enumerate(parts):
        own_gb_qkv[:, cols] = wide[p * b_count : (p + 1) * b_count]
    own_gb_out[...] = wide[3 * b_count : 4 * b_count]

    def sent(n, carry):
        for i in range(2):
            near(i, n).wait_send()
        return carry

    lax.fori_loop(0, others, sent, 0)
    for j in range(planes):
        for i in range(2):
            far(i, j).wait_send()


def settle_body(*refs):
    count = len(refs) // 2
    for n, (source, target) in enumerate(zip(refs[:count], refs[count:])):
        target[...] = source[...].T[: target.shape[0]] if n == 0 else source[...]


def split_three(values):
    top = values.astype(BF16)
    rest = values - top.astype(F32)
    mid = rest.astype(BF16)
    return top, mid, (rest - mid.astype(F32)).astype(BF16)


def post_attn_body(
    kinds, attn_low, hid_s, mask, small_s, w_out, a_out, b_out, router, gain,
    low_out, resid, act_two, gate,
):
    low_out[...], resid[...], act_two[...], gate[...] = post_attn(
        kinds, attn_low[...], hid_s[...], mask[...], small_s[...], w_out, a_out, b_out, router, gain
    )


def post_attn(kinds, attn, hid, mask, sm, w_out, a_out, b_out, router, gain):
    low = (dot(attn, a_out[...]) * mask.astype(F32)).astype(BF16)
    res = hid.astype(F32) + (dot(attn, w_out[...]) + dot(low, b_out[...]))
    act = normed(res, gain)
    logits = dot_nt(act, router[...])
    lane = iota(logits.shape, 1)
    routed = jnp.where(lane < kinds, logits + sm, -1e30)
    top = jnp.max(routed, axis=1, keepdims=True)
    expo = jnp.exp(routed - top)
    prob = expo / jnp.sum(expo, axis=1, keepdims=True)
    return low, res, act, jnp.where(lane < kinds, prob, logits)


def place_slots(experts, small_s, slot, slot_rows):
    tok = slot.shape[0]
    lane = iota((tok, LANES), 1)
    first = small_s[:, CHOICE_LANE : CHOICE_LANE + 1].astype(jnp.int32)
    second = small_s[:, CHOICE_LANE + 1 : CHOICE_LANE + 2].astype(jnp.int32)
    hot = ((first == lane) | (second == lane)) & (lane < experts)
    hot_low = hot_matrix(hot)
    for blk in range(tok // ROW_BLOCK):
        lo, hi = blk * ROW_BLOCK, (blk + 1) * ROW_BLOCK
        tri = hot_matrix(iota((ROW_BLOCK, hi), 1) < lo + iota((ROW_BLOCK, hi), 0))
        rank = dot(tri, hot_low[:hi, :])
        slot[lo:hi, :] = jnp.where(hot[lo:hi, :], rank, -1.0)
    slot_rows[...] = slot[...].T


def fill_slots(eid, gate, act_two, dy_s, mask, slot_rows, target):
    row = slot_rows[pl.ds(eid, 1), :].astype(jnp.int32)
    pick = hot_matrix(row == iota((target.shape[0], row.shape[1]), 0))
    value = lane_value(gate[...], eid)
    scaled = (dy_s[...].astype(F32) * value).astype(BF16)
    target[:, :MODEL_WIDTH] = dot(pick, act_two[...]).astype(BF16)
    target[:, MODEL_WIDTH : 2 * MODEL_WIDTH] = dot(pick, scaled).astype(BF16)
    target[:, 2 * MODEL_WIDTH :] = dot(pick, mask[...]).astype(BF16)


def dispatch_body(experts, eids, small_s, gate, act_two, dy_s, mask, slot, sent, slot_rows):
    step = pl.program_id(0)

    @pl.when(step == 0)
    def _():
        place_slots(experts, small_s, slot, slot_rows)

    fill_slots(eids[step], gate, act_two, dy_s, mask, slot_rows, sent.at[0])


def ffn_math(
    rows, d_out, mask, w_gu, w_dn, a_gu, b_gu, a_dn, b_dn,
    ga_gu, gb_gu, ga_dn, gb_dn, acc_out, acc_dx, acc_low, acc_dlow,
):
    low_gu = (dot(rows, a_gu[...]) * mask).astype(BF16)
    dlow_dn = (dot_nt(d_out, b_dn[...]) * mask).astype(BF16)
    for ref in (acc_out, acc_dx, acc_low, acc_dlow):
        ref[...] = jnp.zeros_like(ref)

    def step(j, carry):
        lo = pl.multiple_of(j * HIDDEN_BLOCK, HIDDEN_BLOCK)
        g_cols = pl.ds(lo, HIDDEN_BLOCK)
        u_cols = pl.ds(pl.multiple_of(FEEDFWD_WIDTH + lo, HIDDEN_BLOCK), HIDDEN_BLOCK)
        gate = dot(rows, w_gu[:, g_cols]) + dot(low_gu, b_gu[:, g_cols])
        up = dot(rows, w_gu[:, u_cols]) + dot(low_gu, b_gu[:, u_cols])
        sig = 1.0 / (1.0 + jnp.exp(-gate))
        silu = gate * sig
        middle = (silu * up).astype(BF16)
        acc_out[...] += dot(middle, w_dn[g_cols, :])
        acc_low[...] += dot(middle, a_dn[g_cols, :])
        d_mid = dot_nt(d_out, w_dn[g_cols, :]) + dot_nt(dlow_dn, a_dn[g_cols, :])
        d_mid = d_mid.astype(BF16).astype(F32)
        d_gate = (d_mid * up * (sig * (1.0 + gate * (1.0 - sig)))).astype(BF16)
        d_up = (d_mid * silu).astype(BF16)
        acc_dx[...] += dot_nt(d_gate, w_gu[:, g_cols]) + dot_nt(d_up, w_gu[:, u_cols])
        acc_dlow[...] += dot_nt(d_gate, b_gu[:, g_cols]) + dot_nt(d_up, b_gu[:, u_cols])
        gb_gu[:, g_cols] += dot_tn(low_gu, d_gate)
        gb_gu[:, u_cols] += dot_tn(low_gu, d_up)
        ga_dn[g_cols, :] += dot_tn(middle, dlow_dn)
        return carry

    lax.fori_loop(0, FEEDFWD_WIDTH // HIDDEN_BLOCK, step, 0)
    low_dn = (acc_low[...] * mask).astype(BF16)
    result = (acc_out[...] + dot(low_dn, b_dn[...])).astype(BF16)
    gb_dn[...] += dot_tn(low_dn, d_out)
    dlow_gu = (acc_dlow[...] * mask).astype(BF16)
    d_rows = (acc_dx[...] + dot_nt(dlow_gu, a_gu[...])).astype(BF16)
    ga_gu[...] += dot_tn(rows, dlow_gu)
    return result, d_rows


def ffn_body(
    came, w_gu, w_dn, a_gu, b_gu, a_dn, b_dn,
    back, ga_gu, gb_gu, ga_dn, gb_dn, acc_out, acc_dx, acc_low, acc_dlow,
):
    @pl.when(pl.program_id(0) == 0)
    def _():
        for ref in (ga_gu, gb_gu, ga_dn, gb_dn):
            ref[...] = jnp.zeros_like(ref)

    back[0, :, :MODEL_WIDTH], back[0, :, MODEL_WIDTH:] = ffn_math(
        came[0, :, :MODEL_WIDTH], came[0, :, MODEL_WIDTH : 2 * MODEL_WIDTH],
        came[0, :, 2 * MODEL_WIDTH :].astype(F32), w_gu, w_dn, a_gu, b_gu, a_dn, b_dn,
        ga_gu, gb_gu, ga_dn, gb_dn, acc_out, acc_dx, acc_low, acc_dlow,
    )


def pair_ffn_body(
    had, last_sent, wide, mid, thin,
    returned, out_ga_gu, out_gb_gu, out_ga_dn, out_gb_dn,
    came, back, ga_gu, gb_gu, ga_dn, gb_dn, w_gu, w_dn, a_gu, b_gu, a_dn, b_dn, acc_out, acc_dx, acc_low, acc_dlow,
    load_sems, came_sems, back_sems, done_sems, last_sems,
):
    dp, z = lax.axis_index("dp"), lax.axis_index("expert")
    core, plane = dp % 2, z % 2

    def peer(k):
        return (dp + (k // 2) * (1 - 2 * core), z + (k % 2) * (1 - 2 * plane))

    start_kernel(None, [(peer(k), None) for k in (1, 2, 3)], 3)

    half = last_sent.shape[0] // 2
    early, late = pl.ds(0, half), pl.ds(half, half)

    def had_in(k):
        return pltpu.make_async_copy(had.at[k], came.at[k], came_sems.at[k])

    early_in = pltpu.make_async_copy(had.at[3, early], came.at[3, early], came_sems.at[3])
    last_out = pltpu.make_async_remote_copy(
        src_ref=last_sent.at[late], dst_ref=came.at[3, late], send_sem=last_sems.at[0],
        recv_sem=last_sems.at[1], device_id=peer(3), device_id_type=MESH_ID,
    )

    def result_out(k):
        return pltpu.make_async_remote_copy(
            src_ref=back.at[k], dst_ref=returned.at[k], send_sem=back_sems.at[k],
            recv_sem=done_sems.at[k], device_id=peer(k), device_id_type=MESH_ID,
        )

    last_out.start()
    for k in (1, 0, 2):
        had_in(k).start()
    early_in.start()

    gu_rows = w_gu.shape[0] // wide.shape[0]
    up_rows = b_gu.shape[0] // wide.shape[0]
    dn_rows = w_dn.shape[0] // wide.shape[0]
    plans = (
        (wide, 0, gu_rows, w_gu), (wide, gu_rows, up_rows, b_gu), (mid, 0, dn_rows, w_dn),
        (mid, dn_rows, up_rows, b_dn), (thin, 0, gu_rows, a_gu), (thin, gu_rows, dn_rows, a_dn),
    )

    def load(d, carry):
        for i, (source, at, count, target) in enumerate(plans):
            pltpu.make_async_copy(
                source.at[d, pl.ds(at, count)],
                target.at[pl.ds(pl.multiple_of(d * count, 16), count)],
                load_sems.at[i],
            ).start()
        return carry

    lax.fori_loop(0, wide.shape[0], load, 0)
    for ref in (ga_gu, gb_gu, ga_dn, gb_dn):
        ref[...] = jnp.zeros_like(ref)
    for i, (_, _, _, target) in enumerate(plans):
        pltpu.make_async_copy(target, target, load_sems.at[i]).wait()

    def source_step(s, carry):
        k = jnp.where(s < 2, 1 + 2 * s, 2 * s - 4)

        @pl.when(k != 3)
        def _():
            had_in(k).wait()

        @pl.when(k == 3)
        def _():
            early_in.wait()
            last_out.wait_recv()

        back[k, :, :MODEL_WIDTH], back[k, :, MODEL_WIDTH:] = ffn_math(
            came[k, :, :MODEL_WIDTH], came[k, :, MODEL_WIDTH : 2 * MODEL_WIDTH],
            came[k, :, 2 * MODEL_WIDTH :].astype(F32), w_gu, w_dn, a_gu, b_gu, a_dn, b_dn,
            ga_gu, gb_gu, ga_dn, gb_dn, acc_out, acc_dx, acc_low, acc_dlow,
        )

        @pl.when(k != 0)
        def _():
            result_out(k).start()

        return carry

    lax.fori_loop(0, 4, source_step, 0)
    for out, total in (
        (out_ga_gu, ga_gu), (out_gb_gu, gb_gu), (out_ga_dn, ga_dn), (out_gb_dn, gb_dn),
    ):
        out[...] = total[...].astype(BF16)
    own_out = pltpu.make_async_copy(back.at[0], returned.at[0], done_sems.at[0])
    own_out.start()
    own_out.wait()
    last_out.wait_send()
    for k in (1, 2, 3):
        result_out(k).wait_send()
        result_out(k).wait_recv()


def combine_body(
    experts, kinds, eids, resid, act_two, dy_s, gate, slot, small_s, low_out, attn_low, mask, came,
    w_out, a_out, b_out, router, const_value, gain,
    out_s, d_resid, d_attended, d_logits, ga_out, gb_out,
):
    @pl.when(pl.program_id(0) == 0)
    def _():
        ga_out[...] = jnp.zeros_like(ga_out)
        gb_out[...] = jnp.zeros_like(gb_out)

    rows = resid.shape[0]
    cap = came.shape[1]
    res = resid[...]
    act = act_two[...].astype(F32)
    dy_low = dy_s[...]
    dy = dy_low.astype(F32)
    lane = iota((rows, LANES), 1)
    levels = gate[...].T
    top = iota((CHOICE_ROWS, rows), 0)
    prob = jnp.where(top < kinds, levels[:CHOICE_ROWS], 0.0)

    def row(values, index):
        return jnp.sum(jnp.where(top == index, values, 0.0), axis=0, keepdims=True)

    picked = small_s[...].T
    first = picked[CHOICE_LANE : CHOICE_LANE + 1]
    second = picked[CHOICE_LANE + 1 : CHOICE_LANE + 2]

    def chosen(kind):
        return jnp.where((first == kind) | (second == kind), 1.0, 0.0)

    has_copy, has_zero, has_one = chosen(experts + 1), chosen(experts + 2), chosen(experts + 3)
    g_copy = has_copy * row(prob, experts + 1)
    g_zero = has_zero * row(prob, experts + 2)
    g_one = has_one * row(prob, experts + 3)

    def pair(at):
        left, right = levels[at : at + 1], levels[at + 1 : at + 2]
        high = jnp.maximum(left, right)
        e_left, e_right = jnp.exp(left - high), jnp.exp(right - high)
        scale = 1.0 / (e_left + e_right)
        return e_left * scale, e_right * scale

    a00, a01 = pair(CONST_LANE)
    a10, a11 = pair(CONST_LANE + 2)
    coef = g_copy + g_zero * a00 + g_one * a10
    factors = [coef, g_zero * a01, g_one * a11]
    factors += [row(prob, eids[k]) for k in range(came.shape[0])]
    spot = iota((LANES, rows), 0)
    columns = jnp.zeros((LANES, rows), F32)
    for n, factor in enumerate(factors):
        columns = jnp.where(spot == n, factor, columns)
    columns = columns.T
    v_zero, v_one = const_value[0:1, :], const_value[1:2, :]
    out = res + columns[:, 0:1] * act + columns[:, 1:2] * v_zero + columns[:, 2:3] * v_one
    d_act = columns[:, 0:1] * dy
    met = jnp.where(lane == 0, jnp.sum(dy * act, axis=1, keepdims=True), 0.0)
    met = jnp.where(lane == 1, jnp.sum(dy * v_zero, axis=1, keepdims=True), met)
    met = jnp.where(lane == 2, jnp.sum(dy * v_one, axis=1, keepdims=True), met)
    for k in range(came.shape[0]):
        place = lane_value(slot[...], eids[k]).astype(jnp.int32)
        pick = hot_matrix(place == iota((rows, cap), 1))
        result = dot(pick, came[k, :, :MODEL_WIDTH])
        d_act = d_act + dot(pick, came[k, :, MODEL_WIDTH:])
        met = jnp.where(lane == 3 + k, jnp.sum(dy * result, axis=1, keepdims=True), met)
        out = out + columns[:, 3 + k : 4 + k] * result
    out_s[...] = out.astype(BF16)
    met = met.T
    along_act, along_zero, along_one = met[0:1], met[1:2], met[2:3]
    d_gate = jnp.zeros((CHOICE_ROWS, rows), F32)
    for k in range(came.shape[0]):
        d_gate = jnp.where(top == eids[k], met[3 + k : 4 + k], d_gate)
    d_gate = jnp.where(top == experts + 1, has_copy * along_act, d_gate)
    d_gate = jnp.where(top == experts + 2, has_zero * (a00 * along_act + a01 * along_zero), d_gate)
    d_gate = jnp.where(top == experts + 3, has_one * (a10 * along_act + a11 * along_one), d_gate)
    d_logit = prob * (d_gate - jnp.sum(prob * d_gate, axis=0, keepdims=True))
    tail = iota((8, rows), 0)
    d_pair = jnp.zeros((8, rows), F32)
    for n, (g_val, left, right, along) in enumerate(
        ((g_zero, a00, a01, along_zero), (g_one, a10, a11, along_one))
    ):
        da_left, da_right = g_val * along_act, g_val * along
        level = left * da_left + right * da_right
        d_pair = jnp.where(tail == 2 * n, left * (da_left - level), d_pair)
        d_pair = jnp.where(tail == 2 * n + 1, right * (da_right - level), d_pair)
    mix = jnp.concatenate(
        [d_logit, jnp.zeros((CONST_LANE - CHOICE_ROWS, rows), F32), d_pair,
         jnp.zeros((LANES - CONST_LANE - 8, rows), F32)],
        axis=0,
    ).T
    d_logits[...] = mix
    mix_hi = mix.astype(BF16)
    mix_lo = (mix - mix_hi.astype(F32)).astype(BF16)
    d_act = d_act + (dot(mix_hi, router[...]) + dot(mix_lo, router[...]))
    scale = lax.rsqrt(jnp.mean(res * res, axis=-1, keepdims=True) + EPSILON)
    weighted = d_act * gain[...].astype(F32)
    d_res = dy + (
        scale * weighted
        - res * (scale * scale * scale) * jnp.mean(res * weighted, axis=-1, keepdims=True)
    )
    d_resid[...] = d_res
    d_attn = d_res.astype(BF16)
    dlow = (dot_nt(d_attn, b_out[...]) * mask[...].astype(F32)).astype(BF16)
    gb_out[...] += dot_tn(low_out[...], d_attn)
    ga_out[...] += dot_tn(attn_low[...], dlow)
    d_attended[...] = (dot_nt(d_attn, w_out[...]) + dot_nt(dlow, a_out[...])).astype(BF16)


def input_grad_body(
    d_query, d_key, d_value, low_qkv, act_one, mask, hid_s, d_resid, w_qkv, a_in, b_out, gain,
    high, lower, ga_qkv, gb_qkv,
):
    @pl.when(pl.program_id(0) == 0)
    def _():
        ga_qkv[...] = jnp.zeros_like(ga_qkv)
        gb_qkv[...] = jnp.zeros_like(gb_qkv)

    d_low = jnp.zeros((d_query.shape[0], LANES), F32)
    d_act = jnp.zeros((d_query.shape[0], MODEL_WIDTH), F32)
    for part, ref in enumerate((d_query, d_key, d_value)):
        cols = slice(part * MODEL_WIDTH, (part + 1) * MODEL_WIDTH)
        grad = ref[...]
        d_low = d_low + dot_nt(grad, b_out[:, cols])
        d_act = d_act + dot_nt(grad, w_qkv[:, cols])
        gb_qkv[:, cols] += dot_tn(low_qkv[...], grad)
    d_low = (d_low * mask[...].astype(F32)).astype(BF16)
    ga_qkv[...] += dot_tn(act_one[...], d_low)
    d_act = d_act + dot_nt(d_low, a_in[...])
    hid = hid_s[...].astype(F32)
    scale = lax.rsqrt(jnp.mean(hid * hid, axis=-1, keepdims=True) + EPSILON)
    weighted = d_act * gain[...].astype(F32)
    grad_hid = d_resid[...] + (
        scale * weighted
        - hid * (scale * scale * scale) * jnp.mean(hid * weighted, axis=-1, keepdims=True)
    )
    top = grad_hid.astype(BF16)
    high[...] = top
    lower[...] = (grad_hid - top.astype(F32)).astype(BF16)


def to_rows_body(place_col, out_s, d_logits, high, lower, out, grad_hidden, grad_gate):
    rows = out.shape[0]
    tok = out_s.shape[0]
    perm = hot_matrix(place_col[...] == iota((rows, tok), 1))
    out[...] = dot(perm, out_s[...]).astype(BF16)
    grad_hidden[...] = dot(perm, high[...]) + dot(perm, lower[...])
    logits = d_logits[...]
    top = logits.astype(BF16)
    rest = logits - top.astype(F32)
    mid = rest.astype(BF16)
    last = (rest - mid.astype(F32)).astype(BF16)
    grad_gate[...] = dot(perm, top) + (dot(perm, mid) + dot(perm, last))


class PairPlan:
    paired = True

    def __init__(self, dp, ex):
        self.ex = ex

    def expert_ids(self):
        own = lax.axis_index("expert") % 2 + 2 * (lax.axis_index("dp") % 2)
        return own ^ jnp.arange(self.ex, dtype=jnp.int32)


class AxisPlan:
    paired = False

    def __init__(self, dp, ex):
        self.dp, self.ex = dp, ex

    def gather(self, shard):
        return lax.all_gather(shard, "dp", axis=0)

    def expert_ids(self):
        return jnp.arange(self.ex, dtype=jnp.int32)

    def exchange(self, values):
        return lax.all_to_all(values, "expert", split_axis=0, concat_axis=0, tiled=True)

    def reduce(self, sums):
        return lax.psum_scatter(sums, "dp", scatter_dimension=0, tiled=True)[0].astype(F32)

    def reduce_all(self, sums):
        return lax.psum_scatter(
            sums, ("dp", "expert"), scatter_dimension=0, tiled=True
        )[0].astype(F32)


def shards(
    dp_size,
    expert_count,
    hidden_input,
    gate_carryover,
    sequence_length,
    token_stream_place,
    expert_choice_index,
    sequence_adapter,
    attention_gain,
    query_key_weight,
    output_weight,
    adapter_in_query,
    adapter_out_query,
    adapter_in_output,
    adapter_out_output,
    feedfwd_gain,
    router_weight,
    constant_gate,
    constant_value,
    gate_upward_weight,
    down_weight,
    adapter_in_gate,
    adapter_out_gate,
    adapter_in_down,
    adapter_out_down,
    output_gradient,
):
    tok = hidden_input.shape[0]
    width = MODEL_WIDTH
    kinds = expert_count + 4
    devices = dp_size * expert_count
    capacity = 5 * tok // (2 * kinds) // 8 * 8 + 8
    cap = -(-capacity // 16) * 16
    blocks = tok // ROW_BLOCK
    plan = (PairPlan if (dp_size, expert_count) == (8, 4) else AxisPlan)(dp_size, expert_count)

    a_rows, b_rows = query_key_weight.shape[0], adapter_out_query.shape[0]
    gu_rows, up_rows, dn_rows = (
        gate_upward_weight.shape[1], adapter_out_gate.shape[1], down_weight.shape[1],
    )
    gains = jnp.stack([attention_gain, feedfwd_gain])
    gain_one, gain_two = gains[0:1], gains[1:2]
    const_value = constant_value.astype(F32)
    sent_width = 2 * width + LANES
    full = whole
    hbm = pl.BlockSpec(memory_space=pl.ANY)
    vmem = pl.BlockSpec(memory_space=pltpu.VMEM)
    pairs = HEAD_COUNT // 2
    lse_rows = -(-HEAD_COUNT // 8) * 8
    smem = pl.BlockSpec(memory_space=pltpu.SMEM)
    eids = plan.expert_ids()
    if plan.paired:
        shapes = [
            sds((tok, width), BF16), sds((tok, width), BF16), sds((tok, LANES), F32),
            sds((tok, width), BF16), sds((tok, LANES), BF16), sds((tok, LANES), BF16),
            sds((1, tok), jnp.int32), sds((tok, LANES), F32), sds((tok, LANES), F32),
            sds((LANES, width), BF16),
            sds((tok, width), BF16), sds((tok, width), BF16), sds((tok, width), BF16),
            sds((width, 3 * width), BF16), sds((width, LANES), BF16), sds((LANES, 3 * width), BF16),
            sds((width, width), BF16), sds((width, LANES), BF16), sds((LANES, width), BF16),
            sds((tok, width), BF16), sds((lse_rows, tok), F32), sds((tok, LANES), BF16),
            sds((tok, width), F32), sds((tok, width), BF16), sds((tok, LANES), F32),
            sds((tok, LANES), F32),
        ]
        shard_rows = -(-(a_rows + b_rows) // 16) * 16
        packed = [
            (gu_rows + up_rows, 2 * FEEDFWD_WIDTH), (dn_rows + up_rows, width),
            (gu_rows + dn_rows, LANES),
        ]
        row_shape = (expert_count, cap, sent_width)
        (
            hid_s, dy_s, small_s, act_one, low_qkv, mask, starts, cosine, sine, router,
            query, key, value, w_qkv, a_qkv, b_qkv, w_out, a_out, b_out,
            attn_low, lse, low_out, resid, act_two, gate, slot,
            wide, mid, thin, came, last_sent,
        ) = pl.pallas_call(
            functools.partial(pair_front_body, kinds, a_rows, b_rows),
            in_specs=[smem] * 2 + [vmem] * 14 + [hbm] * 6,
            out_specs=[hbm] * (FRONT_KEPT + 5),
            out_shape=shapes
            + [sds((dp_size,) + shape, BF16) for shape in packed]
            + [sds(row_shape, BF16), sds(row_shape[1:], BF16)],
            scratch_shapes=[pltpu.VMEM(s.shape, s.dtype) for s in shapes]
            + [
                pltpu.VMEM((devices, shard_rows, 3 * width + LANES), BF16),
                pltpu.VMEM((devices, shard_rows, width + LANES), BF16),
                *[pltpu.VMEM(shape, BF16) for shape in packed],
                pltpu.VMEM((3,) + row_shape[1:], BF16),
                pltpu.VMEM((LANES, tok), F32),
                pltpu.SemaphoreType.DMA((2, 35)), pltpu.SemaphoreType.DMA((2, 35)),
                pltpu.SemaphoreType.DMA((2, 6)),
                pltpu.SemaphoreType.DMA((4, 8)), pltpu.SemaphoreType.DMA((4, 8)),
                pltpu.SemaphoreType.DMA((FRONT_KEPT,)), pltpu.SemaphoreType.DMA((6,)),
                pltpu.SemaphoreType.DMA((5,)), pltpu.SemaphoreType.DMA((4,)),
            ],
            compiler_params=pltpu.CompilerParams(
                vmem_limit_bytes=VMEM_BYTES, collective_id=4, has_side_effects=True
            ),
            name="pair_front",
        )(sequence_length, sequence_adapter, token_stream_place, hidden_input, output_gradient,
          gate_carryover.T, expert_choice_index.T, gains, router_weight.T,
          constant_gate.T,
          query_key_weight, output_weight, adapter_in_query, adapter_in_output, adapter_out_query,
          adapter_out_output, gate_upward_weight, adapter_out_gate, down_weight, adapter_out_down,
          adapter_in_gate, adapter_in_down)
        place = token_stream_place[0]
    else:
        pad_rows = -(a_rows + b_rows) % 16

        def pack(weight, adapter_in, adapter_out):
            lower = jnp.pad(adapter_out, ((0, pad_rows), (0, LANES)))
            return jnp.concatenate([jnp.concatenate([weight, adapter_in], axis=1), lower], axis=0)

        own_qkv = pack(query_key_weight, adapter_in_query, adapter_out_query)
        own_out = pack(output_weight, adapter_in_output, adapter_out_output)
        own_wide = jnp.concatenate([gate_upward_weight[0], adapter_out_gate[0]], axis=0)
        own_mid = jnp.concatenate([down_weight[0], adapter_out_down[0]], axis=0)
        own_thin = jnp.concatenate([adapter_in_gate[0], adapter_in_down[0]], axis=0)

        place = token_stream_place[0]
        ends = jnp.cumsum(sequence_length[0])
        begins = ends - sequence_length[0]
        stream = jnp.arange(tok, dtype=jnp.int32)
        seg = jnp.sum((stream[:, None] >= ends[None, :]).astype(jnp.int32), axis=1)
        seg_hot = seg[:, None] == jnp.arange(ends.shape[0], dtype=jnp.int32)[None, :]
        start = jnp.sum(jnp.where(seg_hot, begins[None, :], 0), axis=1)
        adapter = jnp.sum(jnp.where(seg_hot, sequence_adapter[0][None, :], 0), axis=1)
        half = HEAD_DIM // 2
        freq = jnp.exp(jnp.arange(half, dtype=F32) * (-math.log(10000.0) / half))
        angle = (stream - start).astype(F32)[:, None] * freq[None, :]
        cos, sin = jnp.cos(angle), jnp.sin(angle)
        cosine = jnp.concatenate([cos, cos, cos, cos], axis=1)
        sine = jnp.concatenate([-sin, sin, -sin, sin], axis=1)
        starts = start[None, :]
        mask = (jnp.arange(LANES)[None, :] // ADAPTER_RANK == adapter[:, None]).astype(BF16)
        top, middle, last = split_three(gate_carryover)
        gap = jnp.zeros((tok, 16 - kinds), BF16)
        small = jnp.concatenate(
            [top, gap, middle, gap, last, gap, expert_choice_index.astype(BF16),
             jnp.zeros((tok, LANES - CHOICE_LANE - 2), BF16)],
            axis=1,
        )
        router = jnp.concatenate(
            [router_weight.T, jnp.zeros((CONST_LANE - kinds, width), BF16), constant_gate.T,
             jnp.zeros((LANES - CONST_LANE - 4, width), BF16)],
            axis=0,
        )

        all_qkv = lax.all_gather(own_qkv, ("dp", "expert"), axis=0)
        all_out = lax.all_gather(own_out, ("dp", "expert"), axis=0)
        upper = slice(a_rows, a_rows + b_rows)
        w_qkv = all_qkv[:, :a_rows, : 3 * width].reshape(width, 3 * width)
        a_qkv = all_qkv[:, :a_rows, 3 * width :].reshape(width, LANES)
        b_qkv = all_qkv[:, upper, : 3 * width].reshape(LANES, 3 * width)
        w_out = all_out[:, :a_rows, :width].reshape(width, width)
        a_out = all_out[:, :a_rows, width:].reshape(width, LANES)
        b_out = all_out[:, upper, :width].reshape(LANES, width)
        wide, mid, thin = (plan.gather(w) for w in (own_wide, own_mid, own_thin))
        hid_s, dy_s, small_s, act_one, low_qkv, query, key, value = call(
            proj_in_body,
            (blocks,),
            [full((1, tok)), full((tok, width)), full((tok, width)), full((tok, LANES)),
             row_spec(LANES), row_spec(LANES), row_spec(LANES), full((1, width)),
             full((width, 3 * width)), full((width, LANES)), full((LANES, 3 * width))],
            [row_spec(width), row_spec(width), row_spec(LANES), row_spec(width), row_spec(LANES),
             row_spec(width), row_spec(width), row_spec(width)],
            [sds((tok, width), BF16), sds((tok, width), BF16), sds((tok, LANES), F32),
             sds((tok, width), BF16), sds((tok, LANES), BF16), sds((tok, width), BF16),
             sds((tok, width), BF16), sds((tok, width), BF16)],
            name="proj_in",
        )(place[None, :], hidden_input, output_gradient, small, cosine, sine, mask, gain_one,
          w_qkv, a_qkv, b_qkv)

        attn_low, lse = call(
            attention_fwd_body,
            (pairs,),
            [col_spec(tok)] * 3 + [full((1, tok))],
            [col_spec(tok), full((lse_rows, tok))],
            [sds((tok, width), BF16), sds((lse_rows, tok), F32)],
            name="attention_fwd",
        )(query, key, value, starts)

        low_out, resid, act_two, gate = call(
            functools.partial(post_attn_body, kinds),
            (blocks,),
            [row_spec(width), row_spec(width), row_spec(LANES), row_spec(LANES), full((width, width)),
             full((width, LANES)), full((LANES, width)), full((LANES, width)), full((1, width))],
            [row_spec(LANES), row_spec(width), row_spec(width), row_spec(LANES)],
            [sds((tok, LANES), BF16), sds((tok, width), F32), sds((tok, width), BF16),
             sds((tok, LANES), F32)],
            name="post_attn",
        )(attn_low, hid_s, mask, small_s, w_out, a_out, b_out, router, gain_two)

        slot, sent = call(
            functools.partial(dispatch_body, expert_count),
            (expert_count,),
            [smem, full((tok, LANES)), full((tok, LANES)), full((tok, width)), full((tok, width)),
             full((tok, LANES))],
            [full((tok, LANES)), pl.BlockSpec((1, cap, sent_width), lambda i: (i, 0, 0))],
            [sds((tok, LANES), F32), sds((expert_count, cap, sent_width), BF16)],
            scratch=[pltpu.VMEM((LANES, tok), F32)],
            name="dispatch",
        )(eids, small_s, gate, act_two, dy_s, mask)

    grad_shapes = [
        sds((width, LANES), F32), sds((LANES, 2 * FEEDFWD_WIDTH), F32),
        sds((FEEDFWD_WIDTH, LANES), F32), sds((LANES, width), F32),
    ]
    accumulators = [
        pltpu.VMEM((cap, width), F32), pltpu.VMEM((cap, width), F32),
        pltpu.VMEM((cap, LANES), F32), pltpu.VMEM((cap, LANES), F32),
    ]
    if plan.paired:
        returned, ga_gu, gb_gu, ga_dn, gb_dn = pl.pallas_call(
            pair_ffn_body,
            in_specs=[hbm] * 5,
            out_specs=[hbm] + [vmem] * 4,
            out_shape=[sds((expert_count, cap, 2 * width), BF16)]
            + [sds(g.shape, BF16) for g in grad_shapes],
            scratch_shapes=[
                pltpu.VMEM((expert_count, cap, sent_width), BF16),
                pltpu.VMEM((expert_count, cap, 2 * width), BF16),
                *[pltpu.VMEM(g.shape, F32) for g in grad_shapes],
                pltpu.VMEM((width, 2 * FEEDFWD_WIDTH), BF16), pltpu.VMEM((FEEDFWD_WIDTH, width), BF16),
                pltpu.VMEM((width, LANES), BF16), pltpu.VMEM((LANES, 2 * FEEDFWD_WIDTH), BF16),
                pltpu.VMEM((FEEDFWD_WIDTH, LANES), BF16), pltpu.VMEM((LANES, width), BF16),
                *accumulators,
                pltpu.SemaphoreType.DMA((6,)),
                *[pltpu.SemaphoreType.DMA((expert_count,)) for _ in range(3)],
                pltpu.SemaphoreType.DMA((2,)),
            ],
            compiler_params=pltpu.CompilerParams(
                vmem_limit_bytes=VMEM_BYTES, collective_id=1, has_side_effects=True
            ),
            name="pair_ffn",
        )(came, last_sent, wide, mid, thin)
    else:
        w_gu = wide[:, :gu_rows].reshape(width, 2 * FEEDFWD_WIDTH)
        b_gu = wide[:, gu_rows:].reshape(LANES, 2 * FEEDFWD_WIDTH)
        w_dn = mid[:, :dn_rows].reshape(FEEDFWD_WIDTH, width)
        b_dn = mid[:, dn_rows:].reshape(LANES, width)
        a_gu = thin[:, :gu_rows].reshape(width, LANES)
        a_dn = thin[:, gu_rows:].reshape(FEEDFWD_WIDTH, LANES)
        came = plan.exchange(sent)
        back, ga_gu, gb_gu, ga_dn, gb_dn = call(
            ffn_body,
            (expert_count,),
            [pl.BlockSpec((1, cap, sent_width), lambda i: (i, 0, 0)),
             full((width, 2 * FEEDFWD_WIDTH)), full((FEEDFWD_WIDTH, width)), full((width, LANES)),
             full((LANES, 2 * FEEDFWD_WIDTH)), full((FEEDFWD_WIDTH, LANES)), full((LANES, width))],
            [pl.BlockSpec((1, cap, 2 * width), lambda i: (i, 0, 0)), full((width, LANES)),
             full((LANES, 2 * FEEDFWD_WIDTH)), full((FEEDFWD_WIDTH, LANES)), full((LANES, width))],
            [sds((expert_count, cap, 2 * width), BF16)] + grad_shapes,
            scratch=accumulators,
            name="ffn",
        )(came, w_gu, w_dn, a_gu, b_gu, a_dn, b_dn)
        returned = plan.exchange(back)

    out_s, d_resid, d_attended, d_logits, ga_out, gb_out = call(
        functools.partial(combine_body, expert_count, kinds),
        (tok // ROW_BLOCK,),
        [smem, row_spec(width, ROW_BLOCK), row_spec(width, ROW_BLOCK), row_spec(width, ROW_BLOCK), row_spec(LANES, ROW_BLOCK), row_spec(LANES, ROW_BLOCK),
         row_spec(LANES, ROW_BLOCK), row_spec(LANES, ROW_BLOCK), row_spec(width, ROW_BLOCK), row_spec(LANES, ROW_BLOCK),
         full((expert_count, cap, 2 * width)), full((width, width)), full((width, LANES)),
         full((LANES, width)), full((LANES, width)), full((2, width)), full((1, width))],
        [row_spec(width, ROW_BLOCK), row_spec(width, ROW_BLOCK), row_spec(width, ROW_BLOCK), row_spec(LANES, ROW_BLOCK), full((width, LANES)),
         full((LANES, width))],
        [sds((tok, width), BF16), sds((tok, width), F32), sds((tok, width), BF16),
         sds((tok, LANES), F32), sds((width, LANES), F32), sds((LANES, width), F32)],
        name="combine",
    )(eids, resid, act_two, dy_s, gate, slot, small_s, low_out, attn_low, mask, returned,
      w_out, a_out, b_out, router, const_value, gain_two)

    if plan.paired:
        flow = dict(vmem_limit_bytes=VMEM_BYTES, has_side_effects=True)
        own_shapes = [
            sds((gu_rows, LANES), F32), sds((up_rows, 2 * FEEDFWD_WIDTH), F32),
            sds((dn_rows, LANES), F32), sds((up_rows, width), F32),
        ]
        plane_shapes = [
            sds((width // dp_size, LANES), F32), sds((LANES // dp_size, width), F32),
        ]
        d_query, d_key, d_value, *expert_owned, plane_ga, plane_gb = pl.pallas_call(
            pair_attention_bwd_body,
            grid=(pairs,),
            in_specs=[col_spec(tok)] * 5
            + [full((lse_rows, tok)), full((1, tok)), full((tok, LANES)), full((tok, LANES)),
               full((width, LANES)), full((LANES, width))]
            + [hbm] * 4,
            out_specs=[col_spec(tok)] * 3 + [full(s.shape) for s in own_shapes + plane_shapes],
            out_shape=[sds((tok, width), BF16)] * 3 + own_shapes + plane_shapes,
            scratch_shapes=[pltpu.VMEM((tok, LANES), F32), pltpu.VMEM((tok, LANES), F32)]
            + [pltpu.VMEM((2 * s.shape[0], s.shape[1]), BF16) for s in own_shapes]
            + [pltpu.VMEM((3, 2 * s.shape[0], s.shape[1]), BF16) for s in own_shapes]
            + [pltpu.VMEM((2,) + s.shape, BF16) for s in own_shapes * 2]
            + [pltpu.VMEM((width, LANES), BF16), pltpu.VMEM((LANES, width), BF16)]
            + [pltpu.VMEM((dp_size - 1,) + s.shape, BF16) for s in plane_shapes]
            + [pltpu.SemaphoreType.DMA((4,)), pltpu.SemaphoreType.DMA((4, 3)),
               pltpu.SemaphoreType.DMA((4, 3)), pltpu.SemaphoreType.DMA((4, 2)),
               pltpu.SemaphoreType.DMA((4, 2)), pltpu.SemaphoreType.DMA((2, dp_size)),
               pltpu.SemaphoreType.DMA((2, dp_size))],
            compiler_params=pltpu.CompilerParams(collective_id=2, **flow),
            name="pair_attention_bwd",
        )(query, key, value, d_attended, attn_low, lse, starts, cosine, sine, ga_out, gb_out,
          ga_gu, gb_gu, ga_dn, gb_dn)
        sum_shapes = [(width, LANES), (LANES, 3 * width)]
        got_shapes = [(dp_size - 1, a // dp_size, b) for a, b in sum_shapes]
        thin_rows = -(-a_rows // 16) * 16
        tail_shapes = [
            sds((tok, width), BF16), sds((tok, width), F32), sds((tok, LANES), F32),
            sds((a_rows, LANES), F32), sds((b_rows, 3 * width), F32),
            sds((a_rows, LANES), F32), sds((b_rows, width), F32),
        ]
        tail = pl.pallas_call(
            pair_tail_body,
            in_specs=[vmem] * 8 + [hbm] * 9,
            out_specs=[vmem] * 7,
            out_shape=tail_shapes,
            scratch_shapes=[
                *[pltpu.VMEM((tok, width), BF16) for _ in range(3)],
                pltpu.VMEM((tok, LANES), BF16), pltpu.VMEM((tok, width), BF16),
                pltpu.VMEM((tok, width), BF16), pltpu.VMEM((tok, width), F32),
                pltpu.VMEM((width, 3 * width), BF16), pltpu.VMEM((tok, width), BF16),
                pltpu.VMEM((tok, LANES), F32),
                pltpu.VMEM((tok, width), BF16), pltpu.VMEM((tok, width), BF16),
                pltpu.VMEM((tok, LANES), BF16),
                pltpu.VMEM((width, LANES), F32), pltpu.VMEM((LANES, 3 * width), F32),
                *[pltpu.VMEM(shape, BF16) for shape in sum_shapes + got_shapes],
                pltpu.VMEM((expert_count, thin_rows, 2 * LANES), BF16),
                pltpu.VMEM((expert_count, 4 * b_rows, width), BF16),
                pltpu.VMEM((expert_count - 1, thin_rows, 2 * LANES), BF16),
                pltpu.VMEM((expert_count - 1, 4 * b_rows, width), BF16),
                pltpu.SemaphoreType.DMA((9,)),
                pltpu.SemaphoreType.DMA((2, dp_size - 1)), pltpu.SemaphoreType.DMA((2, dp_size - 1)),
                pltpu.SemaphoreType.DMA((2, expert_count - 1)),
                pltpu.SemaphoreType.DMA((2, expert_count - 1)),
            ],
            compiler_params=pltpu.CompilerParams(collective_id=3, **flow),
            name="pair_tail",
        )(token_stream_place, mask, a_qkv, b_qkv, gain_one, plane_ga, plane_gb, d_logits,
          d_query, d_key, d_value, low_qkv, act_one, hid_s, d_resid, w_qkv, out_s)
        output, grad_hidden, grad_gate, *attn_owned = tail
        small_owned = [*attn_owned, *expert_owned]
        small_specs = [full(v.shape) for v in small_owned]
        grad_gate, output, grad_hidden, *owned = call(
            settle_body,
            (blocks,),
            [row_spec(LANES), row_spec(width), row_spec(width)] + small_specs,
            [pl.BlockSpec((kinds, ROW_BLOCK), lambda i: (0, i)), row_spec(width), row_spec(width)]
            + small_specs,
            [sds((kinds, tok), F32), sds((tok, width), BF16), sds((tok, width), F32)]
            + [sds(v.shape, F32) for v in small_owned],
            name="settle",
        )(grad_gate, output, grad_hidden, *small_owned)
        attn_owned, expert_owned = owned[:4], owned[4:]
        grad_gate = grad_gate.T
        return (
            output, grad_hidden, grad_gate[:, :kinds], *attn_owned,
            *[expert_owned[i][None] for i in range(4)],
        )

    owned_wide = plan.reduce(
        jnp.concatenate([gb_gu, gb_dn], axis=1).astype(BF16).reshape(dp_size, up_rows, -1)
    )
    owned_thin = plan.reduce(
        jnp.concatenate(
            [ga_gu.reshape(dp_size, gu_rows, LANES), ga_dn.reshape(dp_size, dn_rows, LANES)], axis=1
        ).astype(BF16)
    )

    d_query, d_key, d_value = call(
        attention_bwd_body,
        (pairs,),
        [col_spec(tok)] * 5
        + [full((lse_rows, tok)), full((1, tok)), full((tok, LANES)), full((tok, LANES))],
        [col_spec(tok)] * 3,
        [sds((tok, width), BF16)] * 3,
        scratch=[pltpu.VMEM((tok, LANES), F32), pltpu.VMEM((tok, LANES), F32)],
        name="attention_bwd",
    )(query, key, value, d_attended, attn_low, lse, starts, cosine, sine)

    high, lower, ga_qkv, gb_qkv = call(
        input_grad_body,
        (blocks,),
        [row_spec(width)] * 3 + [row_spec(LANES), row_spec(width), row_spec(LANES), row_spec(width),
         row_spec(width), full((width, 3 * width)), full((width, LANES)), full((LANES, 3 * width)),
         full((1, width))],
        [row_spec(width), row_spec(width), full((width, LANES)), full((LANES, 3 * width))],
        [sds((tok, width), BF16), sds((tok, width), BF16), sds((width, LANES), F32),
         sds((LANES, 3 * width), F32)],
        name="input_grad",
    )(d_query, d_key, d_value, low_qkv, act_one, mask, hid_s, d_resid, w_qkv, a_qkv, b_qkv,
      gain_one)

    owned = plan.reduce_all(
        jnp.concatenate(
            [
                ga_qkv.reshape(devices, b_rows, -1),
                ga_out.reshape(devices, b_rows, -1),
                gb_qkv.reshape(devices, b_rows, -1),
                gb_out.reshape(devices, b_rows, -1),
            ],
            axis=2,
        ).astype(BF16)
    )

    output, grad_hidden, grad_gate = call(
        to_rows_body,
        (blocks,),
        [row_spec(1), full((tok, width)), full((tok, LANES)), full((tok, width)),
         full((tok, width))],
        [row_spec(width), row_spec(width), row_spec(LANES)],
        [sds((tok, width), BF16), sds((tok, width), F32), sds((tok, LANES), F32)],
        name="to_rows",
    )(place[:, None], out_s, d_logits, high, lower)

    return (
        output,
        grad_hidden,
        grad_gate[:, :kinds],
        owned[:, :width].reshape(a_rows, LANES),
        owned[:, 2 * width : 5 * width],
        owned[:, width : 2 * width].reshape(a_rows, LANES),
        owned[:, 5 * width :],
        owned_thin[None, :gu_rows],
        owned_wide[None, :, : 2 * FEEDFWD_WIDTH],
        owned_thin[None, gu_rows:],
        owned_wide[None, :, 2 * FEEDFWD_WIDTH :],
    )


def solution(mesh):
    rows = P(("dp", "expert"), None)
    expert_rows = P("expert", "dp", None)
    in_specs = (
        (rows,) * 6 + (P(),) + (rows,) * 6 + (P(),) * 4 + (expert_rows,) * 6 + (rows,)
    )
    out_specs = (rows,) * 7 + (expert_rows,) * 4
    body = functools.partial(shards, mesh.shape["dp"], mesh.shape["expert"])
    return jax.shard_map(body, mesh=mesh, in_specs=in_specs, out_specs=out_specs, check_vma=False)
```

```python
import functools
import math

import jax
import jax.numpy as jnp
from jax import lax
from jax.experimental import pallas as pl
from jax.experimental.pallas import tpu as pltpu
from jax.sharding import PartitionSpec as P

MODEL_WIDTH = 768
HEAD_COUNT = 12
HEAD_DIM = 64
FEEDFWD_WIDTH = 2048
ADAPTER_RANK = 16
ROW_BLOCK = 256
HIDDEN_BLOCK = 1024
LANES = 128
CONST_LANE = 64
CHOICE_LANE = 48
CHOICE_ROWS = 16
EPSILON = 1e-06
VMEM_BYTES = 60 * 2**20
FRONT_KEPT = 26
MESH_ID = pl.DeviceIdType.MESH

F32 = jnp.float32
BF16 = jnp.bfloat16


def dot(a, b):
    return jnp.dot(a, b, preferred_element_type=F32)


def dot_nt(a, b):
    return lax.dot_general(a, b, (((1,), (1,)), ((), ())), preferred_element_type=F32)


def dot_tn(a, b):
    return lax.dot_general(a, b, (((0,), (0,)), ((), ())), preferred_element_type=F32)


def iota(shape, dim):
    return lax.broadcasted_iota(jnp.int32, shape, dim)


def hot_matrix(condition):
    return jnp.where(condition, 1.0, 0.0).astype(BF16)


def whole(shape):
    zeros = (0,) * len(shape)
    return pl.BlockSpec(shape, lambda *_: zeros)


def row_spec(width, rows=ROW_BLOCK):
    return pl.BlockSpec((rows, width), lambda i: (i, 0))


def col_spec(rows, width=LANES):
    return pl.BlockSpec((rows, width), lambda j: (0, j))


def sds(shape, dtype):
    return jax.ShapeDtypeStruct(shape, dtype)


def call(body, grid, in_specs, out_specs, out_shape, scratch=(), name=None):
    return pl.pallas_call(
        body,
        grid=grid,
        in_specs=in_specs,
        out_specs=out_specs,
        out_shape=out_shape,
        scratch_shapes=list(scratch),
        compiler_params=pltpu.CompilerParams(vmem_limit_bytes=VMEM_BYTES),
        name=name,
    )


def half_swap(values):
    lane = iota(values.shape, 1)
    up = pltpu.roll(values, 32, 1)
    down = pltpu.roll(values, LANES - 32, 1)
    return jnp.where(lane % HEAD_DIM < HEAD_DIM // 2, down, up)


def lane_value(values, lane_id):
    return jnp.sum(jnp.where(iota(values.shape, 1) == lane_id, values, 0.0), axis=1, keepdims=True)


def proj_in_body(
    place_row, hidden, upstream, small, cosine, sine, mask, gain, w_qkv, a_in, b_out,
    hid_s, dy_s, small_s, act_one, low_qkv, query, key, value,
):
    rows = hid_s.shape[0]
    base = pl.program_id(0) * rows
    perm = hot_matrix(place_row[...] == base + iota((rows, place_row.shape[1]), 0))
    hid = dot(perm, hidden[...])
    hid_s[...] = hid.astype(BF16)
    dy_s[...] = dot(perm, upstream[...]).astype(BF16)
    parts = dot(perm, small[...])
    small_s[...] = parts + (pltpu.roll(parts, LANES - 16, 1) + pltpu.roll(parts, LANES - 32, 1))
    act = normed(hid, gain)
    act_one[...] = act
    low, q_val, k_val, value[...] = project(
        act, mask[...], cosine[...], sine[...], w_qkv, a_in, b_out
    )
    low_qkv[...] = low
    query[...], key[...] = q_val, k_val


def normed(values, gain):
    scale = lax.rsqrt(jnp.mean(values * values, axis=-1, keepdims=True) + EPSILON)
    return (values * scale * gain[...].astype(F32)).astype(BF16)


def project(act, mask, cos, sin, w_qkv, a_in, b_out):
    low = (dot(act, a_in[...]) * mask.astype(F32)).astype(BF16)
    turned = []
    for start, factor in ((0, HEAD_DIM**-0.5), (MODEL_WIDTH, 1.0)):
        cols = slice(start, start + MODEL_WIDTH)
        vals = dot(act, w_qkv[:, cols]) + dot(low, b_out[:, cols])
        pieces = []
        for c in range(MODEL_WIDTH // LANES):
            piece = vals[:, c * LANES : (c + 1) * LANES]
            piece = (piece * cos + half_swap(piece) * sin).astype(BF16)
            pieces.append(piece if factor == 1.0 else piece * jnp.asarray(factor, BF16))
        turned.append(jnp.concatenate(pieces, axis=1))
    value = dot(act, w_qkv[:, 2 * MODEL_WIDTH :]) + dot(low, b_out[:, 2 * MODEL_WIDTH :])
    return low, turned[0], turned[1], value.astype(BF16)


def head_mask(shape, head):
    lane = iota(shape, 1)
    return (lane >= head * HEAD_DIM) & (lane < (head + 1) * HEAD_DIM)


def attention_fwd_body(query, key, value, starts, attended, lse):
    attention_fwd_pair(pl.program_id(0), query, key, value, starts, attended, lse)


def visible(lo, hi, starts):
    rows = iota((hi, hi - lo), 0)
    return (rows <= lo + iota((hi, hi - lo), 1)) & (rows >= starts[:, lo:hi])


def attention_fwd_pair(pair, query, key, value, starts, attended, lse):
    size = ROW_BLOCK
    zero = jnp.zeros((), BF16)
    for blk in range(query.shape[0] // size):
        lo, hi = blk * size, (blk + 1) * size
        q_blk = query[lo:hi, :]
        k_all = key[:hi, :]
        v_all = value[:hi, :]
        allowed = visible(lo, hi, starts)
        total = jnp.zeros((size, LANES), F32)
        for head in range(2):
            mine = head_mask((size, LANES), head)
            scores = dot_nt(k_all, jnp.where(mine, q_blk, zero))
            scores = jnp.where(allowed, scores, -1000000000.0)
            top = jnp.max(scores, axis=0, keepdims=True)
            expo = jnp.exp(scores - top)
            norm = jnp.sum(expo, axis=0, keepdims=True)
            prob = (expo * (1.0 / norm)).astype(BF16)
            total = jnp.where(mine, dot_tn(prob, v_all), total)
            lse[pl.ds(2 * pair + head, 1), lo:hi] = top + jnp.log(norm)
        attended[lo:hi, :] = total.astype(BF16)


def attention_bwd_body(
    query, key, value, dout, attended, lse, starts, cosine, sine, d_query, d_key, d_value, kacc, vacc
):
    pair = pl.program_id(0)
    tok = query.shape[0]
    size = ROW_BLOCK
    zero = jnp.zeros((), BF16)
    kacc[...] = jnp.zeros_like(kacc)
    vacc[...] = jnp.zeros_like(vacc)
    for blk in range(tok // size):
        lo, hi = blk * size, (blk + 1) * size
        q_blk = query[lo:hi, :]
        do_blk = dout[lo:hi, :]
        k_all = key[:hi, :]
        v_all = value[:hi, :]
        allowed = visible(lo, hi, starts)
        prod = (do_blk.astype(F32) * attended[lo:hi, :].astype(F32)).T
        probs, dscores, q_heads, do_heads = [], [], [], []
        q_total = jnp.zeros((size, LANES), F32)
        for head in range(2):
            mine = head_mask((size, LANES), head)
            q_heads.append(jnp.where(mine, q_blk, zero))
            do_heads.append(jnp.where(mine, do_blk, zero))
            lse_head = lse[pl.ds(2 * pair + head, 1), lo:hi]
            delta = jnp.sum(
                prod[head * HEAD_DIM : (head + 1) * HEAD_DIM], axis=0, keepdims=True
            )
            scores = dot_nt(k_all, q_heads[head])
            prob = jnp.where(allowed, jnp.exp(scores - lse_head), 0.0)
            dprob = dot_nt(v_all, do_heads[head])
            dscores.append((prob * (dprob - delta)).astype(BF16))
            probs.append(prob.astype(BF16))
            k_head = jnp.where(head_mask((hi, LANES), head), k_all, zero)
            q_total = q_total + dot_tn(dscores[head], k_head)
        kacc[:hi, :] += dot(jnp.concatenate(dscores, axis=1), jnp.concatenate(q_heads, axis=0))
        vacc[:hi, :] += dot(jnp.concatenate(probs, axis=1), jnp.concatenate(do_heads, axis=0))
        q_total = q_total * HEAD_DIM**-0.5
        d_query[lo:hi, :] = (
            q_total * cosine[lo:hi, :] - half_swap(q_total) * sine[lo:hi, :]
        ).astype(BF16)
    for blk in range(tok // size):
        lo, hi = blk * size, (blk + 1) * size
        k_total = kacc[lo:hi, :]
        d_key[lo:hi, :] = (
            k_total * cosine[lo:hi, :] - half_swap(k_total) * sine[lo:hi, :]
        ).astype(BF16)
    d_value[...] = vacc[...].astype(BF16)


def start_kernel(send_to, hear_from, count):
    barrier = pltpu.get_barrier_semaphore()
    for device, remote in hear_from:
        if remote is None:
            pl.semaphore_signal(barrier, inc=1, device_id=device, device_id_type=MESH_ID)
        else:

            @pl.when(remote)
            def _(device=device):
                pl.semaphore_signal(barrier, inc=1, device_id=device, device_id_type=MESH_ID)

    pl.semaphore_wait(barrier, count)


def pair_front_body(
    kinds, a_rows, b_rows,
    lengths, adapters, place_row, hidden, upstream, carry, choices, gains,
    router_in, const_in, in_qkv, in_out, in_a_qkv, in_a_out, in_b_qkv, in_b_out,
    in_gu, in_b_gu, in_dn, in_b_dn, in_a_gu, in_a_dn, *rest,
):
    count = FRONT_KEPT
    outs, rest = rest[:count], rest[count:]
    (all_wide, all_mid, all_thin, came, last_sent, came_kinds), rest = rest[:6], rest[6:]
    kept, rest = rest[:count], rest[count:]
    (
        hid_s, dy_s, small_s, act_one, low_qkv, mask, starts, cosine, sine, router,
        query, key, value, w_qkv, a_qkv, b_qkv, w_out, a_out, b_out,
        attn_low, lse, low_out, resid, act_two, gate, slot,
    ) = kept
    (
        g_qkv, g_out, own_wide, own_mid, own_thin, sent, sent_kinds, slot_rows,
        a_send, a_recv, z_send, e_send, e_recv, out_sems, own_sems, row_send, row_recv,
    ) = rest
    gain_one, gain_two = gains[0:1, :], gains[1:2, :]
    dp, z = lax.axis_index("dp"), lax.axis_index("expert")
    core, x_bit, y_bit = dp % 2, dp // 2 % 2, dp // 4
    across = dp + 1 - 2 * core
    x_dev, y_dev = dp + 2 - 4 * x_bit, dp + 4 - 8 * y_bit
    diag = x_dev + 4 - 8 * y_bit
    far = (z + 2) % 4
    home = z // 2
    columns = (dp, x_dev, y_dev, diag)
    tok = hidden.shape[0]
    blocks = tok // ROW_BLOCK

    def remote(source, target, send, recv, device):
        return pltpu.make_async_remote_copy(
            src_ref=source, dst_ref=target, send_sem=send, recv_sem=recv,
            device_id=device, device_id_type=MESH_ID,
        )

    packs = (g_qkv, g_out)

    def at(kind, back):
        return columns[kind] * 4 + (z + 4 - back) % 4

    def shard(p, kind, back, rows=None):
        view = packs[p].at[at(kind, back)]
        if rows is None:
            return view
        half = packs[p].shape[1] // 2
        return view.at[pl.ds(rows * half, half)]

    def z_up(p, t):
        view = shard(p, 0, t)
        return remote(view, view, z_send.at[p, t], a_recv.at[p, t], (dp, z + 1))

    def z_down(p, t):
        view = shard(p, 0, (4 - t) % 4)
        return remote(view, view, z_send.at[p, 3 + t], a_recv.at[p, 2 - t], (dp, z - 1))

    def z_sends(p, t, act):
        @pl.when((z < 3) & (z >= t))
        def _():
            act(z_up(p, t))

        @pl.when((z > 0) & (z + t <= 3))
        def _():
            act(z_down(p, t))

    def to_x(p, back):
        return remote(
            shard(p, 0, back), shard(p, 0, back), a_send.at[p, 3 + back], a_recv.at[p, 3 + back],
            (x_dev, z),
        )

    def to_y(p, back):
        return remote(
            shard(p, 0, back), shard(p, 0, back), a_send.at[p, 7 + back], a_recv.at[p, 7 + back],
            (y_dev, z),
        )

    def relay_y(p, back):
        return remote(
            shard(p, 1, back, 0), shard(p, 1, back, 0), a_send.at[p, 11 + back],
            a_recv.at[p, 11 + back], (y_dev, z),
        )

    def relay_x(p, back):
        return remote(
            shard(p, 2, back, 1), shard(p, 2, back, 1), a_send.at[p, 15 + back],
            a_recv.at[p, 15 + back], (x_dev, z),
        )

    def to_core(p, kind, back):
        sem = 19 + 4 * kind + back
        return remote(
            shard(p, kind, back), shard(p, kind, back), a_send.at[p, sem], a_recv.at[p, sem],
            (across, z),
        )

    half_wide = own_wide.shape[1] // 2
    parts = []
    for own, everything, cols in (
        (own_mid, all_mid, None), (own_thin, all_thin, None),
        (own_wide, all_wide, (0, half_wide)), (own_wide, all_wide, (half_wide, half_wide)),
    ):
        if cols is None:
            parts.append((own, lambda d, ref=everything: ref.at[d]))
        else:
            parts.append(
                (own.at[:, pl.ds(*cols)], lambda d, ref=everything, c=cols: ref.at[d, :, pl.ds(*c)])
            )
    chunks = ((0, 1), (2,), (3,))

    def first_far(a):
        return remote(
            parts[a][0], parts[a][1](dp), e_send.at[a, 0], e_recv.at[a, core],
            (dp - core + home, far),
        )

    def first_across(a):
        return remote(
            parts[a][0], parts[a][1](dp), e_send.at[a, 1], e_recv.at[a, core], (across, z)
        )

    def first_keep(a):
        return pltpu.make_async_copy(parts[a][0], parts[a][1](dp), e_recv.at[a, core])

    def first_arrival(a, i):
        view = parts[a][1](dp - core + i)
        return remote(view, view, e_send.at[a, 0], e_recv.at[a, i], (dp, far))

    def expert_hop(a, column, i, sem, device):
        view = parts[a][1](column - core + i)
        return remote(view, view, e_send.at[a, sem], e_recv.at[a, sem], (device, z))

    def expert_x(a, i):
        return expert_hop(a, dp, i, 2 + i, x_dev)

    def expert_y(a, i):
        return expert_hop(a, dp, i, 4 + i, y_dev)

    def expert_relay_y(a):
        return expert_hop(a, x_dev, 0, 6, y_dev)

    def expert_relay_x(a):
        return expert_hop(a, y_dev, 1, 7, x_dev)

    def expert_first(c):
        for a in chunks[c]:
            first_far(a).start()

            @pl.when(core == home)
            def _(a=a):
                first_keep(a).start()

            @pl.when(core != home)
            def _(a=a):
                first_across(a).start()

    def at_home(step, *args):
        @pl.when(core == home)
        def _():
            step(*args)

    def abroad(step, *args):
        @pl.when(core != home)
        def _():
            step(*args)

    def send_sides(a):
        for i in range(2):
            expert_x(a, i).start()
            expert_y(a, i).start()

    def spread_home(c):
        for a in chunks[c]:
            first_keep(a).wait()
            first_arrival(a, 1 - core).wait_recv()
            send_sides(a)

    def spread_far(c):
        for a in chunks[c]:
            for i in range(2):
                first_arrival(a, i).wait_recv()
            send_sides(a)

    def expert_relay(c):
        for a in chunks[c]:
            for i in range(2):
                expert_hop(a, x_dev, i, 2 + i, x_dev).wait_recv()
            expert_relay_y(a).start()
            for i in range(2):
                expert_hop(a, y_dev, i, 4 + i, y_dev).wait_recv()
            expert_relay_x(a).start()

    def expert_finish(c):
        for a in chunks[c]:
            expert_hop(a, diag, 0, 6, y_dev).wait_recv()
            expert_hop(a, diag, 1, 7, x_dev).wait_recv()
            first_far(a).wait_send()

            @pl.when(core != home)
            def _(a=a):
                first_across(a).wait_send()

            for i in range(2):
                expert_x(a, i).wait_send()
                expert_y(a, i).wait_send()
            expert_relay_y(a).wait_send()
            expert_relay_x(a).wait_send()

    gu_rows, up_rows, dn_rows = in_gu.shape[1], in_b_gu.shape[1], in_dn.shape[1]
    own_loads = [
        pltpu.make_async_copy(source.at[0], target.at[pl.ds(at_row, rows)], own_sems.at[i])
        for i, (source, target, at_row, rows) in enumerate((
            (in_gu, own_wide, 0, gu_rows), (in_b_gu, own_wide, gu_rows, up_rows),
            (in_dn, own_mid, 0, dn_rows), (in_b_dn, own_mid, dn_rows, up_rows),
            (in_a_gu, own_thin, 0, gu_rows), (in_a_dn, own_thin, gu_rows, dn_rows),
        ))
    ]
    for load in own_loads:
        load.start()
    for gathered, weight, adapter_in, adapter_out in (
        (g_qkv, in_qkv, in_a_qkv, in_b_qkv), (g_out, in_out, in_a_out, in_b_out),
    ):
        spare = gathered.shape[1] - a_rows - b_rows
        wide_cols = weight.shape[1]
        gathered[at(0, 0), :, :wide_cols] = jnp.concatenate(
            [weight[...].astype(F32), adapter_out[...].astype(F32), jnp.zeros((spare, wide_cols), F32)],
            axis=0,
        ).astype(BF16)
        gathered[at(0, 0), :, wide_cols:] = jnp.concatenate(
            [adapter_in[...].astype(F32), jnp.zeros((spare + b_rows, LANES), F32)], axis=0
        ).astype(BF16)
    next_z = z + 1 - 2 * (z % 2)
    peers = [(x_dev, z), (y_dev, z), (across, z), (across, far), (across, next_z)]
    peers += [(dp, (z + j) % 4) for j in (1, 2, 3)]
    start_kernel(None, [(device, None) for device in peers], len(peers))
    def send_own(p):
        z_sends(p, 0, lambda copy: copy.start())
        to_x(p, 0).start()
        to_y(p, 0).start()
        to_core(p, 0, 0).start()

    send_own(0)
    router[...] = jnp.concatenate(
        [router_in[...].astype(F32), jnp.zeros((CONST_LANE - kinds, MODEL_WIDTH), F32),
         const_in[...].astype(F32), jnp.zeros((LANES - CONST_LANE - 4, MODEL_WIDTH), F32)],
        axis=0,
    ).astype(BF16)
    small_s[...] = jnp.zeros_like(small_s)
    carry_parts = split_three(carry[...])
    choices_low = choices[...].astype(F32).astype(BF16)
    half_dim = HEAD_DIM // 2
    freq = jnp.exp(
        (iota((1, LANES), 1) % half_dim).astype(F32) * (-math.log(10000.0) / half_dim)
    )
    sign = jnp.where(iota((1, LANES), 1) % HEAD_DIM < half_dim, -1.0, 1.0)

    def block_rows(b):
        return pl.ds(pl.multiple_of(b * ROW_BLOCK, ROW_BLOCK), ROW_BLOCK)

    def arrange(b, carry_on):
        rows = block_rows(b)
        perm = hot_matrix(place_row[...] == b * ROW_BLOCK + iota((ROW_BLOCK, tok), 0))
        hid = dot(perm, hidden[...])
        hid_s[rows, :] = hid.astype(BF16)
        act_one[rows, :] = normed(hid, gain_one)
        return carry_on

    def arrange_rest(b, carry_on):
        rows = block_rows(b)
        perm = hot_matrix(place_row[...] == b * ROW_BLOCK + iota((ROW_BLOCK, tok), 0))
        dy_s[rows, :] = dot(perm, upstream[...]).astype(BF16)
        top, mid, last = carry_parts
        small_s[rows, :kinds] = dot_nt(perm, top) + (dot_nt(perm, mid) + dot_nt(perm, last))
        small_s[rows, CHOICE_LANE : CHOICE_LANE + 2] = dot_nt(perm, choices_low)
        return carry_on

    place = iota((1, tok), 1)
    begin_row = jnp.zeros((1, tok), jnp.int32)
    begin = 0
    for n in range(1, lengths.shape[1]):
        begin = begin + lengths[0, n - 1]
        begin_row = jnp.where(place >= begin, begin, begin_row)
    starts[...] = begin_row

    def positions(b, carry_on):
        rows = block_rows(b)
        stream = b * ROW_BLOCK + iota((ROW_BLOCK, 1), 0)
        start = jnp.zeros((ROW_BLOCK, 1), jnp.int32)
        adapter = start + adapters[0, 0]
        begin = 0
        for n in range(1, lengths.shape[1]):
            begin = begin + lengths[0, n - 1]
            start = jnp.where(stream >= begin, begin, start)
            adapter = jnp.where(stream >= begin, adapters[0, n], adapter)
        mask[rows, :] = hot_matrix(iota((ROW_BLOCK, LANES), 1) // ADAPTER_RANK == adapter)
        angle = (stream - start).astype(F32) * freq
        cosine[rows, :] = jnp.cos(angle)
        sine[rows, :] = jnp.sin(angle) * sign
        return carry_on

    lax.fori_loop(0, blocks, arrange, 0)

    at_end = (z == 0) | (z == 3)
    order = (
        jnp.where(z == 0, 3, 1), jnp.where(at_end, 2, 3),
        jnp.where(z == 0, 1, jnp.where(z == 3, 3, 2)),
    )

    def spread_shard(p, back):
        view = shard(p, 0, back)
        remote(view, view, z_send.at[p, 0], a_recv.at[p, back - 1], (dp, z)).wait_recv()
        to_x(p, back).start()
        to_y(p, back).start()
        to_core(p, 0, back).start()

    def from_z(p, t):
        @pl.when(z > t)
        def _():
            spread_shard(p, 1 + t)

        @pl.when(z + t < 3)
        def _():
            spread_shard(p, 3 - t)

        if t < 2:
            z_sends(p, t + 1, lambda copy: copy.start())

    def from_sides(p, back):
        view = shard(p, 1, back)
        remote(view, view, a_send.at[p, 3 + back], a_recv.at[p, 3 + back], (x_dev, z)).wait_recv()
        relay_y(p, back).start()
        to_core(p, 1, back).start()
        view = shard(p, 2, back)
        remote(view, view, a_send.at[p, 7 + back], a_recv.at[p, 7 + back], (y_dev, z)).wait_recv()
        relay_x(p, back).start()
        to_core(p, 2, back).start()

    def from_diag(p, back):
        view = shard(p, 3, back, 0)
        remote(view, view, a_send.at[p, 11 + back], a_recv.at[p, 11 + back], (y_dev, z)).wait_recv()
        view = shard(p, 3, back, 1)
        remote(view, view, a_send.at[p, 15 + back], a_recv.at[p, 15 + back], (x_dev, z)).wait_recv()
        to_core(p, 3, back).start()

    for t in range(3):
        from_z(0, t)
    send_own(1)
    from_sides(0, 0)
    lax.fori_loop(0, 2, arrange_rest, 0)
    from_sides(0, order[0])
    lax.fori_loop(2, 4, arrange_rest, 0)
    from_sides(0, order[1])
    lax.fori_loop(4, blocks, arrange_rest, 0)
    from_sides(0, order[2])
    for t in range(3):
        from_z(1, t)
    for load in own_loads:
        load.wait()
    for c in range(len(chunks)):
        expert_first(c)
    for back in (0,) + order[:2]:
        from_diag(0, back)
    lax.fori_loop(0, blocks, positions, 0)
    place_slots(4, small_s, slot, slot_rows)
    from_diag(0, order[2])
    core_columns = (across, x_dev + across - dp, y_dev + across - dp, diag + across - dp)

    def from_core(p):
        def body(back, carry):
            for kind in range(4):
                view = packs[p].at[core_columns[kind] * 4 + (z + 4 - back) % 4]
                sem = 19 + 4 * kind + back
                remote(view, view, a_send.at[p, sem], a_recv.at[p, sem], (across, z)).wait_recv()
            return carry

        lax.fori_loop(0, 4, body, 0)

    width = MODEL_WIDTH
    total = g_qkv.shape[0]

    def lay_rows(i, carry, gathered, targets):
        pair = [gathered[2 * i + n, :a_rows, :].astype(F32) for n in range(2)]
        both = jnp.concatenate(pair, axis=0).astype(BF16)
        rows = pl.ds(pl.multiple_of(i * 2 * a_rows, 16), 2 * a_rows)
        start = 0
        for target in targets:
            target[rows, :] = both[:, start : start + target.shape[1]]
            start += target.shape[1]
        return carry

    def lay_ups(i, carry, gathered, target):
        group = 16 // b_rows
        pieces = [
            gathered[group * i + n, a_rows : a_rows + b_rows, : target.shape[1]].astype(F32)
            for n in range(group)
        ]
        rows = pl.ds(pl.multiple_of(i * 16, 16), 16)
        target[rows, :] = jnp.concatenate(pieces, axis=0).astype(BF16)
        return carry

    def lay(gathered, targets, ups):
        lax.fori_loop(
            0, total // 2, functools.partial(lay_rows, gathered=gathered, targets=targets), 0
        )
        lax.fori_loop(
            0, total * b_rows // 16, functools.partial(lay_ups, gathered=gathered, target=ups), 0
        )

    def flush(first, last):
        return [
            pltpu.make_async_copy(kept[i], outs[i], out_sems.at[i]) for i in range(first, last)
        ]

    for back in (0,) + order:
        from_sides(1, back)
    for c in range(len(chunks)):
        at_home(spread_home, c)
    from_core(0)
    lay(g_qkv, (w_qkv, a_qkv), b_qkv)

    def projection(b, carry):
        rows = block_rows(b)
        low_qkv[rows, :], query[rows, :], key[rows, :], value[rows, :] = project(
            act_one[rows, :], mask[rows, :], cosine[rows, :], sine[rows, :], w_qkv, a_qkv, b_qkv
        )

        return carry

    lax.fori_loop(0, blocks, projection, 0)
    abroad(spread_far, 0)
    for copy in flush(0, 16):
        copy.start()
    lse[...] = jnp.zeros_like(lse)

    def attention(pair, carry):
        cols = pl.ds(pl.multiple_of(pair * LANES, LANES), LANES)
        attention_fwd_pair(
            pair, query.at[:, cols], key.at[:, cols], value.at[:, cols], starts,
            attn_low.at[:, cols], lse,
        )

        @pl.when(pair == 0)
        def _():
            for back in (0,) + order:
                from_diag(1, back)
            at_home(expert_relay, 0)

        @pl.when(pair == 2)
        def _():
            at_home(expert_relay, 1)

        @pl.when(pair == 3)
        def _():
            abroad(spread_far, 1)
            abroad(expert_relay, 0)

        @pl.when(pair == 4)
        def _():
            at_home(expert_relay, 2)

        return carry

    lax.fori_loop(0, HEAD_COUNT // 2, attention, 0)
    from_core(1)
    lay(g_out, (w_out, a_out), b_out)
    for copy in flush(16, 21):
        copy.start()

    def after(b, carry):
        rows = block_rows(b)
        low_out[rows, :], resid[rows, :], act_two[rows, :], gate[rows, :] = post_attn(
            kinds, attn_low[rows, :], hid_s[rows, :], mask[rows, :], small_s[rows, :],
            w_out, a_out, b_out, router, gain_two,
        )
        return carry

    lax.fori_loop(0, blocks, after, 0)
    abroad(spread_far, 2)
    abroad(expert_relay, 1)
    for copy in flush(21, FRONT_KEPT):
        copy.start()

    def rows_out(k):
        device = ((dp, next_z), (across, z))[k - 1]
        return remote(sent.at[k], came.at[k], row_send.at[k], row_recv.at[k], device)

    last_local = pltpu.make_async_copy(sent.at[0], last_sent, row_send.at[3])
    own_local = pltpu.make_async_copy(sent.at[0], came.at[0], row_send.at[0])
    some = pl.ds(0, last_sent.shape[0] // 2)
    last_half = remote(
        last_sent.at[some], came.at[3, some], row_send.at[4], row_recv.at[3], (across, next_z)
    )
    def kinds_out(k):
        device = ((dp, next_z), (across, z), (across, next_z))[k - 1]
        return remote(
            sent_kinds.at[k], came_kinds.at[k], row_send.at[4 + k], row_recv.at[3 + k], device
        )

    own_kinds = pltpu.make_async_copy(sent_kinds.at[0], came_kinds.at[0], row_send.at[8])

    def fill(n, carry):
        k = (n + 1) % 4
        eid = (z + k) % 2 + 2 * ((core + k // 2) % 2)
        fill_slots(eid, gate, act_two, dy_s, mask, slot_rows, sent.at[k % 3], sent_kinds.at[k])

        @pl.when(n == 0)
        def _():
            kinds_out(1).start()
            rows_out(1).start()

        @pl.when(n == 1)
        def _():
            kinds_out(2).start()
            rows_out(2).start()

        @pl.when(n == 2)
        def _():
            last_local.start()
            last_local.wait()
            kinds_out(3).start()
            last_half.start()

        return carry

    lax.fori_loop(0, 4, fill, 0)
    own_local.start()
    own_kinds.start()
    abroad(expert_relay, 2)
    for c in range(len(chunks)):
        expert_finish(c)
    for k in (1, 2):
        rows_out(k).wait_recv()
        rows_out(k).wait_send()
    last_half.wait_recv()
    last_half.wait_send()
    own_local.wait()
    own_kinds.wait()
    for k in (1, 2, 3):
        kinds_out(k).wait_recv()
        kinds_out(k).wait_send()

    def attn_sent(n, carry):
        for p in range(2):
            to_x(p, n).wait_send()
            to_y(p, n).wait_send()
            relay_x(p, n).wait_send()
            relay_y(p, n).wait_send()
            for kind in range(4):
                to_core(p, kind, n).wait_send()
        return carry

    lax.fori_loop(0, 4, attn_sent, 0)
    for p in range(2):
        for t in range(3):
            z_sends(p, t, lambda copy: copy.wait_send())
    for copy in flush(0, FRONT_KEPT):
        copy.wait()


def pair_attention_bwd_body(
    query, key, value, dout, attended, lse, starts, cosine, sine, ga_out, gb_out,
    ga_gu, gb_gu, ga_dn, gb_dn,
    d_query, d_key, d_value, own_ga_gu, own_gb_gu, own_ga_dn, own_gb_dn, plane_ga_out, plane_gb_out,
    kacc, vacc, *rest,
):
    mine, got, halves, final = (rest[4 * n : 4 * n + 4] for n in range(4))
    (
        s_ga_out, s_gb_out, r_ga_out, r_gb_out,
        own_sems, side_send, side_recv, end_send, end_recv, near_send, near_recv,
    ) = rest[16:]
    dp, z = lax.axis_index("dp"), lax.axis_index("expert")
    core, spot, half = dp % 2, dp // 2, z // 2
    far = (z + 2) % 4
    across = dp + 1 - 2 * core
    home = core == half
    away = core + half - 2 * core * half
    owners, spots = 8, 4
    sources = (ga_gu, gb_gu, ga_dn, gb_dn)
    outs = (own_ga_gu, own_gb_gu, own_ga_dn, own_gb_dn)
    plane_groups = (
        (s_ga_out, r_ga_out, plane_ga_out), (s_gb_out, r_gb_out, plane_gb_out),
    )

    def remote(source, target, send, recv, device):
        return pltpu.make_async_remote_copy(
            src_ref=source, dst_ref=target, send_sem=send, recv_sem=recv,
            device_id=device, device_id_type=MESH_ID,
        )

    def share(i, d):
        count = plane_groups[i][1].shape[1]
        return plane_groups[i][0].at[pl.ds(pl.multiple_of(d * count, 16), count)]

    def near(i, n):
        goal = (dp + n + 1) % owners
        return remote(
            share(i, goal), plane_groups[i][1].at[n], near_send.at[i, n], near_recv.at[i, n], (goal, z)
        )

    def quarter(i, m):
        count = mine[i].shape[0]
        return sources[i].at[pl.ds(pl.multiple_of(m * count, 16), count)]

    def keep(i):
        return pltpu.make_async_copy(quarter(i, spot), mine[i], own_sems.at[i])

    def side(i, n):
        goal = (spot + n + 1) % spots
        return remote(
            quarter(i, goal), got[i].at[n], side_send.at[i, n], side_recv.at[i, n],
            (2 * goal + core, z),
        )

    def to_across(i):
        return remote(
            halves[i].at[1 - core], final[i].at[0], end_send.at[i, 0], end_recv.at[i, 0], (across, z)
        )

    def to_far(i, h):
        return remote(
            halves[i].at[h], final[i].at[1], end_send.at[i, h], end_recv.at[i, 1],
            (dp - core + h, far),
        )

    step = pl.program_id(0)

    @pl.when(step == 0)
    def _():
        s_ga_out[...] = ga_out[...].astype(BF16)
        s_gb_out[...] = gb_out[...].astype(BF16)
        senders = [((dp - core + half, far), None)]
        senders += [(((dp + n) % owners, z), None) for n in range(1, owners)]
        start_kernel(None, senders, owners - 1 + 2 * away)
        for i in range(4):
            keep(i).start()

        def send_side(n, carry):
            for i in range(4):
                side(i, n).start()
            return carry

        lax.fori_loop(0, spots - 1, send_side, 0)

        def send_near(n, carry):
            for i in range(2):
                near(i, n).start()
            return carry

        lax.fori_loop(0, owners - 1, send_near, 0)

    @pl.when(step == pl.num_programs(0) - 2)
    def _():
        for i in range(4):
            keep(i).wait()
            total = mine[i][...].astype(F32)
            for n in range(spots - 1):
                side(i, n).wait_recv()
                total = total + got[i][n].astype(F32)
            count = halves[i].shape[1]
            for h in range(2):
                halves[i][h] = total[h * count : (h + 1) * count].astype(BF16)

            @pl.when(home)
            def _(i=i):
                to_across(i).start()

            @pl.when(jnp.logical_not(home))
            def _(i=i):
                for h in range(2):
                    to_far(i, h).start()

    attention_bwd_body(
        query, key, value, dout, attended, lse, starts, cosine, sine, d_query, d_key, d_value,
        kacc, vacc,
    )

    @pl.when(step == pl.num_programs(0) - 1)
    def _():
        for i in range(4):
            to_far(i, 0).wait_recv()

            @pl.when(home)
            def _(i=i):
                outs[i][...] = halves[i][core].astype(F32) + final[i][1].astype(F32)
                to_across(i).wait_send()

            @pl.when(jnp.logical_not(home))
            def _(i=i):
                to_across(i).wait_recv()
                outs[i][...] = final[i][0].astype(F32) + final[i][1].astype(F32)
                for h in range(2):
                    to_far(i, h).wait_send()

        def sent_side(n, carry):
            for i in range(4):
                side(i, n).wait_send()
            return carry

        lax.fori_loop(0, spots - 1, sent_side, 0)

        def finish_near(n, carry):
            for i in range(2):
                near(i, n).wait_recv()
                near(i, n).wait_send()
            return carry

        lax.fori_loop(0, owners - 1, finish_near, 0)
        for i, (_, target, out) in enumerate(plane_groups):
            total = share(i, dp)[...].astype(F32)
            for n in range(owners - 1):
                total = total + target[n].astype(F32)
            out[...] = total


def pair_tail_body(
    place_row, mask, a_in, b_out, gain, a_o, b_o, d_logits,
    q_hbm, k_hbm, v_hbm, low_hbm, act_hbm, hid_hbm, resid_hbm, w_hbm, out_hbm,
    out, grad_hidden, grad_gate, own_ga_qkv, own_gb_qkv, own_ga_out, own_gb_out,
    d_query, d_key, d_value, low_qkv, act_one,
    hid_s, d_resid, w_qkv, out_s, place_col, high, lower, d_low_all, ga_sum, gb_sum,
    s_ga_qkv, s_gb_qkv, r_ga_qkv, r_gb_qkv,
    thin_out, wide_out, thin_in, wide_in, load_sems, send_sems, recv_sems, far_send, far_recv,
):
    dp, z = lax.axis_index("dp"), lax.axis_index("expert")
    others, planes = 7, 3
    tok = place_row.shape[1]
    blocks = tok // ROW_BLOCK
    loads = [
        pltpu.make_async_copy(source, target, load_sems.at[i])
        for i, (source, target) in enumerate(
            ((q_hbm, d_query), (k_hbm, d_key), (v_hbm, d_value), (low_hbm, low_qkv),
             (act_hbm, act_one), (w_hbm, w_qkv), (hid_hbm, hid_s), (resid_hbm, d_resid),
             (out_hbm, out_s))
        )
    ]
    for load in loads:
        load.start()
    start_kernel(
        None,
        [(((dp + i) % 8, z), None) for i in range(1, 8)] + [((dp, (z + j) % 4), None) for j in (1, 2, 3)],
        others + planes,
    )
    ga_sum[...] = jnp.zeros_like(ga_sum)
    gb_sum[...] = jnp.zeros_like(gb_sum)
    parts = [slice(p * MODEL_WIDTH, (p + 1) * MODEL_WIDTH) for p in range(3)]
    d_refs = (d_query, d_key, d_value)

    def block_rows(b):
        return pl.ds(pl.multiple_of(b * ROW_BLOCK, ROW_BLOCK), ROW_BLOCK)

    def sums(b, carry):
        rows = block_rows(b)
        low = low_qkv[rows, :]
        d_low = jnp.zeros((ROW_BLOCK, LANES), F32)
        for cols, ref in zip(parts, d_refs):
            grad = ref[rows, :]
            d_low = d_low + dot_nt(grad, b_out[:, cols])
            gb_sum[:, cols] += dot_tn(low, grad)
        d_low = (d_low * mask[rows, :].astype(F32)).astype(BF16)
        d_low_all[rows, :] = d_low
        ga_sum[...] += dot_tn(act_one[rows, :], d_low)
        return carry

    for load in loads[:5]:
        load.wait()
    lax.fori_loop(0, blocks, sums, 0)
    s_ga_qkv[...] = ga_sum[...].astype(BF16)
    s_gb_qkv[...] = gb_sum[...].astype(BF16)
    groups = ((s_ga_qkv, r_ga_qkv), (s_gb_qkv, r_gb_qkv))

    def share(i, d):
        count = groups[i][1].shape[1]
        return groups[i][0].at[pl.ds(pl.multiple_of(d * count, 16), count)]

    def near(i, n):
        goal = (dp + n + 1) % 8
        return pltpu.make_async_remote_copy(
            src_ref=share(i, goal), dst_ref=groups[i][1].at[n], send_sem=send_sems.at[i, n],
            recv_sem=recv_sems.at[i, n], device_id=(goal, z), device_id_type=MESH_ID,
        )

    def send_near(n, carry):
        for i in range(2):
            near(i, n).start()
        return carry

    lax.fori_loop(0, others, send_near, 0)

    for load in loads[5:8]:
        load.wait()

    def back(b, carry):
        rows = block_rows(b)
        d_act = dot_nt(d_low_all[rows, :], a_in[...])
        for cols, ref in zip(parts, d_refs):
            d_act = d_act + dot_nt(ref[rows, :], w_qkv[:, cols])
        hid = hid_s[rows, :].astype(F32)
        scale = lax.rsqrt(jnp.mean(hid * hid, axis=-1, keepdims=True) + EPSILON)
        weighted = d_act * gain[...].astype(F32)
        grad_hid = d_resid[rows, :] + (
            scale * weighted
            - hid * (scale * scale * scale) * jnp.mean(hid * weighted, axis=-1, keepdims=True)
        )
        top = grad_hid.astype(BF16)
        high[rows, :] = top
        lower[rows, :] = (grad_hid - top.astype(F32)).astype(BF16)
        return carry

    lax.fori_loop(0, blocks, back, 0)
    place_col[...] = jnp.broadcast_to(place_row[...].astype(F32), (LANES, tok)).T

    def near_done(n, carry):
        for i in range(2):
            near(i, n).wait_recv()
        return carry

    lax.fori_loop(0, others, near_done, 0)
    totals = []
    for i in range(2):
        total = share(i, dp)[...].astype(F32)
        for n in range(others):
            total = total + groups[i][1][n].astype(F32)
        totals.append(total)
    a_qkv, b_qkv = totals
    a_count, b_count = a_qkv.shape[0] // 4, b_qkv.shape[0] // 4
    for p in range(4):
        a_rows, b_rows = slice(p * a_count, (p + 1) * a_count), slice(p * b_count, (p + 1) * b_count)
        thin_out[p, :a_count, :LANES] = a_qkv[a_rows].astype(BF16)
        thin_out[p, :a_count, LANES:] = a_o[a_rows, :].astype(BF16)
        thin_out[p, a_count:, :] = jnp.zeros((thin_out.shape[1] - a_count, 2 * LANES), BF16)
        wide_out[p] = jnp.concatenate(
            [b_qkv[b_rows, cols] for cols in parts] + [b_o[b_rows, :]], axis=0
        ).astype(BF16)

    def far(i, j):
        goal = (z + j + 1) % 4
        source, target = ((thin_out, thin_in), (wide_out, wide_in))[i]
        return pltpu.make_async_remote_copy(
            src_ref=source.at[goal], dst_ref=target.at[j], send_sem=far_send.at[i, j],
            recv_sem=far_recv.at[i, j], device_id=(dp, goal), device_id_type=MESH_ID,
        )

    for j in range(planes):
        for i in range(2):
            far(i, j).start()
    loads[8].wait()

    top, mid, last = (jnp.where(iota((tok, LANES), 1) < 16, v.astype(F32), 0.0) for v in split_three(d_logits[...]))
    logit_parts = (top + pltpu.roll(mid, 16, 1) + pltpu.roll(last, 32, 1)).astype(BF16)

    def to_rows(b, carry):
        rows = block_rows(b)
        perm = hot_matrix(place_col[rows, 0:1].astype(jnp.int32) == iota((ROW_BLOCK, tok), 1))
        out[rows, :] = dot(perm, out_s[...]).astype(BF16)
        grad_hidden[rows, :] = dot(perm, high[...]) + dot(perm, lower[...])
        moved = dot(perm, logit_parts)
        grad_gate[rows, :] = moved + (
            pltpu.roll(moved, LANES - 16, 1) + pltpu.roll(moved, LANES - 32, 1)
        )
        return carry

    lax.fori_loop(0, blocks, to_rows, 0)
    for j in range(planes):
        for i in range(2):
            far(i, j).wait_recv()
    thin = thin_out[z].astype(F32)
    wide = wide_out[z].astype(F32)
    for j in range(planes):
        thin = thin + thin_in[j].astype(F32)
        wide = wide + wide_in[j].astype(F32)
    own_ga_qkv[...] = thin[:a_count, :LANES]
    own_ga_out[...] = thin[:a_count, LANES:]
    for p, cols in enumerate(parts):
        own_gb_qkv[:, cols] = wide[p * b_count : (p + 1) * b_count]
    own_gb_out[...] = wide[3 * b_count : 4 * b_count]

    def sent(n, carry):
        for i in range(2):
            near(i, n).wait_send()
        return carry

    lax.fori_loop(0, others, sent, 0)
    for j in range(planes):
        for i in range(2):
            far(i, j).wait_send()


def settle_body(*refs):
    count = len(refs) // 2
    for n, (source, target) in enumerate(zip(refs[:count], refs[count:])):
        target[...] = source[...].T[: target.shape[0]] if n == 0 else source[...]


def split_three(values):
    top = values.astype(BF16)
    rest = values - top.astype(F32)
    mid = rest.astype(BF16)
    return top, mid, (rest - mid.astype(F32)).astype(BF16)


def post_attn_body(
    kinds, attn_low, hid_s, mask, small_s, w_out, a_out, b_out, router, gain,
    low_out, resid, act_two, gate,
):
    low_out[...], resid[...], act_two[...], gate[...] = post_attn(
        kinds, attn_low[...], hid_s[...], mask[...], small_s[...], w_out, a_out, b_out, router, gain
    )


def post_attn(kinds, attn, hid, mask, sm, w_out, a_out, b_out, router, gain):
    low = (dot(attn, a_out[...]) * mask.astype(F32)).astype(BF16)
    res = hid.astype(F32) + (dot(attn, w_out[...]) + dot(low, b_out[...]))
    act = normed(res, gain)
    logits = dot_nt(act, router[...])
    lane = iota(logits.shape, 1)
    routed = jnp.where(lane < kinds, logits + sm, -1e30)
    top = jnp.max(routed, axis=1, keepdims=True)
    expo = jnp.exp(routed - top)
    prob = expo / jnp.sum(expo, axis=1, keepdims=True)
    return low, res, act, jnp.where(lane < kinds, prob, logits)


def place_slots(experts, small_s, slot, slot_rows):
    tok = slot.shape[0]
    lane = iota((tok, LANES), 1)
    first = small_s[:, CHOICE_LANE : CHOICE_LANE + 1].astype(jnp.int32)
    second = small_s[:, CHOICE_LANE + 1 : CHOICE_LANE + 2].astype(jnp.int32)
    hot = ((first == lane) | (second == lane)) & (lane < experts)
    hot_low = hot_matrix(hot)
    for blk in range(tok // ROW_BLOCK):
        lo, hi = blk * ROW_BLOCK, (blk + 1) * ROW_BLOCK
        tri = hot_matrix(iota((ROW_BLOCK, hi), 1) < lo + iota((ROW_BLOCK, hi), 0))
        rank = dot(tri, hot_low[:hi, :])
        slot[lo:hi, :] = jnp.where(hot[lo:hi, :], rank, -1.0)
    slot_rows[...] = slot[...].T


def adapter_pattern(rows, cols, first):
    lanes = iota((rows, cols), 1)
    start = ADAPTER_RANK * iota((rows, cols), 0)
    return hot_matrix((lanes == start) if first else ((lanes - start) // ADAPTER_RANK == 0) & (lanes >= start))


def fill_slots(eid, gate, act_two, dy_s, mask, slot_rows, target, kinds_target=None):
    row = slot_rows[pl.ds(eid, 1), :].astype(jnp.int32)
    pick = hot_matrix(row == iota((target.shape[0], row.shape[1]), 0))
    value = lane_value(gate[...], eid)
    scaled = (dy_s[...].astype(F32) * value).astype(BF16)
    target[:, :MODEL_WIDTH] = dot(pick, act_two[...]).astype(BF16)
    target[:, MODEL_WIDTH : 2 * MODEL_WIDTH] = dot(pick, scaled).astype(BF16)
    if kinds_target is None:
        target[:, 2 * MODEL_WIDTH :] = dot(pick, mask[...]).astype(BF16)
    else:
        owner = dot_nt(adapter_pattern(kinds_target.shape[0], LANES, True), mask[...]).astype(BF16)
        kinds_target[:, : target.shape[0]] = dot_nt(owner, pick).astype(BF16)


def dispatch_body(experts, eids, small_s, gate, act_two, dy_s, mask, slot, sent, slot_rows):
    step = pl.program_id(0)

    @pl.when(step == 0)
    def _():
        place_slots(experts, small_s, slot, slot_rows)

    fill_slots(eids[step], gate, act_two, dy_s, mask, slot_rows, sent.at[0])


def ffn_math(
    rows, d_out, mask, w_gu, w_dn, a_gu, b_gu, a_dn, b_dn,
    ga_gu, gb_gu, ga_dn, gb_dn, acc_out, acc_dx, acc_low, acc_dlow,
):
    low_gu = (dot(rows, a_gu[...]) * mask).astype(BF16)
    dlow_dn = (dot_nt(d_out, b_dn[...]) * mask).astype(BF16)
    for ref in (acc_out, acc_dx, acc_low, acc_dlow):
        ref[...] = jnp.zeros_like(ref)

    def step(j, carry):
        lo = pl.multiple_of(j * HIDDEN_BLOCK, HIDDEN_BLOCK)
        g_cols = pl.ds(lo, HIDDEN_BLOCK)
        u_cols = pl.ds(pl.multiple_of(FEEDFWD_WIDTH + lo, HIDDEN_BLOCK), HIDDEN_BLOCK)
        gate = dot(rows, w_gu[:, g_cols]) + dot(low_gu, b_gu[:, g_cols])
        up = dot(rows, w_gu[:, u_cols]) + dot(low_gu, b_gu[:, u_cols])
        sig = 1.0 / (1.0 + jnp.exp(-gate))
        silu = gate * sig
        middle = (silu * up).astype(BF16)
        acc_out[...] += dot(middle, w_dn[g_cols, :])
        acc_low[...] += dot(middle, a_dn[g_cols, :])
        d_mid = dot_nt(d_out, w_dn[g_cols, :]) + dot_nt(dlow_dn, a_dn[g_cols, :])
        d_mid = d_mid.astype(BF16).astype(F32)
        d_gate = (d_mid * up * (sig * (1.0 + gate * (1.0 - sig)))).astype(BF16)
        d_up = (d_mid * silu).astype(BF16)
        acc_dx[...] += dot_nt(d_gate, w_gu[:, g_cols]) + dot_nt(d_up, w_gu[:, u_cols])
        acc_dlow[...] += dot_nt(d_gate, b_gu[:, g_cols]) + dot_nt(d_up, b_gu[:, u_cols])
        gb_gu[:, g_cols] += dot_tn(low_gu, d_gate)
        gb_gu[:, u_cols] += dot_tn(low_gu, d_up)
        ga_dn[g_cols, :] += dot_tn(middle, dlow_dn)
        return carry

    lax.fori_loop(0, FEEDFWD_WIDTH // HIDDEN_BLOCK, step, 0)
    low_dn = (acc_low[...] * mask).astype(BF16)
    result = (acc_out[...] + dot(low_dn, b_dn[...])).astype(BF16)
    gb_dn[...] += dot_tn(low_dn, d_out)
    dlow_gu = (acc_dlow[...] * mask).astype(BF16)
    d_rows = (acc_dx[...] + dot_nt(dlow_gu, a_gu[...])).astype(BF16)
    ga_gu[...] += dot_tn(rows, dlow_gu)
    return result, d_rows


def ffn_body(
    came, w_gu, w_dn, a_gu, b_gu, a_dn, b_dn,
    back, ga_gu, gb_gu, ga_dn, gb_dn, acc_out, acc_dx, acc_low, acc_dlow,
):
    @pl.when(pl.program_id(0) == 0)
    def _():
        for ref in (ga_gu, gb_gu, ga_dn, gb_dn):
            ref[...] = jnp.zeros_like(ref)

    back[0, :, :MODEL_WIDTH], back[0, :, MODEL_WIDTH:] = ffn_math(
        came[0, :, :MODEL_WIDTH], came[0, :, MODEL_WIDTH : 2 * MODEL_WIDTH],
        came[0, :, 2 * MODEL_WIDTH :].astype(F32), w_gu, w_dn, a_gu, b_gu, a_dn, b_dn,
        ga_gu, gb_gu, ga_dn, gb_dn, acc_out, acc_dx, acc_low, acc_dlow,
    )


def pair_ffn_body(
    had, last_sent, kinds, wide, mid, thin,
    returned, out_ga_gu, out_gb_gu, out_ga_dn, out_gb_dn,
    came, back, ga_gu, gb_gu, ga_dn, gb_dn, w_gu, w_dn, a_gu, b_gu, a_dn, b_dn, acc_out, acc_dx, acc_low, acc_dlow,
    load_sems, came_sems, back_sems, done_sems, last_sems,
):
    dp, z = lax.axis_index("dp"), lax.axis_index("expert")
    core, plane = dp % 2, z % 2

    def peer(k):
        return (dp + (k // 2) * (1 - 2 * core), z + (k % 2) * (1 - 2 * plane))

    start_kernel(None, [(peer(k), None) for k in (1, 2, 3)], 3)

    half = last_sent.shape[0] // 2
    early, late = pl.ds(0, half), pl.ds(half, half)

    def had_in(k):
        return pltpu.make_async_copy(had.at[k], came.at[k], came_sems.at[k])

    early_in = pltpu.make_async_copy(had.at[3, early], came.at[3, early], came_sems.at[3])
    last_out = pltpu.make_async_remote_copy(
        src_ref=last_sent.at[late], dst_ref=came.at[3, late], send_sem=last_sems.at[0],
        recv_sem=last_sems.at[1], device_id=peer(3), device_id_type=MESH_ID,
    )

    def result_out(k):
        return pltpu.make_async_remote_copy(
            src_ref=back.at[k], dst_ref=returned.at[k], send_sem=back_sems.at[k],
            recv_sem=done_sems.at[k], device_id=peer(k), device_id_type=MESH_ID,
        )

    last_out.start()
    for k in (1, 0, 2):
        had_in(k).start()
    early_in.start()

    gu_rows = w_gu.shape[0] // wide.shape[0]
    up_rows = b_gu.shape[0] // wide.shape[0]
    dn_rows = w_dn.shape[0] // wide.shape[0]
    plans = (
        (wide, 0, gu_rows, w_gu), (wide, gu_rows, up_rows, b_gu), (mid, 0, dn_rows, w_dn),
        (mid, dn_rows, up_rows, b_dn), (thin, 0, gu_rows, a_gu), (thin, gu_rows, dn_rows, a_dn),
    )

    def load(d, carry):
        for i, (source, at, count, target) in enumerate(plans):
            pltpu.make_async_copy(
                source.at[d, pl.ds(at, count)],
                target.at[pl.ds(pl.multiple_of(d * count, 16), count)],
                load_sems.at[i],
            ).start()
        return carry

    lax.fori_loop(0, wide.shape[0], load, 0)
    for ref in (ga_gu, gb_gu, ga_dn, gb_dn):
        ref[...] = jnp.zeros_like(ref)
    for i, (_, _, _, target) in enumerate(plans):
        pltpu.make_async_copy(target, target, load_sems.at[i]).wait()

    def source_step(s, carry):
        k = jnp.where(s < 2, 1 + 2 * s, 2 * s - 4)

        @pl.when(k != 3)
        def _():
            had_in(k).wait()

        @pl.when(k == 3)
        def _():
            early_in.wait()
            last_out.wait_recv()

        back[k, :, :MODEL_WIDTH], back[k, :, MODEL_WIDTH:] = ffn_math(
            came[k, :, :MODEL_WIDTH], came[k, :, MODEL_WIDTH:],
            dot_tn(kinds[k, :, : came.shape[1]], adapter_pattern(kinds.shape[1], LANES, False)), w_gu, w_dn, a_gu, b_gu, a_dn, b_dn,
            ga_gu, gb_gu, ga_dn, gb_dn, acc_out, acc_dx, acc_low, acc_dlow,
        )

        @pl.when(k != 0)
        def _():
            result_out(k).start()

        return carry

    lax.fori_loop(0, 4, source_step, 0)
    for out, total in (
        (out_ga_gu, ga_gu), (out_gb_gu, gb_gu), (out_ga_dn, ga_dn), (out_gb_dn, gb_dn),
    ):
        out[...] = total[...].astype(BF16)
    own_out = pltpu.make_async_copy(back.at[0], returned.at[0], done_sems.at[0])
    own_out.start()
    own_out.wait()
    last_out.wait_send()
    for k in (1, 2, 3):
        result_out(k).wait_send()
        result_out(k).wait_recv()


def combine_body(
    experts, kinds, eids, resid, act_two, dy_s, gate, slot, small_s, low_out, attn_low, mask, came,
    w_out, a_out, b_out, router, const_value, gain,
    out_s, d_resid, d_attended, d_logits, ga_out, gb_out,
):
    @pl.when(pl.program_id(0) == 0)
    def _():
        ga_out[...] = jnp.zeros_like(ga_out)
        gb_out[...] = jnp.zeros_like(gb_out)

    rows = resid.shape[0]
    cap = came.shape[1]
    res = resid[...]
    act = act_two[...].astype(F32)
    dy_low = dy_s[...]
    dy = dy_low.astype(F32)
    lane = iota((rows, LANES), 1)
    levels = gate[...].T
    top = iota((CHOICE_ROWS, rows), 0)
    prob = jnp.where(top < kinds, levels[:CHOICE_ROWS], 0.0)

    def row(values, index):
        return jnp.sum(jnp.where(top == index, values, 0.0), axis=0, keepdims=True)

    picked = small_s[...].T
    first = picked[CHOICE_LANE : CHOICE_LANE + 1]
    second = picked[CHOICE_LANE + 1 : CHOICE_LANE + 2]

    def chosen(kind):
        return jnp.where((first == kind) | (second == kind), 1.0, 0.0)

    has_copy, has_zero, has_one = chosen(experts + 1), chosen(experts + 2), chosen(experts + 3)
    g_copy = has_copy * row(prob, experts + 1)
    g_zero = has_zero * row(prob, experts + 2)
    g_one = has_one * row(prob, experts + 3)

    def pair(at):
        left, right = levels[at : at + 1], levels[at + 1 : at + 2]
        high = jnp.maximum(left, right)
        e_left, e_right = jnp.exp(left - high), jnp.exp(right - high)
        scale = 1.0 / (e_left + e_right)
        return e_left * scale, e_right * scale

    a00, a01 = pair(CONST_LANE)
    a10, a11 = pair(CONST_LANE + 2)
    coef = g_copy + g_zero * a00 + g_one * a10
    factors = [coef, g_zero * a01, g_one * a11]
    factors += [row(prob, eids[k]) for k in range(came.shape[0])]
    spot = iota((LANES, rows), 0)
    columns = jnp.zeros((LANES, rows), F32)
    for n, factor in enumerate(factors):
        columns = jnp.where(spot == n, factor, columns)
    columns = columns.T
    v_zero, v_one = const_value[0:1, :].astype(F32), const_value[1:2, :].astype(F32)
    out = res + columns[:, 0:1] * act + columns[:, 1:2] * v_zero + columns[:, 2:3] * v_one
    d_act = columns[:, 0:1] * dy
    met = jnp.where(lane == 0, jnp.sum(dy * act, axis=1, keepdims=True), 0.0)
    met = jnp.where(lane == 1, jnp.sum(dy * v_zero, axis=1, keepdims=True), met)
    met = jnp.where(lane == 2, jnp.sum(dy * v_one, axis=1, keepdims=True), met)
    for k in range(came.shape[0]):
        place = lane_value(slot[...], eids[k]).astype(jnp.int32)
        pick = hot_matrix(place == iota((rows, cap), 1))
        result = dot(pick, came[k, :, :MODEL_WIDTH])
        d_act = d_act + dot(pick, came[k, :, MODEL_WIDTH:])
        met = jnp.where(lane == 3 + k, jnp.sum(dy * result, axis=1, keepdims=True), met)
        out = out + columns[:, 3 + k : 4 + k] * result
    out_s[...] = out.astype(BF16)
    met = met.T
    along_act, along_zero, along_one = met[0:1], met[1:2], met[2:3]
    d_gate = jnp.zeros((CHOICE_ROWS, rows), F32)
    for k in range(came.shape[0]):
        d_gate = jnp.where(top == eids[k], met[3 + k : 4 + k], d_gate)
    d_gate = jnp.where(top == experts + 1, has_copy * along_act, d_gate)
    d_gate = jnp.where(top == experts + 2, has_zero * (a00 * along_act + a01 * along_zero), d_gate)
    d_gate = jnp.where(top == experts + 3, has_one * (a10 * along_act + a11 * along_one), d_gate)
    d_logit = prob * (d_gate - jnp.sum(prob * d_gate, axis=0, keepdims=True))
    tail = iota((8, rows), 0)
    d_pair = jnp.zeros((8, rows), F32)
    for n, (g_val, left, right, along) in enumerate(
        ((g_zero, a00, a01, along_zero), (g_one, a10, a11, along_one))
    ):
        da_left, da_right = g_val * along_act, g_val * along
        level = left * da_left + right * da_right
        d_pair = jnp.where(tail == 2 * n, left * (da_left - level), d_pair)
        d_pair = jnp.where(tail == 2 * n + 1, right * (da_right - level), d_pair)
    mix = jnp.concatenate(
        [d_logit, jnp.zeros((CONST_LANE - CHOICE_ROWS, rows), F32), d_pair,
         jnp.zeros((LANES - CONST_LANE - 8, rows), F32)],
        axis=0,
    ).T
    d_logits[...] = mix
    mix_hi = mix.astype(BF16)
    mix_lo = (mix - mix_hi.astype(F32)).astype(BF16)
    d_act = d_act + (dot(mix_hi, router[...]) + dot(mix_lo, router[...]))
    scale = lax.rsqrt(jnp.mean(res * res, axis=-1, keepdims=True) + EPSILON)
    weighted = d_act * gain[...].astype(F32)
    d_res = dy + (
        scale * weighted
        - res * (scale * scale * scale) * jnp.mean(res * weighted, axis=-1, keepdims=True)
    )
    d_resid[...] = d_res
    d_attn = d_res.astype(BF16)
    dlow = (dot_nt(d_attn, b_out[...]) * mask[...].astype(F32)).astype(BF16)
    gb_out[...] += dot_tn(low_out[...], d_attn)
    ga_out[...] += dot_tn(attn_low[...], dlow)
    d_attended[...] = (dot_nt(d_attn, w_out[...]) + dot_nt(dlow, a_out[...])).astype(BF16)


def input_grad_body(
    d_query, d_key, d_value, low_qkv, act_one, mask, hid_s, d_resid, w_qkv, a_in, b_out, gain,
    high, lower, ga_qkv, gb_qkv,
):
    @pl.when(pl.program_id(0) == 0)
    def _():
        ga_qkv[...] = jnp.zeros_like(ga_qkv)
        gb_qkv[...] = jnp.zeros_like(gb_qkv)

    d_low = jnp.zeros((d_query.shape[0], LANES), F32)
    d_act = jnp.zeros((d_query.shape[0], MODEL_WIDTH), F32)
    for part, ref in enumerate((d_query, d_key, d_value)):
        cols = slice(part * MODEL_WIDTH, (part + 1) * MODEL_WIDTH)
        grad = ref[...]
        d_low = d_low + dot_nt(grad, b_out[:, cols])
        d_act = d_act + dot_nt(grad, w_qkv[:, cols])
        gb_qkv[:, cols] += dot_tn(low_qkv[...], grad)
    d_low = (d_low * mask[...].astype(F32)).astype(BF16)
    ga_qkv[...] += dot_tn(act_one[...], d_low)
    d_act = d_act + dot_nt(d_low, a_in[...])
    hid = hid_s[...].astype(F32)
    scale = lax.rsqrt(jnp.mean(hid * hid, axis=-1, keepdims=True) + EPSILON)
    weighted = d_act * gain[...].astype(F32)
    grad_hid = d_resid[...] + (
        scale * weighted
        - hid * (scale * scale * scale) * jnp.mean(hid * weighted, axis=-1, keepdims=True)
    )
    top = grad_hid.astype(BF16)
    high[...] = top
    lower[...] = (grad_hid - top.astype(F32)).astype(BF16)


def to_rows_body(place_col, out_s, d_logits, high, lower, out, grad_hidden, grad_gate):
    rows = out.shape[0]
    tok = out_s.shape[0]
    perm = hot_matrix(place_col[...] == iota((rows, tok), 1))
    out[...] = dot(perm, out_s[...]).astype(BF16)
    grad_hidden[...] = dot(perm, high[...]) + dot(perm, lower[...])
    logits = d_logits[...]
    top = logits.astype(BF16)
    rest = logits - top.astype(F32)
    mid = rest.astype(BF16)
    last = (rest - mid.astype(F32)).astype(BF16)
    grad_gate[...] = dot(perm, top) + (dot(perm, mid) + dot(perm, last))


class PairPlan:
    paired = True

    def __init__(self, dp, ex):
        self.ex = ex

    def expert_ids(self):
        own = lax.axis_index("expert") % 2 + 2 * (lax.axis_index("dp") % 2)
        return own ^ jnp.arange(self.ex, dtype=jnp.int32)


class AxisPlan:
    paired = False

    def __init__(self, dp, ex):
        self.dp, self.ex = dp, ex

    def gather(self, shard):
        return lax.all_gather(shard, "dp", axis=0)

    def expert_ids(self):
        return jnp.arange(self.ex, dtype=jnp.int32)

    def exchange(self, values):
        return lax.all_to_all(values, "expert", split_axis=0, concat_axis=0, tiled=True)

    def reduce(self, sums):
        return lax.psum_scatter(sums, "dp", scatter_dimension=0, tiled=True)[0].astype(F32)

    def reduce_all(self, sums):
        return lax.psum_scatter(
            sums, ("dp", "expert"), scatter_dimension=0, tiled=True
        )[0].astype(F32)


def shards(
    dp_size,
    expert_count,
    hidden_input,
    gate_carryover,
    sequence_length,
    token_stream_place,
    expert_choice_index,
    sequence_adapter,
    attention_gain,
    query_key_weight,
    output_weight,
    adapter_in_query,
    adapter_out_query,
    adapter_in_output,
    adapter_out_output,
    feedfwd_gain,
    router_weight,
    constant_gate,
    constant_value,
    gate_upward_weight,
    down_weight,
    adapter_in_gate,
    adapter_out_gate,
    adapter_in_down,
    adapter_out_down,
    output_gradient,
):
    tok = hidden_input.shape[0]
    width = MODEL_WIDTH
    kinds = expert_count + 4
    devices = dp_size * expert_count
    capacity = 5 * tok // (2 * kinds) // 8 * 8 + 8
    cap = -(-capacity // 16) * 16
    blocks = tok // ROW_BLOCK
    plan = (PairPlan if (dp_size, expert_count) == (8, 4) else AxisPlan)(dp_size, expert_count)

    a_rows, b_rows = query_key_weight.shape[0], adapter_out_query.shape[0]
    gu_rows, up_rows, dn_rows = (
        gate_upward_weight.shape[1], adapter_out_gate.shape[1], down_weight.shape[1],
    )
    gains = jnp.stack([attention_gain, feedfwd_gain])
    gain_one, gain_two = gains[0:1], gains[1:2]
    sent_width = 2 * width + LANES
    full = whole
    hbm = pl.BlockSpec(memory_space=pl.ANY)
    vmem = pl.BlockSpec(memory_space=pltpu.VMEM)
    pairs = HEAD_COUNT // 2
    lse_rows = -(-HEAD_COUNT // 8) * 8
    smem = pl.BlockSpec(memory_space=pltpu.SMEM)
    eids = plan.expert_ids()
    if plan.paired:
        shapes = [
            sds((tok, width), BF16), sds((tok, width), BF16), sds((tok, LANES), F32),
            sds((tok, width), BF16), sds((tok, LANES), BF16), sds((tok, LANES), BF16),
            sds((1, tok), jnp.int32), sds((tok, LANES), F32), sds((tok, LANES), F32),
            sds((LANES, width), BF16),
            sds((tok, width), BF16), sds((tok, width), BF16), sds((tok, width), BF16),
            sds((width, 3 * width), BF16), sds((width, LANES), BF16), sds((LANES, 3 * width), BF16),
            sds((width, width), BF16), sds((width, LANES), BF16), sds((LANES, width), BF16),
            sds((tok, width), BF16), sds((lse_rows, tok), F32), sds((tok, LANES), BF16),
            sds((tok, width), F32), sds((tok, width), BF16), sds((tok, LANES), F32),
            sds((tok, LANES), F32),
        ]
        shard_rows = -(-(a_rows + b_rows) // 16) * 16
        packed = [
            (gu_rows + up_rows, 2 * FEEDFWD_WIDTH), (dn_rows + up_rows, width),
            (gu_rows + dn_rows, LANES),
        ]
        row_shape = (expert_count, cap, 2 * width)
        kinds_shape = (expert_count, 16, -(-cap // LANES) * LANES)
        (
            hid_s, dy_s, small_s, act_one, low_qkv, mask, starts, cosine, sine, router,
            query, key, value, w_qkv, a_qkv, b_qkv, w_out, a_out, b_out,
            attn_low, lse, low_out, resid, act_two, gate, slot,
            wide, mid, thin, came, last_sent, came_kinds,
        ) = pl.pallas_call(
            functools.partial(pair_front_body, kinds, a_rows, b_rows),
            in_specs=[smem] * 2 + [vmem] * 14 + [hbm] * 6,
            out_specs=[hbm] * (FRONT_KEPT + 6),
            out_shape=shapes
            + [sds((dp_size,) + shape, BF16) for shape in packed]
            + [sds(row_shape, BF16), sds(row_shape[1:], BF16), sds(kinds_shape, BF16)],
            scratch_shapes=[pltpu.VMEM(s.shape, s.dtype) for s in shapes]
            + [
                pltpu.VMEM((devices, shard_rows, 3 * width + LANES), BF16),
                pltpu.VMEM((devices, shard_rows, width + LANES), BF16),
                *[pltpu.VMEM(shape, BF16) for shape in packed],
                pltpu.VMEM((3,) + row_shape[1:], BF16),
                pltpu.VMEM(kinds_shape, BF16),
                pltpu.VMEM((LANES, tok), F32),
                pltpu.SemaphoreType.DMA((2, 35)), pltpu.SemaphoreType.DMA((2, 35)),
                pltpu.SemaphoreType.DMA((2, 6)),
                pltpu.SemaphoreType.DMA((4, 8)), pltpu.SemaphoreType.DMA((4, 8)),
                pltpu.SemaphoreType.DMA((FRONT_KEPT,)), pltpu.SemaphoreType.DMA((6,)),
                pltpu.SemaphoreType.DMA((9,)), pltpu.SemaphoreType.DMA((7,)),
            ],
            compiler_params=pltpu.CompilerParams(
                vmem_limit_bytes=VMEM_BYTES, collective_id=4, has_side_effects=True
            ),
            name="pair_front",
        )(sequence_length, sequence_adapter, token_stream_place, hidden_input, output_gradient,
          gate_carryover.T, expert_choice_index.T, gains, router_weight.T,
          constant_gate.T,
          query_key_weight, output_weight, adapter_in_query, adapter_in_output, adapter_out_query,
          adapter_out_output, gate_upward_weight, adapter_out_gate, down_weight, adapter_out_down,
          adapter_in_gate, adapter_in_down)
        place = token_stream_place[0]
    else:
        pad_rows = -(a_rows + b_rows) % 16

        def pack(weight, adapter_in, adapter_out):
            lower = jnp.pad(adapter_out, ((0, pad_rows), (0, LANES)))
            return jnp.concatenate([jnp.concatenate([weight, adapter_in], axis=1), lower], axis=0)

        own_qkv = pack(query_key_weight, adapter_in_query, adapter_out_query)
        own_out = pack(output_weight, adapter_in_output, adapter_out_output)
        own_wide = jnp.concatenate([gate_upward_weight[0], adapter_out_gate[0]], axis=0)
        own_mid = jnp.concatenate([down_weight[0], adapter_out_down[0]], axis=0)
        own_thin = jnp.concatenate([adapter_in_gate[0], adapter_in_down[0]], axis=0)

        place = token_stream_place[0]
        ends = jnp.cumsum(sequence_length[0])
        begins = ends - sequence_length[0]
        stream = jnp.arange(tok, dtype=jnp.int32)
        seg = jnp.sum((stream[:, None] >= ends[None, :]).astype(jnp.int32), axis=1)
        seg_hot = seg[:, None] == jnp.arange(ends.shape[0], dtype=jnp.int32)[None, :]
        start = jnp.sum(jnp.where(seg_hot, begins[None, :], 0), axis=1)
        adapter = jnp.sum(jnp.where(seg_hot, sequence_adapter[0][None, :], 0), axis=1)
        half = HEAD_DIM // 2
        freq = jnp.exp(jnp.arange(half, dtype=F32) * (-math.log(10000.0) / half))
        angle = (stream - start).astype(F32)[:, None] * freq[None, :]
        cos, sin = jnp.cos(angle), jnp.sin(angle)
        cosine = jnp.concatenate([cos, cos, cos, cos], axis=1)
        sine = jnp.concatenate([-sin, sin, -sin, sin], axis=1)
        starts = start[None, :]
        mask = (jnp.arange(LANES)[None, :] // ADAPTER_RANK == adapter[:, None]).astype(BF16)
        top, middle, last = split_three(gate_carryover)
        gap = jnp.zeros((tok, 16 - kinds), BF16)
        small = jnp.concatenate(
            [top, gap, middle, gap, last, gap, expert_choice_index.astype(BF16),
             jnp.zeros((tok, LANES - CHOICE_LANE - 2), BF16)],
            axis=1,
        )
        router = jnp.concatenate(
            [router_weight.T, jnp.zeros((CONST_LANE - kinds, width), BF16), constant_gate.T,
             jnp.zeros((LANES - CONST_LANE - 4, width), BF16)],
            axis=0,
        )

        all_qkv = lax.all_gather(own_qkv, ("dp", "expert"), axis=0)
        all_out = lax.all_gather(own_out, ("dp", "expert"), axis=0)
        upper = slice(a_rows, a_rows + b_rows)
        w_qkv = all_qkv[:, :a_rows, : 3 * width].reshape(width, 3 * width)
        a_qkv = all_qkv[:, :a_rows, 3 * width :].reshape(width, LANES)
        b_qkv = all_qkv[:, upper, : 3 * width].reshape(LANES, 3 * width)
        w_out = all_out[:, :a_rows, :width].reshape(width, width)
        a_out = all_out[:, :a_rows, width:].reshape(width, LANES)
        b_out = all_out[:, upper, :width].reshape(LANES, width)
        wide, mid, thin = (plan.gather(w) for w in (own_wide, own_mid, own_thin))
        hid_s, dy_s, small_s, act_one, low_qkv, query, key, value = call(
            proj_in_body,
            (blocks,),
            [full((1, tok)), full((tok, width)), full((tok, width)), full((tok, LANES)),
             row_spec(LANES), row_spec(LANES), row_spec(LANES), full((1, width)),
             full((width, 3 * width)), full((width, LANES)), full((LANES, 3 * width))],
            [row_spec(width), row_spec(width), row_spec(LANES), row_spec(width), row_spec(LANES),
             row_spec(width), row_spec(width), row_spec(width)],
            [sds((tok, width), BF16), sds((tok, width), BF16), sds((tok, LANES), F32),
             sds((tok, width), BF16), sds((tok, LANES), BF16), sds((tok, width), BF16),
             sds((tok, width), BF16), sds((tok, width), BF16)],
            name="proj_in",
        )(place[None, :], hidden_input, output_gradient, small, cosine, sine, mask, gain_one,
          w_qkv, a_qkv, b_qkv)

        attn_low, lse = call(
            attention_fwd_body,
            (pairs,),
            [col_spec(tok)] * 3 + [full((1, tok))],
            [col_spec(tok), full((lse_rows, tok))],
            [sds((tok, width), BF16), sds((lse_rows, tok), F32)],
            name="attention_fwd",
        )(query, key, value, starts)

        low_out, resid, act_two, gate = call(
            functools.partial(post_attn_body, kinds),
            (blocks,),
            [row_spec(width), row_spec(width), row_spec(LANES), row_spec(LANES), full((width, width)),
             full((width, LANES)), full((LANES, width)), full((LANES, width)), full((1, width))],
            [row_spec(LANES), row_spec(width), row_spec(width), row_spec(LANES)],
            [sds((tok, LANES), BF16), sds((tok, width), F32), sds((tok, width), BF16),
             sds((tok, LANES), F32)],
            name="post_attn",
        )(attn_low, hid_s, mask, small_s, w_out, a_out, b_out, router, gain_two)

        slot, sent = call(
            functools.partial(dispatch_body, expert_count),
            (expert_count,),
            [smem, full((tok, LANES)), full((tok, LANES)), full((tok, width)), full((tok, width)),
             full((tok, LANES))],
            [full((tok, LANES)), pl.BlockSpec((1, cap, sent_width), lambda i: (i, 0, 0))],
            [sds((tok, LANES), F32), sds((expert_count, cap, sent_width), BF16)],
            scratch=[pltpu.VMEM((LANES, tok), F32)],
            name="dispatch",
        )(eids, small_s, gate, act_two, dy_s, mask)

    grad_shapes = [
        sds((width, LANES), F32), sds((LANES, 2 * FEEDFWD_WIDTH), F32),
        sds((FEEDFWD_WIDTH, LANES), F32), sds((LANES, width), F32),
    ]
    accumulators = [
        pltpu.VMEM((cap, width), F32), pltpu.VMEM((cap, width), F32),
        pltpu.VMEM((cap, LANES), F32), pltpu.VMEM((cap, LANES), F32),
    ]
    if plan.paired:
        returned, ga_gu, gb_gu, ga_dn, gb_dn = pl.pallas_call(
            pair_ffn_body,
            in_specs=[hbm] * 2 + [vmem] + [hbm] * 3,
            out_specs=[hbm] + [vmem] * 4,
            out_shape=[sds((expert_count, cap, 2 * width), BF16)]
            + [sds(g.shape, BF16) for g in grad_shapes],
            scratch_shapes=[
                pltpu.VMEM((expert_count, cap, 2 * width), BF16),
                pltpu.VMEM((expert_count, cap, 2 * width), BF16),
                *[pltpu.VMEM(g.shape, F32) for g in grad_shapes],
                pltpu.VMEM((width, 2 * FEEDFWD_WIDTH), BF16), pltpu.VMEM((FEEDFWD_WIDTH, width), BF16),
                pltpu.VMEM((width, LANES), BF16), pltpu.VMEM((LANES, 2 * FEEDFWD_WIDTH), BF16),
                pltpu.VMEM((FEEDFWD_WIDTH, LANES), BF16), pltpu.VMEM((LANES, width), BF16),
                *accumulators,
                pltpu.SemaphoreType.DMA((6,)),
                *[pltpu.SemaphoreType.DMA((expert_count,)) for _ in range(3)],
                pltpu.SemaphoreType.DMA((2,)),
            ],
            compiler_params=pltpu.CompilerParams(
                vmem_limit_bytes=VMEM_BYTES, collective_id=1, has_side_effects=True
            ),
            name="pair_ffn",
        )(came, last_sent, came_kinds, wide, mid, thin)
    else:
        w_gu = wide[:, :gu_rows].reshape(width, 2 * FEEDFWD_WIDTH)
        b_gu = wide[:, gu_rows:].reshape(LANES, 2 * FEEDFWD_WIDTH)
        w_dn = mid[:, :dn_rows].reshape(FEEDFWD_WIDTH, width)
        b_dn = mid[:, dn_rows:].reshape(LANES, width)
        a_gu = thin[:, :gu_rows].reshape(width, LANES)
        a_dn = thin[:, gu_rows:].reshape(FEEDFWD_WIDTH, LANES)
        came = plan.exchange(sent)
        back, ga_gu, gb_gu, ga_dn, gb_dn = call(
            ffn_body,
            (expert_count,),
            [pl.BlockSpec((1, cap, sent_width), lambda i: (i, 0, 0)),
             full((width, 2 * FEEDFWD_WIDTH)), full((FEEDFWD_WIDTH, width)), full((width, LANES)),
             full((LANES, 2 * FEEDFWD_WIDTH)), full((FEEDFWD_WIDTH, LANES)), full((LANES, width))],
            [pl.BlockSpec((1, cap, 2 * width), lambda i: (i, 0, 0)), full((width, LANES)),
             full((LANES, 2 * FEEDFWD_WIDTH)), full((FEEDFWD_WIDTH, LANES)), full((LANES, width))],
            [sds((expert_count, cap, 2 * width), BF16)] + grad_shapes,
            scratch=accumulators,
            name="ffn",
        )(came, w_gu, w_dn, a_gu, b_gu, a_dn, b_dn)
        returned = plan.exchange(back)

    out_s, d_resid, d_attended, d_logits, ga_out, gb_out = call(
        functools.partial(combine_body, expert_count, kinds),
        (tok // ROW_BLOCK,),
        [smem, row_spec(width, ROW_BLOCK), row_spec(width, ROW_BLOCK), row_spec(width, ROW_BLOCK), row_spec(LANES, ROW_BLOCK), row_spec(LANES, ROW_BLOCK),
         row_spec(LANES, ROW_BLOCK), row_spec(LANES, ROW_BLOCK), row_spec(width, ROW_BLOCK), row_spec(LANES, ROW_BLOCK),
         full((expert_count, cap, 2 * width)), full((width, width)), full((width, LANES)),
         full((LANES, width)), full((LANES, width)), full((2, width)), full((1, width))],
        [row_spec(width, ROW_BLOCK), row_spec(width, ROW_BLOCK), row_spec(width, ROW_BLOCK), row_spec(LANES, ROW_BLOCK), full((width, LANES)),
         full((LANES, width))],
        [sds((tok, width), BF16), sds((tok, width), F32), sds((tok, width), BF16),
         sds((tok, LANES), F32), sds((width, LANES), F32), sds((LANES, width), F32)],
        name="combine",
    )(eids, resid, act_two, dy_s, gate, slot, small_s, low_out, attn_low, mask, returned,
      w_out, a_out, b_out, router, constant_value, gain_two)

    if plan.paired:
        flow = dict(vmem_limit_bytes=VMEM_BYTES, has_side_effects=True)
        own_shapes = [
            sds((gu_rows, LANES), F32), sds((up_rows, 2 * FEEDFWD_WIDTH), F32),
            sds((dn_rows, LANES), F32), sds((up_rows, width), F32),
        ]
        plane_shapes = [
            sds((width // dp_size, LANES), F32), sds((LANES // dp_size, width), F32),
        ]
        d_query, d_key, d_value, *expert_owned, plane_ga, plane_gb = pl.pallas_call(
            pair_attention_bwd_body,
            grid=(pairs,),
            in_specs=[col_spec(tok)] * 5
            + [full((lse_rows, tok)), full((1, tok)), full((tok, LANES)), full((tok, LANES)),
               full((width, LANES)), full((LANES, width))]
            + [hbm] * 4,
            out_specs=[col_spec(tok)] * 3 + [full(s.shape) for s in own_shapes + plane_shapes],
            out_shape=[sds((tok, width), BF16)] * 3 + own_shapes + plane_shapes,
            scratch_shapes=[pltpu.VMEM((tok, LANES), F32), pltpu.VMEM((tok, LANES), F32)]
            + [pltpu.VMEM((2 * s.shape[0], s.shape[1]), BF16) for s in own_shapes]
            + [pltpu.VMEM((3, 2 * s.shape[0], s.shape[1]), BF16) for s in own_shapes]
            + [pltpu.VMEM((2,) + s.shape, BF16) for s in own_shapes * 2]
            + [pltpu.VMEM((width, LANES), BF16), pltpu.VMEM((LANES, width), BF16)]
            + [pltpu.VMEM((dp_size - 1,) + s.shape, BF16) for s in plane_shapes]
            + [pltpu.SemaphoreType.DMA((4,)), pltpu.SemaphoreType.DMA((4, 3)),
               pltpu.SemaphoreType.DMA((4, 3)), pltpu.SemaphoreType.DMA((4, 2)),
               pltpu.SemaphoreType.DMA((4, 2)), pltpu.SemaphoreType.DMA((2, dp_size)),
               pltpu.SemaphoreType.DMA((2, dp_size))],
            compiler_params=pltpu.CompilerParams(collective_id=2, **flow),
            name="pair_attention_bwd",
        )(query, key, value, d_attended, attn_low, lse, starts, cosine, sine, ga_out, gb_out,
          ga_gu, gb_gu, ga_dn, gb_dn)
        sum_shapes = [(width, LANES), (LANES, 3 * width)]
        got_shapes = [(dp_size - 1, a // dp_size, b) for a, b in sum_shapes]
        thin_rows = -(-a_rows // 16) * 16
        tail_shapes = [
            sds((tok, width), BF16), sds((tok, width), F32), sds((tok, LANES), F32),
            sds((a_rows, LANES), F32), sds((b_rows, 3 * width), F32),
            sds((a_rows, LANES), F32), sds((b_rows, width), F32),
        ]
        tail = pl.pallas_call(
            pair_tail_body,
            in_specs=[vmem] * 8 + [hbm] * 9,
            out_specs=[vmem] * 7,
            out_shape=tail_shapes,
            scratch_shapes=[
                *[pltpu.VMEM((tok, width), BF16) for _ in range(3)],
                pltpu.VMEM((tok, LANES), BF16), pltpu.VMEM((tok, width), BF16),
                pltpu.VMEM((tok, width), BF16), pltpu.VMEM((tok, width), F32),
                pltpu.VMEM((width, 3 * width), BF16), pltpu.VMEM((tok, width), BF16),
                pltpu.VMEM((tok, LANES), F32),
                pltpu.VMEM((tok, width), BF16), pltpu.VMEM((tok, width), BF16),
                pltpu.VMEM((tok, LANES), BF16),
                pltpu.VMEM((width, LANES), F32), pltpu.VMEM((LANES, 3 * width), F32),
                *[pltpu.VMEM(shape, BF16) for shape in sum_shapes + got_shapes],
                pltpu.VMEM((expert_count, thin_rows, 2 * LANES), BF16),
                pltpu.VMEM((expert_count, 4 * b_rows, width), BF16),
                pltpu.VMEM((expert_count - 1, thin_rows, 2 * LANES), BF16),
                pltpu.VMEM((expert_count - 1, 4 * b_rows, width), BF16),
                pltpu.SemaphoreType.DMA((9,)),
                pltpu.SemaphoreType.DMA((2, dp_size - 1)), pltpu.SemaphoreType.DMA((2, dp_size - 1)),
                pltpu.SemaphoreType.DMA((2, expert_count - 1)),
                pltpu.SemaphoreType.DMA((2, expert_count - 1)),
            ],
            compiler_params=pltpu.CompilerParams(collective_id=3, **flow),
            name="pair_tail",
        )(token_stream_place, mask, a_qkv, b_qkv, gain_one, plane_ga, plane_gb, d_logits,
          d_query, d_key, d_value, low_qkv, act_one, hid_s, d_resid, w_qkv, out_s)
        output, grad_hidden, grad_gate, *attn_owned = tail
        small_owned = [*attn_owned, *expert_owned]
        small_specs = [full(v.shape) for v in small_owned]
        grad_gate, output, grad_hidden, *owned = call(
            settle_body,
            (blocks,),
            [row_spec(LANES), row_spec(width), row_spec(width)] + small_specs,
            [pl.BlockSpec((kinds, ROW_BLOCK), lambda i: (0, i)), row_spec(width), row_spec(width)]
            + small_specs,
            [sds((kinds, tok), F32), sds((tok, width), BF16), sds((tok, width), F32)]
            + [sds(v.shape, F32) for v in small_owned],
            name="settle",
        )(grad_gate, output, grad_hidden, *small_owned)
        attn_owned, expert_owned = owned[:4], owned[4:]
        grad_gate = grad_gate.T
        return (
            output, grad_hidden, grad_gate[:, :kinds], *attn_owned,
            *[expert_owned[i][None] for i in range(4)],
        )

    owned_wide = plan.reduce(
        jnp.concatenate([gb_gu, gb_dn], axis=1).astype(BF16).reshape(dp_size, up_rows, -1)
    )
    owned_thin = plan.reduce(
        jnp.concatenate(
            [ga_gu.reshape(dp_size, gu_rows, LANES), ga_dn.reshape(dp_size, dn_rows, LANES)], axis=1
        ).astype(BF16)
    )

    d_query, d_key, d_value = call(
        attention_bwd_body,
        (pairs,),
        [col_spec(tok)] * 5
        + [full((lse_rows, tok)), full((1, tok)), full((tok, LANES)), full((tok, LANES))],
        [col_spec(tok)] * 3,
        [sds((tok, width), BF16)] * 3,
        scratch=[pltpu.VMEM((tok, LANES), F32), pltpu.VMEM((tok, LANES), F32)],
        name="attention_bwd",
    )(query, key, value, d_attended, attn_low, lse, starts, cosine, sine)

    high, lower, ga_qkv, gb_qkv = call(
        input_grad_body,
        (blocks,),
        [row_spec(width)] * 3 + [row_spec(LANES), row_spec(width), row_spec(LANES), row_spec(width),
         row_spec(width), full((width, 3 * width)), full((width, LANES)), full((LANES, 3 * width)),
         full((1, width))],
        [row_spec(width), row_spec(width), full((width, LANES)), full((LANES, 3 * width))],
        [sds((tok, width), BF16), sds((tok, width), BF16), sds((width, LANES), F32),
         sds((LANES, 3 * width), F32)],
        name="input_grad",
    )(d_query, d_key, d_value, low_qkv, act_one, mask, hid_s, d_resid, w_qkv, a_qkv, b_qkv,
      gain_one)

    owned = plan.reduce_all(
        jnp.concatenate(
            [
                ga_qkv.reshape(devices, b_rows, -1),
                ga_out.reshape(devices, b_rows, -1),
                gb_qkv.reshape(devices, b_rows, -1),
                gb_out.reshape(devices, b_rows, -1),
            ],
            axis=2,
        ).astype(BF16)
    )

    output, grad_hidden, grad_gate = call(
        to_rows_body,
        (blocks,),
        [row_spec(1), full((tok, width)), full((tok, LANES)), full((tok, width)),
         full((tok, width))],
        [row_spec(width), row_spec(width), row_spec(LANES)],
        [sds((tok, width), BF16), sds((tok, width), F32), sds((tok, LANES), F32)],
        name="to_rows",
    )(place[:, None], out_s, d_logits, high, lower)

    return (
        output,
        grad_hidden,
        grad_gate[:, :kinds],
        owned[:, :width].reshape(a_rows, LANES),
        owned[:, 2 * width : 5 * width],
        owned[:, width : 2 * width].reshape(a_rows, LANES),
        owned[:, 5 * width :],
        owned_thin[None, :gu_rows],
        owned_wide[None, :, : 2 * FEEDFWD_WIDTH],
        owned_thin[None, gu_rows:],
        owned_wide[None, :, 2 * FEEDFWD_WIDTH :],
    )


def solution(mesh):
    rows = P(("dp", "expert"), None)
    expert_rows = P("expert", "dp", None)
    in_specs = (
        (rows,) * 6 + (P(),) + (rows,) * 6 + (P(),) * 4 + (expert_rows,) * 6 + (rows,)
    )
    out_specs = (rows,) * 7 + (expert_rows,) * 4
    body = functools.partial(shards, mesh.shape["dp"], mesh.shape["expert"])
    return jax.shard_map(body, mesh=mesh, in_specs=in_specs, out_specs=out_specs, check_vma=False)
```
